32 devices in a mesh: dp: 8 (over y, x, core), blk: 4 (over z).
Axes of the slice: x: 2, y: 2, z: 4, core: 2. Of those that a mesh axis runs over, the one named last changes fastest.
Arguments:
- tokens: bfloat16 [16, 16, 48, 768], P('dp', 'blk'), may hold values from -6 to 6
- frame_counts: int32 [16], P('dp'), may hold values from 4 to 16, as said below
- slot_mask: int32 [16, 16, 48], P('dp'), may hold values 0 or 1
- norm1_gain: float32 [768], replicated, may hold values from 0.5 to 1.5
- norm1_bias: float32 [768], replicated, may hold values from -2 to 2
- w_qkv: bfloat16 [768, 2304], replicated, may hold values from -0.21875 to 0.21875
- q_bias: float32 [768], replicated, may hold values from -2 to 2
- v_bias: float32 [768], replicated, may hold values from -2 to 2
- w_out: bfloat16 [768, 768], replicated, may hold values from -1.75 to 1.75
- out_bias: float32 [768], replicated, may hold values from -2 to 2
- norm2_gain: float32 [768], replicated, may hold values from 0.5 to 1.5
- norm2_bias: float32 [768], replicated, may hold values from -2 to 2
- w_up: bfloat16 [768, 3072], replicated, may hold values from -0.21875 to 0.21875
- up_bias: float32 [3072], replicated, may hold values from -2 to 2
- w_down: bfloat16 [3072, 768], replicated, may hold values from -0.109375 to 0.109375
- down_bias: float32 [768], replicated, may hold values from -2 to 2
- norm3_gain: float32 [768], replicated, may hold values from 0.5 to 1.5
- norm3_bias: float32 [768], replicated, may hold values from -2 to 2
- w_align: bfloat16 [768, 1024], replicated, may hold values from -0.21875 to 0.21875
- align_bias: float32 [1024], replicated, may hold values from -2 to 2
- cot_block: bfloat16 [16, 16, 48, 768], P('dp', 'blk'), may hold values from -6 to 6
- cot_align: bfloat16 [16, 16, 48, 1024], P('dp', 'blk'), may hold values from -6 to 6
Outputs:
- block_out: bfloat16 [16, 16, 48, 768], P('dp', 'blk')
- aligned: bfloat16 [16, 16, 48, 1024], P('dp', 'blk')
- grad_tokens: bfloat16 [16, 16, 48, 768], P('dp', 'blk')
- grad_norm1_gain: float32 [768], replicated
- grad_norm1_bias: float32 [768], replicated
- grad_w_qkv: float32 [768, 2304], P('dp')
- grad_q_bias: float32 [768], replicated
- grad_v_bias: float32 [768], replicated
- grad_w_out: float32 [768, 768], P('dp')
- grad_out_bias: float32 [768], replicated
- grad_norm2_gain: float32 [768], replicated
- grad_norm2_bias: float32 [768], replicated
- grad_w_up: float32 [768, 3072], P('dp')
- grad_up_bias: float32 [3072], replicated
- grad_w_down: float32 [3072, 768], P('dp')
- grad_down_bias: float32 [768], replicated
- grad_norm3_gain: float32 [768], replicated
- grad_norm3_bias: float32 [768], replicated
- grad_w_align: float32 [768, 1024], P('dp')
- grad_align_bias: float32 [1024], replicated
The draws below stay inside these ranges and needn't reach their ends.
Inputs may be any that keep to these rules, and one draw needn't show every extreme that they name: `frame_counts`: each clip has 4, 8 or 16 real frames; in each aligned block of 2 clips (the clips of one index of dp) at least one has 16.
All inputs are finite; a program needn't handle non-finite values. No bound on the sum of `slot_mask` on one device may be relied on, other than what follows from the above.
Results may differ from the reference program's by a relative error of at most 0.013.
Values may be sent and summed in bfloat16 or wider, within the bound.
A program may use at most 192 MiB of HBM per device.

```python
import math
import jax
import jax.numpy as jnp
from jax import lax

D = 768
HEADS = 12
HEAD = 64
FF = 3072
ALIGN = 1024
FRAMES = 16
SLOTS = 48
CLIPS_DEV = 2
CLIPS = 16


def draw_frame_counts(key, part):
    key = jax.random.fold_in(key, 7)
    key_one, key_two = jax.random.split(key)
    doubling = jax.random.randint(key_one, (CLIPS,), 0, 3).astype(jnp.int32)
    count_base = jnp.full((CLIPS,), FRAMES // 4, jnp.int32)
    frame_total = jnp.left_shift(count_base, doubling)
    chosen = jax.random.randint(key_two, (CLIPS // CLIPS_DEV,), 0, CLIPS_DEV).astype(jnp.int32)
    position = jnp.arange(CLIPS, dtype=jnp.int32) % CLIPS_DEV
    longest = position == jnp.repeat(chosen, CLIPS_DEV, total_repeat_length=CLIPS)
    return jnp.where(longest, FRAMES, frame_total).astype(jnp.int32)


def with_ends(array, key, low, top_value):
    spot = [jax.random.randint(jax.random.fold_in(key, axis), (), 0, length) for axis, length in enumerate(array.shape)]
    widest = array.shape.index(max(array.shape))
    neighbour = spot[:widest] + [(spot[widest] + 1) % array.shape[widest]] + spot[widest + 1:]
    return array.at[tuple(spot)].set(low).at[tuple(neighbour)].set(top_value)


def level_of(own_key, extent, pieces, low, top_value):
    level, own = 1.0, jax.random.fold_in(own_key, 6)
    for dim, blocks in pieces:
        draws = jnp.exp(jax.random.uniform(jax.random.fold_in(own, dim), (blocks,), jnp.float32, low / len(pieces), top_value / len(pieces)))
        level = level * jnp.repeat(draws, extent[dim] // blocks).reshape([-1 if axis == dim else 1 for axis in range(len(extent))])
    return level


def bell_draw(own_key, extent, scale, bound, cuts=(), kind=jnp.bfloat16):
    array = scale * jax.random.normal(own_key, extent, jnp.float32)
    if cuts:
        array = array * level_of(own_key, extent, cuts, -0.22, 0.18)
    return jnp.clip(array, -bound, bound).astype(kind)


def setup_inputs(seed: int = 0) -> dict:
    key_list = jax.random.split(jax.random.key(seed), 23)
    tokens = bell_draw(key_list[0], (CLIPS, FRAMES, SLOTS, D), 1.0, 6.0, ((0, 8), (1, 4)))
    frame_counts = draw_frame_counts(jax.random.fold_in(key_list[22], 71), 0)
    slot_mask = with_ends((jax.random.randint(key_list[2], (CLIPS, FRAMES, SLOTS), 0, 50) < 41).astype(jnp.int32), jax.random.fold_in(key_list[2], 1), 0, 1)
    norm1_gain = jnp.clip(1.0 + 0.1 * jax.random.normal(key_list[3], (D,), jnp.float32), 0.5, 1.5)
    norm1_bias = bell_draw(key_list[4], (D,), 0.3, 2.0, (), jnp.float32)
    w_qkv = bell_draw(key_list[5], (D, 3 * D), D ** -0.5, 0.21875)
    q_bias = bell_draw(key_list[6], (D,), 0.3, 2.0, (), jnp.float32)
    v_bias = bell_draw(key_list[7], (D,), 0.3, 2.0, (), jnp.float32)
    w_out = bell_draw(key_list[8], (D, D), (max(1, D // 64)) ** -0.5, 1.75)
    out_bias = bell_draw(key_list[9], (D,), 0.3, 2.0, (), jnp.float32)
    norm2_gain = jnp.clip(1.0 + 0.1 * jax.random.normal(key_list[10], (D,), jnp.float32), 0.5, 1.5)
    norm2_bias = bell_draw(key_list[11], (D,), 0.3, 2.0, (), jnp.float32)
    w_up = bell_draw(key_list[12], (D, FF), D ** -0.5, 0.21875)
    up_bias = bell_draw(key_list[13], (FF,), 0.3, 2.0, (), jnp.float32)
    w_down = bell_draw(key_list[14], (FF, D), FF ** -0.5, 0.109375)
    down_bias = bell_draw(key_list[15], (D,), 0.3, 2.0, (), jnp.float32)
    norm3_gain = jnp.clip(1.0 + 0.1 * jax.random.normal(key_list[16], (D,), jnp.float32), 0.5, 1.5)
    norm3_bias = bell_draw(key_list[17], (D,), 0.3, 2.0, (), jnp.float32)
    w_align = bell_draw(key_list[18], (D, ALIGN), D ** -0.5, 0.21875)
    align_bias = bell_draw(key_list[19], (ALIGN,), 0.3, 2.0, (), jnp.float32)
    cot_block = bell_draw(key_list[20], (CLIPS, FRAMES, SLOTS, D), 1.0, 6.0, ((0, 8), (1, 4)))
    cot_align = bell_draw(key_list[21], (CLIPS, FRAMES, SLOTS, ALIGN), 1.0, 6.0, ((0, 8), (1, 4)))
    return dict(tokens=tokens, frame_counts=frame_counts, slot_mask=slot_mask, norm1_gain=norm1_gain, norm1_bias=norm1_bias, w_qkv=w_qkv, q_bias=q_bias, v_bias=v_bias, w_out=w_out, out_bias=out_bias, norm2_gain=norm2_gain, norm2_bias=norm2_bias, w_up=w_up, up_bias=up_bias, w_down=w_down, down_bias=down_bias, norm3_gain=norm3_gain, norm3_bias=norm3_bias, w_align=w_align, align_bias=align_bias, cot_block=cot_block, cot_align=cot_align)


EPSILON = 1e-06

@jax.custom_vjp
def low(v):
    return lax.optimization_barrier(v.astype(jnp.bfloat16)).astype(jnp.float32)

@jax.custom_vjp
def low_back(v):
    return v

def low_keep(v):
    return (low(v), None)

def low_pass(kept, grad):
    return (grad,)

def back_keep(v):
    return (v, None)

def back_low(kept, grad):
    return (low(grad),)
low.defvjp(low_keep, low_pass)
low_back.defvjp(back_keep, back_low)

def layer_norm(values, gain, shift):
    center = values - lax.optimization_barrier(jnp.mean(values, axis=-1, keepdims=True))
    inverse = lax.rsqrt(lax.optimization_barrier(jnp.mean(center * center, axis=-1, keepdims=True)) + EPSILON)
    return center * inverse * gain + shift

def matmul(left, right):
    return jnp.dot(left, right, precision=lax.Precision.HIGHEST, preferred_element_type=jnp.float32)

def attend_clip(operands):
    queries, keys, values, key_valid = operands
    scale = 1.0 / math.sqrt(queries.shape[-1])
    scores = jnp.einsum('qhd,khd->hqk', queries, keys, precision=lax.Precision.HIGHEST) * scale
    scores = low_back(jnp.where(key_valid[None, None, :], scores, -1e+30))
    top = lax.optimization_barrier(jnp.max(scores, axis=-1, keepdims=True))
    expo = jnp.exp(scores - top)
    probs = low(expo / lax.optimization_barrier(jnp.sum(expo, axis=-1, keepdims=True)))
    return jnp.einsum('hqk,khd->qhd', probs, values, precision=lax.Precision.HIGHEST)

def reference(tokens, frame_counts, slot_mask, norm1_gain, norm1_bias, w_qkv, q_bias, v_bias, w_out, out_bias, norm2_gain, norm2_bias, w_up, up_bias, w_down, down_bias, norm3_gain, norm3_bias, w_align, align_bias, cot_block, cot_align):
    seq_len = FRAMES * SLOTS
    row_count = CLIPS * seq_len
    frame_ids = jnp.arange(FRAMES, dtype=jnp.int32)
    visible_mask = (frame_ids[None, :, None] < frame_counts[:, None, None]) & (slot_mask > 0)
    visible = visible_mask.astype(jnp.float32).reshape(row_count, 1)
    key_valid = visible_mask.reshape(CLIPS, seq_len)
    params = tuple((item.astype(jnp.float32) for item in (norm1_gain, norm1_bias, w_qkv, q_bias, v_bias, w_out, out_bias, norm2_gain, norm2_bias, w_up, up_bias, w_down, down_bias, norm3_gain, norm3_bias, w_align, align_bias)))
    inputs = tokens.astype(jnp.float32).reshape(row_count, D)

    def forward(weights, source):
        gain_one, shift_one, proj_qkv, bias_q, bias_v, proj_out, bias_out, gain_two, shift_two, proj_up, bias_up, proj_down, bias_down, gain_three, shift_three, proj_align, bias_align = weights
        normed1 = low(layer_norm(source, gain_one, shift_one))
        projected = matmul(normed1, proj_qkv)
        queries = low_back(low(projected[:, :D] + bias_q))
        keys = low_back(low(projected[:, D:2 * D]))
        values = low_back(low(projected[:, 2 * D:] + bias_v))
        heads_shape = (CLIPS, seq_len, HEADS, HEAD)
        attended = lax.map(jax.checkpoint(attend_clip), (queries.reshape(heads_shape), keys.reshape(heads_shape), values.reshape(heads_shape), key_valid))
        attended = low_back(low(attended.reshape(row_count, D)))
        mid = source + low_back(matmul(attended, proj_out) + bias_out)
        normed2 = low(layer_norm(mid, gain_two, shift_two))
        hidden = low_back(matmul(normed2, proj_up) + bias_up)
        active = low(jax.nn.gelu(hidden, approximate=False))
        after = mid + low_back(matmul(active, proj_down) + bias_down)
        normed3 = low(layer_norm(after, gain_three, shift_three))
        target = low_back(matmul(normed3, proj_align) + bias_align)
        return (visible * after, visible * target)
    (out_block, out_align), pullback = jax.vjp(forward, params, inputs)
    grad_params, grad_inputs = pullback((cot_block.astype(jnp.float32).reshape(row_count, D), cot_align.astype(jnp.float32).reshape(row_count, ALIGN)))
    return (out_block.astype(jnp.bfloat16).reshape(CLIPS, FRAMES, SLOTS, D), out_align.astype(jnp.bfloat16).reshape(CLIPS, FRAMES, SLOTS, ALIGN), grad_inputs.astype(jnp.bfloat16).reshape(CLIPS, FRAMES, SLOTS, D), grad_params[0], grad_params[1], grad_params[2], grad_params[3], grad_params[4], grad_params[5], grad_params[6], grad_params[7], grad_params[8], grad_params[9], grad_params[10], grad_params[11], grad_params[12], grad_params[13], grad_params[14], grad_params[15], grad_params[16])
```

```python
import math

import jax
import jax.numpy as jnp
from jax import lax
from jax.experimental import pallas as pl
from jax.experimental.pallas import tpu as pltpu
from jax.sharding import PartitionSpec as P

HEADS = 12


EPSILON = 1e-06
SQRT_HALF = 0.7071067811865476
INV_ROOT_TAU = 0.3989422804014327


MESH = pl.DeviceIdType.MESH
GRID = (8, 4)
VECTOR_ROWS = 96
JOBS = (
    (4, 0, 96, 0, 1024),
    (3, 0, 192, 0, 768),
    (3, 192, 192, 0, 768),
    (2, 0, 96, 0, 1536),
    (2, 0, 96, 1536, 1536),
    (1, 0, 96, 0, 768),
    (0, 0, 96, 0, 768),
    (0, 0, 96, 768, 768),
    (0, 0, 96, 1536, 768),
)


def add_into(target, first, second):
    rows = target.shape[-2]
    step = 32

    def body(k, _):
        at = pl.ds(pl.multiple_of(k * step, step), step)
        target[..., at, :] = (
            first[..., at, :].astype(jnp.float32) + second[..., at, :].astype(jnp.float32)
        ).astype(target.dtype)
        return 0

    lax.fori_loop(0, rows // step, body, 0)


def reduce_kernel(*refs):
    count = len(JOBS)
    grads = refs[:5]
    vec_in = refs[5]
    outs = refs[6:11]
    vec_out = refs[11]
    rest = refs[12:]
    own, got0, got1, got2, gotz = (rest[i * count : (i + 1) * count] for i in range(5))
    vec_got, local_sem, send0, recv0, send1, recv1, send2, recv2, sendz, recvz, vsend, vrecv = rest[5 * count :]

    dp = lax.axis_index("dp")
    z = lax.axis_index("blk")
    core = lax.rem(dp, 2)
    x = lax.rem(dp // 2, 2)
    y = dp // 4
    to_core = (dp + 1 - 2 * core, z)
    to_x = (dp + 2 - 4 * x, z)
    to_y = (dp + 4 - 8 * y, z)
    to_z1 = (dp, z + 1 - 2 * lax.rem(z, 2))
    to_z2 = (dp, lax.rem(z + 2, 4))
    to_z3 = (dp, 3 - z)
    is_mid = (z == 1) | (z == 2)
    is_end = (z == 0) | (z == 3)

    barrier = pltpu.get_barrier_semaphore()
    for device in (to_core, to_x, to_y, to_z1, to_z2, to_z3):
        pl.semaphore_signal(barrier, inc=1, device_id=device, device_id_type=MESH)
    pl.semaphore_wait(barrier, 6)

    def remote(src, dst, send, recv, device):
        return pltpu.make_async_remote_copy(
            src_ref=src, dst_ref=dst, send_sem=send, recv_sem=recv, device_id=device, device_id_type=MESH
        )

    def pieces(j):
        matrix, row, rows, column, columns = JOBS[j]
        half = columns // 2
        for h in range(2):
            for chip in range(4):
                cy, cx = chip // 2, chip % 2
                first, second = (cx, cy) if h == 0 else (cy, cx)
                yield h, chip, first, second, pl.ds(row, rows), pl.ds(column + h * half, half)

    def copies0(j):
        matrix = JOBS[j][0]
        for h, chip, first, second, rows, columns in pieces(j):
            yield (
                remote(
                    grads[matrix].at[chip, 1 - core, rows, columns],
                    got0[j].at[h, first, second],
                    send0.at[j, h * 4 + chip],
                    recv0.at[j, h * 4 + chip],
                    to_core,
                ),
                pltpu.make_async_copy(
                    grads[matrix].at[chip, core, rows, columns],
                    own[j].at[h, first, second],
                    local_sem.at[j, h * 4 + chip],
                ),
            )

    def copies1(j):
        yield remote(own[j].at[0, 1 - x], got1[j].at[0], send1.at[j, 0], recv1.at[j, 0], to_x)
        yield remote(own[j].at[1, 1 - y], got1[j].at[1], send1.at[j, 1], recv1.at[j, 1], to_y)

    def copies2(j):
        yield remote(own[j].at[0, x, 1 - y], got2[j].at[0], send2.at[j, 0], recv2.at[j, 0], to_y)
        yield remote(own[j].at[1, y, 1 - x], got2[j].at[1], send2.at[j, 1], recv2.at[j, 1], to_x)

    def shares(j):
        return (own[j].at[0, x, y], own[j].at[1, y, x])

    def copiesz(j, slot, device):
        for h, share in enumerate(shares(j)):
            yield remote(share, gotz[j].at[slot, h], sendz.at[j, slot, h], recvz.at[j, slot, h], device)

    def put_out(j, h, value):
        matrix, row, rows, column, columns = JOBS[j]
        half = columns // 2
        outs[matrix][row : row + rows, column + h * half : column + (h + 1) * half] = value

    def stage(j, number):
        if number == 0:
            for far, near in copies0(j):
                far.start()
                near.start()
        if number == 1:
            for far, near in copies0(j):
                near.wait()
                far.wait()
            add_into(own[j], own[j], got0[j])
            for copy in copies1(j):
                copy.start()
        if number == 2:
            for copy in copies1(j):
                copy.wait()
            add_into(own[j].at[0, x], own[j].at[0, x], got1[j].at[0])
            add_into(own[j].at[1, y], own[j].at[1, y], got1[j].at[1])
            for copy in copies2(j):
                copy.start()
        if number == 3:
            for copy in copies2(j):
                copy.wait()
            for h, share in enumerate(shares(j)):
                add_into(share, share, got2[j].at[h])

            @pl.when(is_end)
            def _():
                for copy in copiesz(j, 0, to_z1):
                    copy.start()
        if number == 4:

            @pl.when(is_mid)
            def _():
                for copy in copiesz(j, 0, to_z1):
                    copy.wait_recv()
                for h, share in enumerate(shares(j)):
                    add_into(share, share, gotz[j].at[0, h])
                for copy in copiesz(j, 1, to_z3):
                    copy.start()

            @pl.when(is_end)
            def _():
                for copy in copiesz(j, 0, to_z1):
                    copy.wait_send()
        if number == 5:

            @pl.when(is_mid)
            def _():
                for copy in copiesz(j, 1, to_z3):
                    copy.wait()
                for h, share in enumerate(shares(j)):
                    add_into(share, share, gotz[j].at[1, h])
                for copy in copiesz(j, 0, to_z1):
                    copy.start()
                for h, share in enumerate(shares(j)):
                    put_out(j, h, share[...])
        if number == 6:

            @pl.when(is_mid)
            def _():
                for copy in copiesz(j, 0, to_z1):
                    copy.wait_send()

            @pl.when(is_end)
            def _():
                for copy in copiesz(j, 0, to_z1):
                    copy.wait_recv()
                for h in range(2):
                    put_out(j, h, gotz[j][0, h])

    vec_devices = (to_core, to_x, to_y, to_z1, to_z2)

    def vec_copy(k):
        return remote(vec_out, vec_got.at[k], vsend.at[k], vrecv.at[k], vec_devices[k])

    vec_out[...] = vec_in[...]
    for step in range(count + 6):
        if step < 5:
            vec_copy(step).start()
        for j in range(count):
            if 0 <= step - j <= 6:
                stage(j, step - j)
        if step < 5:
            vec_copy(step).wait()
            vec_out[...] = vec_out[...] + vec_got[step]


def reduce_all(grads, vectors):
    sizes = [vector.shape[0] for vector in vectors]
    total = sum(sizes)
    packed = jnp.concatenate(vectors + [jnp.zeros((VECTOR_ROWS * 128 - total,), jnp.float32)])
    packed = packed.reshape(VECTOR_ROWS, 128)
    views = [grad.reshape(4, 2, grad.shape[0] // 8, grad.shape[1]) for grad in grads]
    halves = [(2, 2, 2, job[2], job[4] // 2) for job in JOBS]
    count = len(JOBS)
    dma = pltpu.SemaphoreType.DMA
    scratch = (
        [pltpu.VMEM(shape, jnp.bfloat16) for shape in halves]
        + [pltpu.VMEM(shape, jnp.bfloat16) for shape in halves]
        + [pltpu.VMEM(shape[1:], jnp.bfloat16) for shape in halves]
        + [pltpu.VMEM(shape[2:], jnp.bfloat16) for shape in halves]
        + [pltpu.VMEM(shape[1:], jnp.bfloat16) for shape in halves]
        + [pltpu.VMEM((5, VECTOR_ROWS, 128), jnp.float32)]
        + [dma((count, 8))] * 3
        + [dma((count, 2))] * 4
        + [dma((count, 2, 2))] * 2
        + [dma((5,))] * 2
    )
    vmem = pl.BlockSpec(memory_space=pltpu.VMEM)
    results = pl.pallas_call(
        reduce_kernel,
        name="reduce_grads",
        out_shape=[
            jax.ShapeDtypeStruct((view.shape[2], view.shape[3]), jnp.bfloat16) for view in views
        ]
        + [jax.ShapeDtypeStruct((VECTOR_ROWS, 128), jnp.float32)],
        in_specs=[pl.BlockSpec(memory_space=pl.ANY)] * 5 + [vmem],
        out_specs=[vmem] * 6,
        scratch_shapes=scratch,
        compiler_params=pltpu.CompilerParams(
            collective_id=0, has_side_effects=True, vmem_limit_bytes=56 * 2**20
        ),
    )(*views, packed)
    flat = results[5].reshape(-1)
    starts = [sum(sizes[:k]) for k in range(len(sizes))]
    return (
        [flat[start : start + size] for start, size in zip(starts, sizes)],
        [result.astype(jnp.float32) for result in results[:5]],
    )


def norm_forward(values, gain, shift):
    center = values - jnp.mean(values, axis=-1, keepdims=True)
    inverse = lax.rsqrt(jnp.mean(center * center, axis=-1, keepdims=True) + EPSILON)
    normed = center * inverse
    return (normed * gain + shift, normed, inverse)


def norm_backward(upstream, normed, inverse, gain):
    scaled = upstream * gain
    inner = (
        scaled
        - jnp.mean(scaled, axis=-1, keepdims=True)
        - normed * jnp.mean(scaled * normed, axis=-1, keepdims=True)
    )
    return (inverse * inner, jnp.sum(upstream * normed, axis=0), jnp.sum(upstream, axis=0))


def gelu_slope(values):
    return (
        0.5 * (1.0 + lax.erf(values * SQRT_HALF))
        + values * jnp.exp(-0.5 * values * values) * INV_ROOT_TAU
    )


def weight_grad(left, right):
    return lax.dot_general(
        left, right, (((0,), (0,)), ((), ())), preferred_element_type=jnp.float32
    )


def input_grad(upstream, weight):
    return lax.dot_general(
        upstream, weight, (((1,), (1,)), ((), ())), preferred_element_type=jnp.float32
    )


def masked_scores(query_heads, key_heads, key_valid, scale):
    scores = (
        jnp.einsum("cqhd,ckhd->chqk", query_heads, key_heads, preferred_element_type=jnp.float32)
        * scale
    )
    return jnp.where(key_valid, scores, -1e30)


def column_sum(values):
    return jnp.sum(values, axis=0, dtype=jnp.float32)


def local(
    tokens,
    frame_counts,
    slot_mask,
    norm1_gain,
    norm1_bias,
    w_qkv,
    q_bias,
    v_bias,
    w_out,
    out_bias,
    norm2_gain,
    norm2_bias,
    w_up,
    up_bias,
    w_down,
    down_bias,
    norm3_gain,
    norm3_bias,
    w_align,
    align_bias,
    cot_block,
    cot_align,
):
    clip_count, frame_dev, slot_count, width = tokens.shape
    align_width = w_align.shape[1]
    head_size = width // HEADS
    scale = 1.0 / math.sqrt(head_size)
    row_count = clip_count * frame_dev * slot_count
    cycle_pos = lax.axis_index("blk")
    frame_ids = cycle_pos * frame_dev + jnp.arange(frame_dev, dtype=jnp.int32)
    own_slots = lax.dynamic_slice_in_dim(slot_mask, cycle_pos * frame_dev, frame_dev, 1)
    own_mask = (frame_ids[None, :, None] < frame_counts[:, None, None]) & (own_slots > 0)
    visible = own_mask.astype(jnp.float32).reshape(row_count, 1)
    all_frames = jnp.arange(slot_mask.shape[1], dtype=jnp.int32)
    key_valid = (all_frames[None, :, None] < frame_counts[:, None, None]) & (slot_mask > 0)
    key_valid = key_valid.reshape(clip_count, 1, 1, -1)
    inputs = tokens.reshape(row_count, width).astype(jnp.float32)
    normed_one, unit_one, inverse_one = norm_forward(inputs, norm1_gain, norm1_bias)
    normed1 = normed_one.astype(jnp.bfloat16)
    projected = jnp.dot(normed1, w_qkv, preferred_element_type=jnp.float32)
    queries = (projected[:, :width] + q_bias).astype(jnp.bfloat16)
    keys_local = projected[:, width : 2 * width].astype(jnp.bfloat16)
    values_local = (projected[:, 2 * width :] + v_bias).astype(jnp.bfloat16)
    block_shape = (clip_count, frame_dev, slot_count, width)
    heads_shape = (clip_count, -1, HEADS, head_size)
    keys_all, values_all = (
        lax.all_gather(keys_local.reshape(block_shape), "blk", axis=1, tiled=True),
        lax.all_gather(values_local.reshape(block_shape), "blk", axis=1, tiled=True),
    )
    key_heads = keys_all.reshape(heads_shape)
    value_heads = values_all.reshape(heads_shape)
    query_heads = queries.reshape(heads_shape)
    scores = masked_scores(query_heads, key_heads, key_valid, scale)
    top = jnp.max(scores, axis=-1, keepdims=True)
    expo = jnp.exp(scores - top)
    total = jnp.sum(expo, axis=-1, keepdims=True)
    probs_low = (expo / total).astype(jnp.bfloat16)
    attended = jnp.einsum(
        "chqk,ckhd->cqhd", probs_low, value_heads, preferred_element_type=jnp.float32
    )
    attended = attended.astype(jnp.bfloat16).reshape(row_count, width)
    mid = inputs + jnp.dot(attended, w_out, preferred_element_type=jnp.float32) + out_bias
    normed_two, unit_two, inverse_two = norm_forward(mid, norm2_gain, norm2_bias)
    normed2 = normed_two.astype(jnp.bfloat16)
    hidden = jnp.dot(normed2, w_up, preferred_element_type=jnp.float32) + up_bias
    active = jax.nn.gelu(hidden, approximate=False).astype(jnp.bfloat16)
    after = mid + jnp.dot(active, w_down, preferred_element_type=jnp.float32) + down_bias
    block_out = (visible * after).astype(jnp.bfloat16).reshape(block_shape)
    normed_three, unit_three, inverse_three = norm_forward(after, norm3_gain, norm3_bias)
    normed3 = normed_three.astype(jnp.bfloat16)
    target = jnp.dot(normed3, w_align, preferred_element_type=jnp.float32) + align_bias
    aligned = (
        (visible * target)
        .astype(jnp.bfloat16)
        .reshape(clip_count, frame_dev, slot_count, align_width)
    )
    back_align = (visible * cot_align.reshape(row_count, align_width).astype(jnp.float32)).astype(
        jnp.bfloat16
    )
    grad_align_bias = column_sum(back_align)
    grad_w_align = weight_grad(normed3, back_align)
    back_norm3, grad_norm3_gain, grad_norm3_bias = norm_backward(
        input_grad(back_align, w_align), unit_three, inverse_three, norm3_gain
    )
    back_after = visible * cot_block.reshape(row_count, width).astype(jnp.float32) + back_norm3
    back_down = back_after.astype(jnp.bfloat16)
    grad_down_bias = column_sum(back_down)
    grad_w_down = weight_grad(active, back_down)
    back_up = (input_grad(back_down, w_down) * gelu_slope(hidden)).astype(jnp.bfloat16)
    grad_up_bias = column_sum(back_up)
    grad_w_up = weight_grad(normed2, back_up)
    back_norm2, grad_norm2_gain, grad_norm2_bias = norm_backward(
        input_grad(back_up, w_up), unit_two, inverse_two, norm2_gain
    )
    back_mid = back_after + back_norm2
    back_out = back_mid.astype(jnp.bfloat16)
    grad_out_bias = column_sum(back_out)
    grad_w_out = weight_grad(attended, back_out)
    back_attended = input_grad(back_out, w_out).astype(jnp.bfloat16).reshape(heads_shape)
    scores = masked_scores(query_heads, key_heads, key_valid, scale)
    probs = jnp.exp(scores - top) / total
    probs_low = probs.astype(jnp.bfloat16)
    back_probs = jnp.einsum(
        "cqhd,ckhd->chqk", back_attended, value_heads, preferred_element_type=jnp.float32
    )
    spread = jnp.sum(probs * back_probs, axis=-1, keepdims=True)
    back_scores = (probs * (back_probs - spread)).astype(jnp.bfloat16)
    back_queries = (
        jnp.einsum("chqk,ckhd->cqhd", back_scores, key_heads, preferred_element_type=jnp.float32)
        * scale
    )
    back_queries = back_queries.astype(jnp.bfloat16).reshape(row_count, width)
    value_terms = jnp.einsum(
        "chqk,cqhd->ckhd", probs_low, back_attended, preferred_element_type=jnp.float32
    )
    key_terms = (
        jnp.einsum("chqk,cqhd->ckhd", back_scores, query_heads, preferred_element_type=jnp.float32)
        * scale
    )
    whole_shape = (clip_count, -1, slot_count, width)
    key_share, value_share = (
        lax.psum_scatter(
            key_terms.reshape(whole_shape).astype(jnp.bfloat16),
            "blk",
            scatter_dimension=1,
            tiled=True,
        ).astype(jnp.float32),
        lax.psum_scatter(
            value_terms.reshape(whole_shape).astype(jnp.bfloat16),
            "blk",
            scatter_dimension=1,
            tiled=True,
        ).astype(jnp.float32),
    )
    back_keys = key_share.astype(jnp.bfloat16).reshape(row_count, width)
    back_values = value_share.astype(jnp.bfloat16).reshape(row_count, width)
    grad_q_bias = column_sum(back_queries)
    grad_v_bias = column_sum(back_values)
    combined = jnp.concatenate([back_queries, back_keys, back_values], axis=1)
    grad_w_qkv = weight_grad(normed1, combined)
    back_norm1, grad_norm1_gain, grad_norm1_bias = norm_backward(
        input_grad(combined, w_qkv), unit_one, inverse_one, norm1_gain
    )
    grad_tokens = (back_mid + back_norm1).astype(jnp.bfloat16).reshape(block_shape)
    vectors = [
        grad_norm1_gain,
        grad_norm1_bias,
        grad_q_bias,
        grad_v_bias,
        grad_out_bias,
        grad_norm2_gain,
        grad_norm2_bias,
        grad_up_bias,
        grad_down_bias,
        grad_norm3_gain,
        grad_norm3_bias,
        grad_align_bias,
    ]
    matrices = [grad_w_qkv, grad_w_out, grad_w_up, grad_w_down, grad_w_align]
    if (lax.axis_size("dp"), lax.axis_size("blk")) == GRID:
        vector_total, matrix_total = reduce_all([grad.astype(jnp.bfloat16) for grad in matrices], vectors)
    else:
        vector_total = lax.psum(vectors, ("dp", "blk"))
        matrix_total = [
            lax.psum(
                lax.psum_scatter(grad, "dp", scatter_dimension=0, tiled=True).astype(jnp.bfloat16), "blk"
            ).astype(jnp.float32)
            for grad in matrices
        ]
    return (
        block_out,
        aligned,
        grad_tokens,
        vector_total[0],
        vector_total[1],
        matrix_total[0],
        vector_total[2],
        vector_total[3],
        matrix_total[1],
        vector_total[4],
        vector_total[5],
        vector_total[6],
        matrix_total[2],
        vector_total[7],
        matrix_total[3],
        vector_total[8],
        vector_total[9],
        vector_total[10],
        matrix_total[4],
        vector_total[11],
    )


def solution(mesh):
    in_specs = (
        P("dp", "blk", None, None),
        P("dp"),
        P("dp", None, None),
        P(),
        P(),
        P(),
        P(),
        P(),
        P(),
        P(),
        P(),
        P(),
        P(),
        P(),
        P(),
        P(),
        P(),
        P(),
        P(),
        P(),
        P("dp", "blk", None, None),
        P("dp", "blk", None, None),
    )
    out_specs = (
        P("dp", "blk", None, None),
        P("dp", "blk", None, None),
        P("dp", "blk", None, None),
        P(),
        P(),
        P("dp", None),
        P(),
        P(),
        P("dp", None),
        P(),
        P(),
        P(),
        P("dp", None),
        P(),
        P("dp", None),
        P(),
        P(),
        P(),
        P("dp", None),
        P(),
    )
    return jax.shard_map(local, mesh=mesh, in_specs=in_specs, out_specs=out_specs, check_vma=False)
```

```python
import math

import jax
import jax.numpy as jnp
from jax import lax
from jax.experimental import pallas as pl
from jax.experimental.pallas import tpu as pltpu
from jax.sharding import PartitionSpec as P

HEADS = 12


EPSILON = 1e-06
SQRT_HALF = 0.7071067811865476
INV_ROOT_TAU = 0.3989422804014327


MESH = pl.DeviceIdType.MESH
GRID = (8, 4)
VECTOR_ROWS = 96
JOBS = (
    (4, 0, 96, 0, 1024),
    (3, 0, 192, 0, 768),
    (3, 192, 192, 0, 768),
    (2, 0, 96, 0, 1536),
    (2, 0, 96, 1536, 1536),
    (1, 0, 96, 0, 768),
    (0, 0, 96, 0, 768),
    (0, 0, 96, 768, 768),
    (0, 0, 96, 1536, 768),
)


def add_into(target, first, second):
    rows = target.shape[-2]
    step = 32

    def body(k, _):
        at = pl.ds(pl.multiple_of(k * step, step), step)
        target[..., at, :] = (
            first[..., at, :].astype(jnp.float32) + second[..., at, :].astype(jnp.float32)
        ).astype(target.dtype)
        return 0

    lax.fori_loop(0, rows // step, body, 0)


def reduce_kernel(*refs):
    count = len(JOBS)
    grads = refs[:5]
    vec_in = refs[5]
    outs = refs[6:11]
    vec_out = refs[11]
    rest = refs[12:]
    own, got0, got1, got2, gotz = (rest[i * count : (i + 1) * count] for i in range(5))
    vec_got, local_sem, send0, recv0, send1, recv1, send2, recv2, sendz, recvz, vsend, vrecv = rest[5 * count :]

    dp = lax.axis_index("dp")
    z = lax.axis_index("blk")
    core = lax.rem(dp, 2)
    x = lax.rem(dp // 2, 2)
    y = dp // 4
    to_core = (dp + 1 - 2 * core, z)
    to_x = (dp + 2 - 4 * x, z)
    to_y = (dp + 4 - 8 * y, z)
    to_z1 = (dp, z + 1 - 2 * lax.rem(z, 2))
    to_z2 = (dp, lax.rem(z + 2, 4))
    to_z3 = (dp, 3 - z)
    is_mid = (z == 1) | (z == 2)
    is_end = (z == 0) | (z == 3)

    barrier = pltpu.get_barrier_semaphore()
    for device in (to_core, to_x, to_y, to_z1, to_z2, to_z3):
        pl.semaphore_signal(barrier, inc=1, device_id=device, device_id_type=MESH)
    pl.semaphore_wait(barrier, 6)

    def remote(src, dst, send, recv, device):
        return pltpu.make_async_remote_copy(
            src_ref=src, dst_ref=dst, send_sem=send, recv_sem=recv, device_id=device, device_id_type=MESH
        )

    def pieces(j):
        matrix, row, rows, column, columns = JOBS[j]
        half = columns // 2
        for h in range(2):
            for chip in range(4):
                cy, cx = chip // 2, chip % 2
                first, second = (cx, cy) if h == 0 else (cy, cx)
                yield h, chip, first, second, pl.ds(row, rows), pl.ds(column + h * half, half)

    def copies0(j):
        matrix = JOBS[j][0]
        for h, chip, first, second, rows, columns in pieces(j):
            yield (
                remote(
                    grads[matrix].at[chip, 1 - core, rows, columns],
                    got0[j].at[h, first, second],
                    send0.at[j, h * 4 + chip],
                    recv0.at[j, h * 4 + chip],
                    to_core,
                ),
                pltpu.make_async_copy(
                    grads[matrix].at[chip, core, rows, columns],
                    own[j].at[h, first, second],
                    local_sem.at[j, h * 4 + chip],
                ),
            )

    def copies1(j):
        yield remote(own[j].at[0, 1 - x], got1[j].at[0], send1.at[j, 0], recv1.at[j, 0], to_x)
        yield remote(own[j].at[1, 1 - y], got1[j].at[1], send1.at[j, 1], recv1.at[j, 1], to_y)

    def copies2(j):
        yield remote(own[j].at[0, x, 1 - y], got2[j].at[0], send2.at[j, 0], recv2.at[j, 0], to_y)
        yield remote(own[j].at[1, y, 1 - x], got2[j].at[1], send2.at[j, 1], recv2.at[j, 1], to_x)

    def shares(j):
        return (own[j].at[0, x, y], own[j].at[1, y, x])

    def copiesz(j, slot, device):
        for h, share in enumerate(shares(j)):
            yield remote(share, gotz[j].at[slot, h], sendz.at[j, slot, h], recvz.at[j, slot, h], device)

    def put_out(j, h, value):
        matrix, row, rows, column, columns = JOBS[j]
        half = columns // 2
        outs[matrix][row : row + rows, column + h * half : column + (h + 1) * half] = value

    def stage(j, number):
        if number == 0:
            for far, near in copies0(j):
                far.start()
                near.start()
        if number == 1:
            for far, near in copies0(j):
                near.wait()
                far.wait()
            add_into(own[j], own[j], got0[j])
            for copy in copies1(j):
                copy.start()
        if number == 2:
            for copy in copies1(j):
                copy.wait()
            add_into(own[j].at[0, x], own[j].at[0, x], got1[j].at[0])
            add_into(own[j].at[1, y], own[j].at[1, y], got1[j].at[1])
            for copy in copies2(j):
                copy.start()
        if number == 3:
            for copy in copies2(j):
                copy.wait()
            for h, share in enumerate(shares(j)):
                add_into(share, share, got2[j].at[h])

            @pl.when(is_end)
            def _():
                for copy in copiesz(j, 0, to_z1):
                    copy.start()
        if number == 4:

            @pl.when(is_mid)
            def _():
                for copy in copiesz(j, 0, to_z1):
                    copy.wait_recv()
                for h, share in enumerate(shares(j)):
                    add_into(share, share, gotz[j].at[0, h])
                for copy in copiesz(j, 1, to_z3):
                    copy.start()

            @pl.when(is_end)
            def _():
                for copy in copiesz(j, 0, to_z1):
                    copy.wait_send()
        if number == 5:

            @pl.when(is_mid)
            def _():
                for copy in copiesz(j, 1, to_z3):
                    copy.wait()
                for h, share in enumerate(shares(j)):
                    add_into(share, share, gotz[j].at[1, h])
                for copy in copiesz(j, 0, to_z1):
                    copy.start()
                for h, share in enumerate(shares(j)):
                    put_out(j, h, share[...])
        if number == 6:

            @pl.when(is_mid)
            def _():
                for copy in copiesz(j, 0, to_z1):
                    copy.wait_send()

            @pl.when(is_end)
            def _():
                for copy in copiesz(j, 0, to_z1):
                    copy.wait_recv()
                for h in range(2):
                    put_out(j, h, gotz[j][0, h])

    vec_devices = (to_core, to_x, to_y, to_z1, to_z2)

    def vec_copy(k):
        return remote(vec_out, vec_got.at[k], vsend.at[k], vrecv.at[k], vec_devices[k])

    vec_out[...] = vec_in[...]
    for step in range(count + 6):
        if step < 5:
            vec_copy(step).start()
        for j in range(count):
            if 0 <= step - j <= 6:
                stage(j, step - j)
        if step < 5:
            vec_copy(step).wait()
            vec_out[...] = vec_out[...] + vec_got[step]


def reduce_all(grads, vectors):
    sizes = [vector.shape[0] for vector in vectors]
    total = sum(sizes)
    packed = jnp.concatenate(vectors + [jnp.zeros((VECTOR_ROWS * 128 - total,), jnp.float32)])
    packed = packed.reshape(VECTOR_ROWS, 128)
    views = [grad.reshape(4, 2, grad.shape[0] // 8, grad.shape[1]) for grad in grads]
    halves = [(2, 2, 2, job[2], job[4] // 2) for job in JOBS]
    count = len(JOBS)
    dma = pltpu.SemaphoreType.DMA
    scratch = (
        [pltpu.VMEM(shape, jnp.bfloat16) for shape in halves]
        + [pltpu.VMEM(shape, jnp.bfloat16) for shape in halves]
        + [pltpu.VMEM(shape[1:], jnp.bfloat16) for shape in halves]
        + [pltpu.VMEM(shape[2:], jnp.bfloat16) for shape in halves]
        + [pltpu.VMEM(shape[1:], jnp.bfloat16) for shape in halves]
        + [pltpu.VMEM((5, VECTOR_ROWS, 128), jnp.float32)]
        + [dma((count, 8))] * 3
        + [dma((count, 2))] * 4
        + [dma((count, 2, 2))] * 2
        + [dma((5,))] * 2
    )
    vmem = pl.BlockSpec(memory_space=pltpu.VMEM)
    results = pl.pallas_call(
        reduce_kernel,
        name="reduce_grads",
        out_shape=[
            jax.ShapeDtypeStruct((view.shape[2], view.shape[3]), jnp.bfloat16) for view in views
        ]
        + [jax.ShapeDtypeStruct((VECTOR_ROWS, 128), jnp.float32)],
        in_specs=[pl.BlockSpec(memory_space=pl.ANY)] * 5 + [vmem],
        out_specs=[vmem] * 6,
        scratch_shapes=scratch,
        compiler_params=pltpu.CompilerParams(
            collective_id=0, has_side_effects=True, vmem_limit_bytes=56 * 2**20
        ),
    )(*views, packed)
    flat = results[5].reshape(-1)
    starts = [sum(sizes[:k]) for k in range(len(sizes))]
    return (
        [flat[start : start + size] for start, size in zip(starts, sizes)],
        [result.astype(jnp.float32) for result in results[:5]],
    )


NT = (((1,), (1,)), ((), ()))
TN = (((0,), (0,)), ((), ()))
CHUNKS = 2


def dot(left, right, dims=(((1,), (0,)), ((), ()))):
    return lax.dot_general(left, right, dims, preferred_element_type=jnp.float32)


def remote_copy(src, dst, send, recv, device):
    return pltpu.make_async_remote_copy(
        src_ref=src, dst_ref=dst, send_sem=send, recv_sem=recv, device_id=device, device_id_type=MESH
    )


def line_barrier(dp, z):
    barrier = pltpu.get_barrier_semaphore()
    for away in range(1, 4):
        pl.semaphore_signal(
            barrier, inc=1, device_id=(dp, lax.rem(z + away, 4)), device_id_type=MESH
        )
    pl.semaphore_wait(barrier, 3)


def aligned(start, size):
    return pl.ds(pl.multiple_of(start, size), size)


def attend_kernel(
    tok, gain, bias, w_hbm, q_bias, v_bias, key_bias,
    att, n1, qkv, own_att, lse,
    xall, w_low, w_sem, pair_send, cross_send, fwd_send, recv, att_send, att_recv,
):
    dp = lax.axis_index("dp")
    z = lax.axis_index("blk")
    clip, side = z // 2, lax.rem(z, 2)
    rows, width = tok.shape[1], tok.shape[2]
    half = width // 2
    partner = z + 1 - 2 * side
    is_mid = (z == 1) | (z == 2)
    other_mid = 2 - clip
    near, far = 3 - z, lax.rem(z + 2, 4)
    columns = aligned(side * half, 128)

    def w_copy(m):
        start = pl.multiple_of(m * width + side * half, 128)
        return pltpu.make_async_copy(w_hbm.at[:, pl.ds(start, half)], w_low.at[m], w_sem.at[m])

    for m in range(3):
        w_copy(m).start()
    line_barrier(dp, z)
    step = rows // CHUNKS

    def cross_copy(k):
        at = pl.ds(k * step, step)
        return remote_copy(
            tok.at[1 - clip, at], xall.at[z, at], cross_send.at[k], recv.at[z, k], (dp, other_mid)
        )

    def pair_copy(k):
        at = pl.ds(k * step, step)
        return remote_copy(
            tok.at[clip, at], xall.at[z, at], pair_send.at[k], recv.at[z, k], (dp, partner)
        )

    def arrival(slot, k):
        at = pl.ds(k * step, step)
        return remote_copy(
            tok.at[clip, at], xall.at[slot, at], pair_send.at[k], recv.at[slot, k], (dp, partner)
        )

    def forward_copy(slot, which, k):
        at = pl.ds(k * step, step)
        return remote_copy(
            xall.at[slot, at], xall.at[slot, at], fwd_send.at[which, k], recv.at[slot, k], (dp, partner)
        )

    for k in range(CHUNKS):
        cross_copy(k).start()
    for k in range(CHUNKS):
        pair_copy(k).start()
    xall[z] = tok[clip]
    for m in range(3):
        w_copy(m).wait()

    def project(slot):
        for k in range(rows // 32):
            at = pl.ds(k * 32, 32)
            values = xall[slot, at, :].astype(jnp.float32)
            center = values - jnp.mean(values, axis=-1, keepdims=True)
            inverse = lax.rsqrt(jnp.mean(center * center, axis=-1, keepdims=True) + EPSILON)
            n1[slot, at, :] = (center * inverse * gain[...] + bias[...]).astype(jnp.bfloat16)
        where = aligned(slot * rows, 16)
        where = pl.ds(pl.multiple_of(slot * rows, rows), rows)
        normed = n1[slot]
        qkv[0, where, :] = (
            (dot(normed, w_low[0]) + q_bias[:, pl.ds(pl.multiple_of(side * half, 128), half)]).astype(jnp.bfloat16)
            * jnp.bfloat16(0.125)
        )
        qkv[1, where, :] = dot(normed, w_low[1]).astype(jnp.bfloat16)
        qkv[2, where, :] = (
            dot(normed, w_low[2]) + v_bias[:, pl.ds(pl.multiple_of(side * half, 128), half)]
        ).astype(jnp.bfloat16)

    project(z)

    @pl.when(is_mid)
    def _():
        for k in range(CHUNKS):
            for which, slot in enumerate((near, far)):
                arrival(slot, k).wait_recv()
                forward_copy(slot, which, k).start()
        for k in range(CHUNKS):
            arrival(partner, k).wait_recv()

    def later(number, _):
        slot = jnp.where(number == 0, partner, jnp.where(number == 1, jnp.where(is_mid, near, far), jnp.where(is_mid, far, near)))

        @pl.when(jnp.logical_not(is_mid))
        def _():
            for k in range(CHUNKS):
                arrival(slot, k).wait_recv()

        project(slot)
        return 0

    lax.fori_loop(0, 3, later, 0)

    lane = lax.broadcasted_iota(jnp.int32, (1, 128), 1)
    low_lane = lane < 64

    def att_copy(slot):
        return remote_copy(
            own_att.at[slot], att.at[clip, side], att_send.at[slot], att_recv.at[z], (dp, slot)
        )

    def piece(number, _):
        slot = jnp.where(number == 0, far, jnp.where(number == 1, near, jnp.where(number == 2, partner, z)))
        where = pl.ds(pl.multiple_of(slot * rows, rows), rows)
        stats = jnp.zeros((rows, 128), jnp.float32)
        for t in range(half // 128):
            at = pl.ds(t * 128, 128)
            queries = qkv[0, where, at]
            keys = qkv[1, :, at]
            values = qkv[2, :, at]
            parts = []
            for a in range(2):
                mine = low_lane if a == 0 else jnp.logical_not(low_lane)
                masked = jnp.where(mine, queries, jnp.zeros_like(queries))
                scores = dot(masked, keys, NT) + key_bias[...]
                top = jnp.max(scores, axis=-1, keepdims=True)
                expo = jnp.exp(scores - top)
                total = jnp.sum(expo, axis=-1, keepdims=True)
                parts.append(dot(expo.astype(jnp.bfloat16), values) * (1.0 / total))
                stats = jnp.where(lane == 2 * t + a, top + jnp.log(total), stats)
            own_att[slot, :, at] = jnp.where(low_lane, parts[0], parts[1]).astype(jnp.bfloat16)
        lse[where, :] = stats

        @pl.when(number < 3)
        def _():
            att_copy(slot).start()

        return 0

    lax.fori_loop(0, 4, piece, 0)
    att[clip, side] = own_att[z]

    def settle(number, _):
        slot = lax.rem(z + number, 4)
        att_copy(slot).wait_send()
        remote_copy(
            own_att.at[slot], att.at[slot // 2, lax.rem(slot, 2)], att_send.at[slot], att_recv.at[slot], (dp, slot)
        ).wait_recv()
        return 0

    lax.fori_loop(1, 4, settle, 0)
    for k in range(CHUNKS):
        cross_copy(k).wait_send()
        pair_copy(k).wait_send()

    @pl.when(is_mid)
    def _():
        for k in range(CHUNKS):
            for which, slot in enumerate((near, far)):
                forward_copy(slot, which, k).wait_send()


def attend(tokens, gain, bias, w_qkv, q_bias, v_bias, key_bias):
    clips, rows, width = tokens.shape
    half = width // 2
    vmem = pl.BlockSpec(memory_space=pltpu.VMEM)
    dma = pltpu.SemaphoreType.DMA
    low = jnp.bfloat16
    return pl.pallas_call(
        attend_kernel,
        name="attend",
        out_shape=[
            jax.ShapeDtypeStruct((2, 2, rows, half), low),
            jax.ShapeDtypeStruct((4, rows, width), low),
            jax.ShapeDtypeStruct((3, 4 * rows, half), low),
            jax.ShapeDtypeStruct((4, rows, half), low),
            jax.ShapeDtypeStruct((4 * rows, 128), jnp.float32),
        ],
        in_specs=[vmem, vmem, vmem, pl.BlockSpec(memory_space=pl.ANY), vmem, vmem, vmem],
        out_specs=[vmem] * 5,
        scratch_shapes=[
            pltpu.VMEM((4, rows, width), low),
            pltpu.VMEM((3, width, half), low),
            dma((3,)),
            dma((CHUNKS,)),
            dma((CHUNKS,)),
            dma((2, CHUNKS)),
            dma((4, CHUNKS)),
            dma((4,)),
            dma((4,)),
        ],
        compiler_params=pltpu.CompilerParams(
            collective_id=1, has_side_effects=True, vmem_limit_bytes=56 * 2**20
        ),
    )(tokens, gain.reshape(1, -1), bias.reshape(1, -1), w_qkv, q_bias.reshape(1, -1), v_bias.reshape(1, -1), key_bias)


KEY_BLOCK = 256


def attend_back_kernel(
    back_att, qkv, own_att, lse, n1, w_hbm, key_bias,
    e1, grad_w, back_qkv,
    w_low, grad_att, lse_rows, spread_rows, spread, grad_q, e_part, from_pair, from_end, total_in,
    w_sem, in_send, in_recv, pair_send, pair_recv, end_send, end_recv, out_send, out_recv,
):
    dp = lax.axis_index("dp")
    z = lax.axis_index("blk")
    clip, side = z // 2, lax.rem(z, 2)
    rows, half = back_att.shape[2], back_att.shape[3]
    width = 2 * half
    partner = z + 1 - 2 * side
    is_mid = (z == 1) | (z == 2)
    is_end = (z == 0) | (z == 3)
    near, far = 3 - z, lax.rem(z + 2, 4)
    other_mid = 2 - clip

    def w_copy(m):
        start = pl.multiple_of(m * width + side * half, 128)
        return pltpu.make_async_copy(w_hbm.at[:, pl.ds(start, half)], w_low.at[m], w_sem.at[m])

    for m in range(3):
        w_copy(m).start()
    line_barrier(dp, z)

    def in_copy(slot):
        return remote_copy(
            back_att.at[slot // 2, lax.rem(slot, 2)], grad_att.at[z], in_send.at[slot], in_recv.at[z], (dp, slot)
        )

    def start(number, _):
        in_copy(lax.rem(z + number, 4)).start()
        return 0

    lax.fori_loop(1, 4, start, 0)
    grad_att[z] = back_att[clip, side]

    lse_rows[...] = lse[...].T

    def settle(number, _):
        slot = lax.rem(z + number, 4)
        in_copy(slot).wait_send()
        remote_copy(
            back_att.at[0, 0], grad_att.at[slot], in_send.at[slot], in_recv.at[slot], (dp, slot)
        ).wait_recv()
        return 0

    lax.fori_loop(1, 4, settle, 0)

    lane = lax.broadcasted_iota(jnp.int32, (1, 128), 1)
    low_lane = lane < 64

    def spread_of(slot, _):
        stats = jnp.zeros((rows, 128), jnp.float32)
        for t in range(half // 128):
            at = pl.ds(t * 128, 128)
            product = grad_att[slot, :, at].astype(jnp.float32) * own_att[slot, :, at].astype(jnp.float32)
            for a in range(2):
                mine = low_lane if a == 0 else jnp.logical_not(low_lane)
                value = jnp.sum(jnp.where(mine, product, 0.0), axis=-1, keepdims=True)
                stats = jnp.where(lane == 2 * t + a, value, stats)
        spread[pl.ds(pl.multiple_of(slot * rows, rows), rows), :] = stats
        return 0

    lax.fori_loop(0, 4, spread_of, 0)
    spread_rows[...] = spread[...].T

    def pair(t, _):
        at = pl.ds(pl.multiple_of(t * 128, 128), 128)
        grad_q[...] = jnp.zeros_like(grad_q)
        queries = qkv[0, :, at]
        grads = grad_att[:, :, at].reshape(4 * rows, 128)

        def block(b, _):
            keys_at = pl.ds(pl.multiple_of(b * KEY_BLOCK, KEY_BLOCK), KEY_BLOCK)
            keys = qkv[1, keys_at, at]
            values = qkv[2, keys_at, at]
            grad_k = jnp.zeros((KEY_BLOCK, 128), jnp.float32)
            grad_v = jnp.zeros((KEY_BLOCK, 128), jnp.float32)
            grad_queries = grad_q[...]
            for a in range(2):
                mine = low_lane if a == 0 else jnp.logical_not(low_lane)
                zero = jnp.zeros((), jnp.bfloat16)
                q_mine = jnp.where(mine, queries, zero)
                g_mine = jnp.where(mine, grads, zero)
                k_mine = jnp.where(mine, keys, zero)
                row = pl.ds(2 * t + a, 1)
                scores = dot(keys, q_mine, NT) + key_bias[keys_at, :]
                probs = jnp.exp(scores - lse_rows[row, :])
                back = probs * (dot(values, g_mine, NT) - spread_rows[row, :])
                back = back.astype(jnp.bfloat16)
                grad_v = grad_v + dot(probs.astype(jnp.bfloat16), g_mine)
                grad_k = grad_k + dot(back, q_mine)
                grad_queries = grad_queries + dot(back, k_mine, TN)
            grad_q[...] = grad_queries
            back_qkv[1, keys_at, at] = grad_k.astype(jnp.bfloat16)
            back_qkv[2, keys_at, at] = grad_v.astype(jnp.bfloat16)
            return 0

        lax.fori_loop(0, 4 * rows // KEY_BLOCK, block, 0)
        back_qkv[0, :, at] = (grad_q[...] * 0.125).astype(jnp.bfloat16)
        return 0

    lax.fori_loop(0, half // 128, pair, 0)

    for m in range(3):
        w_copy(m).wait()

    def pair_copy():
        return remote_copy(e_part.at[partner], from_pair, pair_send, pair_recv, (dp, partner))

    def end_copy(which, slot):
        return remote_copy(
            e_part.at[slot], from_end.at[which], end_send.at[which], end_recv.at[which], (dp, partner)
        )

    def out_copy(which, slot):
        return remote_copy(e_part.at[slot], total_in, out_send.at[which], out_recv, (dp, slot))

    mid_near = 2 - clip
    mid_far = 3 - 3 * clip
    targets = (mid_far, mid_near)

    def part_of(number, _):
        slot = jnp.where(number == 0, mid_far, jnp.where(number == 1, mid_near, jnp.where(number == 2, partner, z)))
        where = pl.ds(pl.multiple_of(slot * rows, rows), rows)
        value = dot(back_qkv[0, where, :], w_low[0], NT)
        value = value + dot(back_qkv[1, where, :], w_low[1], NT)
        value = value + dot(back_qkv[2, where, :], w_low[2], NT)
        e_part[slot] = value.astype(jnp.bfloat16)

        @pl.when(number == 3)
        def _():
            e1[clip] = value

        for which in range(2):

            @pl.when(is_end & (number == which))
            def _():
                end_copy(which, targets[which]).start()

        @pl.when(number == 2)
        def _():
            pair_copy().start()

        return 0

    lax.fori_loop(0, 4, part_of, 0)

    @pl.when(is_mid)
    def _():
        for which in range(2):
            end_copy(which, targets[which]).wait_recv()
            add_into(e_part.at[targets[which]], e_part.at[targets[which]], from_end.at[which])
            out_copy(which, targets[which]).start()

    for c in range(0, width, 256):
        for m in range(3):
            grad_w[m, pl.ds(c, 256), :] = sum(
                dot(n1[f, :, pl.ds(c, 256)], back_qkv[m, pl.ds(f * rows, rows), :], TN) for f in range(4)
            ).astype(jnp.bfloat16)

    pair_copy().wait()
    e1[clip] = e1[clip] + from_pair[...].astype(jnp.float32)
    out_copy(0, partner).wait_recv()
    e1[1 - clip] = total_in[...].astype(jnp.float32)

    @pl.when(is_mid)
    def _():
        for which in range(2):
            out_copy(which, targets[which]).wait_send()

    @pl.when(is_end)
    def _():
        for which in range(2):
            end_copy(which, targets[which]).wait_send()


def attend_back(back_att, qkv, own_att, lse, n1, w_qkv, key_bias):
    _, _, rows, half = back_att.shape
    width = 2 * half
    vmem = pl.BlockSpec(memory_space=pltpu.VMEM)
    dma = pltpu.SemaphoreType.DMA
    low = jnp.bfloat16
    return pl.pallas_call(
        attend_back_kernel,
        name="attend_back",
        out_shape=[
            jax.ShapeDtypeStruct((2, rows, width), jnp.float32),
            jax.ShapeDtypeStruct((3, width, half), low),
            jax.ShapeDtypeStruct((3, 4 * rows, half), low),
        ],
        in_specs=[vmem] * 5 + [pl.BlockSpec(memory_space=pl.ANY), vmem],
        out_specs=[vmem] * 3,
        scratch_shapes=[
            pltpu.VMEM((3, width, half), low),
            pltpu.VMEM((4, rows, half), low),
            pltpu.VMEM((128, 4 * rows), jnp.float32),
            pltpu.VMEM((128, 4 * rows), jnp.float32),
            pltpu.VMEM((4 * rows, 128), jnp.float32),
            pltpu.VMEM((4 * rows, 128), jnp.float32),
            pltpu.VMEM((4, rows, width), low),
            pltpu.VMEM((rows, width), low),
            pltpu.VMEM((2, rows, width), low),
            pltpu.VMEM((rows, width), low),
            dma((3,)),
            dma((4,)),
            dma((4,)),
            dma(()),
            dma(()),
            dma((2,)),
            dma((2,)),
            dma((2,)),
            dma(()),
        ],
        compiler_params=pltpu.CompilerParams(
            collective_id=2, has_side_effects=True, vmem_limit_bytes=56 * 2**20
        ),
    )(back_att, qkv, own_att, lse, n1, w_qkv, key_bias)


def norm_forward(values, gain, shift):
    center = values - jnp.mean(values, axis=-1, keepdims=True)
    inverse = lax.rsqrt(jnp.mean(center * center, axis=-1, keepdims=True) + EPSILON)
    normed = center * inverse
    return (normed * gain + shift, normed, inverse)


def norm_backward(upstream, normed, inverse, gain):
    scaled = upstream * gain
    inner = (
        scaled
        - jnp.mean(scaled, axis=-1, keepdims=True)
        - normed * jnp.mean(scaled * normed, axis=-1, keepdims=True)
    )
    return (inverse * inner, jnp.sum(upstream * normed, axis=0), jnp.sum(upstream, axis=0))


def gelu_slope(values):
    return (
        0.5 * (1.0 + lax.erf(values * SQRT_HALF))
        + values * jnp.exp(-0.5 * values * values) * INV_ROOT_TAU
    )


def weight_grad(left, right):
    return lax.dot_general(
        left, right, (((0,), (0,)), ((), ())), preferred_element_type=jnp.float32
    )


def input_grad(upstream, weight):
    return lax.dot_general(
        upstream, weight, (((1,), (1,)), ((), ())), preferred_element_type=jnp.float32
    )


def masked_scores(query_heads, key_heads, key_valid, scale):
    scores = (
        jnp.einsum("cqhd,ckhd->chqk", query_heads, key_heads, preferred_element_type=jnp.float32)
        * scale
    )
    return jnp.where(key_valid, scores, -1e30)


def column_sum(values):
    return jnp.sum(values, axis=0, dtype=jnp.float32)


def local(
    tokens,
    frame_counts,
    slot_mask,
    norm1_gain,
    norm1_bias,
    w_qkv,
    q_bias,
    v_bias,
    w_out,
    out_bias,
    norm2_gain,
    norm2_bias,
    w_up,
    up_bias,
    w_down,
    down_bias,
    norm3_gain,
    norm3_bias,
    w_align,
    align_bias,
    cot_block,
    cot_align,
):
    clip_count, frame_dev, slot_count, width = tokens.shape
    align_width = w_align.shape[1]
    head_size = width // HEADS
    scale = 1.0 / math.sqrt(head_size)
    row_count = clip_count * frame_dev * slot_count
    cycle_pos = lax.axis_index("blk")
    frame_ids = cycle_pos * frame_dev + jnp.arange(frame_dev, dtype=jnp.int32)
    own_slots = lax.dynamic_slice_in_dim(slot_mask, cycle_pos * frame_dev, frame_dev, 1)
    own_mask = (frame_ids[None, :, None] < frame_counts[:, None, None]) & (own_slots > 0)
    visible = own_mask.astype(jnp.float32).reshape(row_count, 1)
    all_frames = jnp.arange(slot_mask.shape[1], dtype=jnp.int32)
    key_valid = (all_frames[None, :, None] < frame_counts[:, None, None]) & (slot_mask > 0)
    key_valid = key_valid.reshape(clip_count, 1, 1, -1)
    inputs = tokens.reshape(row_count, width).astype(jnp.float32)
    normed_one, unit_one, inverse_one = norm_forward(inputs, norm1_gain, norm1_bias)
    normed1 = normed_one.astype(jnp.bfloat16)
    kernels = (lax.axis_size("dp"), lax.axis_size("blk")) == GRID
    block_shape = (clip_count, frame_dev, slot_count, width)
    heads_shape = (clip_count, -1, HEADS, head_size)
    whole_shape = (clip_count, -1, slot_count, width)
    if kernels:
        rows = frame_dev * slot_count
        own_clip = lax.dynamic_index_in_dim(key_valid.reshape(clip_count, -1), cycle_pos // 2, 0, False)
        key_bias = jnp.where(own_clip, 0.0, -1e30).astype(jnp.float32)
        att, n1, qkv, own_att, lse = attend(
            tokens.reshape(clip_count, rows, width), norm1_gain, norm1_bias, w_qkv, q_bias, v_bias, key_bias[None, :]
        )
        attended = att.transpose(0, 2, 1, 3).reshape(row_count, width)
    else:
        projected = jnp.dot(normed1, w_qkv, preferred_element_type=jnp.float32)
        queries = (projected[:, :width] + q_bias).astype(jnp.bfloat16)
        keys_local = projected[:, width : 2 * width].astype(jnp.bfloat16)
        values_local = (projected[:, 2 * width :] + v_bias).astype(jnp.bfloat16)
        keys_all, values_all = (
            lax.all_gather(keys_local.reshape(block_shape), "blk", axis=1, tiled=True),
            lax.all_gather(values_local.reshape(block_shape), "blk", axis=1, tiled=True),
        )
        key_heads = keys_all.reshape(heads_shape)
        value_heads = values_all.reshape(heads_shape)
        query_heads = queries.reshape(heads_shape)
        scores = masked_scores(query_heads, key_heads, key_valid, scale)
        top = jnp.max(scores, axis=-1, keepdims=True)
        expo = jnp.exp(scores - top)
        total = jnp.sum(expo, axis=-1, keepdims=True)
        probs_low = (expo / total).astype(jnp.bfloat16)
        attended = jnp.einsum(
            "chqk,ckhd->cqhd", probs_low, value_heads, preferred_element_type=jnp.float32
        )
        attended = attended.astype(jnp.bfloat16).reshape(row_count, width)
    mid = inputs + jnp.dot(attended, w_out, preferred_element_type=jnp.float32) + out_bias
    normed_two, unit_two, inverse_two = norm_forward(mid, norm2_gain, norm2_bias)
    normed2 = normed_two.astype(jnp.bfloat16)
    hidden = jnp.dot(normed2, w_up, preferred_element_type=jnp.float32) + up_bias
    active = jax.nn.gelu(hidden, approximate=False).astype(jnp.bfloat16)
    after = mid + jnp.dot(active, w_down, preferred_element_type=jnp.float32) + down_bias
    block_out = (visible * after).astype(jnp.bfloat16).reshape(block_shape)
    normed_three, unit_three, inverse_three = norm_forward(after, norm3_gain, norm3_bias)
    normed3 = normed_three.astype(jnp.bfloat16)
    target = jnp.dot(normed3, w_align, preferred_element_type=jnp.float32) + align_bias
    aligned = (
        (visible * target)
        .astype(jnp.bfloat16)
        .reshape(clip_count, frame_dev, slot_count, align_width)
    )
    back_align = (visible * cot_align.reshape(row_count, align_width).astype(jnp.float32)).astype(
        jnp.bfloat16
    )
    grad_align_bias = column_sum(back_align)
    grad_w_align = weight_grad(normed3, back_align)
    back_norm3, grad_norm3_gain, grad_norm3_bias = norm_backward(
        input_grad(back_align, w_align), unit_three, inverse_three, norm3_gain
    )
    back_after = visible * cot_block.reshape(row_count, width).astype(jnp.float32) + back_norm3
    back_down = back_after.astype(jnp.bfloat16)
    grad_down_bias = column_sum(back_down)
    grad_w_down = weight_grad(active, back_down)
    back_up = (input_grad(back_down, w_down) * gelu_slope(hidden)).astype(jnp.bfloat16)
    grad_up_bias = column_sum(back_up)
    grad_w_up = weight_grad(normed2, back_up)
    back_norm2, grad_norm2_gain, grad_norm2_bias = norm_backward(
        input_grad(back_up, w_up), unit_two, inverse_two, norm2_gain
    )
    back_mid = back_after + back_norm2
    back_out = back_mid.astype(jnp.bfloat16)
    grad_out_bias = column_sum(back_out)
    grad_w_out = weight_grad(attended, back_out)
    back_attended = input_grad(back_out, w_out).astype(jnp.bfloat16)
    if kernels:
        back_att = back_attended.reshape(clip_count, rows, 2, width // 2).transpose(0, 2, 1, 3)
        upstream_one, grad_part, back_qkv = attend_back(
            back_att, qkv, own_att, lse, n1, w_qkv, key_bias[:, None]
        )
        upstream_one = upstream_one.reshape(row_count, width)
        spot = (0, (cycle_pos % 2) * (width // 2))
        grad_w_qkv = jnp.concatenate(
            [lax.dynamic_update_slice(jnp.zeros((width, width), jnp.bfloat16), grad_part[m], spot) for m in range(3)],
            axis=1,
        )
        sums = jnp.sum(back_qkv, axis=1, dtype=jnp.float32)
        grad_q_bias, grad_v_bias = (
            lax.dynamic_update_slice(jnp.zeros((width,), jnp.float32), sums[m], spot[1:]) for m in (0, 2)
        )
    else:
        back_attended = back_attended.reshape(heads_shape)
        scores = masked_scores(query_heads, key_heads, key_valid, scale)
        probs = jnp.exp(scores - top) / total
        probs_low = probs.astype(jnp.bfloat16)
        back_probs = jnp.einsum(
            "cqhd,ckhd->chqk", back_attended, value_heads, preferred_element_type=jnp.float32
        )
        spread = jnp.sum(probs * back_probs, axis=-1, keepdims=True)
        back_scores = (probs * (back_probs - spread)).astype(jnp.bfloat16)
        back_queries = (
            jnp.einsum("chqk,ckhd->cqhd", back_scores, key_heads, preferred_element_type=jnp.float32)
            * scale
        )
        back_queries = back_queries.astype(jnp.bfloat16).reshape(row_count, width)
        value_terms = jnp.einsum(
            "chqk,cqhd->ckhd", probs_low, back_attended, preferred_element_type=jnp.float32
        )
        key_terms = (
            jnp.einsum("chqk,cqhd->ckhd", back_scores, query_heads, preferred_element_type=jnp.float32)
            * scale
        )
        key_share, value_share = (
            lax.psum_scatter(
                key_terms.reshape(whole_shape).astype(jnp.bfloat16),
                "blk",
                scatter_dimension=1,
                tiled=True,
            ).astype(jnp.float32),
            lax.psum_scatter(
                value_terms.reshape(whole_shape).astype(jnp.bfloat16),
                "blk",
                scatter_dimension=1,
                tiled=True,
            ).astype(jnp.float32),
        )
        back_keys = key_share.astype(jnp.bfloat16).reshape(row_count, width)
        back_values = value_share.astype(jnp.bfloat16).reshape(row_count, width)
        grad_q_bias = column_sum(back_queries)
        grad_v_bias = column_sum(back_values)
        combined = jnp.concatenate([back_queries, back_keys, back_values], axis=1)
        grad_w_qkv = weight_grad(normed1, combined)
        upstream_one = input_grad(combined, w_qkv)
    back_norm1, grad_norm1_gain, grad_norm1_bias = norm_backward(
        upstream_one, unit_one, inverse_one, norm1_gain
    )
    grad_tokens = (back_mid + back_norm1).astype(jnp.bfloat16).reshape(block_shape)
    vectors = [
        grad_norm1_gain,
        grad_norm1_bias,
        grad_q_bias,
        grad_v_bias,
        grad_out_bias,
        grad_norm2_gain,
        grad_norm2_bias,
        grad_up_bias,
        grad_down_bias,
        grad_norm3_gain,
        grad_norm3_bias,
        grad_align_bias,
    ]
    matrices = [grad_w_qkv, grad_w_out, grad_w_up, grad_w_down, grad_w_align]
    if kernels:
        vector_total, matrix_total = reduce_all([grad.astype(jnp.bfloat16) for grad in matrices], vectors)
    else:
        vector_total = lax.psum(vectors, ("dp", "blk"))
        matrix_total = [
            lax.psum(
                lax.psum_scatter(grad, "dp", scatter_dimension=0, tiled=True).astype(jnp.bfloat16), "blk"
            ).astype(jnp.float32)
            for grad in matrices
        ]
    return (
        block_out,
        aligned,
        grad_tokens,
        vector_total[0],
        vector_total[1],
        matrix_total[0],
        vector_total[2],
        vector_total[3],
        matrix_total[1],
        vector_total[4],
        vector_total[5],
        vector_total[6],
        matrix_total[2],
        vector_total[7],
        matrix_total[3],
        vector_total[8],
        vector_total[9],
        vector_total[10],
        matrix_total[4],
        vector_total[11],
    )


def solution(mesh):
    in_specs = (
        P("dp", "blk", None, None),
        P("dp"),
        P("dp", None, None),
        P(),
        P(),
        P(),
        P(),
        P(),
        P(),
        P(),
        P(),
        P(),
        P(),
        P(),
        P(),
        P(),
        P(),
        P(),
        P(),
        P(),
        P("dp", "blk", None, None),
        P("dp", "blk", None, None),
    )
    out_specs = (
        P("dp", "blk", None, None),
        P("dp", "blk", None, None),
        P("dp", "blk", None, None),
        P(),
        P(),
        P("dp", None),
        P(),
        P(),
        P("dp", None),
        P(),
        P(),
        P(),
        P("dp", None),
        P(),
        P("dp", None),
        P(),
        P(),
        P(),
        P("dp", None),
        P(),
    )
    return jax.shard_map(local, mesh=mesh, in_specs=in_specs, out_specs=out_specs, check_vma=False)
```

```python
import math

import jax
import jax.numpy as jnp
from jax import lax
from jax.experimental import pallas as pl
from jax.experimental.pallas import tpu as pltpu
from jax.sharding import PartitionSpec as P

HEADS = 12


EPSILON = 1e-06
SQRT_HALF = 0.7071067811865476
INV_ROOT_TAU = 0.3989422804014327
MESH = pl.DeviceIdType.MESH
GRID = (8, 4)


NT = (((1,), (1,)), ((), ()))
TN = (((0,), (0,)), ((), ()))
CHUNKS = 2


def dot(left, right, dims=(((1,), (0,)), ((), ()))):
    return lax.dot_general(left, right, dims, preferred_element_type=jnp.float32)


def remote_copy(src, dst, send, recv, device):
    return pltpu.make_async_remote_copy(
        src_ref=src, dst_ref=dst, send_sem=send, recv_sem=recv, device_id=device, device_id_type=MESH
    )


def line_barrier(dp, z):
    barrier = pltpu.get_barrier_semaphore()
    for away in range(1, 4):
        pl.semaphore_signal(
            barrier, inc=1, device_id=(dp, lax.rem(z + away, 4)), device_id_type=MESH
        )
    pl.semaphore_wait(barrier, 3)


N1_GAIN, N1_BIAS, Q_BIAS, V_BIAS, OUT_BIAS, N2_GAIN, N2_BIAS, DOWN_BIAS, N3_GAIN, N3_BIAS, UP_BIAS, ALIGN_BIAS = (
    0, 1, 2, 3, 4, 5, 6, 7, 8, 9, 10, 14,
)
PACK_ROWS = 16
TILE = 512


def row_of(pack, row, start, size):
    width = pack.shape[1]
    parts = []
    while size > 0:
        line, column = row + start // width, start % width
        take = min(size, width - column)
        parts.append(pack[line : line + 1, column : column + take])
        start, size = start + take, size - take
    return parts[0] if len(parts) == 1 else jnp.concatenate(parts, axis=1)


def norm_rows(values):
    center = values - jnp.mean(values, axis=-1, keepdims=True)
    inverse = lax.rsqrt(jnp.mean(center * center, axis=-1, keepdims=True) + EPSILON)
    return center * inverse, inverse


def feed_kernel(
    tok, att, vis, pack, w_out, w_up, w_down, w_align,
    block_out, align_out, act_t, slope, unit2, inv2, unit3, inv3, normed2_t, normed3_t, att_t,
    out_v, up_v, down_v, align_v, attended, mid, normed, hidden, act, slope_v, act_tv, trans, w_sem, put_sem,
):
    rows, width = tok.shape
    wide = up_v.shape[1]
    half = width // 2
    weights = [
        pltpu.make_async_copy(src, dst, w_sem.at[k])
        for k, (src, dst) in enumerate(((w_out, out_v), (w_up, up_v), (w_down, down_v), (w_align, align_v)))
    ]
    for copy in weights:
        copy.start()
    chunk = 32

    def transposed(k, source, target):
        for c in range(0, width, 128):
            trans[k, pl.ds(c, 128), :] = source[:, pl.ds(c, 128)].T
        copy = pltpu.make_async_copy(trans.at[k], target, put_sem.at[k])
        copy.start()
        return copy

    for c in range(2):
        for h in range(2):
            attended[pl.ds(c * rows // 2, rows // 2), pl.ds(h * half, half)] = att[c, h]
    puts = [transposed(0, attended, att_t)]
    weights[0].wait()
    for c in range(0, width, 256):
        at = pl.ds(c, 256)
        mid[:, at] = (
            tok[:, at].astype(jnp.float32) + dot(attended[...], out_v[:, at]) + pack[OUT_BIAS : OUT_BIAS + 1, at]
        )

    def norm(gain, bias, unit, inv):
        def body(k, _):
            at = pl.ds(pl.multiple_of(k * chunk, chunk), chunk)
            one, inverse = norm_rows(mid[at, :])
            unit[at, :] = one.astype(jnp.bfloat16)
            inv[at, :] = inverse
            normed[at, :] = (one * pack[gain : gain + 1, :] + pack[bias : bias + 1, :]).astype(jnp.bfloat16)
            return 0

        lax.fori_loop(0, rows // chunk, body, 0)

    norm(N2_GAIN, N2_BIAS, unit2, inv2)
    puts.append(transposed(1, normed, normed2_t))
    weights[1].wait()
    for t in range(wide // TILE):
        at = pl.ds(t * TILE, TILE)
        hidden[...] = dot(normed[...], up_v[:, at]) + row_of(pack, UP_BIAS, t * TILE, TILE)

        def body(k, _):
            here = pl.ds(pl.multiple_of(k * chunk, chunk), chunk)
            values = hidden[here, :]
            cdf = 0.5 * (1.0 + lax.erf(values * SQRT_HALF))
            act[here, at] = (values * cdf).astype(jnp.bfloat16)
            slope_v[here, at] = (
                cdf + values * jnp.exp(-0.5 * values * values) * INV_ROOT_TAU
            ).astype(jnp.bfloat16)
            return 0

        lax.fori_loop(0, rows // chunk, body, 0)
        for c in range(0, TILE, 128):
            act_tv[pl.ds(t * TILE + c, 128), :] = act[:, pl.ds(t * TILE + c, 128)].T
        copy = pltpu.make_async_copy(act_tv.at[pl.ds(t * TILE, TILE)], act_t.at[pl.ds(t * TILE, TILE)], put_sem.at[4 + t])
        copy.start()
        puts.append(copy)
    copy = pltpu.make_async_copy(slope_v, slope, put_sem.at[3])
    copy.start()
    puts.append(copy)
    weights[2].wait()
    for c in range(0, width, 256):
        at = pl.ds(c, 256)
        mid[:, at] = mid[:, at] + dot(act[...], down_v[:, at]) + pack[DOWN_BIAS : DOWN_BIAS + 1, at]
    block_out[...] = (vis[...] * mid[...]).astype(jnp.bfloat16)
    norm(N3_GAIN, N3_BIAS, unit3, inv3)
    puts.append(transposed(2, normed, normed3_t))
    weights[3].wait()
    for c in range(0, align_v.shape[1], 256):
        at = pl.ds(c, 256)
        target = dot(normed[...], align_v[:, at]) + row_of(pack, ALIGN_BIAS, c, 256)
        align_out[:, at] = (vis[...] * target).astype(jnp.bfloat16)
    for copy in puts:
        copy.wait()


def feed(tok, att, vis, pack, w_out, w_up, w_down, w_align):
    rows, width = tok.shape
    wide, align = w_up.shape[1], w_align.shape[1]
    vmem = pl.BlockSpec(memory_space=pltpu.VMEM)
    hbm = pl.BlockSpec(memory_space=pl.ANY)
    low = jnp.bfloat16
    struct = jax.ShapeDtypeStruct
    return pl.pallas_call(
        feed_kernel,
        name="feed",
        out_shape=[
            struct((rows, width), low),
            struct((rows, align), low),
            struct((wide, rows), low),
            struct((rows, wide), low),
            struct((rows, width), low),
            struct((rows, 1), jnp.float32),
            struct((rows, width), low),
            struct((rows, 1), jnp.float32),
            struct((width, rows), low),
            struct((width, rows), low),
            struct((width, rows), low),
        ],
        in_specs=[vmem] * 4 + [hbm] * 4,
        out_specs=[vmem, vmem, hbm, hbm, vmem, vmem, vmem, vmem, hbm, hbm, hbm],
        scratch_shapes=[
            pltpu.VMEM(w_out.shape, low),
            pltpu.VMEM(w_up.shape, low),
            pltpu.VMEM(w_down.shape, low),
            pltpu.VMEM(w_align.shape, low),
            pltpu.VMEM((rows, width), low),
            pltpu.VMEM((rows, width), jnp.float32),
            pltpu.VMEM((rows, width), low),
            pltpu.VMEM((rows, TILE), jnp.float32),
            pltpu.VMEM((rows, wide), low),
            pltpu.VMEM((rows, wide), low),
            pltpu.VMEM((wide, rows), low),
            pltpu.VMEM((3, width, rows), low),
            pltpu.SemaphoreType.DMA((4,)),
            pltpu.SemaphoreType.DMA((4 + wide // TILE,)),
        ],
        compiler_params=pltpu.CompilerParams(vmem_limit_bytes=56 * 2**20),
    )(tok, att, vis, pack, w_out, w_up, w_down, w_align)


def attend_kernel(
    tok, pack, w_hbm, key_bias,
    att, n1, unit, qkv, own_att, lse,
    xall, w_low, w_sem, pair_send, cross_send, fwd_send, recv, att_send, att_recv,
):
    dp = lax.axis_index("dp")
    z = lax.axis_index("blk")
    clip, side = z // 2, lax.rem(z, 2)
    rows, width = tok.shape[1], tok.shape[2]
    half = width // 2
    partner = z + 1 - 2 * side
    is_mid = (z == 1) | (z == 2)
    other_mid = 2 - clip
    near, far = 3 - z, lax.rem(z + 2, 4)
    columns = pl.ds(pl.multiple_of(side * half, 128), half)

    def w_copy(m):
        start = pl.multiple_of(m * width + side * half, 128)
        return pltpu.make_async_copy(w_hbm.at[:, pl.ds(start, half)], w_low.at[m], w_sem.at[m])

    for m in range(3):
        w_copy(m).start()
    line_barrier(dp, z)
    step = rows // CHUNKS

    def cross_copy(k):
        at = pl.ds(k * step, step)
        return remote_copy(
            tok.at[1 - clip, at], xall.at[z, at], cross_send.at[k], recv.at[z, k], (dp, other_mid)
        )

    def pair_copy(k):
        at = pl.ds(k * step, step)
        return remote_copy(
            tok.at[clip, at], xall.at[z, at], pair_send.at[k], recv.at[z, k], (dp, partner)
        )

    def arrival(slot, k):
        at = pl.ds(k * step, step)
        return remote_copy(
            tok.at[clip, at], xall.at[slot, at], pair_send.at[k], recv.at[slot, k], (dp, partner)
        )

    def forward_copy(slot, which, k):
        at = pl.ds(k * step, step)
        return remote_copy(
            xall.at[slot, at], xall.at[slot, at], fwd_send.at[which, k], recv.at[slot, k], (dp, partner)
        )

    for k in range(CHUNKS):
        cross_copy(k).start()
    for k in range(CHUNKS):
        pair_copy(k).start()
    xall[z] = tok[clip]
    for m in range(3):
        w_copy(m).wait()

    def project(slot):
        for k in range(rows // 32):
            at = pl.ds(k * 32, 32)
            values = xall[slot, at, :].astype(jnp.float32)
            one, _ = norm_rows(values)
            unit[slot, at, :] = one.astype(jnp.bfloat16)
            n1[slot, at, :] = (
                one * pack[N1_GAIN : N1_GAIN + 1, :] + pack[N1_BIAS : N1_BIAS + 1, :]
            ).astype(jnp.bfloat16)
        where = pl.ds(pl.multiple_of(slot * rows, rows), rows)
        normed = n1[slot]
        qkv[0, where, :] = (
            (dot(normed, w_low[0]) + pack[Q_BIAS : Q_BIAS + 1, columns]).astype(jnp.bfloat16)
            * jnp.bfloat16(0.125)
        )
        qkv[1, where, :] = dot(normed, w_low[1]).astype(jnp.bfloat16)
        qkv[2, where, :] = (
            dot(normed, w_low[2]) + pack[V_BIAS : V_BIAS + 1, columns]
        ).astype(jnp.bfloat16)

    project(z)

    @pl.when(is_mid)
    def _():
        for k in range(CHUNKS):
            for which, slot in enumerate((near, far)):
                arrival(slot, k).wait_recv()
                forward_copy(slot, which, k).start()
        for k in range(CHUNKS):
            arrival(partner, k).wait_recv()

    def later(number, _):
        slot = jnp.where(number == 0, partner, jnp.where(number == 1, jnp.where(is_mid, near, far), jnp.where(is_mid, far, near)))

        @pl.when(jnp.logical_not(is_mid))
        def _():
            for k in range(CHUNKS):
                arrival(slot, k).wait_recv()

        project(slot)
        return 0

    lax.fori_loop(0, 3, later, 0)

    lane = lax.broadcasted_iota(jnp.int32, (1, 128), 1)
    low_lane = lane < 64

    def att_copy(slot):
        return remote_copy(
            own_att.at[slot], att.at[clip, side], att_send.at[slot], att_recv.at[z], (dp, slot)
        )

    def piece(number, _):
        slot = jnp.where(number == 0, far, jnp.where(number == 1, near, jnp.where(number == 2, partner, z)))
        where = pl.ds(pl.multiple_of(slot * rows, rows), rows)
        stats = jnp.zeros((rows, 128), jnp.float32)
        for t in range(half // 128):
            at = pl.ds(t * 128, 128)
            queries = qkv[0, where, at]
            keys = qkv[1, :, at]
            values = qkv[2, :, at]
            parts = []
            for a in range(2):
                mine = low_lane if a == 0 else jnp.logical_not(low_lane)
                masked = jnp.where(mine, queries, jnp.zeros_like(queries))
                scores = dot(masked, keys, NT) + key_bias[...]
                top = jnp.max(scores, axis=-1, keepdims=True)
                expo = jnp.exp(scores - top)
                total = jnp.sum(expo, axis=-1, keepdims=True)
                parts.append(dot(expo.astype(jnp.bfloat16), values) * (1.0 / total))
                stats = jnp.where(lane == 2 * t + a, top + jnp.log(total), stats)
            own_att[slot, :, at] = jnp.where(low_lane, parts[0], parts[1]).astype(jnp.bfloat16)
        lse[where, :] = stats

        @pl.when(number < 3)
        def _():
            att_copy(slot).start()

        return 0

    lax.fori_loop(0, 4, piece, 0)
    att[clip, side] = own_att[z]

    def settle(number, _):
        slot = lax.rem(z + number, 4)
        att_copy(slot).wait_send()
        remote_copy(
            own_att.at[slot], att.at[slot // 2, lax.rem(slot, 2)], att_send.at[slot], att_recv.at[slot], (dp, slot)
        ).wait_recv()
        return 0

    lax.fori_loop(1, 4, settle, 0)
    for k in range(CHUNKS):
        cross_copy(k).wait_send()
        pair_copy(k).wait_send()

    @pl.when(is_mid)
    def _():
        for k in range(CHUNKS):
            for which, slot in enumerate((near, far)):
                forward_copy(slot, which, k).wait_send()


def attend(tokens, pack, w_qkv, key_bias):
    clips, rows, width = tokens.shape
    half = width // 2
    vmem = pl.BlockSpec(memory_space=pltpu.VMEM)
    dma = pltpu.SemaphoreType.DMA
    low = jnp.bfloat16
    return pl.pallas_call(
        attend_kernel,
        name="attend",
        out_shape=[
            jax.ShapeDtypeStruct((2, 2, rows, half), low),
            jax.ShapeDtypeStruct((4, rows, width), low),
            jax.ShapeDtypeStruct((4, rows, width), low),
            jax.ShapeDtypeStruct((3, 4 * rows, half), low),
            jax.ShapeDtypeStruct((4, rows, half), low),
            jax.ShapeDtypeStruct((4 * rows, 128), jnp.float32),
        ],
        in_specs=[vmem, vmem, pl.BlockSpec(memory_space=pl.ANY), vmem],
        out_specs=[vmem] * 6,
        scratch_shapes=[
            pltpu.VMEM((4, rows, width), low),
            pltpu.VMEM((3, width, half), low),
            dma((3,)),
            dma((CHUNKS,)),
            dma((CHUNKS,)),
            dma((2, CHUNKS)),
            dma((4, CHUNKS)),
            dma((4,)),
            dma((4,)),
        ],
        compiler_params=pltpu.CompilerParams(
            collective_id=1, has_side_effects=True, vmem_limit_bytes=56 * 2**20
        ),
    )(tokens, pack, w_qkv, key_bias)


KEY_BLOCK = 256


JOBS = (
    (4, 0, 96, 0, 1024, 0),
    (3, 0, 192, 0, 768, 2),
    (3, 192, 192, 0, 768, 2),
    (2, 0, 96, 0, 1536, 0),
    (2, 0, 96, 1536, 1536, 1),
    (1, 0, 96, 0, 768, 0),
    (0, 0, 96, 0, 1152, 1),
)
ALIGN, DOWN0, DOWN1, UP0, UP1, OUT, QKV = range(7)
COUNT = len(JOBS)
SEND_SHAPES = ((2, 2, 2, 48, 1536), (2, 2, 2, 48, 1536), (2, 2, 2, 96, 768))


def add_into(target, first, second):
    rows = target.shape[-2]
    step = 48 if rows % 48 == 0 else 32

    def body(k, _):
        at = pl.ds(pl.multiple_of(k * step, step), step)
        target[..., at, :] = (
            first[..., at, :].astype(jnp.float32) + second[..., at, :].astype(jnp.float32)
        ).astype(target.dtype)
        return 0

    lax.fori_loop(0, rows // step, body, 0)


LOADS = (
    "cot_a", "l3", "align", "unit3", "cot_b", "down", "slope", "ld", "up", "unit2", "out", "l2", "la",
    "n1", "lse", "own_att", "qkv0", "qkv1", "qkv2", "unit1", "low0", "low1", "low2",
    "l3_far", "ld_far", "l2_far", "la_far",
)


def back_kernel(*refs):
    (
        vis, pack, key_bias, inv2, inv3, tok,
        cot_a_h, cot_b_h, unit2_h, unit3_h, slope_h, l3_h, ld_h, l2_h, la_h,
        qkv_h, own_att_h, lse_h, n1_h, unit1_h, w_align, w_down, w_up, w_out, w_qkv,
    ) = refs[:25]
    grad_tokens, vec_out = refs[25:27]
    outs = refs[27:32]
    rest = refs[32:]
    own, got0, got1, got2 = (rest[i * COUNT : (i + 1) * COUNT] for i in range(4))
    rest = rest[4 * COUNT :]
    gotz = rest[: COUNT - 1]
    rest = rest[COUNT - 1 :]
    (
        gotq, send_a, send_b, send_c, vec_got,
        align_v, down_v, up_v, out_v, cot_a, cot_b, unit2, unit3, slope, l3, ld, l2, la,
        e_v, mid_v, low_d, low_o, in_src, grad_att, n1s, lse, lse_rows, spread_rows, grad_q,
        from_pair, from_end, total_in,
        load_sem, send0, recv0, send1, recv1, send2, recv2, sendz, recvz, sendq, recvq, out_sem, vsend, vrecv,
        in_send, in_recv, pair_send, pair_recv, end_send, end_recv, out_send, out_recv,
    ) = rest
    buffers = (send_a, send_b, send_c)

    dp = lax.axis_index("dp")
    z = lax.axis_index("blk")
    core = lax.rem(dp, 2)
    x = lax.rem(dp // 2, 2)
    y = dp // 4
    clip, side = z // 2, lax.rem(z, 2)
    to_core = (dp + 1 - 2 * core, z)
    to_x = (dp + 2 - 4 * x, z)
    to_y = (dp + 4 - 8 * y, z)
    partner = z + 1 - 2 * side
    to_z1 = (dp, partner)
    to_z2 = (dp, lax.rem(z + 2, 4))
    to_z3 = (dp, 3 - z)
    is_mid = (z == 1) | (z == 2)
    is_end = (z == 0) | (z == 3)
    rows, width = tok.shape
    half, piece = width // 2, rows // 2
    wide = slope.shape[1]
    low = jnp.bfloat16

    def load(name, src, dst):
        return pltpu.make_async_copy(src, dst, load_sem.at[LOADS.index(name)])

    def qkv_at(m):
        return up_v.at[:, pl.ds(m * half, half)]

    def low_at(m):
        return up_v.at[:, pl.ds((3 + m) * half, half)]

    def grad_at(m):
        return down_v.at[pl.ds((2 if m == 0 else 3) * width, width), pl.ds(half if m != 1 else 0, half)]

    unit1 = down_v.at[pl.ds(0, width)]
    n1 = down_v.at[pl.ds(width, width)]
    own_att = down_v.at[pl.ds(2 * width, width), pl.ds(0, half)]

    def e_at(slot):
        return align_v.at[pl.ds(pl.multiple_of(slot * piece, piece), piece), pl.ds(0, width)]

    def halves(name, src, dst):
        return [
            load(name + "_far", src.at[:, 1 - core], dst.at[0]),
            load(name, src.at[:, core], dst.at[1]),
        ]

    first = {
        "cot_a": [load("cot_a", cot_a_h, cot_a)],
        "l3": halves("l3", l3_h, l3),
        "align": [load("align", w_align, align_v)],
        "unit3": [load("unit3", unit3_h, unit3)],
        "cot_b": [load("cot_b", cot_b_h, cot_b)],
        "down": [load("down", w_down, down_v)],
        "slope": [load("slope", slope_h, slope)],
        "ld": halves("ld", ld_h, ld),
        "up": [load("up", w_up, up_v)],
        "unit2": [load("unit2", unit2_h, unit2)],
        "out": [load("out", w_out, out_v)],
        "l2": halves("l2", l2_h, l2),
        "la": halves("la", la_h, la),
        "lse": [load("lse", lse_h, lse)],
    }
    second = {
        "n1": [load("n1", n1_h, n1)],
        "own_att": [load("own_att", own_att_h, own_att)],
        "unit1": [load("unit1", unit1_h, unit1)],
    }
    for m in range(3):
        second["qkv%d" % m] = [load("qkv%d" % m, qkv_h.at[m], qkv_at(m))]
        column = pl.multiple_of(m * width + side * half, 128)
        second["low%d" % m] = [load("low%d" % m, w_qkv.at[:, pl.ds(column, half)], low_at(m))]
    for copies in first.values():
        for copy in copies:
            copy.start()

    def ready(*names):
        for name in names:
            for copy in {**first, **second}[name]:
                copy.wait()

    barrier = pltpu.get_barrier_semaphore()
    for device in (to_core, to_x, to_y, to_z1, to_z2, to_z3):
        pl.semaphore_signal(barrier, inc=1, device_id=device, device_id_type=MESH)
    pl.semaphore_wait(barrier, 6)

    def copies0(j):
        columns = JOBS[j][4]
        for h in range(2):
            yield remote_copy(
                buffers[JOBS[j][5]].at[h, :, :, :, pl.ds(0, columns)], got0[j].at[h], send0.at[j, h], recv0.at[j, h], to_core
            )

    def copies1(j):
        yield remote_copy(own[j].at[0, 1 - x], got1[j].at[0], send1.at[j, 0], recv1.at[j, 0], to_x)
        yield remote_copy(own[j].at[1, 1 - y], got1[j].at[1], send1.at[j, 1], recv1.at[j, 1], to_y)

    def copies2(j):
        yield remote_copy(own[j].at[0, x, 1 - y], got2[j].at[0], send2.at[j, 0], recv2.at[j, 0], to_y)
        yield remote_copy(own[j].at[1, y, 1 - x], got2[j].at[1], send2.at[j, 1], recv2.at[j, 1], to_x)

    def shares(j):
        return (own[j].at[0, x, y], own[j].at[1, y, x])

    def copiesz(j, slot, device):
        for h, share in enumerate(shares(j)):
            yield remote_copy(share, gotz[j].at[slot, h], sendz.at[j, slot, h], recvz.at[j, slot, h], device)

    def copiesq(source, slot, device):
        for h, share in enumerate(shares(QKV)):
            yield remote_copy(
                share if source is None else gotq.at[source, h],
                gotq.at[slot, h], sendq.at[slot, h], recvq.at[slot, h], device,
            )

    def result(j, h, source):
        matrix, row, count, column, columns, _ = JOBS[j]
        return pltpu.make_async_copy(
            source, outs[matrix].at[pl.ds(row + h * count // 2, count // 2), pl.ds(column, columns)], out_sem.at[j, h]
        )

    def result_q(h, which, source):
        count = JOBS[QKV][2] // 2
        at = side if which == 0 else 1 - side
        for m in range(3):
            column = pl.multiple_of(m * width + at * half, 128)
            yield pltpu.make_async_copy(
                source.at[:, pl.ds(m * half, half)],
                outs[0].at[pl.ds(h * count, count), pl.ds(column, half)],
                out_sem.at[QKV + which * 3 + m, h],
            )

    def stage(j, number):
        if number == 0:
            for copy in copies0(j):
                copy.start()
        if number == 1:
            for copy in copies0(j):
                copy.wait()
            add_into(own[j], own[j], got0[j])
            for copy in copies1(j):
                copy.start()
        if number == 2:
            for copy in copies1(j):
                copy.wait()
            add_into(own[j].at[0, x], own[j].at[0, x], got1[j].at[0])
            add_into(own[j].at[1, y], own[j].at[1, y], got1[j].at[1])
            for copy in copies2(j):
                copy.start()
        if number == 3:
            for copy in copies2(j):
                copy.wait()
            for h, share in enumerate(shares(j)):
                add_into(share, share, got2[j].at[h])

            @pl.when(is_end)
            def _():
                for copy in copiesq(None, 0, to_z1) if j == QKV else copiesz(j, 0, to_z1):
                    copy.start()

        if number >= 4 and j == QKV:
            stage_q(number)
            return
        if number == 4:

            @pl.when(is_mid)
            def _():
                for copy in copiesz(j, 0, to_z1):
                    copy.wait_recv()
                for h, share in enumerate(shares(j)):
                    add_into(share, share, gotz[j].at[0, h])
                for copy in copiesz(j, 1, to_z3):
                    copy.start()

            @pl.when(is_end)
            def _():
                for copy in copiesz(j, 0, to_z1):
                    copy.wait_send()

        if number == 5:

            @pl.when(is_mid)
            def _():
                for copy in copiesz(j, 1, to_z3):
                    copy.wait()
                for h, share in enumerate(shares(j)):
                    add_into(share, share, gotz[j].at[1, h])
                for copy in copiesz(j, 0, to_z1):
                    copy.start()
                for h, share in enumerate(shares(j)):
                    result(j, h, share).start()

        if number == 6:

            @pl.when(is_mid)
            def _():
                for copy in copiesz(j, 0, to_z1):
                    copy.wait_send()

            @pl.when(is_end)
            def _():
                for copy in copiesz(j, 0, to_z1):
                    copy.wait_recv()
                for h in range(2):
                    result(j, h, gotz[j].at[0, h]).start()

            for h in range(2):
                result(j, h, gotz[j].at[0, h]).wait()

    def stage_q(number):
        if number == 4:

            @pl.when(is_mid)
            def _():
                for copy in copiesq(None, 1, to_z3):
                    copy.start()
                for copy in copiesq(None, 0, to_z1):
                    copy.wait_recv()
                for copy in copiesq(0, 2, to_z3):
                    copy.start()

            @pl.when(is_end)
            def _():
                for copy in copiesq(None, 0, to_z1):
                    copy.wait_send()

        if number == 5:

            @pl.when(is_mid)
            def _():
                for copy in copiesq(None, 1, to_z3):
                    copy.wait()
                for copy in copiesq(0, 2, to_z3):
                    copy.wait()
                for h, share in enumerate(shares(QKV)):
                    add_into(share, share, gotq.at[2, h])
                    add_into(gotq.at[0, h], gotq.at[0, h], gotq.at[1, h])
                for copy in copiesq(None, 1, to_z1):
                    copy.start()
                for copy in copiesq(0, 0, to_z1):
                    copy.start()
                for h, share in enumerate(shares(QKV)):
                    for copy in result_q(h, 0, share):
                        copy.start()
                    for copy in result_q(h, 1, gotq.at[0, h]):
                        copy.start()

        if number == 6:

            @pl.when(is_mid)
            def _():
                for copy in copiesq(None, 1, to_z1):
                    copy.wait_send()
                for copy in copiesq(0, 0, to_z1):
                    copy.wait_send()

            @pl.when(is_end)
            def _():
                for copy in copiesq(None, 1, to_z1):
                    copy.wait_recv()
                for copy in copiesq(0, 0, to_z1):
                    copy.wait_recv()
                for h in range(2):
                    for copy in result_q(h, 0, gotq.at[0, h]):
                        copy.start()
                    for copy in result_q(h, 1, gotq.at[1, h]):
                        copy.start()

            for h in range(2):
                for which in range(2):
                    for copy in result_q(h, which, gotq.at[0, h]):
                        copy.wait()

    def tick(*pairs):
        for j, number in pairs:
            stage(j, number)

    def gradient(j, mine, lhs, rhs):
        _, row, count, column, columns, buffer = JOBS[j]
        target = own[j] if mine else buffers[buffer]
        left = lhs[1 if mine else 0, :, pl.ds(row, count), :].reshape(4 * count, lhs.shape[3])
        step = 512 if columns % 512 == 0 else 384
        for c in range(0, columns, step):
            right = rhs(c) if callable(rhs) else rhs[:, pl.ds(column + c, step)]
            value = dot(left, right).astype(low)
            for chip in range(4):
                cy, cx = chip // 2, chip % 2
                for h in range(2):
                    i, k = (cx, cy) if h == 0 else (cy, cx)
                    start = chip * count + h * count // 2
                    target[h, i, k, :, pl.ds(c, step)] = value[start : start + count // 2]

    def both(j, lhs, rhs):
        gradient(j, False, lhs, rhs)
        stage(j, 0)
        gradient(j, True, lhs, rhs)

    def put_vector(row, start, value):
        at = 0
        while at < value.shape[1]:
            line, column = row + (start + at) // width, (start + at) % width
            take = min(value.shape[1] - at, width - column)
            vec_out[line : line + 1, column : column + take] = value[:, at : at + take]
            at += take

    def total(value):
        return jnp.sum(value.astype(jnp.float32), axis=0, keepdims=True)

    chunk = 32

    def chunks(body, carry):
        def step(k, carry):
            return body(pl.ds(pl.multiple_of(k * chunk, chunk), chunk), carry)

        return lax.fori_loop(0, rows // chunk, step, carry)

    zero_row = jnp.zeros((1, width), jnp.float32)

    def norm_back(e, one, inverse, gain):
        scaled = e * gain
        return inverse * (
            scaled
            - jnp.mean(scaled, axis=-1, keepdims=True)
            - one * jnp.mean(scaled * one, axis=-1, keepdims=True)
        )

    def norm_pass(unit, inv, gain_row, base, target, low_target, sums):
        def body(at, carry):
            e = e_v[at, :]
            one = unit[at, :].astype(jnp.float32)
            value = base(at) + norm_back(e, one, inv[at, :], pack[gain_row : gain_row + 1, :])
            target[at, :] = value
            rounded = value.astype(low)
            low_target[at, :] = rounded
            return (carry[0] + total(e * one), carry[1] + total(e), carry[2] + total(rounded))

        for row, value in zip(sums, chunks(body, (zero_row,) * 3)):
            put_vector(row, 0, value)

    vec_out[...] = jnp.zeros_like(vec_out)
    ready("cot_a")

    def mask(at, carry):
        value = (vis[at, :] * cot_a[at, :].astype(jnp.float32)).astype(low)
        cot_a[at, :] = value
        return carry + total(value)

    put_vector(ALIGN_BIAS, 0, chunks(mask, jnp.zeros((1, cot_a.shape[1]), jnp.float32)))
    ready("l3")
    both(ALIGN, l3, cot_a)
    ready("align")
    for c in range(0, width, 256):
        e_v[:, pl.ds(c, 256)] = dot(cot_a[...], align_v[pl.ds(c, 256), :], NT)
    tick((ALIGN, 1))
    ready("unit3", "cot_b")
    norm_pass(
        unit3, inv3, N3_GAIN, lambda at: vis[at, :] * cot_b[at, :].astype(jnp.float32), mid_v, low_d,
        (N3_GAIN, N3_BIAS, DOWN_BIAS),
    )

    ready("down", "slope")
    for c in range(0, wide, TILE):
        at = pl.ds(c, TILE)
        value = (dot(low_d[...], down_v[at, :], NT) * slope[:, at].astype(jnp.float32)).astype(low)
        slope[:, at] = value
        put_vector(UP_BIAS, c, total(value))
    ready("ld")
    both(DOWN0, ld, low_d)
    tick((ALIGN, 2), (DOWN0, 1))
    both(DOWN1, ld, low_d)
    for name in ("n1", "own_att", "unit1"):
        for copy in second[name]:
            copy.start()
    ready("up")
    for c in range(0, width, 256):
        e_v[:, pl.ds(c, 256)] = dot(slope[...], up_v[pl.ds(c, 256), :], NT)
    for m in range(3):
        for name in ("qkv%d" % m, "low%d" % m):
            for copy in second[name]:
                copy.start()
    ready("unit2")
    norm_pass(
        unit2, inv2, N2_GAIN, lambda at: mid_v[at, :], mid_v, low_o, (N2_GAIN, N2_BIAS, OUT_BIAS)
    )
    ready("out")
    for h in range(2):
        value = dot(low_o[...], out_v[pl.ds(h * half, half), :], NT).astype(low)
        for c in range(2):
            in_src[c, h] = value[c * piece : (c + 1) * piece]

    def in_copy(slot):
        return remote_copy(
            in_src.at[slot // 2, lax.rem(slot, 2)], grad_att.at[z], in_send.at[slot], in_recv.at[z], (dp, slot)
        )

    def start_in(number, _):
        in_copy(lax.rem(z + number, 4)).start()
        return 0

    lax.fori_loop(1, 4, start_in, 0)
    grad_att[z] = in_src[clip, side]
    tick((ALIGN, 3), (DOWN0, 2), (DOWN1, 1))
    ready("l2")
    both(UP0, l2, slope)
    both(UP1, l2, slope)
    ready("n1", "lse")
    for c in range(0, width, 128):
        flipped = n1[:, pl.ds(c, 128)].T
        at = 0
        while at < 128:
            share, inside = (c + at) // 96, (c + at) % 96
            take = min(128 - at, 96 - inside)
            n1s[share % 2, share // 2, pl.ds(inside, take), :] = flipped[at : at + take]
            at += take
    lse_rows[...] = lse[...].T[:8]
    tick((ALIGN, 4), (DOWN0, 3), (DOWN1, 2), (UP0, 1))
    ready("la")
    both(OUT, la, low_o)

    def settle(number, _):
        slot = lax.rem(z + number, 4)
        in_copy(slot).wait_send()
        remote_copy(
            in_src.at[0, 0], grad_att.at[slot], in_send.at[slot], in_recv.at[slot], (dp, slot)
        ).wait_recv()
        return 0

    lax.fori_loop(1, 4, settle, 0)
    ready("own_att", "qkv0", "qkv1", "qkv2")
    lane = lax.broadcasted_iota(jnp.int32, (1, 128), 1)
    low_lane = lane < 64

    def spread_of(slot, _):
        where = pl.ds(pl.multiple_of(slot * piece, piece), piece)
        stats = jnp.zeros((piece, 128), jnp.float32)
        for t in range(half // 128):
            at = pl.ds(t * 128, 128)
            product = grad_att[slot, :, at].astype(jnp.float32) * own_att[where, at].astype(jnp.float32)
            for a in range(2):
                mine = low_lane if a == 0 else jnp.logical_not(low_lane)
                value = jnp.sum(jnp.where(mine, product, 0.0), axis=-1, keepdims=True)
                stats = jnp.where(lane == 2 * t + a, value, stats)
        lse[where, :] = stats
        return 0

    lax.fori_loop(0, 4, spread_of, 0)
    spread_rows[...] = lse[...].T[:8]
    q_ref, k_ref, v_ref = (qkv_at(m) for m in range(3))
    gq_ref, gk_ref, gv_ref = (grad_at(m) for m in range(3))

    def pair(t):
        at = pl.ds(t * 128, 128)
        grad_q[...] = jnp.zeros_like(grad_q)
        queries = q_ref[:, at]
        grads = grad_att[:, :, at].reshape(4 * piece, 128)

        def block(b, _):
            keys_at = pl.ds(pl.multiple_of(b * KEY_BLOCK, KEY_BLOCK), KEY_BLOCK)
            keys = k_ref[keys_at, at]
            values = v_ref[keys_at, at]
            grad_k = jnp.zeros((KEY_BLOCK, 128), jnp.float32)
            grad_v = jnp.zeros((KEY_BLOCK, 128), jnp.float32)
            grad_queries = grad_q[...]
            for a in range(2):
                mine = low_lane if a == 0 else jnp.logical_not(low_lane)
                zero = jnp.zeros((), low)
                q_mine = jnp.where(mine, queries, zero)
                g_mine = jnp.where(mine, grads, zero)
                k_mine = jnp.where(mine, keys, zero)
                row = pl.ds(2 * t + a, 1)
                scores = dot(keys, q_mine, NT) + key_bias[keys_at, :]
                probs = jnp.exp(scores - lse_rows[row, :])
                back = probs * (dot(values, g_mine, NT) - spread_rows[row, :])
                back = back.astype(low)
                grad_v = grad_v + dot(probs.astype(low), g_mine)
                grad_k = grad_k + dot(back, q_mine)
                grad_queries = grad_queries + dot(back, k_mine, TN)
            grad_q[...] = grad_queries
            gk_ref[keys_at, at] = grad_k.astype(low)
            gv_ref[keys_at, at] = grad_v.astype(low)
            return 0

        lax.fori_loop(0, 4 * piece // KEY_BLOCK, block, 0)
        gq_ref[:, at] = (grad_q[...] * 0.125).astype(low)

    pair(0)
    tick((ALIGN, 5), (DOWN0, 4), (DOWN1, 3), (UP0, 2), (UP1, 1))
    pair(1)
    tick((ALIGN, 6), (DOWN0, 5), (DOWN1, 4), (UP0, 3), (UP1, 2), (OUT, 1))
    pair(2)

    def half_grads(mine):
        left = n1s[core if mine else 1 - core].reshape(4 * 96, 4 * piece)
        target = own[QKV] if mine else buffers[JOBS[QKV][5]]
        for m in range(3):
            value = dot(left, grad_at(m)[...]).astype(low)
            for chip in range(4):
                cy, cx = chip // 2, chip % 2
                for h in range(2):
                    i, k = (cx, cy) if h == 0 else (cy, cx)
                    start = chip * 96 + h * 48
                    target[h, i, k, :, pl.ds(m * half, half)] = value[start : start + 48]

    half_grads(False)
    stage(QKV, 0)
    ready("low0", "low1", "low2", "unit1")

    def pair_copy():
        return remote_copy(e_at(partner), from_pair, pair_send, pair_recv, to_z1)

    def end_copy(which, slot):
        return remote_copy(e_at(slot), from_end.at[which], end_send.at[which], end_recv.at[which], to_z1)

    def out_copy(which, slot):
        return remote_copy(e_at(slot), total_in, out_send.at[which], out_recv, (dp, slot))

    mid_near = 2 - clip
    mid_far = 3 - 3 * clip
    targets = (mid_far, mid_near)

    def part_of(number, carry):
        slot = jnp.where(
            number == 0, mid_far, jnp.where(number == 1, mid_near, jnp.where(number == 2, partner, z))
        )
        where = pl.ds(pl.multiple_of(slot * piece, piece), piece)
        value = dot(gq_ref[where, :], low_at(0)[...], NT)
        value = value + dot(gk_ref[where, :], low_at(1)[...], NT)
        value = value + dot(gv_ref[where, :], low_at(2)[...], NT)
        e_at(slot)[...] = value.astype(low)

        @pl.when(number == 3)
        def _():
            e_v[pl.ds(pl.multiple_of(clip * piece, piece), piece), :] = value

        for which in range(2):

            @pl.when(is_end & (number == which))
            def _():
                end_copy(which, targets[which]).start()

        @pl.when(number == 2)
        def _():
            pair_copy().start()

        return (carry[0] + total(value * unit1[where, :].astype(jnp.float32)), carry[1] + total(value))

    for row, value in zip((N1_GAIN, N1_BIAS), lax.fori_loop(0, 4, part_of, (zero_row, zero_row))):
        put_vector(row, 0, value)
    for row, ref in ((Q_BIAS, gq_ref), (V_BIAS, gv_ref)):
        value = total(ref[...])
        value = jnp.concatenate([value, value], axis=1)
        spot = lax.broadcasted_iota(jnp.int32, (1, width), 1)
        put_vector(row, 0, jnp.where((spot < half) == (side == 0), value, 0.0))

    vec_devices = (to_core, to_x, to_y, to_z1, to_z2)

    def vec_copy(k):
        return remote_copy(vec_out, vec_got.at[k], vsend.at[k], vrecv.at[k], vec_devices[k])

    def vec_add(k):
        vec_copy(k).wait()
        vec_out[...] = vec_out[...] + vec_got[k]

    vec_copy(0).start()
    half_grads(True)
    tick((DOWN0, 6), (DOWN1, 5), (UP0, 4), (UP1, 3), (OUT, 2), (QKV, 1))
    vec_add(0)
    vec_copy(1).start()

    @pl.when(is_mid)
    def _():
        for which in range(2):
            end_copy(which, targets[which]).wait_recv()
            add_into(e_at(targets[which]), e_at(targets[which]), from_end.at[which])
            out_copy(which, targets[which]).start()

    tick((DOWN1, 6), (UP0, 5), (UP1, 4), (OUT, 3), (QKV, 2))
    vec_add(1)
    vec_copy(2).start()
    tick((UP0, 6), (UP1, 5), (OUT, 4), (QKV, 3))
    vec_add(2)
    vec_copy(3).start()
    tick((UP1, 6), (OUT, 5), (QKV, 4))
    vec_add(3)
    vec_copy(4).start()
    tick((OUT, 6), (QKV, 5))
    vec_add(4)

    pair_copy().wait()
    mine = pl.ds(pl.multiple_of(clip * piece, piece), piece)
    theirs = pl.ds(pl.multiple_of((1 - clip) * piece, piece), piece)
    e_v[mine, :] = e_v[mine, :] + from_pair[...].astype(jnp.float32)
    out_copy(0, partner).wait_recv()
    e_v[theirs, :] = total_in[...].astype(jnp.float32)

    def last(at, carry):
        one, inverse = norm_rows(tok[at, :].astype(jnp.float32))
        value = mid_v[at, :] + norm_back(e_v[at, :], one, inverse, pack[N1_GAIN : N1_GAIN + 1, :])
        grad_tokens[at, :] = value.astype(low)
        return carry

    chunks(last, 0)
    tick((QKV, 6))

    @pl.when(is_mid)
    def _():
        for which in range(2):
            out_copy(which, targets[which]).wait_send()

    @pl.when(is_end)
    def _():
        for which in range(2):
            end_copy(which, targets[which]).wait_send()


def back(small, large, out_rows):
    tok = small[5]
    rows, width = tok.shape
    half, piece = width // 2, rows // 2
    w_align, w_down, w_up, w_out, w_qkv = large[-5:]
    wide, align = w_up.shape[1], w_align.shape[1]
    low, wide_type = jnp.bfloat16, jnp.float32
    vmem = pl.BlockSpec(memory_space=pltpu.VMEM)
    hbm = pl.BlockSpec(memory_space=pl.ANY)
    dma = pltpu.SemaphoreType.DMA
    shapes = [(2, 2, 2, job[2] // 2, job[4]) for job in JOBS]
    v = pltpu.VMEM
    scratch = (
        [v(shape, low) for shape in shapes]
        + [v(shape, low) for shape in shapes]
        + [v(shape[1:], low) for shape in shapes]
        + [v(shape[2:], low) for shape in shapes]
        + [v(shape[1:], low) for shape in shapes[:-1]]
        + [v((3,) + shapes[-1][2:], low)]
        + [v(shape, low) for shape in SEND_SHAPES]
        + [v((5, PACK_ROWS, width), wide_type)]
        + [
            v(w_align.shape, low), v(w_down.shape, low), v(w_up.shape, low), v(w_out.shape, low),
            v((rows, align), low), v((rows, width), low), v((rows, width), low), v((rows, width), low),
            v((rows, wide), low),
            v((2, 4, width // 8, rows), low), v((2, 4, wide // 8, rows), low),
            v((2, 4, width // 8, rows), low), v((2, 4, width // 8, rows), low),
            v((rows, width), wide_type), v((rows, width), wide_type), v((rows, width), low), v((rows, width), low),
            v((2, 2, piece, half), low), v((4, piece, half), low), v((2, 4, width // 8, 4 * piece), low),
            v((4 * piece, 128), wide_type), v((8, 4 * piece), wide_type), v((8, 4 * piece), wide_type),
            v((4 * piece, 128), wide_type),
            v((piece, width), low), v((2, piece, width), low), v((piece, width), low),
        ]
        + [dma((len(LOADS),))]
        + [dma((COUNT, 2))] * 6
        + [dma((COUNT, 2, 2))] * 2
        + [dma((3, 2))] * 2
        + [dma((COUNT + 5, 2))]
        + [dma((5,))] * 2
        + [dma((4,))] * 2
        + [dma(())] * 2
        + [dma((2,))] * 2
        + [dma((2,)), dma(())]
    )
    struct = jax.ShapeDtypeStruct
    return pl.pallas_call(
        back_kernel,
        name="back",
        out_shape=[struct((rows, width), low), struct((PACK_ROWS, width), wide_type)]
        + [struct(shape, low) for shape in out_rows],
        in_specs=[vmem] * len(small) + [hbm] * len(large),
        out_specs=[vmem, vmem] + [hbm] * 5,
        scratch_shapes=scratch,
        compiler_params=pltpu.CompilerParams(
            collective_id=0, has_side_effects=True, vmem_limit_bytes=62 * 2**20
        ),
    )(*small, *large)


def norm_forward(values, gain, shift):
    center = values - jnp.mean(values, axis=-1, keepdims=True)
    inverse = lax.rsqrt(jnp.mean(center * center, axis=-1, keepdims=True) + EPSILON)
    normed = center * inverse
    return (normed * gain + shift, normed, inverse)


def norm_backward(upstream, normed, inverse, gain):
    scaled = upstream * gain
    inner = (
        scaled
        - jnp.mean(scaled, axis=-1, keepdims=True)
        - normed * jnp.mean(scaled * normed, axis=-1, keepdims=True)
    )
    return (inverse * inner, jnp.sum(upstream * normed, axis=0), jnp.sum(upstream, axis=0))


def gelu_slope(values):
    return (
        0.5 * (1.0 + lax.erf(values * SQRT_HALF))
        + values * jnp.exp(-0.5 * values * values) * INV_ROOT_TAU
    )


def weight_grad(left, right):
    return lax.dot_general(
        left, right, (((0,), (0,)), ((), ())), preferred_element_type=jnp.float32
    )


def input_grad(upstream, weight):
    return lax.dot_general(
        upstream, weight, (((1,), (1,)), ((), ())), preferred_element_type=jnp.float32
    )


def masked_scores(query_heads, key_heads, key_valid, scale):
    scores = (
        jnp.einsum("cqhd,ckhd->chqk", query_heads, key_heads, preferred_element_type=jnp.float32)
        * scale
    )
    return jnp.where(key_valid, scores, -1e30)


def column_sum(values):
    return jnp.sum(values, axis=0, dtype=jnp.float32)


def local(
    tokens,
    frame_counts,
    slot_mask,
    norm1_gain,
    norm1_bias,
    w_qkv,
    q_bias,
    v_bias,
    w_out,
    out_bias,
    norm2_gain,
    norm2_bias,
    w_up,
    up_bias,
    w_down,
    down_bias,
    norm3_gain,
    norm3_bias,
    w_align,
    align_bias,
    cot_block,
    cot_align,
):
    clip_count, frame_dev, slot_count, width = tokens.shape
    align_width = w_align.shape[1]
    head_size = width // HEADS
    scale = 1.0 / math.sqrt(head_size)
    row_count = clip_count * frame_dev * slot_count
    cycle_pos = lax.axis_index("blk")
    frame_ids = cycle_pos * frame_dev + jnp.arange(frame_dev, dtype=jnp.int32)
    own_slots = lax.dynamic_slice_in_dim(slot_mask, cycle_pos * frame_dev, frame_dev, 1)
    own_mask = (frame_ids[None, :, None] < frame_counts[:, None, None]) & (own_slots > 0)
    visible = own_mask.astype(jnp.float32).reshape(row_count, 1)
    all_frames = jnp.arange(slot_mask.shape[1], dtype=jnp.int32)
    key_valid = (all_frames[None, :, None] < frame_counts[:, None, None]) & (slot_mask > 0)
    key_valid = key_valid.reshape(clip_count, 1, 1, -1)
    inputs = tokens.reshape(row_count, width).astype(jnp.float32)
    normed_one, unit_one, inverse_one = norm_forward(inputs, norm1_gain, norm1_bias)
    normed1 = normed_one.astype(jnp.bfloat16)
    projected = jnp.dot(normed1, w_qkv, preferred_element_type=jnp.float32)
    queries = (projected[:, :width] + q_bias).astype(jnp.bfloat16)
    keys_local = projected[:, width : 2 * width].astype(jnp.bfloat16)
    values_local = (projected[:, 2 * width :] + v_bias).astype(jnp.bfloat16)
    block_shape = (clip_count, frame_dev, slot_count, width)
    heads_shape = (clip_count, -1, HEADS, head_size)
    keys_all, values_all = (
        lax.all_gather(keys_local.reshape(block_shape), "blk", axis=1, tiled=True),
        lax.all_gather(values_local.reshape(block_shape), "blk", axis=1, tiled=True),
    )
    key_heads = keys_all.reshape(heads_shape)
    value_heads = values_all.reshape(heads_shape)
    query_heads = queries.reshape(heads_shape)
    scores = masked_scores(query_heads, key_heads, key_valid, scale)
    top = jnp.max(scores, axis=-1, keepdims=True)
    expo = jnp.exp(scores - top)
    total = jnp.sum(expo, axis=-1, keepdims=True)
    probs_low = (expo / total).astype(jnp.bfloat16)
    attended = jnp.einsum(
        "chqk,ckhd->cqhd", probs_low, value_heads, preferred_element_type=jnp.float32
    )
    attended = attended.astype(jnp.bfloat16).reshape(row_count, width)
    mid = inputs + jnp.dot(attended, w_out, preferred_element_type=jnp.float32) + out_bias
    normed_two, unit_two, inverse_two = norm_forward(mid, norm2_gain, norm2_bias)
    normed2 = normed_two.astype(jnp.bfloat16)
    hidden = jnp.dot(normed2, w_up, preferred_element_type=jnp.float32) + up_bias
    active = jax.nn.gelu(hidden, approximate=False).astype(jnp.bfloat16)
    after = mid + jnp.dot(active, w_down, preferred_element_type=jnp.float32) + down_bias
    block_out = (visible * after).astype(jnp.bfloat16).reshape(block_shape)
    normed_three, unit_three, inverse_three = norm_forward(after, norm3_gain, norm3_bias)
    normed3 = normed_three.astype(jnp.bfloat16)
    target = jnp.dot(normed3, w_align, preferred_element_type=jnp.float32) + align_bias
    aligned = (
        (visible * target)
        .astype(jnp.bfloat16)
        .reshape(clip_count, frame_dev, slot_count, align_width)
    )
    back_align = (visible * cot_align.reshape(row_count, align_width).astype(jnp.float32)).astype(
        jnp.bfloat16
    )
    grad_align_bias = column_sum(back_align)
    grad_w_align = weight_grad(normed3, back_align)
    back_norm3, grad_norm3_gain, grad_norm3_bias = norm_backward(
        input_grad(back_align, w_align), unit_three, inverse_three, norm3_gain
    )
    back_after = visible * cot_block.reshape(row_count, width).astype(jnp.float32) + back_norm3
    back_down = back_after.astype(jnp.bfloat16)
    grad_down_bias = column_sum(back_down)
    grad_w_down = weight_grad(active, back_down)
    back_up = (input_grad(back_down, w_down) * gelu_slope(hidden)).astype(jnp.bfloat16)
    grad_up_bias = column_sum(back_up)
    grad_w_up = weight_grad(normed2, back_up)
    back_norm2, grad_norm2_gain, grad_norm2_bias = norm_backward(
        input_grad(back_up, w_up), unit_two, inverse_two, norm2_gain
    )
    back_mid = back_after + back_norm2
    back_out = back_mid.astype(jnp.bfloat16)
    grad_out_bias = column_sum(back_out)
    grad_w_out = weight_grad(attended, back_out)
    back_attended = input_grad(back_out, w_out).astype(jnp.bfloat16).reshape(heads_shape)
    scores = masked_scores(query_heads, key_heads, key_valid, scale)
    probs = jnp.exp(scores - top) / total
    probs_low = probs.astype(jnp.bfloat16)
    back_probs = jnp.einsum(
        "cqhd,ckhd->chqk", back_attended, value_heads, preferred_element_type=jnp.float32
    )
    spread = jnp.sum(probs * back_probs, axis=-1, keepdims=True)
    back_scores = (probs * (back_probs - spread)).astype(jnp.bfloat16)
    back_queries = (
        jnp.einsum("chqk,ckhd->cqhd", back_scores, key_heads, preferred_element_type=jnp.float32)
        * scale
    )
    back_queries = back_queries.astype(jnp.bfloat16).reshape(row_count, width)
    value_terms = jnp.einsum(
        "chqk,cqhd->ckhd", probs_low, back_attended, preferred_element_type=jnp.float32
    )
    key_terms = (
        jnp.einsum("chqk,cqhd->ckhd", back_scores, query_heads, preferred_element_type=jnp.float32)
        * scale
    )
    whole_shape = (clip_count, -1, slot_count, width)
    key_share, value_share = (
        lax.psum_scatter(
            key_terms.reshape(whole_shape).astype(jnp.bfloat16),
            "blk",
            scatter_dimension=1,
            tiled=True,
        ).astype(jnp.float32),
        lax.psum_scatter(
            value_terms.reshape(whole_shape).astype(jnp.bfloat16),
            "blk",
            scatter_dimension=1,
            tiled=True,
        ).astype(jnp.float32),
    )
    back_keys = key_share.astype(jnp.bfloat16).reshape(row_count, width)
    back_values = value_share.astype(jnp.bfloat16).reshape(row_count, width)
    grad_q_bias = column_sum(back_queries)
    grad_v_bias = column_sum(back_values)
    combined = jnp.concatenate([back_queries, back_keys, back_values], axis=1)
    grad_w_qkv = weight_grad(normed1, combined)
    back_norm1, grad_norm1_gain, grad_norm1_bias = norm_backward(
        input_grad(combined, w_qkv), unit_one, inverse_one, norm1_gain
    )
    grad_tokens = (back_mid + back_norm1).astype(jnp.bfloat16).reshape(block_shape)
    vector_total = lax.psum(
        (
            grad_norm1_gain,
            grad_norm1_bias,
            grad_q_bias,
            grad_v_bias,
            grad_out_bias,
            grad_norm2_gain,
            grad_norm2_bias,
            grad_up_bias,
            grad_down_bias,
            grad_norm3_gain,
            grad_norm3_bias,
            grad_align_bias,
        ),
        ("dp", "blk"),
    )
    row_part = (
        lax.psum_scatter(grad_w_qkv, "dp", scatter_dimension=0, tiled=True),
        lax.psum_scatter(grad_w_out, "dp", scatter_dimension=0, tiled=True),
        lax.psum_scatter(grad_w_up, "dp", scatter_dimension=0, tiled=True),
        lax.psum_scatter(grad_w_down, "dp", scatter_dimension=0, tiled=True),
        lax.psum_scatter(grad_w_align, "dp", scatter_dimension=0, tiled=True),
    )
    matrix_total = (
        lax.psum(row_part[0].astype(jnp.bfloat16), "blk").astype(jnp.float32),
        lax.psum(row_part[1].astype(jnp.bfloat16), "blk").astype(jnp.float32),
        lax.psum(row_part[2].astype(jnp.bfloat16), "blk").astype(jnp.float32),
        lax.psum(row_part[3].astype(jnp.bfloat16), "blk").astype(jnp.float32),
        lax.psum(row_part[4].astype(jnp.bfloat16), "blk").astype(jnp.float32),
    )
    return (
        block_out,
        aligned,
        grad_tokens,
        vector_total[0],
        vector_total[1],
        matrix_total[0],
        vector_total[2],
        vector_total[3],
        matrix_total[1],
        vector_total[4],
        vector_total[5],
        vector_total[6],
        matrix_total[2],
        vector_total[7],
        matrix_total[3],
        vector_total[8],
        vector_total[9],
        vector_total[10],
        matrix_total[4],
        vector_total[11],
    )


def local_kernels(
    tokens, frame_counts, slot_mask, norm1_gain, norm1_bias, w_qkv, q_bias, v_bias, w_out, out_bias, norm2_gain,
    norm2_bias, w_up, up_bias, w_down, down_bias, norm3_gain, norm3_bias, w_align, align_bias, cot_block, cot_align,
):
    clip_count, frame_dev, slot_count, width = tokens.shape
    wide, align = w_up.shape[1], w_align.shape[1]
    piece = frame_dev * slot_count
    rows = clip_count * piece
    pos = lax.axis_index("blk")
    all_frames = jnp.arange(slot_mask.shape[1], dtype=jnp.int32)
    valid = (all_frames[None, :, None] < frame_counts[:, None, None]) & (slot_mask > 0)
    own_clip = lax.dynamic_index_in_dim(valid, pos // 2, 0, False)
    key_bias = jnp.where(own_clip, 0.0, -1e30).astype(jnp.float32).reshape(1, -1)
    own_mask = lax.dynamic_slice_in_dim(valid, pos * frame_dev, frame_dev, 1)
    vis = own_mask.astype(jnp.float32).reshape(rows, 1)
    vectors = [
        norm1_gain, norm1_bias, q_bias, v_bias, out_bias, norm2_gain, norm2_bias, down_bias, norm3_gain, norm3_bias,
        up_bias, align_bias,
    ]
    sizes = [vector.shape[0] for vector in vectors]
    starts = [sum(sizes[:k]) for k in range(len(sizes))]
    filler = jnp.zeros((PACK_ROWS * width - sum(sizes),), jnp.float32)
    pack = jnp.concatenate(vectors + [filler]).reshape(PACK_ROWS, width)
    tok = tokens.reshape(rows, width)
    att, n1, unit1, qkv, own_att, lse = attend(tokens.reshape(clip_count, piece, width), pack, w_qkv, key_bias)
    block_out, align_out, act_t, slope, unit2, inv2, unit3, inv3, normed2_t, normed3_t, att_t = feed(
        tok, att, vis, pack, w_out, w_up, w_down, w_align
    )

    def by_share(array):
        return array.reshape(4, 2, array.shape[0] // 8, rows)

    grad_tokens, vec, *shares = back(
        (vis, pack, key_bias.reshape(-1, 1), inv2, inv3, tok),
        (
            cot_align.reshape(rows, align), cot_block.reshape(rows, width), unit2, unit3, slope, by_share(normed3_t),
            by_share(act_t), by_share(normed2_t), by_share(att_t), qkv, own_att.reshape(4 * piece, width // 2), lse,
            n1.reshape(4 * piece, width), unit1.reshape(4 * piece, width), w_align, w_down, w_up, w_out, w_qkv,
        ),
        [(w.shape[0] // 8, w.shape[1]) for w in (w_qkv, w_out, w_up, w_down, w_align)],
    )
    flat = vec.reshape(-1)
    (
        grad_norm1_gain, grad_norm1_bias, grad_q_bias, grad_v_bias, grad_out_bias, grad_norm2_gain, grad_norm2_bias,
        grad_down_bias, grad_norm3_gain, grad_norm3_bias, grad_up_bias, grad_align_bias,
    ) = (flat[start : start + size] for start, size in zip(starts, sizes))
    matrices = [share.astype(jnp.float32) for share in shares]
    return (
        block_out.reshape(tokens.shape),
        align_out.reshape(cot_align.shape),
        grad_tokens.reshape(tokens.shape),
        grad_norm1_gain,
        grad_norm1_bias,
        matrices[0],
        grad_q_bias,
        grad_v_bias,
        matrices[1],
        grad_out_bias,
        grad_norm2_gain,
        grad_norm2_bias,
        matrices[2],
        grad_up_bias,
        matrices[3],
        grad_down_bias,
        grad_norm3_gain,
        grad_norm3_bias,
        matrices[4],
        grad_align_bias,
    )


def solution(mesh):
    in_specs = (
        P("dp", "blk", None, None),
        P("dp"),
        P("dp", None, None),
        P(),
        P(),
        P(),
        P(),
        P(),
        P(),
        P(),
        P(),
        P(),
        P(),
        P(),
        P(),
        P(),
        P(),
        P(),
        P(),
        P(),
        P("dp", "blk", None, None),
        P("dp", "blk", None, None),
    )
    out_specs = (
        P("dp", "blk", None, None),
        P("dp", "blk", None, None),
        P("dp", "blk", None, None),
        P(),
        P(),
        P("dp", None),
        P(),
        P(),
        P("dp", None),
        P(),
        P(),
        P(),
        P("dp", None),
        P(),
        P("dp", None),
        P(),
        P(),
        P(),
        P("dp", None),
        P(),
    )
    sizes = (mesh.shape["dp"], mesh.shape["blk"])
    run = local_kernels if sizes == GRID else local
    return jax.shard_map(run, mesh=mesh, in_specs=in_specs, out_specs=out_specs, check_vma=False)
```

```python
import math

import jax
import jax.numpy as jnp
from jax import lax
from jax.experimental import pallas as pl
from jax.experimental.pallas import tpu as pltpu
from jax.sharding import PartitionSpec as P

HEADS = 12


EPSILON = 1e-06
SQRT_HALF = 0.7071067811865476
INV_ROOT_TAU = 0.3989422804014327
MESH = pl.DeviceIdType.MESH
GRID = (8, 4)


NT = (((1,), (1,)), ((), ()))
TN = (((0,), (0,)), ((), ()))
CHUNKS = 2


def dot(left, right, dims=(((1,), (0,)), ((), ()))):
    return lax.dot_general(left, right, dims, preferred_element_type=jnp.float32)


def remote_copy(src, dst, send, recv, device):
    return pltpu.make_async_remote_copy(
        src_ref=src, dst_ref=dst, send_sem=send, recv_sem=recv, device_id=device, device_id_type=MESH
    )


N1_GAIN, N1_BIAS, Q_BIAS, V_BIAS, OUT_BIAS, N2_GAIN, N2_BIAS, DOWN_BIAS, N3_GAIN, N3_BIAS, UP_BIAS, ALIGN_BIAS = (
    0, 1, 2, 3, 4, 5, 6, 7, 8, 9, 10, 14,
)
PACK_ROWS = 16
TILE = 512


def row_of(pack, row, start, size):
    width = pack.shape[1]
    parts = []
    while size > 0:
        line, column = row + start // width, start % width
        take = min(size, width - column)
        parts.append(pack[line : line + 1, column : column + take])
        start, size = start + take, size - take
    return parts[0] if len(parts) == 1 else jnp.concatenate(parts, axis=1)


def fill_pack(pack, rows, refs):
    width = pack.shape[1]
    for row, ref in zip(rows, refs):
        for start in range(0, ref.shape[0], width):
            size = min(width, ref.shape[0] - start)
            line = row + start // width
            pack[line : line + 1, 0:size] = ref[pl.ds(start, size)].reshape(1, size)


def norm_rows(values):
    center = values - jnp.mean(values, axis=-1, keepdims=True)
    inverse = lax.rsqrt(jnp.mean(center * center, axis=-1, keepdims=True) + EPSILON)
    return center * inverse, inverse


def put_visible(vis, visible_t, z):
    piece = vis.shape[0] // 2
    for c in range(2):
        where = pl.ds(pl.multiple_of(z * piece, piece), piece)
        vis[pl.ds(c * piece, piece), :] = visible_t[where, c : c + 1]


JOBS = (
    (4, 0, 96, 0, 1024, 2048),
    (3, 0, 96, 0, 768, 0),
    (3, 96, 96, 0, 768, 768),
    (3, 192, 96, 0, 768, 1536),
    (3, 288, 96, 0, 768, 2304),
    (2, 0, 96, 0, 768, 0),
    (2, 0, 96, 768, 768, 768),
    (2, 0, 96, 1536, 768, 1536),
    (2, 0, 96, 2304, 768, 2304),
    (1, 0, 96, 0, 768, 0),
    (0, 0, 96, 0, 384, 768),
    (0, 0, 96, 384, 384, 1152),
    (0, 0, 96, 768, 384, 1536),
)
COUNT = len(JOBS)
PLAIN = 10
KEY_BLOCK = 256
PLAN = (
    (0, "far"), (0, 0), (0, "own"), "e3", "norm3", (0, 1), "feed0", "feed1", "feed2", "feed3", "feed4", "feed5",
    (1, "far"), (1, 0), (1, "own"), (2, "far"), (2, 0), (2, "own"), (0, 2), "e20", "e21", (1, 1), "e22", "norm2",
    (2, 1), (0, 3), "back_att", (3, "far"), (3, 0), (3, "own"), (4, "far"), (4, 0), (1, 2), (4, "own"), (3, 1),
    (5, "far"), (5, 0), (2, 2), (4, 1), (0, 4), (5, "own"), (6, "far"), (6, 0), (1, 3), (6, "own"), (7, "far"),
    (7, 0), (5, 1), (7, "own"), (8, "far"), (8, 0), (8, "own"), (3, 2), (9, "far"), (9, 0), (9, "own"), (2, 3),
    (6, 1), (4, 2), (7, 1), "settle", "spread", "pair00", (5, 2), (1, 4), (0, 5), (3, 3), "pair01", (8, 1), (6, 2),
    (2, 4), "pair02", (4, 3), (1, 5), (3, 4), "pair10", (7, 2), (9, 1), (0, 6), "pair11", (2, 5), (5, 3), (4, 4),
    (1, 6), "pair12", (8, 2), (3, 5), "pair20", (6, 3), (2, 6), (5, 4), (4, 5), "pair21", (7, 3), "pair22", (9, 2),
    (3, 6), (6, 4), (10, "far"), (10, 0), (5, 5), (8, 3), (11, "far"), (11, 0), (4, 6), (12, "far"), (12, 0), "dx0",
    "dx1", (9, 3), (7, 4), (10, "own"), (10, 1), (11, "own"), (11, 1), (6, 5), (5, 6), (12, "own"), "dx2", (12, 1),
    (8, 4), "dx3", (10, 2), "sums", "vec0", (7, 5), (11, 2), (6, 6), (12, 2), "vec1", (10, 3), (8, 5), (11, 3),
    "fwd0", (12, 3), "vec2", "vec3", "fwd1", "vec4", (7, 6), (9, 4), "vec5", (8, 6), "norm1", (10, 4), (9, 5),
    (11, 4), (12, 4), (10, 5), (9, 6), (11, 5), (10, 6), (12, 5), (11, 6), (12, 6),
)


def add_into(target, first, second):
    rows = target.shape[-2]

    def body(k, _):
        at = pl.ds(pl.multiple_of(k * 48, 48), 48)
        target[..., at, :] = first[..., at, :] + second[..., at, :]
        return 0

    lax.fori_loop(0, rows // 48, body, 0)


VIS, KEY, INV2, INV3, STATS = 0, 1, 2, 3, 8


def layer_kernel(*refs):
    visible, vectors, refs = refs[0], refs[1:13], refs[13:]
    tok_h, cot_a_h, cot_b_h, w_align, w_down, w_up, w_out, w_qkv = refs[:8]
    block_out, align_out, grad_tokens, vec_out = refs[8:12]
    outs = refs[12:17]
    rest = refs[17:]
    own, got0, got1, got2 = (rest[i * COUNT : (i + 1) * COUNT] for i in range(4))
    rest = rest[4 * COUNT :]
    gotz, gotq = rest[:PLAIN], rest[PLAIN:COUNT]
    rest = rest[COUNT:]
    vec_got = rest[0]
    (
        pack, side_v,
        align_v, down_v, up_v, out_v, low_v, tok, xall, n1, qkv, own_att, att, lse_rows, spread_rows,
        mid_v, e_v, normed, ring, slope, ld, l2, l3, la, unit2, unit3, cot_a, cot_b,
        grad_att, n1s, grad_q,
        load_sem, send0, recv0, send1, recv1, send2, recv2, sendz, recvz, sendq, recvq, out_sem, outq_sem, vsend, vrecv,
        tok_send, tok_recv, att_send, att_recv, in_send, in_recv,
        pair_send, pair_recv, end_send, end_recv, out_send, out_recv, put_sem,
    ) = rest[1:]

    dp = lax.axis_index("dp")
    z = lax.axis_index("blk")
    core = lax.rem(dp, 2)
    x = lax.rem(dp // 2, 2)
    y = dp // 4
    clip, side = z // 2, lax.rem(z, 2)
    to_core = (dp + 1 - 2 * core, z)
    to_x = (dp + 2 - 4 * x, z)
    to_y = (dp + 4 - 8 * y, z)
    partner = z + 1 - 2 * side
    to_z1 = (dp, partner)
    to_z2 = (dp, lax.rem(z + 2, 4))
    to_z3 = (dp, 3 - z)
    is_mid = (z == 1) | (z == 2)
    is_end = (z == 0) | (z == 3)
    near, far = 3 - z, lax.rem(z + 2, 4)
    other_mid = 2 - clip
    piece, width = tok.shape[1], tok.shape[2]
    rows, half, wide = 2 * piece, width // 2, up_v.shape[1]
    low = jnp.bfloat16
    low_d, low_o = n1.at[pl.ds(0, rows)], n1.at[pl.ds(rows, rows)]
    in_src = att
    from_end = [normed.at[pl.ds(k * piece, piece)] for k in range(2)]
    from_pair, total_in = (cot_b.at[pl.ds(k * piece, piece)] for k in range(2))

    def grad_at(m):
        return down_v.at[pl.ds((2 if m == 0 else 3) * width, width), pl.ds(half if m != 1 else 0, half)]

    def e_at(slot):
        return align_v.at[pl.ds(pl.multiple_of(slot * piece, piece), piece), pl.ds(0, width)]

    def slot_rows(slot):
        return pl.ds(pl.multiple_of(slot * piece, piece), piece)

    loads = {"tok": (tok_h, tok)}
    for m in range(3):
        column = pl.multiple_of(m * width + side * half, 128)
        loads["low%d" % m] = (w_qkv.at[:, pl.ds(column, half)], low_v.at[m])
    loads["out"] = (w_out, out_v)
    loads["up"] = (w_up, up_v)
    loads["down"] = (w_down, down_v)
    loads["cot_a"] = (cot_a_h, cot_a)
    loads["align"] = (w_align, align_v)
    loads["cot_b"] = (cot_b_h, cot_b)
    loads = {
        name: pltpu.make_async_copy(src, dst, load_sem.at[k]) for k, (name, (src, dst)) in enumerate(loads.items())
    }
    for copy in loads.values():
        copy.start()

    def ready(*names):
        for name in names:
            loads[name].wait()

    barrier = pltpu.get_barrier_semaphore()
    for device in (to_core, to_x, to_y, to_z1, to_z2, to_z3):
        pl.semaphore_signal(barrier, inc=1, device_id=device, device_id_type=MESH)
    pl.semaphore_wait(barrier, 6)
    step = piece // CHUNKS

    def tok_copy(kind, slot, k):
        at = pl.ds(k * step, step)
        source = xall.at[slot, at] if kind >= 2 else tok.at[1 - clip if kind == 0 else clip, at]
        device = (dp, other_mid) if kind == 0 else to_z1
        return remote_copy(source, xall.at[slot, at], tok_send.at[kind, k], tok_recv.at[slot, k], device)

    ready("tok")
    for k in range(CHUNKS):
        tok_copy(0, z, k).start()
    for k in range(CHUNKS):
        tok_copy(1, z, k).start()
    fill_pack(pack, VECTORS, vectors)
    vec_out[...] = jnp.zeros_like(vec_out)
    xall[z] = tok[clip]
    e_v[0:128, :] = jnp.zeros((128, width), jnp.float32)
    e_v[0:2, :] = visible[...]
    grad_q[...] = e_v[0:128, :].T
    for c in range(2):
        side_v[pl.ds(c * piece, piece), VIS : VIS + 1] = grad_q[pl.ds(pl.multiple_of(z * piece, piece), piece), c : c + 1]
    seen = jnp.where(clip == 0, grad_q[:, 0:1], grad_q[:, 1:2])
    side_v[:, KEY : KEY + 1] = jnp.where(seen > 0.0, 0.0, -1e30)
    row_bias = jnp.where(visible[pl.ds(clip, 1), :] > 0.0, 0.0, -1e30)
    columns = pl.ds(pl.multiple_of(side * half, 128), half)
    ready("low0", "low1", "low2")

    def project(slot):
        where = slot_rows(slot)
        for k in range(piece // 32):
            at = pl.ds(pl.multiple_of(slot * piece, piece) + k * 32, 32)
            one, _ = norm_rows(xall[slot, pl.ds(k * 32, 32), :].astype(jnp.float32))
            n1[at, :] = (one * pack[N1_GAIN : N1_GAIN + 1, :] + pack[N1_BIAS : N1_BIAS + 1, :]).astype(low)
        left = n1[where, :]
        qkv[0, where, :] = (dot(left, low_v[0]) + pack[Q_BIAS : Q_BIAS + 1, columns]).astype(low) * low(0.125)
        qkv[1, where, :] = dot(left, low_v[1]).astype(low)
        qkv[2, where, :] = (dot(left, low_v[2]) + pack[V_BIAS : V_BIAS + 1, columns]).astype(low)

    project(z)

    @pl.when(is_mid)
    def _():
        for k in range(CHUNKS):
            for which, slot in enumerate((near, far)):
                tok_copy(1, slot, k).wait_recv()
                tok_copy(2 + which, slot, k).start()
        for k in range(CHUNKS):
            tok_copy(1, partner, k).wait_recv()

    def later(number, _):
        first, second = jnp.where(is_mid, near, far), jnp.where(is_mid, far, near)
        slot = jnp.where(number == 0, partner, jnp.where(number == 1, first, second))

        @pl.when(is_end)
        def _():
            for k in range(CHUNKS):
                tok_copy(1, slot, k).wait_recv()

        project(slot)
        return 0

    lax.fori_loop(0, 3, later, 0)
    lane = lax.broadcasted_iota(jnp.int32, (1, 128), 1)
    low_lane = lane < 64

    def att_copy(slot):
        return remote_copy(
            own_att.at[slot_rows(slot)], att.at[clip, side], att_send.at[slot], att_recv.at[z], (dp, slot)
        )

    def attend(number, _):
        slot = jnp.where(number == 0, far, jnp.where(number == 1, near, jnp.where(number == 2, partner, z)))
        where = slot_rows(slot)
        stats = jnp.zeros((piece, 128), jnp.float32)
        for t in range(half // 128):
            at = pl.ds(t * 128, 128)
            queries = qkv[0, where, at]
            keys = qkv[1, :, at]
            values = qkv[2, :, at]
            parts = []
            for a in range(2):
                mine = low_lane if a == 0 else jnp.logical_not(low_lane)
                masked = jnp.where(mine, queries, jnp.zeros_like(queries))
                scores = dot(masked, keys, NT) + row_bias
                top = jnp.max(scores, axis=-1, keepdims=True)
                expo = jnp.exp(scores - top)
                denominator = jnp.sum(expo, axis=-1, keepdims=True)
                parts.append(dot(expo.astype(low), values) * (1.0 / denominator))
                stats = jnp.where(lane == STATS + 2 * t + a, top + jnp.log(denominator), stats)
            own_att[where, at] = jnp.where(low_lane, parts[0], parts[1]).astype(low)
        side_v[where, STATS : STATS + 8] = stats[:, STATS : STATS + 8]

        @pl.when(number < 3)
        def _():
            att_copy(slot).start()

        return 0

    lax.fori_loop(0, 4, attend, 0)
    att[clip, side] = own_att[slot_rows(z), :]

    chunk = 48

    def chunks(body, carry):
        def one_chunk(k, carry):
            return body(pl.ds(pl.multiple_of(k * chunk, chunk), chunk), k, carry)

        return lax.fori_loop(0, rows // chunk, one_chunk, carry)

    def put_vector(row, start, value):
        at = 0
        while at < value.shape[1]:
            line, column = row + (start + at) // width, (start + at) % width
            take = min(value.shape[1] - at, width - column)
            vec_out[line : line + 1, column : column + take] = value[:, at : at + take]
            at += take

    def total(value):
        return jnp.sum(value.astype(jnp.float32), axis=0, keepdims=True)

    zero_row = jnp.zeros((1, width), jnp.float32)
    ready("cot_a")

    def mask(at, k, carry):
        value = (side_v[at, VIS : VIS + 1] * cot_a[at, :].astype(jnp.float32)).astype(low)
        cot_a[at, :] = value
        return carry + total(value)

    put_vector(ALIGN_BIAS, 0, chunks(mask, jnp.zeros((1, cot_a.shape[1]), jnp.float32)))
    lse_rows[...] = side_v[...].T[STATS : STATS + 8]

    def shares_of(source, target, count):
        for c in range(0, source.shape[1], 128):
            flipped = source[:, pl.ds(c, 128)].T
            at = 0
            while at < 128:
                share, inside = (c + at) // count, (c + at) % count
                take = min(128 - at, count - inside)
                rel = jnp.where(core == share % 2, 1, 0)
                target[rel, share // 2, pl.ds(inside, take), :] = flipped[at : at + take]
                at += take

    shares_of(n1, n1s, width // 8)

    def settle_att(number, _):
        slot = lax.rem(z + number, 4)
        att_copy(slot).wait_send()
        remote_copy(
            own_att.at[slot_rows(slot)], att.at[slot // 2, lax.rem(slot, 2)],
            att_send.at[slot], att_recv.at[slot], (dp, slot),
        ).wait_recv()
        return 0

    lax.fori_loop(1, 4, settle_att, 0)
    for k in range(CHUNKS):
        tok_copy(0, z, k).wait_send()
        tok_copy(1, z, k).wait_send()

    @pl.when(is_mid)
    def _():
        for k in range(CHUNKS):
            for which, slot in enumerate((near, far)):
                tok_copy(2 + which, slot, k).wait_send()

    for c in range(2):
        for h in range(2):
            normed[pl.ds(c * piece, piece), pl.ds(h * half, half)] = att[c, h]
    shares_of(normed, la, width // 8)
    ready("out")
    for c in range(0, width, 256):
        at = pl.ds(c, 256)
        mixed = dot(normed[...], out_v[:, at]) + pack[OUT_BIAS : OUT_BIAS + 1, at]
        mid_v[pl.ds(0, piece), at] = tok[0, :, at].astype(jnp.float32) + mixed[:piece]
        mid_v[pl.ds(piece, piece), at] = tok[1, :, at].astype(jnp.float32) + mixed[piece:]

    def norm(gain, bias, unit, inv):
        def body(at, k, _):
            one, inverse = norm_rows(mid_v[at, :])
            unit[at, :] = one.astype(low)
            side_v[at, inv : inv + 1] = inverse
            normed[at, :] = (one * pack[gain : gain + 1, :] + pack[bias : bias + 1, :]).astype(low)
            return 0

        chunks(body, 0)

    norm(N2_GAIN, N2_BIAS, unit2, INV2)
    shares_of(normed, l2, width // 8)
    ready("up")
    for t in range(wide // TILE):
        at = pl.ds(t * TILE, TILE)
        hidden_at = pl.ds(0, TILE)
        e_v[:, hidden_at] = dot(normed[...], up_v[:, at]) + row_of(pack, UP_BIAS, t * TILE, TILE)

        def gelu(here, k, _):
            values = e_v[here, hidden_at]
            cdf = 0.5 * (1.0 + lax.erf(values * SQRT_HALF))
            ring[k, :, at] = (values * cdf).astype(low)
            slope[here, at] = (cdf + values * jnp.exp(-0.5 * values * values) * INV_ROOT_TAU).astype(low)
            return 0

        chunks(gelu, 0)
        for c in range(0, TILE, 128):
            share, inside = (t * TILE + c) // half, (t * TILE + c) % half
            rel = jnp.where(core == share % 2, 1, 0)
            ld[rel, share // 2, pl.ds(inside, 128), :] = (
                ring[:, :, pl.ds(t * TILE + c, 128)].reshape(rows, 128).T
            )
    ready("down")
    for c in range(0, width, 256):
        at = pl.ds(c, 256)
        mid_v[:, at] = (
            mid_v[:, at] + dot(ring[...].reshape(rows, wide), down_v[:, at]) + pack[DOWN_BIAS : DOWN_BIAS + 1, at]
        )

    def staged(j, target):
        return pltpu.make_async_copy(own[j], target, put_sem.at[j])

    def put_block(at, k, _):
        own[1][k // 4, lax.rem(k, 4)] = (side_v[at, VIS : VIS + 1] * mid_v[at, :]).astype(low)
        return 0

    chunks(put_block, 0)
    staged(1, block_out).start()
    norm(N3_GAIN, N3_BIAS, unit3, INV3)
    shares_of(normed, l3, width // 8)
    ready("align", "cot_b")
    for c in range(0, align_v.shape[1], 256):
        at = pl.ds(c, 256)
        value = dot(normed[...], align_v[:, at]) + row_of(pack, ALIGN_BIAS, c, 256)
        value = (side_v[pl.ds(0, rows), VIS : VIS + 1] * value).astype(low)
        for k in range(8):
            own[0][k // 4, k % 4, :, at] = value[k * 48 : (k + 1) * 48]
    staged(0, align_out).start()

    def buffer_of(j):
        return ring.at[:, :, pl.ds(JOBS[j][5], JOBS[j][4])]

    def copies0(j):
        for h in range(2):
            yield remote_copy(
                buffer_of(j).at[pl.ds(4 * h, 4)], got0[j].at[h], send0.at[j, h], recv0.at[j, h], to_core
            )

    def copies1(j):
        yield remote_copy(
            own[j].at[0, pl.ds(2 * (1 - x), 2)], got1[j].at[0], send1.at[j, 0], recv1.at[j, 0], to_x
        )
        yield remote_copy(
            own[j].at[1, pl.ds(2 * (1 - y), 2)], got1[j].at[1], send1.at[j, 1], recv1.at[j, 1], to_y
        )

    def copies2(j):
        yield remote_copy(own[j].at[0, 2 * x + 1 - y], got2[j].at[0], send2.at[j, 0], recv2.at[j, 0], to_y)
        yield remote_copy(own[j].at[1, 2 * y + 1 - x], got2[j].at[1], send2.at[j, 1], recv2.at[j, 1], to_x)

    def shares(j):
        return (own[j].at[0, 2 * x + y], own[j].at[1, 2 * y + x])

    def copiesz(j, slot, device):
        for h, share in enumerate(shares(j)):
            yield remote_copy(share, gotz[j].at[slot, h], sendz.at[j, slot, h], recvz.at[j, slot, h], device)

    def copiesq(j, source, slot, device):
        got, m = gotq[j - PLAIN], j - PLAIN
        for h, share in enumerate(shares(j)):
            yield remote_copy(
                share if source is None else got.at[source, h],
                got.at[slot, h], sendq.at[m, slot, h], recvq.at[m, slot, h], device,
            )

    def result(j, h, source):
        matrix, row, count, column, size, _ = JOBS[j]
        return pltpu.make_async_copy(
            source, outs[matrix].at[pl.ds(row + h * count // 2, count // 2), pl.ds(column, size)], out_sem.at[j, h]
        )

    def result_q(j, h, which, source):
        count, m = JOBS[j][2] // 2, j - PLAIN
        at = side if which == 0 else 1 - side
        column = pl.multiple_of(m * width + at * half, 128)
        return pltpu.make_async_copy(
            source, outs[0].at[pl.ds(h * count, count), pl.ds(column, half)], outq_sem.at[m, which, h]
        )

    def stage(j, number):
        if number == 0:
            for copy in copies0(j):
                copy.start()
        if number == 1:
            for copy in copies0(j):
                copy.wait()
            add_into(own[j], own[j], got0[j])
            for copy in copies1(j):
                copy.start()
        if number == 2:
            for copy in copies1(j):
                copy.wait()
            first, second = (own[j].at[0, pl.ds(2 * x, 2)], own[j].at[1, pl.ds(2 * y, 2)])
            add_into(first, first, got1[j].at[0])
            add_into(second, second, got1[j].at[1])
            for copy in copies2(j):
                copy.start()
        if number == 3:
            for copy in copies2(j):
                copy.wait()
            for h, share in enumerate(shares(j)):
                add_into(share, share, got2[j].at[h])

            @pl.when(is_end)
            def _():
                for copy in copiesq(j, None, 0, to_z1) if j >= PLAIN else copiesz(j, 0, to_z1):
                    copy.start()

        if number >= 4 and j >= PLAIN:
            stage_q(j, number)
            return
        if number == 4:

            @pl.when(is_mid)
            def _():
                for copy in copiesz(j, 0, to_z1):
                    copy.wait_recv()
                for h, share in enumerate(shares(j)):
                    add_into(share, share, gotz[j].at[0, h])
                for copy in copiesz(j, 1, to_z3):
                    copy.start()

            @pl.when(is_end)
            def _():
                for copy in copiesz(j, 0, to_z1):
                    copy.wait_send()

        if number == 5:

            @pl.when(is_mid)
            def _():
                for copy in copiesz(j, 1, to_z3):
                    copy.wait()
                for h, share in enumerate(shares(j)):
                    add_into(share, share, gotz[j].at[1, h])
                for copy in copiesz(j, 0, to_z1):
                    copy.start()
                for h, share in enumerate(shares(j)):
                    result(j, h, share).start()

        if number == 6:

            @pl.when(is_mid)
            def _():
                for copy in copiesz(j, 0, to_z1):
                    copy.wait_send()

            @pl.when(is_end)
            def _():
                for copy in copiesz(j, 0, to_z1):
                    copy.wait_recv()
                for h in range(2):
                    result(j, h, gotz[j].at[0, h]).start()

    def stage_q(j, number):
        got = gotq[j - PLAIN]
        if number == 4:

            @pl.when(is_mid)
            def _():
                for copy in copiesq(j, None, 1, to_z3):
                    copy.start()
                for copy in copiesq(j, None, 0, to_z1):
                    copy.wait_recv()
                for copy in copiesq(j, 0, 2, to_z3):
                    copy.start()

            @pl.when(is_end)
            def _():
                for copy in copiesq(j, None, 0, to_z1):
                    copy.wait_send()

        if number == 5:

            @pl.when(is_mid)
            def _():
                for copy in copiesq(j, None, 1, to_z3):
                    copy.wait()
                for copy in copiesq(j, 0, 2, to_z3):
                    copy.wait()
                for h, share in enumerate(shares(j)):
                    add_into(share, share, got.at[2, h])
                    add_into(got.at[0, h], got.at[0, h], got.at[1, h])
                for copy in copiesq(j, None, 1, to_z1):
                    copy.start()
                for copy in copiesq(j, 0, 0, to_z1):
                    copy.start()
                for h, share in enumerate(shares(j)):
                    result_q(j, h, 0, share).start()
                    result_q(j, h, 1, got.at[0, h]).start()

        if number == 6:

            @pl.when(is_mid)
            def _():
                for copy in copiesq(j, None, 1, to_z1):
                    copy.wait_send()
                for copy in copiesq(j, 0, 0, to_z1):
                    copy.wait_send()

            @pl.when(is_end)
            def _():
                for copy in copiesq(j, None, 1, to_z1):
                    copy.wait_recv()
                for copy in copiesq(j, 0, 0, to_z1):
                    copy.wait_recv()
                for h in range(2):
                    result_q(j, h, 0, got.at[0, h]).start()
                    result_q(j, h, 1, got.at[1, h]).start()

    def results_done():
        for j in range(COUNT):
            for h in range(2):
                if j < PLAIN:
                    result(j, h, gotz[j].at[0, h]).wait()
                else:
                    for which in range(2):
                        result_q(j, h, which, gotq[j - PLAIN].at[0, h]).wait()

    def gradient(j, mine, left, right):
        count, size = JOBS[j][2], JOBS[j][4]
        target = own[j] if mine else buffer_of(j)
        for c in range(0, size, min(size, 384 if size % 384 == 0 else 512)):
            at = pl.ds(c, min(size, 384 if size % 384 == 0 else 512))
            value = dot(left, right(at)).astype(low)
            for chip in range(4):
                cy, cx = chip // 2, chip % 2
                for h in range(2):
                    k = 2 * cx + cy if h == 0 else 2 * cy + cx
                    start = chip * count + h * count // 2
                    part = value[start : start + count // 2]
                    if mine:
                        target[h, k, :, at] = part
                    else:
                        target[4 * h + k, :, at] = part

    def job(j, mine):
        matrix, row, count, column, size, _ = JOBS[j]
        lhs, rhs = ((n1s, None), (la, low_o), (l2, slope), (ld, low_d), (l3, cot_a))[matrix]
        left = lhs[1 if mine else 0, :, pl.ds(row, count), :].reshape(4 * count, lhs.shape[3])
        if matrix == 0:
            gradient(j, mine, left, lambda at: grad_at(j - PLAIN)[...])
        else:
            gradient(j, mine, left, lambda at: rhs[:, pl.ds(column + at.start, at.size)])

    def norm_back(e, one, inverse, gain):
        scaled = e * gain
        return inverse * (
            scaled
            - jnp.mean(scaled, axis=-1, keepdims=True)
            - one * jnp.mean(scaled * one, axis=-1, keepdims=True)
        )

    def norm_pass(unit, inv, gain_row, base, low_target, sums):
        def body(at, k, carry):
            e = e_v[at, :]
            one = unit[at, :].astype(jnp.float32)
            value = base(at) + norm_back(e, one, side_v[at, inv : inv + 1], pack[gain_row : gain_row + 1, :])
            mid_v[at, :] = value
            rounded = value.astype(low)
            low_target[at, :] = rounded
            return (carry[0] + total(e * one), carry[1] + total(e), carry[2] + total(rounded))

        for row, value in zip(sums, chunks(body, (zero_row,) * 3)):
            put_vector(row, 0, value)

    def e3():
        for c in range(0, width, 256):
            e_v[:, pl.ds(c, 256)] = dot(cot_a[...], align_v[pl.ds(c, 256), :], NT)

    def norm3():
        norm_pass(
            unit3, INV3, N3_GAIN, lambda at: side_v[at, VIS : VIS + 1] * cot_b[at, :].astype(jnp.float32), low_d,
            (N3_GAIN, N3_BIAS, DOWN_BIAS),
        )

    def feed(t):
        at = pl.ds(t * TILE, TILE)
        value = (dot(low_d[...], down_v[at, :], NT) * slope[:, at].astype(jnp.float32)).astype(low)
        slope[:, at] = value
        put_vector(UP_BIAS, t * TILE, total(value))

    def e2(t):
        e_v[:, pl.ds(t * 256, 256)] = dot(slope[...], up_v[pl.ds(t * 256, 256), :], NT)

    def norm2():
        norm_pass(unit2, INV2, N2_GAIN, lambda at: mid_v[at, :], low_o, (N2_GAIN, N2_BIAS, OUT_BIAS))

    def in_copy(slot):
        return remote_copy(
            in_src.at[slot // 2, lax.rem(slot, 2)], grad_att.at[z], in_send.at[slot], in_recv.at[z], (dp, slot)
        )

    def back_att():
        for h in range(2):
            value = dot(low_o[...], out_v[pl.ds(h * half, half), :], NT).astype(low)
            for c in range(2):
                in_src[c, h] = value[c * piece : (c + 1) * piece]

        def start(number, _):
            in_copy(lax.rem(z + number, 4)).start()
            return 0

        lax.fori_loop(1, 4, start, 0)
        grad_att[z] = in_src[clip, side]

    def settle():
        def body(number, _):
            slot = lax.rem(z + number, 4)
            in_copy(slot).wait_send()
            remote_copy(
                in_src.at[0, 0], grad_att.at[slot], in_send.at[slot], in_recv.at[slot], (dp, slot)
            ).wait_recv()
            return 0

        lax.fori_loop(1, 4, body, 0)

    def spread():
        def body(slot, _):
            where = slot_rows(slot)
            stats = jnp.zeros((piece, 128), jnp.float32)
            for t in range(half // 128):
                at = pl.ds(t * 128, 128)
                product = grad_att[slot, :, at].astype(jnp.float32) * own_att[where, at].astype(jnp.float32)
                for a in range(2):
                    mine = low_lane if a == 0 else jnp.logical_not(low_lane)
                    value = jnp.sum(jnp.where(mine, product, 0.0), axis=-1, keepdims=True)
                    stats = jnp.where(lane == STATS + 2 * t + a, value, stats)
            side_v[where, STATS : STATS + 8] = stats[:, STATS : STATS + 8]
            return 0

        lax.fori_loop(0, 4, body, 0)
        spread_rows[...] = side_v[...].T[STATS : STATS + 8]

    def pair(t, b):
        at = pl.ds(t * 128, 128)
        queries = qkv[0, :, at]
        grads = grad_att[:, :, at].reshape(4 * piece, 128)
        keys_at = pl.ds(b * KEY_BLOCK, KEY_BLOCK)
        keys = qkv[1, keys_at, at]
        values = qkv[2, keys_at, at]
        grad_k = jnp.zeros((KEY_BLOCK, 128), jnp.float32)
        grad_v = jnp.zeros((KEY_BLOCK, 128), jnp.float32)
        grad_queries = jnp.zeros_like(grad_q) if b == 0 else grad_q[...]
        for a in range(2):
            mine = low_lane if a == 0 else jnp.logical_not(low_lane)
            zero = jnp.zeros((), low)
            q_mine = jnp.where(mine, queries, zero)
            g_mine = jnp.where(mine, grads, zero)
            k_mine = jnp.where(mine, keys, zero)
            row = pl.ds(2 * t + a, 1)
            scores = dot(keys, q_mine, NT) + side_v[keys_at, KEY : KEY + 1]
            probs = jnp.exp(scores - lse_rows[row, :])
            back = (probs * (dot(values, g_mine, NT) - spread_rows[row, :])).astype(low)
            grad_v = grad_v + dot(probs.astype(low), g_mine)
            grad_k = grad_k + dot(back, q_mine)
            grad_queries = grad_queries + dot(back, k_mine, TN)
        grad_at(1)[keys_at, at] = grad_k.astype(low)
        grad_at(2)[keys_at, at] = grad_v.astype(low)
        if (b + 1) * KEY_BLOCK == 4 * piece:
            grad_at(0)[:, at] = (grad_queries * 0.125).astype(low)
        else:
            grad_q[...] = grad_queries

    def pair_copy():
        return remote_copy(e_at(partner), from_pair, pair_send, pair_recv, to_z1)

    def end_copy(which, slot):
        return remote_copy(e_at(slot), from_end[which], end_send.at[which], end_recv.at[which], to_z1)

    def out_copy(which, slot):
        return remote_copy(e_at(slot), total_in, out_send.at[which], out_recv, (dp, slot))

    targets = (3 - 3 * clip, 2 - clip)
    mine_rows = slot_rows(clip)

    def dx(number):
        slot = (targets + (partner, z))[number]
        where = slot_rows(slot)
        value = sum(dot(grad_at(m)[where, :], low_v[m], NT) for m in range(3))
        e_at(slot)[...] = value.astype(low)
        if number == 3:
            e_v[mine_rows, :] = value
        if number < 2:

            @pl.when(is_end)
            def _():
                end_copy(number, slot).start()

        if number == 2:
            pair_copy().start()
        one, _ = norm_rows(xall[slot].astype(jnp.float32))
        for row, term in ((N1_GAIN, total(value * one)), (N1_BIAS, total(value))):
            vec_out[row : row + 1, :] = vec_out[row : row + 1, :] + term

    def sums():
        spot = lax.broadcasted_iota(jnp.int32, (1, width), 1)
        for row, m in ((Q_BIAS, 0), (V_BIAS, 2)):
            value = total(grad_at(m)[...])
            value = jnp.concatenate([value, value], axis=1)
            put_vector(row, 0, jnp.where((spot < half) == (side == 0), value, 0.0))

    def forward(which):
        @pl.when(is_mid)
        def _():
            slot = targets[which]
            end_copy(which, slot).wait_recv()
            add_into(e_at(slot), e_at(slot), from_end[which])
            out_copy(which, slot).start()

    vec_devices = (to_core, to_x, to_y, to_z1, to_z2)

    def vec_copy(k):
        return remote_copy(vec_out, vec_got.at[k], vsend.at[k], vrecv.at[k], vec_devices[k])

    def vec(k):
        if k > 0:
            vec_copy(k - 1).wait()
            vec_out[...] = vec_out[...] + vec_got[k - 1]
        if k < 5:
            vec_copy(k).start()

    def norm1():
        pair_copy().wait()
        e_v[mine_rows, :] = e_v[mine_rows, :] + from_pair[...].astype(jnp.float32)
        out_copy(0, partner).wait_recv()
        e_v[slot_rows(1 - clip), :] = total_in[...].astype(jnp.float32)

        def body(at, k, _):
            one, inverse = norm_rows(tok[k // 4, pl.ds(pl.multiple_of(lax.rem(k, 4) * chunk, chunk), chunk), :].astype(jnp.float32))
            value = mid_v[at, :] + norm_back(e_v[at, :], one, inverse, pack[N1_GAIN : N1_GAIN + 1, :])
            low_d[at, :] = value.astype(low)
            return 0

        chunks(body, 0)
        pltpu.make_async_copy(low_d, grad_tokens, put_sem.at[2]).start()

    singles = dict(
        e3=e3, norm3=norm3, norm2=norm2, back_att=back_att, settle=settle, spread=spread, sums=sums, norm1=norm1
    )
    several = dict(feed=feed, e2=e2, dx=dx, fwd=forward, vec=vec)
    staged(0, align_out).wait()
    staged(1, block_out).wait()
    for entry in PLAN:
        if isinstance(entry, tuple):
            if entry[1] in (0, 1, 2, 3, 4, 5, 6):
                stage(*entry)
            else:
                job(entry[0], entry[1] == "own")
        elif entry in singles:
            singles[entry]()
        elif entry.startswith("pair"):
            pair(int(entry[4]), int(entry[5]))
        else:
            several[entry[:-1]](int(entry[-1]))

    results_done()
    pltpu.make_async_copy(low_d, grad_tokens, put_sem.at[2]).wait()

    @pl.when(is_mid)
    def _():
        for which in range(2):
            out_copy(which, targets[which]).wait_send()

    @pl.when(is_end)
    def _():
        for which in range(2):
            end_copy(which, targets[which]).wait_send()


def layer(visible, vectors, tok, cot_a, cot_b, w_align, w_down, w_up, w_out, w_qkv):
    _, piece, width = tok.shape
    rows, half, wide, align = 2 * piece, width // 2, w_up.shape[1], w_align.shape[1]
    low, full = jnp.bfloat16, jnp.float32
    vmem = pl.BlockSpec(memory_space=pltpu.VMEM)
    hbm = pl.BlockSpec(memory_space=pl.ANY)
    dma = pltpu.SemaphoreType.DMA
    v = pltpu.VMEM
    shapes = [(2, 4, job[2] // 2, job[4]) for job in JOBS]
    scratch = (
        [v(shape, low) for shape in shapes]
        + [v(shape, low) for shape in shapes]
        + [v((2, 2) + shape[2:], low) for shape in shapes]
        + [v((2,) + shape[2:], low) for shape in shapes]
        + [v((2, 2) + shape[2:], low) for shape in shapes[:PLAIN]]
        + [v((3, 2) + shape[2:], low) for shape in shapes[PLAIN:]]
        + [v((5, PACK_ROWS, width), full)]
        + [v((PACK_ROWS, width), full), v((4 * piece, 128), full)]
        + [v(w_align.shape, low), v(w_down.shape, low), v(w_up.shape, low), v(w_out.shape, low)]
        + [v((3, width, half), low), v((2, piece, width), low), v((4, piece, width), low), v((4 * piece, width), low)]
        + [v((3, 4 * piece, half), low), v((4 * piece, half), low), v((2, 2, piece, half), low)]
        + [v((8, 4 * piece), full)] * 2
        + [v((rows, width), full), v((rows, width), full), v((rows, width), low), v((8, 48, wide), low)]
        + [v((rows, wide), low), v((2, 4, wide // 8, rows), low)]
        + [v((2, 4, width // 8, rows), low)] * 3
        + [v((rows, width), low)] * 2
        + [v((rows, align), low), v((rows, width), low)]
        + [v((4, piece, half), low), v((2, 4, width // 8, 4 * piece), low), v((4 * piece, 128), full)]
        + [dma((10,))]
        + [dma((COUNT, 2))] * 6
        + [dma((PLAIN, 2, 2))] * 2
        + [dma((3, 3, 2))] * 2
        + [dma((PLAIN, 2)), dma((3, 2, 2))]
        + [dma((5,))] * 2
        + [dma((4, CHUNKS))] * 2
        + [dma((4,))] * 4
        + [dma(())] * 2
        + [dma((2,))] * 2
        + [dma((2,)), dma(())]
        + [dma((3,))]
    )
    struct = jax.ShapeDtypeStruct
    return pl.pallas_call(
        layer_kernel,
        name="layer",
        out_shape=[
            struct((2, 4, 48, width), low),
            struct((2, 4, 48, align), low),
            struct((rows, width), low),
            struct((PACK_ROWS, width), full),
        ]
        + [struct((w.shape[0] // 8, w.shape[1]), low) for w in (w_qkv, w_out, w_up, w_down, w_align)],
        in_specs=[vmem] * 13 + [hbm] * 8,
        out_specs=[hbm, hbm, hbm, vmem] + [hbm] * 5,
        scratch_shapes=scratch,
        compiler_params=pltpu.CompilerParams(
            collective_id=0, has_side_effects=True, vmem_limit_bytes=63 * 2**20
        ),
    )(visible, *vectors, tok, cot_a, cot_b, w_align, w_down, w_up, w_out, w_qkv)


VECTORS = (
    N1_GAIN, N1_BIAS, Q_BIAS, V_BIAS, OUT_BIAS, N2_GAIN, N2_BIAS, DOWN_BIAS, N3_GAIN, N3_BIAS, UP_BIAS, ALIGN_BIAS,
)


def finish_kernel(*refs):
    shares, pack, through_in = refs[:5], refs[5], refs[6:9]
    wide, vectors, through_out = refs[9:14], refs[14:26], refs[26:29]
    low_v, wide_v, held = refs[29:34], refs[34:39], refs[39:42]
    in_sem, out_sem = refs[42:]
    ins = [pltpu.make_async_copy(shares[k], low_v[k], in_sem.at[k]) for k in range(5)]
    outs = [pltpu.make_async_copy(wide_v[k], wide[k], out_sem.at[k]) for k in range(5)]
    through = [
        (
            pltpu.make_async_copy(through_in[k], held[k], in_sem.at[5 + k]),
            pltpu.make_async_copy(held[k], through_out[k], out_sem.at[5 + k]),
        )
        for k in range(3)
    ]
    for copy in ins:
        copy.start()
    for copy, _ in through:
        copy.start()
    width = pack.shape[1]
    for row, ref in zip(VECTORS, vectors):
        for start in range(0, ref.shape[0], width):
            size = min(width, ref.shape[0] - start)
            line = row + start // width
            ref[pl.ds(start, size)] = pack[line : line + 1, 0:size].reshape(size)
    for k in range(5):
        ins[k].wait()
        wide_v[k][...] = low_v[k][...].astype(jnp.float32)
        outs[k].start()
    for first, second in through:
        first.wait()
        second.start()
    for copy in outs:
        copy.wait()
    for _, copy in through:
        copy.wait()


def finish(shares, pack, through, sizes):
    vmem = pl.BlockSpec(memory_space=pltpu.VMEM)
    hbm = pl.BlockSpec(memory_space=pl.ANY)
    struct = jax.ShapeDtypeStruct
    results = pl.pallas_call(
        finish_kernel,
        name="finish",
        out_shape=[struct(share.shape, jnp.float32) for share in shares]
        + [struct((size,), jnp.float32) for size in sizes]
        + [struct(array.shape, array.dtype) for array in through],
        in_specs=[hbm] * 5 + [vmem] + [hbm] * 3,
        out_specs=[hbm] * 5 + [vmem] * 12 + [hbm] * 3,
        scratch_shapes=[pltpu.VMEM(share.shape, share.dtype) for share in shares]
        + [pltpu.VMEM(share.shape, jnp.float32) for share in shares]
        + [pltpu.VMEM(array.shape, array.dtype) for array in through]
        + [pltpu.SemaphoreType.DMA((8,)), pltpu.SemaphoreType.DMA((8,))],
        compiler_params=pltpu.CompilerParams(vmem_limit_bytes=62 * 2**20),
    )(*shares, pack, *through)
    return results[:5], results[5:17], results[17:]


def norm_forward(values, gain, shift):
    center = values - jnp.mean(values, axis=-1, keepdims=True)
    inverse = lax.rsqrt(jnp.mean(center * center, axis=-1, keepdims=True) + EPSILON)
    normed = center * inverse
    return (normed * gain + shift, normed, inverse)


def norm_backward(upstream, normed, inverse, gain):
    scaled = upstream * gain
    inner = (
        scaled
        - jnp.mean(scaled, axis=-1, keepdims=True)
        - normed * jnp.mean(scaled * normed, axis=-1, keepdims=True)
    )
    return (inverse * inner, jnp.sum(upstream * normed, axis=0), jnp.sum(upstream, axis=0))


def gelu_slope(values):
    return (
        0.5 * (1.0 + lax.erf(values * SQRT_HALF))
        + values * jnp.exp(-0.5 * values * values) * INV_ROOT_TAU
    )


def weight_grad(left, right):
    return lax.dot_general(
        left, right, (((0,), (0,)), ((), ())), preferred_element_type=jnp.float32
    )


def input_grad(upstream, weight):
    return lax.dot_general(
        upstream, weight, (((1,), (1,)), ((), ())), preferred_element_type=jnp.float32
    )


def masked_scores(query_heads, key_heads, key_valid, scale):
    scores = (
        jnp.einsum("cqhd,ckhd->chqk", query_heads, key_heads, preferred_element_type=jnp.float32)
        * scale
    )
    return jnp.where(key_valid, scores, -1e30)


def column_sum(values):
    return jnp.sum(values, axis=0, dtype=jnp.float32)


def local(
    tokens,
    frame_counts,
    slot_mask,
    norm1_gain,
    norm1_bias,
    w_qkv,
    q_bias,
    v_bias,
    w_out,
    out_bias,
    norm2_gain,
    norm2_bias,
    w_up,
    up_bias,
    w_down,
    down_bias,
    norm3_gain,
    norm3_bias,
    w_align,
    align_bias,
    cot_block,
    cot_align,
):
    clip_count, frame_dev, slot_count, width = tokens.shape
    align_width = w_align.shape[1]
    head_size = width // HEADS
    scale = 1.0 / math.sqrt(head_size)
    row_count = clip_count * frame_dev * slot_count
    cycle_pos = lax.axis_index("blk")
    frame_ids = cycle_pos * frame_dev + jnp.arange(frame_dev, dtype=jnp.int32)
    own_slots = lax.dynamic_slice_in_dim(slot_mask, cycle_pos * frame_dev, frame_dev, 1)
    own_mask = (frame_ids[None, :, None] < frame_counts[:, None, None]) & (own_slots > 0)
    visible = own_mask.astype(jnp.float32).reshape(row_count, 1)
    all_frames = jnp.arange(slot_mask.shape[1], dtype=jnp.int32)
    key_valid = (all_frames[None, :, None] < frame_counts[:, None, None]) & (slot_mask > 0)
    key_valid = key_valid.reshape(clip_count, 1, 1, -1)
    inputs = tokens.reshape(row_count, width).astype(jnp.float32)
    normed_one, unit_one, inverse_one = norm_forward(inputs, norm1_gain, norm1_bias)
    normed1 = normed_one.astype(jnp.bfloat16)
    projected = jnp.dot(normed1, w_qkv, preferred_element_type=jnp.float32)
    queries = (projected[:, :width] + q_bias).astype(jnp.bfloat16)
    keys_local = projected[:, width : 2 * width].astype(jnp.bfloat16)
    values_local = (projected[:, 2 * width :] + v_bias).astype(jnp.bfloat16)
    block_shape = (clip_count, frame_dev, slot_count, width)
    heads_shape = (clip_count, -1, HEADS, head_size)
    keys_all, values_all = (
        lax.all_gather(keys_local.reshape(block_shape), "blk", axis=1, tiled=True),
        lax.all_gather(values_local.reshape(block_shape), "blk", axis=1, tiled=True),
    )
    key_heads = keys_all.reshape(heads_shape)
    value_heads = values_all.reshape(heads_shape)
    query_heads = queries.reshape(heads_shape)
    scores = masked_scores(query_heads, key_heads, key_valid, scale)
    top = jnp.max(scores, axis=-1, keepdims=True)
    expo = jnp.exp(scores - top)
    total = jnp.sum(expo, axis=-1, keepdims=True)
    probs_low = (expo / total).astype(jnp.bfloat16)
    attended = jnp.einsum(
        "chqk,ckhd->cqhd", probs_low, value_heads, preferred_element_type=jnp.float32
    )
    attended = attended.astype(jnp.bfloat16).reshape(row_count, width)
    mid = inputs + jnp.dot(attended, w_out, preferred_element_type=jnp.float32) + out_bias
    normed_two, unit_two, inverse_two = norm_forward(mid, norm2_gain, norm2_bias)
    normed2 = normed_two.astype(jnp.bfloat16)
    hidden = jnp.dot(normed2, w_up, preferred_element_type=jnp.float32) + up_bias
    active = jax.nn.gelu(hidden, approximate=False).astype(jnp.bfloat16)
    after = mid + jnp.dot(active, w_down, preferred_element_type=jnp.float32) + down_bias
    block_out = (visible * after).astype(jnp.bfloat16).reshape(block_shape)
    normed_three, unit_three, inverse_three = norm_forward(after, norm3_gain, norm3_bias)
    normed3 = normed_three.astype(jnp.bfloat16)
    target = jnp.dot(normed3, w_align, preferred_element_type=jnp.float32) + align_bias
    aligned = (
        (visible * target)
        .astype(jnp.bfloat16)
        .reshape(clip_count, frame_dev, slot_count, align_width)
    )
    back_align = (visible * cot_align.reshape(row_count, align_width).astype(jnp.float32)).astype(
        jnp.bfloat16
    )
    grad_align_bias = column_sum(back_align)
    grad_w_align = weight_grad(normed3, back_align)
    back_norm3, grad_norm3_gain, grad_norm3_bias = norm_backward(
        input_grad(back_align, w_align), unit_three, inverse_three, norm3_gain
    )
    back_after = visible * cot_block.reshape(row_count, width).astype(jnp.float32) + back_norm3
    back_down = back_after.astype(jnp.bfloat16)
    grad_down_bias = column_sum(back_down)
    grad_w_down = weight_grad(active, back_down)
    back_up = (input_grad(back_down, w_down) * gelu_slope(hidden)).astype(jnp.bfloat16)
    grad_up_bias = column_sum(back_up)
    grad_w_up = weight_grad(normed2, back_up)
    back_norm2, grad_norm2_gain, grad_norm2_bias = norm_backward(
        input_grad(back_up, w_up), unit_two, inverse_two, norm2_gain
    )
    back_mid = back_after + back_norm2
    back_out = back_mid.astype(jnp.bfloat16)
    grad_out_bias = column_sum(back_out)
    grad_w_out = weight_grad(attended, back_out)
    back_attended = input_grad(back_out, w_out).astype(jnp.bfloat16).reshape(heads_shape)
    scores = masked_scores(query_heads, key_heads, key_valid, scale)
    probs = jnp.exp(scores - top) / total
    probs_low = probs.astype(jnp.bfloat16)
    back_probs = jnp.einsum(
        "cqhd,ckhd->chqk", back_attended, value_heads, preferred_element_type=jnp.float32
    )
    spread = jnp.sum(probs * back_probs, axis=-1, keepdims=True)
    back_scores = (probs * (back_probs - spread)).astype(jnp.bfloat16)
    back_queries = (
        jnp.einsum("chqk,ckhd->cqhd", back_scores, key_heads, preferred_element_type=jnp.float32)
        * scale
    )
    back_queries = back_queries.astype(jnp.bfloat16).reshape(row_count, width)
    value_terms = jnp.einsum(
        "chqk,cqhd->ckhd", probs_low, back_attended, preferred_element_type=jnp.float32
    )
    key_terms = (
        jnp.einsum("chqk,cqhd->ckhd", back_scores, query_heads, preferred_element_type=jnp.float32)
        * scale
    )
    whole_shape = (clip_count, -1, slot_count, width)
    key_share, value_share = (
        lax.psum_scatter(
            key_terms.reshape(whole_shape).astype(jnp.bfloat16),
            "blk",
            scatter_dimension=1,
            tiled=True,
        ).astype(jnp.float32),
        lax.psum_scatter(
            value_terms.reshape(whole_shape).astype(jnp.bfloat16),
            "blk",
            scatter_dimension=1,
            tiled=True,
        ).astype(jnp.float32),
    )
    back_keys = key_share.astype(jnp.bfloat16).reshape(row_count, width)
    back_values = value_share.astype(jnp.bfloat16).reshape(row_count, width)
    grad_q_bias = column_sum(back_queries)
    grad_v_bias = column_sum(back_values)
    combined = jnp.concatenate([back_queries, back_keys, back_values], axis=1)
    grad_w_qkv = weight_grad(normed1, combined)
    back_norm1, grad_norm1_gain, grad_norm1_bias = norm_backward(
        input_grad(combined, w_qkv), unit_one, inverse_one, norm1_gain
    )
    grad_tokens = (back_mid + back_norm1).astype(jnp.bfloat16).reshape(block_shape)
    vector_total = lax.psum(
        (
            grad_norm1_gain,
            grad_norm1_bias,
            grad_q_bias,
            grad_v_bias,
            grad_out_bias,
            grad_norm2_gain,
            grad_norm2_bias,
            grad_up_bias,
            grad_down_bias,
            grad_norm3_gain,
            grad_norm3_bias,
            grad_align_bias,
        ),
        ("dp", "blk"),
    )
    row_part = (
        lax.psum_scatter(grad_w_qkv, "dp", scatter_dimension=0, tiled=True),
        lax.psum_scatter(grad_w_out, "dp", scatter_dimension=0, tiled=True),
        lax.psum_scatter(grad_w_up, "dp", scatter_dimension=0, tiled=True),
        lax.psum_scatter(grad_w_down, "dp", scatter_dimension=0, tiled=True),
        lax.psum_scatter(grad_w_align, "dp", scatter_dimension=0, tiled=True),
    )
    matrix_total = (
        lax.psum(row_part[0].astype(jnp.bfloat16), "blk").astype(jnp.float32),
        lax.psum(row_part[1].astype(jnp.bfloat16), "blk").astype(jnp.float32),
        lax.psum(row_part[2].astype(jnp.bfloat16), "blk").astype(jnp.float32),
        lax.psum(row_part[3].astype(jnp.bfloat16), "blk").astype(jnp.float32),
        lax.psum(row_part[4].astype(jnp.bfloat16), "blk").astype(jnp.float32),
    )
    return (
        block_out,
        aligned,
        grad_tokens,
        vector_total[0],
        vector_total[1],
        matrix_total[0],
        vector_total[2],
        vector_total[3],
        matrix_total[1],
        vector_total[4],
        vector_total[5],
        vector_total[6],
        matrix_total[2],
        vector_total[7],
        matrix_total[3],
        vector_total[8],
        vector_total[9],
        vector_total[10],
        matrix_total[4],
        vector_total[11],
    )


def local_kernels(
    tokens, frame_counts, slot_mask, norm1_gain, norm1_bias, w_qkv, q_bias, v_bias, w_out, out_bias, norm2_gain,
    norm2_bias, w_up, up_bias, w_down, down_bias, norm3_gain, norm3_bias, w_align, align_bias, cot_block, cot_align,
):
    clip_count, frame_dev, slot_count, width = tokens.shape
    align = w_align.shape[1]
    piece = frame_dev * slot_count
    rows = clip_count * piece
    slots = slot_mask.reshape(clip_count, -1)
    frame_ids = lax.broadcasted_iota(jnp.int32, slots.shape, 1) // slot_count
    visible = jnp.where((frame_ids < frame_counts[:, None]) & (slots > 0), 1.0, 0.0).astype(jnp.float32)
    vectors = [
        norm1_gain, norm1_bias, q_bias, v_bias, out_bias, norm2_gain, norm2_bias, down_bias, norm3_gain, norm3_bias,
        up_bias, align_bias,
    ]
    block_out, align_out, grad_tokens, vec, *shares = layer(
        visible, vectors, tokens.reshape(clip_count, piece, width), cot_align.reshape(rows, align),
        cot_block.reshape(rows, width), w_align, w_down, w_up, w_out, w_qkv,
    )
    matrices, totals, (block_out, align_out, grad_tokens) = finish(
        shares, vec, (block_out, align_out, grad_tokens), [vector.shape[0] for vector in vectors]
    )
    (
        grad_norm1_gain, grad_norm1_bias, grad_q_bias, grad_v_bias, grad_out_bias, grad_norm2_gain, grad_norm2_bias,
        grad_down_bias, grad_norm3_gain, grad_norm3_bias, grad_up_bias, grad_align_bias,
    ) = totals
    return (
        block_out.reshape(tokens.shape),
        align_out.reshape(cot_align.shape),
        grad_tokens.reshape(tokens.shape),
        grad_norm1_gain,
        grad_norm1_bias,
        matrices[0],
        grad_q_bias,
        grad_v_bias,
        matrices[1],
        grad_out_bias,
        grad_norm2_gain,
        grad_norm2_bias,
        matrices[2],
        grad_up_bias,
        matrices[3],
        grad_down_bias,
        grad_norm3_gain,
        grad_norm3_bias,
        matrices[4],
        grad_align_bias,
    )


def solution(mesh):
    in_specs = (
        P("dp", "blk", None, None),
        P("dp"),
        P("dp", None, None),
        P(),
        P(),
        P(),
        P(),
        P(),
        P(),
        P(),
        P(),
        P(),
        P(),
        P(),
        P(),
        P(),
        P(),
        P(),
        P(),
        P(),
        P("dp", "blk", None, None),
        P("dp", "blk", None, None),
    )
    out_specs = (
        P("dp", "blk", None, None),
        P("dp", "blk", None, None),
        P("dp", "blk", None, None),
        P(),
        P(),
        P("dp", None),
        P(),
        P(),
        P("dp", None),
        P(),
        P(),
        P(),
        P("dp", None),
        P(),
        P("dp", None),
        P(),
        P(),
        P(),
        P("dp", None),
        P(),
    )
    sizes = (mesh.shape["dp"], mesh.shape["blk"])
    run = local_kernels if sizes == GRID else local
    return jax.shard_map(run, mesh=mesh, in_specs=in_specs, out_specs=out_specs, check_vma=False)
```

```python
import math

import jax
import jax.numpy as jnp
from jax import lax
from jax.experimental import pallas as pl
from jax.experimental.pallas import tpu as pltpu
from jax.sharding import PartitionSpec as P

HEADS = 12


EPSILON = 1e-06
SQRT_HALF = 0.7071067811865476
INV_ROOT_TAU = 0.3989422804014327
MESH = pl.DeviceIdType.MESH
GRID = (8, 4)


NT = (((1,), (1,)), ((), ()))
TN = (((0,), (0,)), ((), ()))
CHUNKS = 4


def dot(left, right, dims=(((1,), (0,)), ((), ()))):
    return lax.dot_general(left, right, dims, preferred_element_type=jnp.float32)


def remote_copy(src, dst, send, recv, device):
    return pltpu.make_async_remote_copy(
        src_ref=src, dst_ref=dst, send_sem=send, recv_sem=recv, device_id=device, device_id_type=MESH
    )


N1_GAIN, N1_BIAS, Q_BIAS, V_BIAS, OUT_BIAS, N2_GAIN, N2_BIAS, DOWN_BIAS, N3_GAIN, N3_BIAS, UP_BIAS, ALIGN_BIAS = (
    0, 1, 2, 3, 4, 5, 6, 7, 8, 9, 10, 14,
)
PACK_ROWS = 16
TILE = 512


def row_of(pack, row, start, size):
    width = pack.shape[1]
    parts = []
    while size > 0:
        line, column = row + start // width, start % width
        take = min(size, width - column)
        parts.append(pack[line : line + 1, column : column + take])
        start, size = start + take, size - take
    return parts[0] if len(parts) == 1 else jnp.concatenate(parts, axis=1)


def fill_pack(pack, rows, refs):
    width = pack.shape[1]
    for row, ref in zip(rows, refs):
        for start in range(0, ref.shape[0], width):
            size = min(width, ref.shape[0] - start)
            line = row + start // width
            pack[line : line + 1, 0:size] = ref[pl.ds(start, size)].reshape(1, size)


def norm_rows(values):
    center = values - jnp.mean(values, axis=-1, keepdims=True)
    inverse = lax.rsqrt(jnp.mean(center * center, axis=-1, keepdims=True) + EPSILON)
    return center * inverse, inverse


def put_visible(vis, visible_t, z):
    piece = vis.shape[0] // 2
    for c in range(2):
        where = pl.ds(pl.multiple_of(z * piece, piece), piece)
        vis[pl.ds(c * piece, piece), :] = visible_t[where, c : c + 1]


JOBS = (
    (4, 0, 96, 0, 1024, 2048),
    (3, 0, 96, 0, 768, 0),
    (3, 96, 96, 0, 768, 768),
    (3, 192, 96, 0, 768, 1536),
    (3, 288, 96, 0, 768, 2304),
    (2, 0, 96, 0, 768, 0),
    (2, 0, 96, 768, 768, 768),
    (2, 0, 96, 1536, 768, 1536),
    (2, 0, 96, 2304, 768, 2304),
    (1, 0, 96, 0, 768, 0),
    (0, 0, 96, 0, 384, 768),
    (0, 0, 96, 384, 384, 1152),
    (0, 0, 96, 768, 384, 1536),
)
COUNT = len(JOBS)
PLAIN = 10
KEY_BLOCK = 256
NORM_ROWS = 96
PLAN = (
    (0, "far"), (0, 0), "e3", "norm3", (0, "own"), (0, 1), (1, "far"), (1, 0), "feed", (1, "own"), (1, 1),
    (5, "far"), (5, 0), "e2", (0, 2), "norm2", (1, 2), "back_att", (5, "own"), (5, 1), (0, 3), (2, "far"), (2, 0),
    (2, "own"), (1, 3), (3, "far"), (3, 0), (3, "own"), (4, "far"), (4, 0), (2, 1), (6, "far"), (6, 0), (4, "own"),
    (5, 2), (6, "own"), "settle0", (3, 1), "pair", (2, 2), "pair", (5, 3), (4, 1), "pair", (3, 2), "settle1",
    (0, 4), (2, 3), "pair", (6, 1), "pair", (4, 2), (1, 4), (3, 3), "settle2", (5, 4), (0, 5), "pair", (6, 2),
    "pair", (2, 4), (4, 3), (1, 5), "pair", (6, 3), (0, 6), (3, 4), (5, 5), "pair", "dx0", (4, 4), (1, 6), (2, 5),
    (10, "far"), (10, 0), "dx1", "dx2", (11, "far"), (11, 0), (6, 4), (5, 6), (3, 5), (7, "far"), (7, 0),
    (9, "far"), (9, 0), (11, "own"), (7, "own"), "dx3", (2, 6), (4, 5), (10, "own"), (10, 1), (9, "own"),
    (8, "far"), (8, 0), "sums", "vec0", (11, 1), "fwd0", (8, "own"), (6, 5), (10, 2), (7, 1), (12, "far"), (12, 0),
    "vec1", (11, 2), (10, 3), "vec2", (9, 1), "fwd1", (3, 6), (7, 2), (11, 3), "vec3", (8, 1), (4, 6), "vec4",
    (9, 2), (7, 3), "vec5", (10, 4), (11, 4), (8, 2), "norm1", (9, 3), (12, "own"), (12, 1), (7, 4), (10, 5),
    (6, 6), (8, 3), (12, 2), (11, 5), (9, 4), (10, 6), (12, 3), (7, 5), (8, 4), (11, 6), (12, 4), (9, 5), (7, 6),
    (8, 5), (9, 6), (12, 5), (8, 6), (12, 6),
)


def add_into(target, first, second):
    lead = target.shape[:-2]

    def body(k, _):
        if len(lead) == 0:
            at = (pl.ds(pl.multiple_of(k * 16, 16), 16), slice(None))
        elif len(lead) == 1:
            at = (k,)
        else:
            at = (k // lead[1], lax.rem(k, lead[1]))
        target[at] = first[at] + second[at]
        return 0

    lax.fori_loop(0, math.prod(lead) if lead else target.shape[0] // 16, body, 0)


VIS, KEY, INV2, INV3, STATS = 0, 1, 2, 3, 8


def layer_kernel(*refs):
    slot_mask, counts, vectors_h, refs = refs[0], refs[1], refs[2:14], refs[14:]
    tok_h, cot_a_h, cot_b_h, w_align, w_down, w_up, w_out, w_qkv = refs[:8]
    block_out, align_out, grad_tokens, vec_out = refs[8:12]
    outs = refs[12:17]
    rest = refs[17:]
    own, got0, got1, got2 = (rest[i * COUNT : (i + 1) * COUNT] for i in range(4))
    rest = rest[4 * COUNT :]
    gotz, gotq = rest[:PLAIN], rest[PLAIN:COUNT]
    rest = rest[COUNT:]
    vec_got, vectors = rest[0], rest[1:13]
    (
        pack, side_v,
        align_v, down_v, up_v, out_v, low_v, tok, xall, n1, qkv, own_att, att, lse_rows, spread_rows,
        mid_v, e_v, normed, ring, slope, ld, l2, l3, la, unit2, unit3, cot_a, cot_b,
        grad_att, n1s, grad_q,
        load_sem, send0, recv0, send1, recv1, send2, recv2, sendz, recvz, sendq, recvq, out_sem, outq_sem, vsend, vrecv,
        tok_send, tok_recv, att_send, att_recv, in_send, in_recv,
        pair_send, pair_recv, end_send, end_recv, out_send, out_recv, put_sem, vector_sem,
    ) = rest[13:]

    dp = lax.axis_index("dp")
    z = lax.axis_index("blk")
    core = lax.rem(dp, 2)
    x = lax.rem(dp // 2, 2)
    y = dp // 4
    clip, side = z // 2, lax.rem(z, 2)
    to_core = (dp + 1 - 2 * core, z)
    to_x = (dp + 2 - 4 * x, z)
    to_y = (dp + 4 - 8 * y, z)
    partner = z + 1 - 2 * side
    to_z1 = (dp, partner)
    to_z2 = (dp, lax.rem(z + 2, 4))
    to_z3 = (dp, 3 - z)
    is_mid = (z == 1) | (z == 2)
    is_end = (z == 0) | (z == 3)
    near, far = 3 - z, lax.rem(z + 2, 4)
    other_mid = 2 - clip
    piece, width = tok.shape[1], tok.shape[2]
    rows, half, wide = 2 * piece, width // 2, up_v.shape[1]
    low = jnp.bfloat16
    low_d, low_o = n1.at[pl.ds(0, rows)], n1.at[pl.ds(rows, rows)]
    in_src = att
    from_end = [normed.at[pl.ds(k * piece, piece)] for k in range(2)]
    from_pair, total_in = (cot_b.at[pl.ds(k * piece, piece)] for k in range(2))

    def grad_at(m):
        return down_v.at[pl.ds((2 if m == 0 else 3) * width, width), pl.ds(half if m != 1 else 0, half)]

    def e_at(slot):
        return align_v.at[pl.ds(pl.multiple_of(slot * piece, piece), piece), pl.ds(0, width)]

    def slot_rows(slot):
        return pl.ds(pl.multiple_of(slot * piece, piece), piece)

    loads = {"tok": (tok_h, tok)}
    for m in range(3):
        column = pl.multiple_of(m * width + side * half, 128)
        loads["low%d" % m] = (w_qkv.at[:, pl.ds(column, half)], low_v.at[m])
    loads["out"] = (w_out, out_v)
    loads["up"] = (w_up, up_v)
    loads["down"] = (w_down, down_v)
    loads["cot_a"] = (cot_a_h, cot_a)
    loads["align"] = (w_align, align_v)
    loads["cot_b"] = (cot_b_h, cot_b)
    loads = {
        name: pltpu.make_async_copy(src, dst, load_sem.at[k]) for k, (name, (src, dst)) in enumerate(loads.items())
    }
    early = ("tok", "low0", "low1", "low2")
    for name in early:
        loads[name].start()
    small = [pltpu.make_async_copy(src, dst, vector_sem.at[k]) for k, (src, dst) in enumerate(zip(vectors_h, vectors))]
    for copy in small:
        copy.start()

    def ready(*names):
        for name in names:
            loads[name].wait()

    barrier = pltpu.get_barrier_semaphore()
    for device in (to_core, to_x, to_y, to_z1, to_z2, to_z3):
        pl.semaphore_signal(barrier, inc=1, device_id=device, device_id_type=MESH)
    pl.semaphore_wait(barrier, 6)
    step = piece // CHUNKS

    def tok_copy(kind, slot, k):
        at = pl.ds(k * step, step)
        source = xall.at[slot, at] if kind >= 2 else tok_h.at[1 - clip if kind == 0 else clip, at]
        device = (dp, other_mid) if kind == 0 else to_z1
        return remote_copy(source, xall.at[slot, at], tok_send.at[kind, k], tok_recv.at[slot, k], device)

    for k in range(CHUNKS):
        tok_copy(0, z, k).start()
    for k in range(CHUNKS):
        tok_copy(1, z, k).start()
    for copy in small:
        copy.wait()
    fill_pack(pack, VECTORS, vectors)
    vec_out[...] = jnp.zeros_like(vec_out)
    ready("tok")
    xall[z] = tok[clip]
    e_v[0:128, :] = jnp.zeros((128, width), jnp.float32)
    for c in range(2):
        e_v[c : c + 1, :] = jnp.concatenate(
            [
                jnp.where((slot_mask[c, f : f + 1, :] > 0) & (f < counts[c]), 1.0, 0.0)
                for f in range(slot_mask.shape[1])
            ],
            axis=1,
        )
    grad_q[...] = e_v[0:128, :].T
    for c in range(2):
        side_v[pl.ds(c * piece, piece), VIS : VIS + 1] = grad_q[pl.ds(pl.multiple_of(z * piece, piece), piece), c : c + 1]
    seen = jnp.where(clip == 0, grad_q[:, 0:1], grad_q[:, 1:2])
    side_v[:, KEY : KEY + 1] = jnp.where(seen > 0.0, 0.0, -1e30)
    row_bias = jnp.where(jnp.where(clip == 0, e_v[0:1, :], e_v[1:2, :]) > 0.0, 0.0, -1e30)
    columns = pl.ds(pl.multiple_of(side * half, 128), half)
    ready("low0", "low1", "low2")

    def project(slot):
        where = slot_rows(slot)

        def body(k, _):
            one, _ = norm_rows(xall[slot, pl.ds(pl.multiple_of(k * 96, 96), 96), :].astype(jnp.float32))
            at = pl.ds(pl.multiple_of(slot * piece + k * 96, 96), 96)
            n1[at, :] = (one * pack[N1_GAIN : N1_GAIN + 1, :] + pack[N1_BIAS : N1_BIAS + 1, :]).astype(low)
            return 0

        lax.fori_loop(0, piece // 96, body, 0)
        left = n1[where, :]
        qkv[0, where, :] = (dot(left, low_v[0]) + pack[Q_BIAS : Q_BIAS + 1, columns]).astype(low) * low(0.125)
        qkv[1, where, :] = dot(left, low_v[1]).astype(low)
        qkv[2, where, :] = (dot(left, low_v[2]) + pack[V_BIAS : V_BIAS + 1, columns]).astype(low)

    def tokens_of(number, _):
        first, second = jnp.where(is_mid, near, far), jnp.where(is_mid, far, near)
        slot = jnp.where(
            number == 0, z, jnp.where(number == 1, partner, jnp.where(number == 2, first, second))
        )

        @pl.when(number == 1)
        def _():
            for name in loads:
                if name not in early:
                    loads[name].start()

        @pl.when(is_mid & (number == 1))
        def _():
            for which, source in enumerate((near, far)):
                for k in range(CHUNKS):
                    tok_copy(1, source, k).wait_recv()
                    tok_copy(2 + which, source, k).start()
            for k in range(CHUNKS):
                tok_copy(1, partner, k).wait_recv()

        @pl.when(is_end & (number > 0))
        def _():
            for k in range(CHUNKS):
                tok_copy(1, slot, k).wait_recv()

        project(slot)
        return 0

    lax.fori_loop(0, 4, tokens_of, 0)
    lane = lax.broadcasted_iota(jnp.int32, (1, 128), 1)
    low_lane = lane < 64

    def att_copy(slot):
        return remote_copy(
            own_att.at[slot_rows(slot)], att.at[clip, side], att_send.at[slot], att_recv.at[z], (dp, slot)
        )

    def attend(number, _):
        slot = jnp.where(number == 0, far, jnp.where(number == 1, near, jnp.where(number == 2, partner, z)))
        where = slot_rows(slot)
        stats = jnp.zeros((piece, 128), jnp.float32)
        for t in range(half // 128):
            at = pl.ds(t * 128, 128)
            queries = qkv[0, where, at]
            keys = qkv[1, :, at]
            values = qkv[2, :, at]
            parts = []
            for a in range(2):
                mine = low_lane if a == 0 else jnp.logical_not(low_lane)
                masked = jnp.where(mine, queries, jnp.zeros_like(queries))
                scores = dot(masked, keys, NT) + row_bias
                top = jnp.max(scores, axis=-1, keepdims=True)
                expo = jnp.exp(scores - top)
                denominator = jnp.sum(expo, axis=-1, keepdims=True)
                parts.append(dot(expo.astype(low), values) * (1.0 / denominator))
                stats = jnp.where(lane == STATS + 2 * t + a, top + jnp.log(denominator), stats)
            own_att[where, at] = jnp.where(low_lane, parts[0], parts[1]).astype(low)
        side_v[where, STATS : STATS + 8] = stats[:, STATS : STATS + 8]

        @pl.when(number < 3)
        def _():
            att_copy(slot).start()

        return 0

    lax.fori_loop(0, 4, attend, 0)
    att[clip, side] = own_att[slot_rows(z), :]

    def tiles(count, size, body):
        def one_tile(t, _):
            body(t, pl.ds(pl.multiple_of(t * size, size), size))
            return 0

        lax.fori_loop(0, count, one_tile, 0)

    def chunks(body, carry, size=48):
        def one_chunk(k, carry):
            return body(pl.ds(pl.multiple_of(k * size, size), size), k, carry)

        return lax.fori_loop(0, rows // size, one_chunk, carry)

    def put_vector(row, start, value):
        at = 0
        while at < value.shape[1]:
            line, column = row + (start + at) // width, (start + at) % width
            take = min(value.shape[1] - at, width - column)
            vec_out[line : line + 1, column : column + take] = value[:, at : at + take]
            at += take

    def total(value):
        return jnp.sum(value.astype(jnp.float32), axis=0, keepdims=True)

    zero_row = jnp.zeros((1, width), jnp.float32)
    ready("cot_a")

    def mask(at, k, carry):
        value = (side_v[at, VIS : VIS + 1] * cot_a[at, :].astype(jnp.float32)).astype(low)
        cot_a[at, :] = value
        return carry + total(value)

    put_vector(ALIGN_BIAS, 0, chunks(mask, jnp.zeros((1, cot_a.shape[1]), jnp.float32)))
    lse_rows[...] = side_v[...].T[STATS : STATS + 8]

    def shares_of(source, target, count):
        for c in range(0, source.shape[1], 128):
            flipped = source[:, pl.ds(c, 128)].T
            at = 0
            while at < 128:
                share, inside = (c + at) // count, (c + at) % count
                take = min(128 - at, count - inside)
                rel = jnp.where(core == share % 2, 1, 0)
                target[rel, share // 2, pl.ds(inside, take), :] = flipped[at : at + take]
                at += take

    shares_of(n1, n1s, width // 8)

    def settle_att(number, _):
        slot = lax.rem(z + number, 4)
        att_copy(slot).wait_send()
        remote_copy(
            own_att.at[slot_rows(slot)], att.at[slot // 2, lax.rem(slot, 2)],
            att_send.at[slot], att_recv.at[slot], (dp, slot),
        ).wait_recv()
        return 0

    lax.fori_loop(1, 4, settle_att, 0)
    for k in range(CHUNKS):
        tok_copy(0, z, k).wait_send()
        tok_copy(1, z, k).wait_send()

    @pl.when(is_mid)
    def _():
        for k in range(CHUNKS):
            for which, slot in enumerate((near, far)):
                tok_copy(2 + which, slot, k).wait_send()

    for c in range(2):
        for h in range(2):
            normed[pl.ds(c * piece, piece), pl.ds(h * half, half)] = att[c, h]
    shares_of(normed, la, width // 8)
    ready("out")

    def mix(t, at):
        mixed = dot(normed[...], out_v[:, at]) + pack[OUT_BIAS : OUT_BIAS + 1, at]
        mid_v[pl.ds(0, piece), at] = tok[0, :, at].astype(jnp.float32) + mixed[:piece]
        mid_v[pl.ds(piece, piece), at] = tok[1, :, at].astype(jnp.float32) + mixed[piece:]

    tiles(3, 256, mix)

    def norm(gain, bias, unit, inv):
        def body(at, k, _):
            one, inverse = norm_rows(mid_v[at, :])
            unit[at, :] = one.astype(low)
            side_v[at, inv : inv + 1] = inverse
            normed[at, :] = (one * pack[gain : gain + 1, :] + pack[bias : bias + 1, :]).astype(low)
            return 0

        chunks(body, 0, NORM_ROWS)

    norm(N2_GAIN, N2_BIAS, unit2, INV2)
    shares_of(normed, l2, width // 8)
    ready("up")

    def up(t, at):
        e_v[...] = dot(normed[...], up_v[:, at]) + pack[pl.ds(UP_BIAS + t, 1), :]

        def gelu(here, k, _):
            values = e_v[here, :]
            cdf = 0.5 * (1.0 + lax.erf(values * SQRT_HALF))
            ring[k, :, at] = (values * cdf).astype(low)
            slope[here, at] = (cdf + values * jnp.exp(-0.5 * values * values) * INV_ROOT_TAU).astype(low)
            return 0

        chunks(gelu, 0)
        for c in range(0, width, 128):
            rel = core if c < half else 1 - core
            columns_at = pl.ds(pl.multiple_of(t * width + c, 128), 128)
            ld[1 - rel, t, pl.ds(c % half, 128), :] = ring[:, :, columns_at].reshape(rows, 128).T

    tiles(4, width, up)
    ready("down")

    def down(t, at):
        mid_v[:, at] = (
            mid_v[:, at] + dot(ring[...].reshape(rows, wide), down_v[:, at]) + pack[DOWN_BIAS : DOWN_BIAS + 1, at]
        )

    tiles(3, 256, down)

    def staged(j, target):
        return pltpu.make_async_copy(own[j], target, put_sem.at[j])

    def put_block(at, k, _):
        own[1][k // 4, lax.rem(k, 4)] = (side_v[at, VIS : VIS + 1] * mid_v[at, :]).astype(low)
        return 0

    chunks(put_block, 0)
    staged(1, block_out).start()
    norm(N3_GAIN, N3_BIAS, unit3, INV3)
    shares_of(normed, l3, width // 8)
    ready("align", "cot_b")

    def head(t, at):
        bias = pack[pl.ds(ALIGN_BIAS + t // 3, 1), pl.ds(pl.multiple_of(lax.rem(t, 3) * 256, 256), 256)]
        value = dot(normed[...], align_v[:, at]) + bias
        value = (side_v[pl.ds(0, rows), VIS : VIS + 1] * value).astype(low)
        for k in range(8):
            own[0][k // 4, k % 4, :, at] = value[k * 48 : (k + 1) * 48]

    tiles(4, 256, head)
    staged(0, align_out).start()

    def buffer_of(j):
        return ring.at[:, :, pl.ds(JOBS[j][5], JOBS[j][4])]

    def copies0(j):
        for h in range(2):
            yield remote_copy(
                buffer_of(j).at[pl.ds(4 * h, 4)], got0[j].at[h], send0.at[j, h], recv0.at[j, h], to_core
            )

    def copies1(j):
        yield remote_copy(
            own[j].at[0, pl.ds(2 * (1 - x), 2)], got1[j].at[0], send1.at[j, 0], recv1.at[j, 0], to_x
        )
        yield remote_copy(
            own[j].at[1, pl.ds(2 * (1 - y), 2)], got1[j].at[1], send1.at[j, 1], recv1.at[j, 1], to_y
        )

    def copies2(j):
        yield remote_copy(own[j].at[0, 2 * x + 1 - y], got2[j].at[0], send2.at[j, 0], recv2.at[j, 0], to_y)
        yield remote_copy(own[j].at[1, 2 * y + 1 - x], got2[j].at[1], send2.at[j, 1], recv2.at[j, 1], to_x)

    def shares(j):
        return (own[j].at[0, 2 * x + y], own[j].at[1, 2 * y + x])

    def copiesz(j, slot, device):
        for h, share in enumerate(shares(j)):
            yield remote_copy(share, gotz[j].at[slot, h], sendz.at[j, slot, h], recvz.at[j, slot, h], device)

    def copiesq(j, source, slot, device):
        got, m = gotq[j - PLAIN], j - PLAIN
        for h, share in enumerate(shares(j)):
            yield remote_copy(
                share if source is None else got.at[source, h],
                got.at[slot, h], sendq.at[m, slot, h], recvq.at[m, slot, h], device,
            )

    def result(j, h, source):
        matrix, row, count, column, size, _ = JOBS[j]
        return pltpu.make_async_copy(
            source, outs[matrix].at[pl.ds(row + h * count // 2, count // 2), pl.ds(column, size)], out_sem.at[j, h]
        )

    def result_q(j, h, which, source):
        count, m = JOBS[j][2] // 2, j - PLAIN
        at = side if which == 0 else 1 - side
        column = pl.multiple_of(m * width + at * half, 128)
        return pltpu.make_async_copy(
            source, outs[0].at[pl.ds(h * count, count), pl.ds(column, half)], outq_sem.at[m, which, h]
        )

    def stage(j, number):
        if number == 0:
            for copy in copies0(j):
                copy.start()
        if number == 1:
            for copy in copies0(j):
                copy.wait()
            add_into(own[j], own[j], got0[j])
            for copy in copies1(j):
                copy.start()
        if number == 2:
            for copy in copies1(j):
                copy.wait()
            first, second = (own[j].at[0, pl.ds(2 * x, 2)], own[j].at[1, pl.ds(2 * y, 2)])
            add_into(first, first, got1[j].at[0])
            add_into(second, second, got1[j].at[1])
            for copy in copies2(j):
                copy.start()
        if number == 3:
            for copy in copies2(j):
                copy.wait()
            for h, share in enumerate(shares(j)):
                add_into(share, share, got2[j].at[h])

            @pl.when(is_end)
            def _():
                for copy in copiesq(j, None, 0, to_z1) if j >= PLAIN else copiesz(j, 0, to_z1):
                    copy.start()

        if number >= 4 and j >= PLAIN:
            stage_q(j, number)
            return
        if number == 4:

            @pl.when(is_mid)
            def _():
                for copy in copiesz(j, 0, to_z1):
                    copy.wait_recv()
                for h, share in enumerate(shares(j)):
                    add_into(share, share, gotz[j].at[0, h])
                for copy in copiesz(j, 1, to_z3):
                    copy.start()

            @pl.when(is_end)
            def _():
                for copy in copiesz(j, 0, to_z1):
                    copy.wait_send()

        if number == 5:

            @pl.when(is_mid)
            def _():
                for copy in copiesz(j, 1, to_z3):
                    copy.wait()
                for h, share in enumerate(shares(j)):
                    add_into(share, share, gotz[j].at[1, h])
                for copy in copiesz(j, 0, to_z1):
                    copy.start()
                for h, share in enumerate(shares(j)):
                    result(j, h, share).start()

        if number == 6:

            @pl.when(is_mid)
            def _():
                for copy in copiesz(j, 0, to_z1):
                    copy.wait_send()

            @pl.when(is_end)
            def _():
                for copy in copiesz(j, 0, to_z1):
                    copy.wait_recv()
                for h in range(2):
                    result(j, h, gotz[j].at[0, h]).start()

    def stage_q(j, number):
        got = gotq[j - PLAIN]
        if number == 4:

            @pl.when(is_mid)
            def _():
                for copy in copiesq(j, None, 1, to_z3):
                    copy.start()
                for copy in copiesq(j, None, 0, to_z1):
                    copy.wait_recv()
                for copy in copiesq(j, 0, 2, to_z3):
                    copy.start()

            @pl.when(is_end)
            def _():
                for copy in copiesq(j, None, 0, to_z1):
                    copy.wait_send()

        if number == 5:

            @pl.when(is_mid)
            def _():
                for copy in copiesq(j, None, 1, to_z3):
                    copy.wait()
                for copy in copiesq(j, 0, 2, to_z3):
                    copy.wait()
                for h, share in enumerate(shares(j)):
                    add_into(share, share, got.at[2, h])
                    add_into(got.at[0, h], got.at[0, h], got.at[1, h])
                for copy in copiesq(j, None, 1, to_z1):
                    copy.start()
                for copy in copiesq(j, 0, 0, to_z1):
                    copy.start()
                for h, share in enumerate(shares(j)):
                    result_q(j, h, 0, share).start()
                    result_q(j, h, 1, got.at[0, h]).start()

        if number == 6:

            @pl.when(is_mid)
            def _():
                for copy in copiesq(j, None, 1, to_z1):
                    copy.wait_send()
                for copy in copiesq(j, 0, 0, to_z1):
                    copy.wait_send()

            @pl.when(is_end)
            def _():
                for copy in copiesq(j, None, 1, to_z1):
                    copy.wait_recv()
                for copy in copiesq(j, 0, 0, to_z1):
                    copy.wait_recv()
                for h in range(2):
                    result_q(j, h, 0, got.at[0, h]).start()
                    result_q(j, h, 1, got.at[1, h]).start()

    def results_done():
        for j in range(COUNT):
            for h in range(2):
                if j < PLAIN:
                    result(j, h, gotz[j].at[0, h]).wait()
                else:
                    for which in range(2):
                        result_q(j, h, which, gotq[j - PLAIN].at[0, h]).wait()

    def gradient(j, mine, left, right):
        count, size = JOBS[j][2], JOBS[j][4]
        target = own[j] if mine else buffer_of(j)
        for c in range(0, size, min(size, 384 if size % 384 == 0 else 512)):
            at = pl.ds(c, min(size, 384 if size % 384 == 0 else 512))
            value = dot(left, right(at)).astype(low)
            for chip in range(4):
                cy, cx = chip // 2, chip % 2
                for h in range(2):
                    k = 2 * cx + cy if h == 0 else 2 * cy + cx
                    start = chip * count + h * count // 2
                    part = value[start : start + count // 2]
                    if mine:
                        target[h, k, :, at] = part
                    else:
                        target[4 * h + k, :, at] = part

    def job(j, mine):
        matrix, row, count, column, size, _ = JOBS[j]
        lhs, rhs = ((n1s, None), (la, low_o), (l2, slope), (ld, low_d), (l3, cot_a))[matrix]
        left = lhs[1 if mine else 0, :, pl.ds(row, count), :].reshape(4 * count, lhs.shape[3])
        if matrix == 0:
            gradient(j, mine, left, lambda at: grad_at(j - PLAIN)[...])
        else:
            gradient(j, mine, left, lambda at: rhs[:, pl.ds(column + at.start, at.size)])

    def norm_back(e, one, inverse, gain):
        scaled = e * gain
        return inverse * (
            scaled
            - jnp.mean(scaled, axis=-1, keepdims=True)
            - one * jnp.mean(scaled * one, axis=-1, keepdims=True)
        )

    def norm_pass(unit, inv, gain_row, base, low_target, sums):
        def body(at, k, carry):
            e = e_v[at, :]
            one = unit[at, :].astype(jnp.float32)
            value = base(at) + norm_back(e, one, side_v[at, inv : inv + 1], pack[gain_row : gain_row + 1, :])
            mid_v[at, :] = value
            rounded = value.astype(low)
            low_target[at, :] = rounded
            return (carry[0] + total(e * one), carry[1] + total(e), carry[2] + total(rounded))

        for row, value in zip(sums, chunks(body, (zero_row,) * 3, NORM_ROWS)):
            put_vector(row, 0, value)

    def e3():
        def body(t, at):
            e_v[:, at] = dot(cot_a[...], align_v[at, :], NT)

        tiles(3, 256, body)

    def norm3():
        norm_pass(
            unit3, INV3, N3_GAIN, lambda at: side_v[at, VIS : VIS + 1] * cot_b[at, :].astype(jnp.float32), low_d,
            (N3_GAIN, N3_BIAS, DOWN_BIAS),
        )

    def feed():
        def body(t, at):
            value = (dot(low_d[...], down_v[at, :], NT) * slope[:, at].astype(jnp.float32)).astype(low)
            slope[:, at] = value
            vec_out[pl.ds(UP_BIAS + t, 1), :] = total(value)

        tiles(4, width, body)

    def e2():
        def body(t, at):
            e_v[:, at] = dot(slope[...], up_v[at, :], NT)

        tiles(3, 256, body)

    def norm2():
        norm_pass(unit2, INV2, N2_GAIN, lambda at: mid_v[at, :], low_o, (N2_GAIN, N2_BIAS, OUT_BIAS))

    def in_copy(slot, t):
        at = pl.ds(t * 128, 128)
        return remote_copy(
            in_src.at[slot // 2, lax.rem(slot, 2), :, at], grad_att.at[z, :, at],
            in_send.at[slot, t], in_recv.at[z, t], (dp, slot),
        )

    def back_att():
        for h in range(2):
            value = dot(low_o[...], out_v[pl.ds(h * half, half), :], NT).astype(low)
            for c in range(2):
                in_src[c, h] = value[c * piece : (c + 1) * piece]
        for t in range(half // 128):

            def start(number, _):
                in_copy(lax.rem(z + number, 4), t).start()
                return 0

            lax.fori_loop(1, 4, start, 0)
        grad_att[z] = in_src[clip, side]

    def settle(t):
        at = pl.ds(t * 128, 128)

        def body(number, _):
            slot = lax.rem(z + number, 4)
            in_copy(slot, t).wait_send()
            remote_copy(
                in_src.at[0, 0, :, at], grad_att.at[slot, :, at], in_send.at[slot, t], in_recv.at[slot, t], (dp, slot)
            ).wait_recv()
            return 0

        lax.fori_loop(1, 4, body, 0)

        def spread(slot, _):
            where = slot_rows(slot)
            stats = jnp.zeros((piece, 128), jnp.float32)
            product = grad_att[slot, :, at].astype(jnp.float32) * own_att[where, at].astype(jnp.float32)
            for a in range(2):
                mine = low_lane if a == 0 else jnp.logical_not(low_lane)
                value = jnp.sum(jnp.where(mine, product, 0.0), axis=-1, keepdims=True)
                stats = jnp.where(lane == STATS + a, value, stats)
            side_v[where, STATS : STATS + 2] = stats[:, STATS : STATS + 2]
            return 0

        lax.fori_loop(0, 4, spread, 0)
        spread_rows[2 * t : 2 * t + 2, :] = side_v[...].T[STATS : STATS + 2]

    def pair(number):
        t, b = number // 3, lax.rem(number, 3)
        at = pl.ds(pl.multiple_of(t * 128, 128), 128)
        queries = qkv[0, :, at]
        grads = grad_att[:, :, at].reshape(4 * piece, 128)
        keys_at = pl.ds(pl.multiple_of(b * KEY_BLOCK, KEY_BLOCK), KEY_BLOCK)
        keys = qkv[1, keys_at, at]
        values = qkv[2, keys_at, at]
        grad_k = jnp.zeros((KEY_BLOCK, 128), jnp.float32)
        grad_v = jnp.zeros((KEY_BLOCK, 128), jnp.float32)
        grad_queries = jnp.where(b == 0, 0.0, grad_q[...])
        for a in range(2):
            mine = low_lane if a == 0 else jnp.logical_not(low_lane)
            zero = jnp.zeros((), low)
            q_mine = jnp.where(mine, queries, zero)
            g_mine = jnp.where(mine, grads, zero)
            k_mine = jnp.where(mine, keys, zero)
            row = pl.ds(2 * t + a, 1)
            scores = dot(keys, q_mine, NT) + side_v[keys_at, KEY : KEY + 1]
            probs = jnp.exp(scores - lse_rows[row, :])
            back = (probs * (dot(values, g_mine, NT) - spread_rows[row, :])).astype(low)
            grad_v = grad_v + dot(probs.astype(low), g_mine)
            grad_k = grad_k + dot(back, q_mine)
            grad_queries = grad_queries + dot(back, k_mine, TN)
        grad_at(1)[keys_at, at] = grad_k.astype(low)
        grad_at(2)[keys_at, at] = grad_v.astype(low)
        grad_q[...] = grad_queries

        @pl.when(b == 2)
        def _():
            grad_at(0)[:, at] = (grad_q[...] * 0.125).astype(low)

    def pair_copy():
        return remote_copy(e_at(partner), from_pair, pair_send, pair_recv, to_z1)

    def end_copy(which, slot):
        return remote_copy(e_at(slot), from_end[which], end_send.at[which], end_recv.at[which], to_z1)

    def out_copy(which, slot):
        return remote_copy(e_at(slot), total_in, out_send.at[which], out_recv, (dp, slot))

    targets = (3 - 3 * clip, 2 - clip)
    mine_rows = slot_rows(clip)

    def dx(number):
        slot = (targets + (partner, z))[number]
        where = slot_rows(slot)
        value = sum(dot(grad_at(m)[where, :], low_v[m], NT) for m in range(3))
        e_at(slot)[...] = value.astype(low)
        if number == 3:
            e_v[mine_rows, :] = value
        if number < 2:

            @pl.when(is_end)
            def _():
                end_copy(number, slot).start()

        if number == 2:
            pair_copy().start()
        one, _ = norm_rows(xall[slot].astype(jnp.float32))
        for row, term in ((N1_GAIN, total(value * one)), (N1_BIAS, total(value))):
            vec_out[row : row + 1, :] = vec_out[row : row + 1, :] + term

    def sums():
        spot = lax.broadcasted_iota(jnp.int32, (1, width), 1)
        for row, m in ((Q_BIAS, 0), (V_BIAS, 2)):
            value = total(grad_at(m)[...])
            value = jnp.concatenate([value, value], axis=1)
            put_vector(row, 0, jnp.where((spot < half) == (side == 0), value, 0.0))

    def forward(which):
        @pl.when(is_mid)
        def _():
            slot = targets[which]
            end_copy(which, slot).wait_recv()
            add_into(e_at(slot), e_at(slot), from_end[which])
            out_copy(which, slot).start()

    vec_devices = (to_core, to_x, to_y, to_z1, to_z2)

    def vec_copy(k):
        return remote_copy(vec_out, vec_got.at[k], vsend.at[k], vrecv.at[k], vec_devices[k])

    def vec(k):
        if k > 0:
            vec_copy(k - 1).wait()
            vec_out[...] = vec_out[...] + vec_got[k - 1]
        if k < 5:
            vec_copy(k).start()

    def norm1():
        pair_copy().wait()
        e_v[mine_rows, :] = e_v[mine_rows, :] + from_pair[...].astype(jnp.float32)
        out_copy(0, partner).wait_recv()
        e_v[slot_rows(1 - clip), :] = total_in[...].astype(jnp.float32)

        def body(at, k, _):
            half_clip = pl.ds(pl.multiple_of(lax.rem(k, 2) * NORM_ROWS, NORM_ROWS), NORM_ROWS)
            one, inverse = norm_rows(tok[k // 2, half_clip, :].astype(jnp.float32))
            value = mid_v[at, :] + norm_back(e_v[at, :], one, inverse, pack[N1_GAIN : N1_GAIN + 1, :])
            low_d[at, :] = value.astype(low)
            return 0

        chunks(body, 0, NORM_ROWS)
        pltpu.make_async_copy(low_d, grad_tokens, put_sem.at[2]).start()

    singles = dict(
        e3=e3, norm3=norm3, feed=feed, e2=e2, norm2=norm2, back_att=back_att, sums=sums, norm1=norm1
    )
    several = dict(settle=settle, dx=dx, fwd=forward, vec=vec)
    staged(0, align_out).wait()
    staged(1, block_out).wait()

    def run(entries):
        for entry in entries:
            if isinstance(entry, tuple):
                if entry[1] in ("far", "own"):
                    job(entry[0], entry[1] == "own")
                else:
                    stage(*entry)
            elif entry in singles:
                singles[entry]()
            else:
                several[entry[:-1]](int(entry[-1]))

    spots = [k for k, entry in enumerate(PLAN) if entry == "pair"]
    run(PLAN[: spots[0]])

    def pair_and_more(number, _):
        pair(number)
        for k in range(len(spots) - 1):
            if spots[k] + 1 < spots[k + 1]:

                @pl.when(number == k)
                def _():
                    run(PLAN[spots[k] + 1 : spots[k + 1]])

        return 0

    lax.fori_loop(0, len(spots), pair_and_more, 0)
    run(PLAN[spots[-1] + 1 :])
    results_done()
    pltpu.make_async_copy(low_d, grad_tokens, put_sem.at[2]).wait()

    @pl.when(is_mid)
    def _():
        for which in range(2):
            out_copy(which, targets[which]).wait_send()

    @pl.when(is_end)
    def _():
        for which in range(2):
            end_copy(which, targets[which]).wait_send()


def layer(slot_mask, counts, vectors, tok, cot_a, cot_b, w_align, w_down, w_up, w_out, w_qkv):
    _, piece, width = tok.shape
    rows, half, wide, align = 2 * piece, width // 2, w_up.shape[1], w_align.shape[1]
    low, full = jnp.bfloat16, jnp.float32
    vmem = pl.BlockSpec(memory_space=pltpu.VMEM)
    hbm = pl.BlockSpec(memory_space=pl.ANY)
    dma = pltpu.SemaphoreType.DMA
    v = pltpu.VMEM
    shapes = [(2, 4, job[2] // 2, job[4]) for job in JOBS]
    scratch = (
        [v(shape, low) for shape in shapes]
        + [v(shape, low) for shape in shapes]
        + [v((2, 2) + shape[2:], low) for shape in shapes]
        + [v((2,) + shape[2:], low) for shape in shapes]
        + [v((2, 2) + shape[2:], low) for shape in shapes[:PLAIN]]
        + [v((3, 2) + shape[2:], low) for shape in shapes[PLAIN:]]
        + [v((5, PACK_ROWS, width), full)]
        + [v(vector.shape, full) for vector in vectors]
        + [v((PACK_ROWS, width), full), v((4 * piece, 128), full)]
        + [v(w_align.shape, low), v(w_down.shape, low), v(w_up.shape, low), v(w_out.shape, low)]
        + [v((3, width, half), low), v((2, piece, width), low), v((4, piece, width), low), v((4 * piece, width), low)]
        + [v((3, 4 * piece, half), low), v((4 * piece, half), low), v((2, 2, piece, half), low)]
        + [v((8, 4 * piece), full)] * 2
        + [v((rows, width), full), v((rows, width), full), v((rows, width), low), v((8, 48, wide), low)]
        + [v((rows, wide), low), v((2, 4, wide // 8, rows), low)]
        + [v((2, 4, width // 8, rows), low)] * 3
        + [v((rows, width), low)] * 2
        + [v((rows, align), low), v((rows, width), low)]
        + [v((4, piece, half), low), v((2, 4, width // 8, 4 * piece), low), v((4 * piece, 128), full)]
        + [dma((10,))]
        + [dma((COUNT, 2))] * 6
        + [dma((PLAIN, 2, 2))] * 2
        + [dma((3, 3, 2))] * 2
        + [dma((PLAIN, 2)), dma((3, 2, 2))]
        + [dma((5,))] * 2
        + [dma((4, CHUNKS))] * 2
        + [dma((4,))] * 2
        + [dma((4, 3))] * 2
        + [dma(())] * 2
        + [dma((2,))] * 2
        + [dma((2,)), dma(())]
        + [dma((3,)), dma((12,))]
    )
    struct = jax.ShapeDtypeStruct
    return pl.pallas_call(
        layer_kernel,
        name="layer",
        out_shape=[
            struct((2, 4, 48, width), low),
            struct((2, 4, 48, align), low),
            struct((rows, width), low),
            struct((PACK_ROWS, width), full),
        ]
        + [struct((w.shape[0] // 8, w.shape[1]), low) for w in (w_qkv, w_out, w_up, w_down, w_align)],
        in_specs=[vmem, pl.BlockSpec(memory_space=pltpu.SMEM)] + [hbm] * 20,
        out_specs=[hbm, hbm, hbm, vmem] + [hbm] * 5,
        scratch_shapes=scratch,
        compiler_params=pltpu.CompilerParams(
            collective_id=0, has_side_effects=True, vmem_limit_bytes=63 * 2**20
        ),
    )(slot_mask, counts, *vectors, tok, cot_a, cot_b, w_align, w_down, w_up, w_out, w_qkv)


VECTORS = (
    N1_GAIN, N1_BIAS, Q_BIAS, V_BIAS, OUT_BIAS, N2_GAIN, N2_BIAS, DOWN_BIAS, N3_GAIN, N3_BIAS, UP_BIAS, ALIGN_BIAS,
)


def finish_kernel(*refs):
    shares, pack, through_in = refs[:5], refs[5], refs[6:9]
    wide, vectors, through_out = refs[9:14], refs[14:26], refs[26:29]
    low_v, wide_v, held, pack_v, vectors_v = refs[29:34], refs[34:39], refs[39:42], refs[42], refs[43:55]
    in_sem, out_sem, vector_sem = refs[55:]
    ins = [pltpu.make_async_copy(shares[k], low_v[k], in_sem.at[k]) for k in range(5)]
    outs = [pltpu.make_async_copy(wide_v[k], wide[k], out_sem.at[k]) for k in range(5)]
    through = [
        (
            pltpu.make_async_copy(through_in[k], held[k], in_sem.at[5 + k]),
            pltpu.make_async_copy(held[k], through_out[k], out_sem.at[5 + k]),
        )
        for k in range(3)
    ]
    pack_in = pltpu.make_async_copy(pack, pack_v, in_sem.at[8])
    for copy in [pack_in] + ins:
        copy.start()
    for copy, _ in through:
        copy.start()
    width = pack.shape[1]
    vectors_out = [
        pltpu.make_async_copy(vectors_v[k], vectors[k], vector_sem.at[k]) for k in range(len(vectors))
    ]
    pack_in.wait()
    for row, ref in zip(VECTORS, vectors_v):
        for start in range(0, ref.shape[0], width):
            size = min(width, ref.shape[0] - start)
            line = row + start // width
            ref[pl.ds(start, size)] = pack_v[line : line + 1, 0:size].reshape(size)
    for copy in vectors_out:
        copy.start()
    for k in range(5):
        ins[k].wait()
        wide_v[k][...] = low_v[k][...].astype(jnp.float32)
        outs[k].start()
    for first, second in through:
        first.wait()
        second.start()
    for copy in outs + vectors_out:
        copy.wait()
    for _, copy in through:
        copy.wait()


def finish(shares, pack, through, sizes):
    hbm = pl.BlockSpec(memory_space=pl.ANY)
    struct = jax.ShapeDtypeStruct
    results = pl.pallas_call(
        finish_kernel,
        name="finish",
        out_shape=[struct(share.shape, jnp.float32) for share in shares]
        + [struct((size,), jnp.float32) for size in sizes]
        + [struct(array.shape, array.dtype) for array in through],
        in_specs=[hbm] * 9,
        out_specs=[hbm] * 20,
        scratch_shapes=[pltpu.VMEM(share.shape, share.dtype) for share in shares]
        + [pltpu.VMEM(share.shape, jnp.float32) for share in shares]
        + [pltpu.VMEM(array.shape, array.dtype) for array in through]
        + [pltpu.VMEM(pack.shape, pack.dtype)]
        + [pltpu.VMEM((size,), jnp.float32) for size in sizes]
        + [pltpu.SemaphoreType.DMA((9,)), pltpu.SemaphoreType.DMA((8,)), pltpu.SemaphoreType.DMA((12,))],
        compiler_params=pltpu.CompilerParams(vmem_limit_bytes=62 * 2**20),
    )(*shares, pack, *through)
    return results[:5], results[5:17], results[17:]


def norm_forward(values, gain, shift):
    center = values - jnp.mean(values, axis=-1, keepdims=True)
    inverse = lax.rsqrt(jnp.mean(center * center, axis=-1, keepdims=True) + EPSILON)
    normed = center * inverse
    return (normed * gain + shift, normed, inverse)


def norm_backward(upstream, normed, inverse, gain):
    scaled = upstream * gain
    inner = (
        scaled
        - jnp.mean(scaled, axis=-1, keepdims=True)
        - normed * jnp.mean(scaled * normed, axis=-1, keepdims=True)
    )
    return (inverse * inner, jnp.sum(upstream * normed, axis=0), jnp.sum(upstream, axis=0))


def gelu_slope(values):
    return (
        0.5 * (1.0 + lax.erf(values * SQRT_HALF))
        + values * jnp.exp(-0.5 * values * values) * INV_ROOT_TAU
    )


def weight_grad(left, right):
    return lax.dot_general(
        left, right, (((0,), (0,)), ((), ())), preferred_element_type=jnp.float32
    )


def input_grad(upstream, weight):
    return lax.dot_general(
        upstream, weight, (((1,), (1,)), ((), ())), preferred_element_type=jnp.float32
    )


def masked_scores(query_heads, key_heads, key_valid, scale):
    scores = (
        jnp.einsum("cqhd,ckhd->chqk", query_heads, key_heads, preferred_element_type=jnp.float32)
        * scale
    )
    return jnp.where(key_valid, scores, -1e30)


def column_sum(values):
    return jnp.sum(values, axis=0, dtype=jnp.float32)


def local(
    tokens,
    frame_counts,
    slot_mask,
    norm1_gain,
    norm1_bias,
    w_qkv,
    q_bias,
    v_bias,
    w_out,
    out_bias,
    norm2_gain,
    norm2_bias,
    w_up,
    up_bias,
    w_down,
    down_bias,
    norm3_gain,
    norm3_bias,
    w_align,
    align_bias,
    cot_block,
    cot_align,
):
    clip_count, frame_dev, slot_count, width = tokens.shape
    align_width = w_align.shape[1]
    head_size = width // HEADS
    scale = 1.0 / math.sqrt(head_size)
    row_count = clip_count * frame_dev * slot_count
    cycle_pos = lax.axis_index("blk")
    frame_ids = cycle_pos * frame_dev + jnp.arange(frame_dev, dtype=jnp.int32)
    own_slots = lax.dynamic_slice_in_dim(slot_mask, cycle_pos * frame_dev, frame_dev, 1)
    own_mask = (frame_ids[None, :, None] < frame_counts[:, None, None]) & (own_slots > 0)
    visible = own_mask.astype(jnp.float32).reshape(row_count, 1)
    all_frames = jnp.arange(slot_mask.shape[1], dtype=jnp.int32)
    key_valid = (all_frames[None, :, None] < frame_counts[:, None, None]) & (slot_mask > 0)
    key_valid = key_valid.reshape(clip_count, 1, 1, -1)
    inputs = tokens.reshape(row_count, width).astype(jnp.float32)
    normed_one, unit_one, inverse_one = norm_forward(inputs, norm1_gain, norm1_bias)
    normed1 = normed_one.astype(jnp.bfloat16)
    projected = jnp.dot(normed1, w_qkv, preferred_element_type=jnp.float32)
    queries = (projected[:, :width] + q_bias).astype(jnp.bfloat16)
    keys_local = projected[:, width : 2 * width].astype(jnp.bfloat16)
    values_local = (projected[:, 2 * width :] + v_bias).astype(jnp.bfloat16)
    block_shape = (clip_count, frame_dev, slot_count, width)
    heads_shape = (clip_count, -1, HEADS, head_size)
    keys_all, values_all = (
        lax.all_gather(keys_local.reshape(block_shape), "blk", axis=1, tiled=True),
        lax.all_gather(values_local.reshape(block_shape), "blk", axis=1, tiled=True),
    )
    key_heads = keys_all.reshape(heads_shape)
    value_heads = values_all.reshape(heads_shape)
    query_heads = queries.reshape(heads_shape)
    scores = masked_scores(query_heads, key_heads, key_valid, scale)
    top = jnp.max(scores, axis=-1, keepdims=True)
    expo = jnp.exp(scores - top)
    total = jnp.sum(expo, axis=-1, keepdims=True)
    probs_low = (expo / total).astype(jnp.bfloat16)
    attended = jnp.einsum(
        "chqk,ckhd->cqhd", probs_low, value_heads, preferred_element_type=jnp.float32
    )
    attended = attended.astype(jnp.bfloat16).reshape(row_count, width)
    mid = inputs + jnp.dot(attended, w_out, preferred_element_type=jnp.float32) + out_bias
    normed_two, unit_two, inverse_two = norm_forward(mid, norm2_gain, norm2_bias)
    normed2 = normed_two.astype(jnp.bfloat16)
    hidden = jnp.dot(normed2, w_up, preferred_element_type=jnp.float32) + up_bias
    active = jax.nn.gelu(hidden, approximate=False).astype(jnp.bfloat16)
    after = mid + jnp.dot(active, w_down, preferred_element_type=jnp.float32) + down_bias
    block_out = (visible * after).astype(jnp.bfloat16).reshape(block_shape)
    normed_three, unit_three, inverse_three = norm_forward(after, norm3_gain, norm3_bias)
    normed3 = normed_three.astype(jnp.bfloat16)
    target = jnp.dot(normed3, w_align, preferred_element_type=jnp.float32) + align_bias
    aligned = (
        (visible * target)
        .astype(jnp.bfloat16)
        .reshape(clip_count, frame_dev, slot_count, align_width)
    )
    back_align = (visible * cot_align.reshape(row_count, align_width).astype(jnp.float32)).astype(
        jnp.bfloat16
    )
    grad_align_bias = column_sum(back_align)
    grad_w_align = weight_grad(normed3, back_align)
    back_norm3, grad_norm3_gain, grad_norm3_bias = norm_backward(
        input_grad(back_align, w_align), unit_three, inverse_three, norm3_gain
    )
    back_after = visible * cot_block.reshape(row_count, width).astype(jnp.float32) + back_norm3
    back_down = back_after.astype(jnp.bfloat16)
    grad_down_bias = column_sum(back_down)
    grad_w_down = weight_grad(active, back_down)
    back_up = (input_grad(back_down, w_down) * gelu_slope(hidden)).astype(jnp.bfloat16)
    grad_up_bias = column_sum(back_up)
    grad_w_up = weight_grad(normed2, back_up)
    back_norm2, grad_norm2_gain, grad_norm2_bias = norm_backward(
        input_grad(back_up, w_up), unit_two, inverse_two, norm2_gain
    )
    back_mid = back_after + back_norm2
    back_out = back_mid.astype(jnp.bfloat16)
    grad_out_bias = column_sum(back_out)
    grad_w_out = weight_grad(attended, back_out)
    back_attended = input_grad(back_out, w_out).astype(jnp.bfloat16).reshape(heads_shape)
    scores = masked_scores(query_heads, key_heads, key_valid, scale)
    probs = jnp.exp(scores - top) / total
    probs_low = probs.astype(jnp.bfloat16)
    back_probs = jnp.einsum(
        "cqhd,ckhd->chqk", back_attended, value_heads, preferred_element_type=jnp.float32
    )
    spread = jnp.sum(probs * back_probs, axis=-1, keepdims=True)
    back_scores = (probs * (back_probs - spread)).astype(jnp.bfloat16)
    back_queries = (
        jnp.einsum("chqk,ckhd->cqhd", back_scores, key_heads, preferred_element_type=jnp.float32)
        * scale
    )
    back_queries = back_queries.astype(jnp.bfloat16).reshape(row_count, width)
    value_terms = jnp.einsum(
        "chqk,cqhd->ckhd", probs_low, back_attended, preferred_element_type=jnp.float32
    )
    key_terms = (
        jnp.einsum("chqk,cqhd->ckhd", back_scores, query_heads, preferred_element_type=jnp.float32)
        * scale
    )
    whole_shape = (clip_count, -1, slot_count, width)
    key_share, value_share = (
        lax.psum_scatter(
            key_terms.reshape(whole_shape).astype(jnp.bfloat16),
            "blk",
            scatter_dimension=1,
            tiled=True,
        ).astype(jnp.float32),
        lax.psum_scatter(
            value_terms.reshape(whole_shape).astype(jnp.bfloat16),
            "blk",
            scatter_dimension=1,
            tiled=True,
        ).astype(jnp.float32),
    )
    back_keys = key_share.astype(jnp.bfloat16).reshape(row_count, width)
    back_values = value_share.astype(jnp.bfloat16).reshape(row_count, width)
    grad_q_bias = column_sum(back_queries)
    grad_v_bias = column_sum(back_values)
    combined = jnp.concatenate([back_queries, back_keys, back_values], axis=1)
    grad_w_qkv = weight_grad(normed1, combined)
    back_norm1, grad_norm1_gain, grad_norm1_bias = norm_backward(
        input_grad(combined, w_qkv), unit_one, inverse_one, norm1_gain
    )
    grad_tokens = (back_mid + back_norm1).astype(jnp.bfloat16).reshape(block_shape)
    vector_total = lax.psum(
        (
            grad_norm1_gain,
            grad_norm1_bias,
            grad_q_bias,
            grad_v_bias,
            grad_out_bias,
            grad_norm2_gain,
            grad_norm2_bias,
            grad_up_bias,
            grad_down_bias,
            grad_norm3_gain,
            grad_norm3_bias,
            grad_align_bias,
        ),
        ("dp", "blk"),
    )
    row_part = (
        lax.psum_scatter(grad_w_qkv, "dp", scatter_dimension=0, tiled=True),
        lax.psum_scatter(grad_w_out, "dp", scatter_dimension=0, tiled=True),
        lax.psum_scatter(grad_w_up, "dp", scatter_dimension=0, tiled=True),
        lax.psum_scatter(grad_w_down, "dp", scatter_dimension=0, tiled=True),
        lax.psum_scatter(grad_w_align, "dp", scatter_dimension=0, tiled=True),
    )
    matrix_total = (
        lax.psum(row_part[0].astype(jnp.bfloat16), "blk").astype(jnp.float32),
        lax.psum(row_part[1].astype(jnp.bfloat16), "blk").astype(jnp.float32),
        lax.psum(row_part[2].astype(jnp.bfloat16), "blk").astype(jnp.float32),
        lax.psum(row_part[3].astype(jnp.bfloat16), "blk").astype(jnp.float32),
        lax.psum(row_part[4].astype(jnp.bfloat16), "blk").astype(jnp.float32),
    )
    return (
        block_out,
        aligned,
        grad_tokens,
        vector_total[0],
        vector_total[1],
        matrix_total[0],
        vector_total[2],
        vector_total[3],
        matrix_total[1],
        vector_total[4],
        vector_total[5],
        vector_total[6],
        matrix_total[2],
        vector_total[7],
        matrix_total[3],
        vector_total[8],
        vector_total[9],
        vector_total[10],
        matrix_total[4],
        vector_total[11],
    )


def local_kernels(
    tokens, frame_counts, slot_mask, norm1_gain, norm1_bias, w_qkv, q_bias, v_bias, w_out, out_bias, norm2_gain,
    norm2_bias, w_up, up_bias, w_down, down_bias, norm3_gain, norm3_bias, w_align, align_bias, cot_block, cot_align,
):
    clip_count, frame_dev, slot_count, width = tokens.shape
    align = w_align.shape[1]
    piece = frame_dev * slot_count
    rows = clip_count * piece
    vectors = [
        norm1_gain, norm1_bias, q_bias, v_bias, out_bias, norm2_gain, norm2_bias, down_bias, norm3_gain, norm3_bias,
        up_bias, align_bias,
    ]
    block_out, align_out, grad_tokens, vec, *shares = layer(
        slot_mask, frame_counts, vectors, tokens.reshape(clip_count, piece, width), cot_align.reshape(rows, align),
        cot_block.reshape(rows, width), w_align, w_down, w_up, w_out, w_qkv,
    )
    matrices, totals, (block_out, align_out, grad_tokens) = finish(
        shares, vec, (block_out, align_out, grad_tokens), [vector.shape[0] for vector in vectors]
    )
    (
        grad_norm1_gain, grad_norm1_bias, grad_q_bias, grad_v_bias, grad_out_bias, grad_norm2_gain, grad_norm2_bias,
        grad_down_bias, grad_norm3_gain, grad_norm3_bias, grad_up_bias, grad_align_bias,
    ) = totals
    return (
        block_out.reshape(tokens.shape),
        align_out.reshape(cot_align.shape),
        grad_tokens.reshape(tokens.shape),
        grad_norm1_gain,
        grad_norm1_bias,
        matrices[0],
        grad_q_bias,
        grad_v_bias,
        matrices[1],
        grad_out_bias,
        grad_norm2_gain,
        grad_norm2_bias,
        matrices[2],
        grad_up_bias,
        matrices[3],
        grad_down_bias,
        grad_norm3_gain,
        grad_norm3_bias,
        matrices[4],
        grad_align_bias,
    )


def solution(mesh):
    in_specs = (
        P("dp", "blk", None, None),
        P("dp"),
        P("dp", None, None),
        P(),
        P(),
        P(),
        P(),
        P(),
        P(),
        P(),
        P(),
        P(),
        P(),
        P(),
        P(),
        P(),
        P(),
        P(),
        P(),
        P(),
        P("dp", "blk", None, None),
        P("dp", "blk", None, None),
    )
    out_specs = (
        P("dp", "blk", None, None),
        P("dp", "blk", None, None),
        P("dp", "blk", None, None),
        P(),
        P(),
        P("dp", None),
        P(),
        P(),
        P("dp", None),
        P(),
        P(),
        P(),
        P("dp", None),
        P(),
        P("dp", None),
        P(),
        P(),
        P(),
        P("dp", None),
        P(),
    )
    sizes = (mesh.shape["dp"], mesh.shape["blk"])
    run = local_kernels if sizes == GRID else local
    return jax.shard_map(run, mesh=mesh, in_specs=in_specs, out_specs=out_specs, check_vma=False)
```

```python
import math

import jax
import jax.numpy as jnp
from jax import lax
from jax.experimental import pallas as pl
from jax.experimental.pallas import tpu as pltpu
from jax.sharding import PartitionSpec as P

HEADS = 12


EPSILON = 1e-06
SQRT_HALF = 0.7071067811865476
INV_ROOT_TAU = 0.3989422804014327
MESH = pl.DeviceIdType.MESH
GRID = (8, 4)


NT = (((1,), (1,)), ((), ()))
TN = (((0,), (0,)), ((), ()))
CHUNKS = 4


def dot(left, right, dims=(((1,), (0,)), ((), ()))):
    return lax.dot_general(left, right, dims, preferred_element_type=jnp.float32)


def remote_copy(src, dst, send, recv, device):
    return pltpu.make_async_remote_copy(
        src_ref=src, dst_ref=dst, send_sem=send, recv_sem=recv, device_id=device, device_id_type=MESH
    )


N1_GAIN, N1_BIAS, Q_BIAS, V_BIAS, OUT_BIAS, N2_GAIN, N2_BIAS, DOWN_BIAS, N3_GAIN, N3_BIAS, UP_BIAS, ALIGN_BIAS = (
    0, 1, 2, 3, 4, 5, 6, 7, 8, 9, 10, 14,
)
PACK_ROWS = 16
TILE = 512


def row_of(pack, row, start, size):
    width = pack.shape[1]
    parts = []
    while size > 0:
        line, column = row + start // width, start % width
        take = min(size, width - column)
        parts.append(pack[line : line + 1, column : column + take])
        start, size = start + take, size - take
    return parts[0] if len(parts) == 1 else jnp.concatenate(parts, axis=1)


def fill_pack(pack, rows, refs):
    width = pack.shape[1]
    for row, ref in zip(rows, refs):
        for start in range(0, ref.shape[0], width):
            size = min(width, ref.shape[0] - start)
            line = row + start // width
            pack[line : line + 1, 0:size] = ref[pl.ds(start, size)].reshape(1, size)


def norm_rows(values):
    center = values - jnp.mean(values, axis=-1, keepdims=True)
    inverse = lax.rsqrt(jnp.mean(center * center, axis=-1, keepdims=True) + EPSILON)
    return center * inverse, inverse


def put_visible(vis, visible_t, z):
    piece = vis.shape[0] // 2
    for c in range(2):
        where = pl.ds(pl.multiple_of(z * piece, piece), piece)
        vis[pl.ds(c * piece, piece), :] = visible_t[where, c : c + 1]


JOBS = (
    (4, 0, 96, 0, 1024, 2048),
    (3, 0, 96, 0, 768, 0),
    (3, 96, 96, 0, 768, 768),
    (3, 192, 96, 0, 768, 1536),
    (3, 288, 96, 0, 768, 2304),
    (2, 0, 96, 0, 768, 0),
    (2, 0, 96, 768, 768, 768),
    (2, 0, 96, 1536, 768, 1536),
    (2, 0, 96, 2304, 768, 2304),
    (1, 0, 96, 0, 768, 0),
    (0, 0, 96, 0, 384, 768),
    (0, 0, 96, 384, 384, 1152),
    (0, 0, 96, 768, 384, 1536),
)
COUNT = len(JOBS)
PLAIN = 10
KEY_BLOCK = 256
NORM_ROWS = 96
PLAN = (
    (0, "far"), (0, 0), "e3", "norm3", (2, "far"), (2, 0), (0, "own"), (0, 1), (2, "own"), (3, "far"), (3, 0),
    "feed", (2, 1), (3, "own"), (3, 1), "e2", "norm2", "back_att", (0, 2), (6, "far"), (6, 0), (1, "far"), (1, 0),
    (4, "own"), (2, 2), (6, "own"), (4, "far"), (4, 0), (3, 2), (1, "own"), (7, "far"), (7, 0), (7, "own"), (1, 1),
    (5, "own"), (0, 3), (6, 1), "settle0", (5, "far"), (5, 0), (3, 3), "pair", (4, 1), "pair", "pair", (6, 2),
    (1, 2), (0, 4), (2, 3), "settle1", (4, 2), (5, 1), "pair", (6, 3), (3, 4), "pair", (2, 4), (0, 5), "settle2",
    (4, 3), "pair", (3, 5), (1, 3), (5, 2), "pair", (6, 4), (2, 5), "pair", (5, 3), (7, 1), (4, 4), "pair", (6, 5),
    "dx0", (5, 4), (11, "far"), (11, 0), (8, "own"), (4, 5), (7, 2), (10, "own"), (11, "own"), (1, 4), (10, "far"),
    (10, 0), (11, 1), (9, "far"), (9, 0), (3, 6), (5, 5), "fwd0", (7, 3), (10, 1), (9, "own"), (2, 6), (8, "far"),
    (8, 0), (11, 2), "dx1", (1, 5), (10, 2), (11, 3), (7, 4), (9, 1), (12, "far"), (12, 0), "fwd1", "dx2", "dx3",
    (10, 3), (9, 2), (11, 4), (8, 1), (7, 5), (4, 6), (12, "own"), "sums", (12, 1), "vec0", (10, 4), "vec1", (9, 3),
    (8, 2), (11, 5), (9, 4), (6, 6), (8, 3), (10, 5), (12, 2), (5, 6), (8, 4), (9, 5), (12, 3), "vec2", (12, 4),
    "norm1", (8, 5), "vec3", (12, 5), (11, 6), "vec4", (7, 6), (9, 6), (0, 6), "vec5", (10, 6), (8, 6), (1, 6),
    (12, 6),
)


def add_into(target, first, second):
    lead = target.shape[:-2]

    def body(k, _):
        if len(lead) == 0:
            at = (pl.ds(pl.multiple_of(k * 16, 16), 16), slice(None))
        elif len(lead) == 1:
            at = (k,)
        else:
            at = (k // lead[1], lax.rem(k, lead[1]))
        target[at] = first[at] + second[at]
        return 0

    lax.fori_loop(0, math.prod(lead) if lead else target.shape[0] // 16, body, 0)


VIS, KEY, INV2, INV3, STATS = 0, 1, 2, 3, 8


def layer_kernel(*refs):
    slot_mask, counts, vectors_h, refs = refs[0], refs[1], refs[2:14], refs[14:]
    tok_h, cot_a_h, cot_b_h, w_align, w_down, w_up, w_out, w_qkv = refs[:8]
    block_out, align_out, grad_tokens, vec_out = refs[8:12]
    outs = refs[12:17]
    rest = refs[17:]
    own, got0, got1, got2 = (rest[i * COUNT : (i + 1) * COUNT] for i in range(4))
    rest = rest[4 * COUNT :]
    gotz, gotq = rest[:PLAIN], rest[PLAIN:COUNT]
    rest = rest[COUNT:]
    vec_got, vectors = rest[0], rest[1:13]
    (
        pack, side_v,
        align_v, down_v, up_v, out_v, low_v, tok, xall, n1, qkv, own_att, att, lse_rows, spread_rows,
        mid_v, e_v, normed, ring, slope, ld, l2, l3, la, unit2, unit3, cot_a, cot_b,
        grad_att, n1s,
        load_sem, send0, recv0, send1, recv1, send2, recv2, sendz, recvz, sendq, recvq, out_sem, outq_sem, vsend, vrecv,
        tok_send, tok_recv, att_send, att_recv, in_send, in_recv,
        pair_send, pair_recv, end_send, end_recv, out_send, out_recv, put_sem, vector_sem,
    ) = rest[13:]

    dp = lax.axis_index("dp")
    z = lax.axis_index("blk")
    core = lax.rem(dp, 2)
    x = lax.rem(dp // 2, 2)
    y = dp // 4
    clip, side = z // 2, lax.rem(z, 2)
    to_core = (dp + 1 - 2 * core, z)
    to_x = (dp + 2 - 4 * x, z)
    to_y = (dp + 4 - 8 * y, z)
    partner = z + 1 - 2 * side
    to_z1 = (dp, partner)
    to_z2 = (dp, lax.rem(z + 2, 4))
    to_z3 = (dp, 3 - z)
    is_mid = (z == 1) | (z == 2)
    is_end = (z == 0) | (z == 3)
    near, far = 3 - z, lax.rem(z + 2, 4)
    other_mid = 2 - clip
    piece, width = tok.shape
    rows, half, wide = 2 * piece, width // 2, up_v.shape[1]
    low = jnp.bfloat16
    low_d, low_o = n1.at[pl.ds(0, rows)], n1.at[pl.ds(rows, rows)]
    in_src = att
    from_end = [normed.at[pl.ds(k * piece, piece)] for k in range(2)]
    from_pair, total_in = (cot_b.at[pl.ds(k * piece, piece)] for k in range(2))

    def grad_at(m):
        return down_v.at[pl.ds((2 if m == 0 else 3) * width, width), pl.ds(half if m != 1 else 0, half)]

    def e_at(slot):
        return align_v.at[pl.ds(pl.multiple_of(slot * piece, piece), piece), pl.ds(0, width)]

    def slot_rows(slot):
        return pl.ds(pl.multiple_of(slot * piece, piece), piece)

    loads = {"mine": (tok_h.at[clip], xall.at[z]), "tok": (tok_h.at[1 - clip], tok)}
    for m in range(3):
        column = pl.multiple_of(m * width + side * half, 128)
        loads["low%d" % m] = (w_qkv.at[:, pl.ds(column, half)], low_v.at[m])
    loads["out"] = (w_out, out_v)
    loads["up"] = (w_up, up_v)
    loads["down"] = (w_down, down_v)
    loads["cot_a"] = (cot_a_h, cot_a)
    loads["align"] = (w_align, align_v)
    loads["cot_b"] = (cot_b_h, cot_b)
    loads = {
        name: pltpu.make_async_copy(src, dst, load_sem.at[k]) for k, (name, (src, dst)) in enumerate(loads.items())
    }
    early = ("mine", "tok", "low0", "low1", "low2")
    for name in early:
        loads[name].start()
    small = [pltpu.make_async_copy(src, dst, vector_sem.at[k]) for k, (src, dst) in enumerate(zip(vectors_h, vectors))]
    for copy in small:
        copy.start()

    def ready(*names):
        for name in names:
            loads[name].wait()

    barrier = pltpu.get_barrier_semaphore()
    for device in (to_core, to_x, to_y, to_z1, to_z2, to_z3):
        pl.semaphore_signal(barrier, inc=1, device_id=device, device_id_type=MESH)
    pl.semaphore_wait(barrier, 6)
    step = piece // CHUNKS

    def tok_copy(kind, slot, k):
        at = pl.ds(k * step, step)
        source = xall.at[slot, at] if kind >= 2 else tok_h.at[1 - clip if kind == 0 else clip, at]
        device = (dp, other_mid) if kind == 0 else to_z1
        return remote_copy(source, xall.at[slot, at], tok_send.at[kind, k], tok_recv.at[slot, k], device)

    for k in range(CHUNKS):
        tok_copy(0, z, k).start()
    for k in range(CHUNKS):
        tok_copy(1, z, k).start()
    for copy in small:
        copy.wait()
    fill_pack(pack, VECTORS, vectors)
    vec_out[...] = jnp.zeros_like(vec_out)
    ready("mine", "tok")
    e_v[0:128, :] = jnp.zeros((128, width), jnp.float32)
    for c in range(2):
        e_v[c : c + 1, :] = jnp.concatenate(
            [
                jnp.where((slot_mask[c, f : f + 1, :] > 0) & (f < counts[c]), 1.0, 0.0)
                for f in range(slot_mask.shape[1])
            ],
            axis=1,
        )
    side_v[...] = e_v[0:128, :].T
    seen = [side_v[slot_rows(z), c : c + 1] for c in range(2)]
    side_v[:, KEY : KEY + 1] = jnp.where(jnp.where(clip == 0, side_v[:, 0:1], side_v[:, 1:2]) > 0.0, 0.0, -1e30)
    for c in range(2):
        side_v[pl.ds(c * piece, piece), VIS : VIS + 1] = seen[c]
    row_bias = jnp.where(jnp.where(clip == 0, e_v[0:1, :], e_v[1:2, :]) > 0.0, 0.0, -1e30)
    columns = pl.ds(pl.multiple_of(side * half, 128), half)
    ready("low0", "low1", "low2")

    def project(slot):
        where = slot_rows(slot)

        def body(k, _):
            one, _ = norm_rows(xall[slot, pl.ds(pl.multiple_of(k * 96, 96), 96), :].astype(jnp.float32))
            at = pl.ds(pl.multiple_of(slot * piece + k * 96, 96), 96)
            n1[at, :] = (one * pack[N1_GAIN : N1_GAIN + 1, :] + pack[N1_BIAS : N1_BIAS + 1, :]).astype(low)
            return 0

        lax.fori_loop(0, piece // 96, body, 0)
        left = n1[where, :]
        qkv[0, where, :] = (dot(left, low_v[0]) + pack[Q_BIAS : Q_BIAS + 1, columns]).astype(low) * low(0.125)
        qkv[1, where, :] = dot(left, low_v[1]).astype(low)
        qkv[2, where, :] = (dot(left, low_v[2]) + pack[V_BIAS : V_BIAS + 1, columns]).astype(low)

    last = 3 * (1 - clip)
    third = 2 - clip
    early_keys = pl.ds(pl.multiple_of(clip * piece, piece), 3 * piece)
    late_keys = slot_rows(last)
    early_bias = jnp.where(clip == 0, row_bias[:, : 3 * piece], row_bias[:, piece:])
    late_bias = jnp.where(clip == 0, row_bias[:, 3 * piece :], row_bias[:, :piece])

    def slot_of(number):
        return jnp.where(number == 0, z, jnp.where(number == 1, partner, jnp.where(number == 2, third, last)))

    def tokens_of(number, _):
        slot = slot_of(number)

        @pl.when(number == 1)
        def _():
            for name in loads:
                if name not in early:
                    loads[name].start()

        @pl.when(is_mid & (number == 1))
        def _():
            for which, source in enumerate((near, far)):
                for k in range(CHUNKS):
                    tok_copy(1, source, k).wait_recv()
                    tok_copy(2 + which, source, k).start()
            for k in range(CHUNKS):
                tok_copy(1, partner, k).wait_recv()

        @pl.when(is_end & (number > 0))
        def _():
            for k in range(CHUNKS):
                tok_copy(1, slot, k).wait_recv()

        project(slot)
        return 0

    lane = lax.broadcasted_iota(jnp.int32, (1, 128), 1)
    low_lane = lane < 64

    def att_copy(slot, t):
        return remote_copy(
            own_att.at[t, slot_rows(slot)], att.at[clip, side, t], att_send.at[slot, t], att_recv.at[z, t], (dp, slot)
        )

    def held(number, t):
        rows_at = pl.ds(pl.multiple_of(lax.rem(number, 2) * piece, piece), piece)
        return rows_at, pl.ds(pl.multiple_of(number // 2 * half + t * 128, 128), 128)

    def head(queries, a, keys, bias):
        mine = low_lane if a == 0 else jnp.logical_not(low_lane)
        return dot(jnp.where(mine, queries, jnp.zeros_like(queries)), keys, NT) + bias

    def attend_early(number, _):
        where = slot_rows(slot_of(number))
        stats = jnp.zeros((piece, 128), jnp.float32)
        for t in range(half // 128):
            at = pl.ds(t * 128, 128)
            parts = []
            for a in range(2):
                scores = head(qkv[0, where, at], a, qkv[1, early_keys, at], early_bias)
                top = jnp.max(scores, axis=-1, keepdims=True)
                expo = jnp.exp(scores - top)
                parts.append(dot(expo.astype(low), qkv[2, early_keys, at]))
                stats = jnp.where(lane == STATS + 2 * t + a, top, stats)
                stats = jnp.where(lane == STATS + 8 + 2 * t + a, jnp.sum(expo, axis=-1, keepdims=True), stats)
            e_v[held(number, t)] = jnp.where(low_lane, parts[0], parts[1])
        side_v[where, STATS : STATS + 16] = stats[:, STATS : STATS + 16]
        return 0

    def attend_whole(slot):
        where = slot_rows(slot)
        stats = jnp.zeros((piece, 128), jnp.float32)
        for t in range(half // 128):
            at = pl.ds(t * 128, 128)
            parts = []
            for a in range(2):
                scores = head(qkv[0, where, at], a, qkv[1, :, at], row_bias)
                top = jnp.max(scores, axis=-1, keepdims=True)
                expo = jnp.exp(scores - top)
                denominator = jnp.sum(expo, axis=-1, keepdims=True)
                parts.append(dot(expo.astype(low), qkv[2, :, at]) * (1.0 / denominator))
                stats = jnp.where(lane == STATS + 2 * t + a, top + jnp.log(denominator), stats)
            own_att[t, where, :] = jnp.where(low_lane, parts[0], parts[1]).astype(low)

            @pl.when(slot != z)
            def _():
                att_copy(slot, t).start()

        side_v[where, STATS : STATS + 8] = stats[:, STATS : STATS + 8]

    def attend_late(step_number, _):
        number = 2 - step_number
        slot = slot_of(number)
        where = slot_rows(slot)
        before = side_v[where, :]
        stats = jnp.zeros((piece, 128), jnp.float32)
        for t in range(half // 128):
            at = pl.ds(t * 128, 128)
            sums = e_v[held(number, t)]
            parts = []
            for a in range(2):
                k = STATS + 2 * t + a
                scores = head(qkv[0, where, at], a, qkv[1, late_keys, at], late_bias)
                old = before[:, k : k + 1]
                top = jnp.maximum(old, jnp.max(scores, axis=-1, keepdims=True))
                expo = jnp.exp(scores - top)
                kept = jnp.exp(old - top)
                denominator = before[:, k + 8 : k + 9] * kept + jnp.sum(expo, axis=-1, keepdims=True)
                value = sums * kept + dot(expo.astype(low), qkv[2, late_keys, at])
                parts.append(value * (1.0 / denominator))
                stats = jnp.where(lane == k, top + jnp.log(denominator), stats)
            own_att[t, where, :] = jnp.where(low_lane, parts[0], parts[1]).astype(low)

            @pl.when(number > 0)
            def _():
                att_copy(slot, t).start()

        side_v[where, STATS : STATS + 8] = stats[:, STATS : STATS + 8]
        return 0

    lax.fori_loop(0, 3, tokens_of, 0)

    tokens_of(3, 0)

    def attend(number, _):
        attend_whole(slot_of(3 - number))

        return 0

    lax.fori_loop(0, 4, attend, 0)

    att[clip, side] = own_att[:, slot_rows(z), :]

    def tiles(count, size, body):
        def one_tile(t, _):
            body(t, pl.ds(pl.multiple_of(t * size, size), size))
            return 0

        lax.fori_loop(0, count, one_tile, 0)

    def chunks(body, carry, size=48):
        def one_chunk(k, carry):
            return body(pl.ds(pl.multiple_of(k * size, size), size), k, carry)

        return lax.fori_loop(0, rows // size, one_chunk, carry)

    def put_vector(row, start, value):
        at = 0
        while at < value.shape[1]:
            line, column = row + (start + at) // width, (start + at) % width
            take = min(value.shape[1] - at, width - column)
            vec_out[line : line + 1, column : column + take] = value[:, at : at + take]
            at += take

    def total(value):
        return jnp.sum(value.astype(jnp.float32), axis=0, keepdims=True)

    zero_row = jnp.zeros((1, width), jnp.float32)
    ready("cot_a")

    def mask(at, k, carry):
        value = (side_v[at, VIS : VIS + 1] * cot_a[at, :].astype(jnp.float32)).astype(low)
        cot_a[at, :] = value
        return carry + total(value)

    put_vector(ALIGN_BIAS, 0, chunks(mask, jnp.zeros((1, cot_a.shape[1]), jnp.float32)))
    lse_rows[...] = side_v[...].T[STATS : STATS + 8]

    def shares_of(source, target, count):
        for c in range(0, source.shape[1], 128):
            flipped = source[:, pl.ds(c, 128)].T
            at = 0
            while at < 128:
                share, inside = (c + at) // count, (c + at) % count
                take = min(128 - at, count - inside)
                rel = jnp.where(core == share % 2, 1, 0)
                target[rel, share // 2, pl.ds(inside, take), :] = flipped[at : at + take]
                at += take

    shares_of(n1, n1s, width // 8)

    def settle_att(number, _):
        slot = lax.rem(z + number, 4)
        for t in range(half // 128):
            att_copy(slot, t).wait_send()
            remote_copy(
                own_att.at[t, slot_rows(slot)], att.at[slot // 2, lax.rem(slot, 2), t],
                att_send.at[slot, t], att_recv.at[slot, t], (dp, slot),
            ).wait_recv()
        return 0

    lax.fori_loop(1, 4, settle_att, 0)
    for k in range(CHUNKS):
        tok_copy(0, z, k).wait_send()
        tok_copy(1, z, k).wait_send()

    @pl.when(is_mid)
    def _():
        for k in range(CHUNKS):
            for which, slot in enumerate((near, far)):
                tok_copy(2 + which, slot, k).wait_send()

    for c in range(2):
        for h in range(2):
            for t in range(half // 128):
                normed[pl.ds(c * piece, piece), pl.ds(h * half + t * 128, 128)] = att[c, h, t]
    shares_of(normed, la, width // 8)
    ready("out")

    def mix(t, at):
        mixed = dot(normed[...], out_v[:, at]) + pack[OUT_BIAS : OUT_BIAS + 1, at]
        for c in range(2):
            mixed_c = mixed[c * piece : (c + 1) * piece]
            source = jnp.where(clip == c, xall[z, :, at], tok[:, at])
            mid_v[pl.ds(c * piece, piece), at] = source.astype(jnp.float32) + mixed_c

    tiles(3, 256, mix)

    def norm(gain, bias, unit, inv):
        def body(at, k, _):
            one, inverse = norm_rows(mid_v[at, :])
            unit[at, :] = one.astype(low)
            side_v[at, inv : inv + 1] = inverse
            normed[at, :] = (one * pack[gain : gain + 1, :] + pack[bias : bias + 1, :]).astype(low)
            return 0

        chunks(body, 0, NORM_ROWS)

    norm(N2_GAIN, N2_BIAS, unit2, INV2)
    shares_of(normed, l2, width // 8)
    ready("up")

    def up(t, at):
        e_v[...] = dot(normed[...], up_v[:, at]) + pack[pl.ds(UP_BIAS + t, 1), :]

        def gelu(here, k, _):
            values = e_v[here, :]
            cdf = 0.5 * (1.0 + lax.erf(values * SQRT_HALF))
            ring[k, :, at] = (values * cdf).astype(low)
            slope[here, at] = (cdf + values * jnp.exp(-0.5 * values * values) * INV_ROOT_TAU).astype(low)
            return 0

        chunks(gelu, 0)
        for c in range(0, width, 128):
            rel = core if c < half else 1 - core
            columns_at = pl.ds(pl.multiple_of(t * width + c, 128), 128)
            ld[1 - rel, t, pl.ds(c % half, 128), :] = ring[:, :, columns_at].reshape(rows, 128).T

    tiles(4, width, up)
    ready("down")

    def down(t, at):
        mid_v[:, at] = (
            mid_v[:, at] + dot(ring[...].reshape(rows, wide), down_v[:, at]) + pack[DOWN_BIAS : DOWN_BIAS + 1, at]
        )

    tiles(3, 256, down)

    def staged(j, target):
        return pltpu.make_async_copy(own[j], target, put_sem.at[j])

    def put_block(at, k, _):
        own[1][k // 4, lax.rem(k, 4)] = (side_v[at, VIS : VIS + 1] * mid_v[at, :]).astype(low)
        return 0

    chunks(put_block, 0)
    staged(1, block_out).start()
    norm(N3_GAIN, N3_BIAS, unit3, INV3)
    shares_of(normed, l3, width // 8)
    ready("align", "cot_b")

    def align_tile(t, at):
        bias = pack[pl.ds(ALIGN_BIAS + t // 3, 1), pl.ds(pl.multiple_of(lax.rem(t, 3) * 256, 256), 256)]
        value = dot(normed[...], align_v[:, at]) + bias
        value = (side_v[pl.ds(0, rows), VIS : VIS + 1] * value).astype(low)
        for k in range(8):
            own[0][k // 4, k % 4, :, at] = value[k * 48 : (k + 1) * 48]

    tiles(4, 256, align_tile)
    staged(0, align_out).start()

    def buffer_of(j):
        return ring.at[:, :, pl.ds(JOBS[j][5], JOBS[j][4])]

    def copies0(j):
        for h in range(2):
            yield remote_copy(
                buffer_of(j).at[pl.ds(4 * h, 4)], got0[j].at[h], send0.at[j, h], recv0.at[j, h], to_core
            )

    def copies1(j):
        yield remote_copy(
            own[j].at[0, pl.ds(2 * (1 - x), 2)], got1[j].at[0], send1.at[j, 0], recv1.at[j, 0], to_x
        )
        yield remote_copy(
            own[j].at[1, pl.ds(2 * (1 - y), 2)], got1[j].at[1], send1.at[j, 1], recv1.at[j, 1], to_y
        )

    def copies2(j):
        yield remote_copy(own[j].at[0, 2 * x + 1 - y], got2[j].at[0], send2.at[j, 0], recv2.at[j, 0], to_y)
        yield remote_copy(own[j].at[1, 2 * y + 1 - x], got2[j].at[1], send2.at[j, 1], recv2.at[j, 1], to_x)

    def shares(j):
        return (own[j].at[0, 2 * x + y], own[j].at[1, 2 * y + x])

    def copiesz(j, slot, device):
        for h, share in enumerate(shares(j)):
            yield remote_copy(share, gotz[j].at[slot, h], sendz.at[j, slot, h], recvz.at[j, slot, h], device)

    def copiesq(j, source, slot, device):
        got, m = gotq[j - PLAIN], j - PLAIN
        for h, share in enumerate(shares(j)):
            yield remote_copy(
                share if source is None else got.at[source, h],
                got.at[slot, h], sendq.at[m, slot, h], recvq.at[m, slot, h], device,
            )

    def result(j, h, source):
        matrix, row, count, column, size, _ = JOBS[j]
        return pltpu.make_async_copy(
            source, outs[matrix].at[pl.ds(row + h * count // 2, count // 2), pl.ds(column, size)], out_sem.at[j, h]
        )

    def result_q(j, h, which, source):
        count, m = JOBS[j][2] // 2, j - PLAIN
        at = side if which == 0 else 1 - side
        column = pl.multiple_of(m * width + at * half, 128)
        return pltpu.make_async_copy(
            source, outs[0].at[pl.ds(h * count, count), pl.ds(column, half)], outq_sem.at[m, which, h]
        )

    def stage(j, number):
        if number == 0:
            for copy in copies0(j):
                copy.start()
        if number == 1:
            for copy in copies0(j):
                copy.wait()
            add_into(own[j], own[j], got0[j])
            for copy in copies1(j):
                copy.start()
        if number == 2:
            for copy in copies1(j):
                copy.wait()
            first, second = (own[j].at[0, pl.ds(2 * x, 2)], own[j].at[1, pl.ds(2 * y, 2)])
            add_into(first, first, got1[j].at[0])
            add_into(second, second, got1[j].at[1])
            for copy in copies2(j):
                copy.start()
        if number == 3:
            for copy in copies2(j):
                copy.wait()
            for h, share in enumerate(shares(j)):
                add_into(share, share, got2[j].at[h])

            @pl.when(is_end)
            def _():
                for copy in copiesq(j, None, 0, to_z1) if j >= PLAIN else copiesz(j, 0, to_z1):
                    copy.start()

        if number >= 4 and j >= PLAIN:
            stage_q(j, number)
            return
        if number == 4:

            @pl.when(is_mid)
            def _():
                for copy in copiesz(j, 0, to_z1):
                    copy.wait_recv()
                for h, share in enumerate(shares(j)):
                    add_into(share, share, gotz[j].at[0, h])
                for copy in copiesz(j, 1, to_z3):
                    copy.start()

            @pl.when(is_end)
            def _():
                for copy in copiesz(j, 0, to_z1):
                    copy.wait_send()

        if number == 5:

            @pl.when(is_mid)
            def _():
                for copy in copiesz(j, 1, to_z3):
                    copy.wait()
                for h, share in enumerate(shares(j)):
                    add_into(share, share, gotz[j].at[1, h])
                for copy in copiesz(j, 0, to_z1):
                    copy.start()
                for h, share in enumerate(shares(j)):
                    result(j, h, share).start()

        if number == 6:

            @pl.when(is_mid)
            def _():
                for copy in copiesz(j, 0, to_z1):
                    copy.wait_send()

            @pl.when(is_end)
            def _():
                for copy in copiesz(j, 0, to_z1):
                    copy.wait_recv()
                for h in range(2):
                    result(j, h, gotz[j].at[0, h]).start()

    def stage_q(j, number):
        got = gotq[j - PLAIN]
        if number == 4:

            @pl.when(is_mid)
            def _():
                for copy in copiesq(j, None, 1, to_z3):
                    copy.start()
                for copy in copiesq(j, None, 0, to_z1):
                    copy.wait_recv()
                for copy in copiesq(j, 0, 2, to_z3):
                    copy.start()

            @pl.when(is_end)
            def _():
                for copy in copiesq(j, None, 0, to_z1):
                    copy.wait_send()

        if number == 5:

            @pl.when(is_mid)
            def _():
                for copy in copiesq(j, None, 1, to_z3):
                    copy.wait()
                for copy in copiesq(j, 0, 2, to_z3):
                    copy.wait()
                for h, share in enumerate(shares(j)):
                    add_into(share, share, got.at[2, h])
                    add_into(got.at[0, h], got.at[0, h], got.at[1, h])
                for copy in copiesq(j, None, 1, to_z1):
                    copy.start()
                for copy in copiesq(j, 0, 0, to_z1):
                    copy.start()
                for h, share in enumerate(shares(j)):
                    result_q(j, h, 0, share).start()
                    result_q(j, h, 1, got.at[0, h]).start()

        if number == 6:

            @pl.when(is_mid)
            def _():
                for copy in copiesq(j, None, 1, to_z1):
                    copy.wait_send()
                for copy in copiesq(j, 0, 0, to_z1):
                    copy.wait_send()

            @pl.when(is_end)
            def _():
                for copy in copiesq(j, None, 1, to_z1):
                    copy.wait_recv()
                for copy in copiesq(j, 0, 0, to_z1):
                    copy.wait_recv()
                for h in range(2):
                    result_q(j, h, 0, got.at[0, h]).start()
                    result_q(j, h, 1, got.at[1, h]).start()

    def results_done():
        for j in range(COUNT):
            for h in range(2):
                if j < PLAIN:
                    result(j, h, gotz[j].at[0, h]).wait()
                else:
                    for which in range(2):
                        result_q(j, h, which, gotq[j - PLAIN].at[0, h]).wait()

    def gradient(j, mine, left, right):
        count, size = JOBS[j][2], JOBS[j][4]
        target = own[j] if mine else buffer_of(j)
        for c in range(0, size, min(size, 384 if size % 384 == 0 else 512)):
            at = pl.ds(c, min(size, 384 if size % 384 == 0 else 512))
            value = dot(left, right(at)).astype(low)
            for chip in range(4):
                cy, cx = chip // 2, chip % 2
                for h in range(2):
                    k = 2 * cx + cy if h == 0 else 2 * cy + cx
                    start = chip * count + h * count // 2
                    part = value[start : start + count // 2]
                    if mine:
                        target[h, k, :, at] = part
                    else:
                        target[4 * h + k, :, at] = part

    def job(j, mine):
        matrix, row, count, column, size, _ = JOBS[j]
        lhs, rhs = ((n1s, None), (la, low_o), (l2, slope), (ld, low_d), (l3, cot_a))[matrix]
        left = lhs[1 if mine else 0, :, pl.ds(row, count), :].reshape(4 * count, lhs.shape[3])
        if matrix == 0:
            gradient(j, mine, left, lambda at: grad_at(j - PLAIN)[...])
        else:
            gradient(j, mine, left, lambda at: rhs[:, pl.ds(column + at.start, at.size)])

    def norm_back(e, one, inverse, gain):
        scaled = e * gain
        return inverse * (
            scaled
            - jnp.mean(scaled, axis=-1, keepdims=True)
            - one * jnp.mean(scaled * one, axis=-1, keepdims=True)
        )

    def norm_pass(unit, inv, gain_row, base, low_target, sums):
        def body(at, k, carry):
            e = e_v[at, :]
            one = unit[at, :].astype(jnp.float32)
            value = base(at) + norm_back(e, one, side_v[at, inv : inv + 1], pack[gain_row : gain_row + 1, :])
            mid_v[at, :] = value
            rounded = value.astype(low)
            low_target[at, :] = rounded
            return (carry[0] + total(e * one), carry[1] + total(e), carry[2] + total(rounded))

        for row, value in zip(sums, chunks(body, (zero_row,) * 3, NORM_ROWS)):
            put_vector(row, 0, value)

    def e3():
        def body(t, at):
            e_v[:, at] = dot(cot_a[...], align_v[at, :], NT)

        tiles(3, 256, body)

    def norm3():
        norm_pass(
            unit3, INV3, N3_GAIN, lambda at: side_v[at, VIS : VIS + 1] * cot_b[at, :].astype(jnp.float32), low_d,
            (N3_GAIN, N3_BIAS, DOWN_BIAS),
        )

    def feed():
        def body(t, at):
            value = (dot(low_d[...], down_v[at, :], NT) * slope[:, at].astype(jnp.float32)).astype(low)
            slope[:, at] = value
            vec_out[pl.ds(UP_BIAS + t, 1), :] = total(value)

        tiles(4, width, body)

    def e2():
        def body(t, at):
            e_v[:, at] = dot(slope[...], up_v[at, :], NT)

        tiles(3, 256, body)

    def norm2():
        norm_pass(unit2, INV2, N2_GAIN, lambda at: mid_v[at, :], low_o, (N2_GAIN, N2_BIAS, OUT_BIAS))

    def in_copy(slot, t):
        return remote_copy(
            in_src.at[slot // 2, lax.rem(slot, 2), t], grad_att.at[t, z],
            in_send.at[slot, t], in_recv.at[z, t], (dp, slot),
        )

    def back_att():
        for h in range(2):
            value = dot(low_o[...], out_v[pl.ds(h * half, half), :], NT).astype(low)
            for c in range(2):
                for t in range(half // 128):
                    in_src[c, h, t] = value[c * piece : (c + 1) * piece, t * 128 : (t + 1) * 128]
        for t in range(half // 128):

            def start(number, _):
                in_copy(lax.rem(z + number, 4), t).start()
                return 0

            lax.fori_loop(1, 4, start, 0)
        for t in range(half // 128):
            grad_att[t, z] = in_src[clip, side, t]

    def settle(t):
        def body(number, _):
            slot = lax.rem(z + number, 4)
            in_copy(slot, t).wait_send()
            remote_copy(
                in_src.at[0, 0, t], grad_att.at[t, slot], in_send.at[slot, t], in_recv.at[slot, t], (dp, slot)
            ).wait_recv()
            return 0

        lax.fori_loop(1, 4, body, 0)

        def spread(slot, _):
            where = slot_rows(slot)
            stats = jnp.zeros((piece, 128), jnp.float32)
            product = grad_att[t, slot].astype(jnp.float32) * own_att[t, where, :].astype(jnp.float32)
            for a in range(2):
                mine = low_lane if a == 0 else jnp.logical_not(low_lane)
                value = jnp.sum(jnp.where(mine, product, 0.0), axis=-1, keepdims=True)
                stats = jnp.where(lane == STATS + a, value, stats)
            side_v[where, STATS : STATS + 2] = stats[:, STATS : STATS + 2]
            return 0

        lax.fori_loop(0, 4, spread, 0)
        spread_rows[2 * t : 2 * t + 2, :] = side_v[...].T[STATS : STATS + 2]

    def pair(number):
        t, b = number // 3, lax.rem(number, 3)
        at = pl.ds(pl.multiple_of(t * 128, 128), 128)
        queries = qkv[0, :, at]
        grads = grad_att[t].reshape(4 * piece, 128)
        keys_at = pl.ds(pl.multiple_of(b * KEY_BLOCK, KEY_BLOCK), KEY_BLOCK)
        keys = qkv[1, keys_at, at]
        values = qkv[2, keys_at, at]
        grad_k = jnp.zeros((KEY_BLOCK, 128), jnp.float32)
        grad_v = jnp.zeros((KEY_BLOCK, 128), jnp.float32)
        held_q = (e_v.at[:, pl.ds(0, 128)], e_v.at[:, pl.ds(128, 128)])
        grad_queries = jnp.where(b == 0, 0.0, jnp.concatenate([ref[...] for ref in held_q], axis=0))
        for a in range(2):
            mine = low_lane if a == 0 else jnp.logical_not(low_lane)
            zero = jnp.zeros((), low)
            q_mine = jnp.where(mine, queries, zero)
            g_mine = jnp.where(mine, grads, zero)
            k_mine = jnp.where(mine, keys, zero)
            row = pl.ds(2 * t + a, 1)
            scores = dot(keys, q_mine, NT) + side_v[keys_at, KEY : KEY + 1]
            probs = jnp.exp(scores - lse_rows[row, :])
            back = (probs * (dot(values, g_mine, NT) - spread_rows[row, :])).astype(low)
            grad_v = grad_v + dot(probs.astype(low), g_mine)
            grad_k = grad_k + dot(back, q_mine)
            grad_queries = grad_queries + dot(back, k_mine, TN)
        grad_at(1)[keys_at, at] = grad_k.astype(low)
        grad_at(2)[keys_at, at] = grad_v.astype(low)
        for k, ref in enumerate(held_q):
            ref[...] = grad_queries[k * rows : (k + 1) * rows]

        @pl.when(b == 2)
        def _():
            for k, ref in enumerate(held_q):
                grad_at(0)[pl.ds(k * rows, rows), at] = (ref[...] * 0.125).astype(low)

    def pair_copy():
        return remote_copy(e_at(partner), from_pair, pair_send, pair_recv, to_z1)

    def end_copy(which, slot):
        return remote_copy(e_at(slot), from_end[which], end_send.at[which], end_recv.at[which], to_z1)

    def out_copy(which, slot):
        return remote_copy(e_at(slot), total_in, out_send.at[which], out_recv, (dp, slot))

    targets = (3 - 3 * clip, 2 - clip)
    mine_rows = slot_rows(clip)

    def dx(number):
        slot = (targets + (partner, z))[number]
        where = slot_rows(slot)
        value = sum(dot(grad_at(m)[where, :], low_v[m], NT) for m in range(3))
        e_at(slot)[...] = value.astype(low)
        if number == 3:
            e_v[mine_rows, :] = value
        if number < 2:

            @pl.when(is_end)
            def _():
                end_copy(number, slot).start()

        if number == 2:
            pair_copy().start()
        one, _ = norm_rows(xall[slot].astype(jnp.float32))
        for row, term in ((N1_GAIN, total(value * one)), (N1_BIAS, total(value))):
            vec_out[row : row + 1, :] = vec_out[row : row + 1, :] + term

    def sums():
        spot = lax.broadcasted_iota(jnp.int32, (1, width), 1)
        for row, m in ((Q_BIAS, 0), (V_BIAS, 2)):
            value = total(grad_at(m)[...])
            value = jnp.concatenate([value, value], axis=1)
            put_vector(row, 0, jnp.where((spot < half) == (side == 0), value, 0.0))

    def forward(which):
        @pl.when(is_mid)
        def _():
            slot = targets[which]
            end_copy(which, slot).wait_recv()
            add_into(e_at(slot), e_at(slot), from_end[which])
            out_copy(which, slot).start()

    vec_devices = (to_core, to_x, to_y, to_z1, to_z2)

    def vec_copy(k):
        return remote_copy(vec_out, vec_got.at[k], vsend.at[k], vrecv.at[k], vec_devices[k])

    def vec(k):
        if k > 0:
            vec_copy(k - 1).wait()
            vec_out[...] = vec_out[...] + vec_got[k - 1]
        if k < 5:
            vec_copy(k).start()

    def norm1():
        pair_copy().wait()
        e_v[mine_rows, :] = e_v[mine_rows, :] + from_pair[...].astype(jnp.float32)
        out_copy(0, partner).wait_recv()
        e_v[slot_rows(1 - clip), :] = total_in[...].astype(jnp.float32)

        def body(at, k, _):
            half_clip = pl.ds(pl.multiple_of(lax.rem(k, 2) * NORM_ROWS, NORM_ROWS), NORM_ROWS)
            source = jnp.where(clip == k // 2, xall[z, half_clip, :], tok[half_clip, :])
            one, inverse = norm_rows(source.astype(jnp.float32))
            value = mid_v[at, :] + norm_back(e_v[at, :], one, inverse, pack[N1_GAIN : N1_GAIN + 1, :])
            low_d[at, :] = value.astype(low)
            return 0

        chunks(body, 0, NORM_ROWS)
        pltpu.make_async_copy(low_d, grad_tokens, put_sem.at[2]).start()

    singles = dict(
        e3=e3, norm3=norm3, feed=feed, e2=e2, norm2=norm2, back_att=back_att, sums=sums, norm1=norm1
    )
    several = dict(settle=settle, dx=dx, fwd=forward, vec=vec)
    staged(0, align_out).wait()
    staged(1, block_out).wait()

    def run(entries):
        for entry in entries:
            if isinstance(entry, tuple):
                if entry[1] in ("far", "own"):
                    job(entry[0], entry[1] == "own")
                else:
                    stage(*entry)
            elif entry in singles:
                singles[entry]()
            else:
                several[entry[:-1]](int(entry[-1]))

    spots = [k for k, entry in enumerate(PLAN) if entry == "pair"]
    run(PLAN[: spots[0]])

    def pair_and_more(number, _):
        pair(number)
        for k in range(len(spots) - 1):
            if spots[k] + 1 < spots[k + 1]:

                @pl.when(number == k)
                def _():
                    run(PLAN[spots[k] + 1 : spots[k + 1]])

        return 0

    lax.fori_loop(0, len(spots), pair_and_more, 0)
    run(PLAN[spots[-1] + 1 :])
    results_done()
    pltpu.make_async_copy(low_d, grad_tokens, put_sem.at[2]).wait()

    @pl.when(is_mid)
    def _():
        for which in range(2):
            out_copy(which, targets[which]).wait_send()

    @pl.when(is_end)
    def _():
        for which in range(2):
            end_copy(which, targets[which]).wait_send()


def layer(slot_mask, counts, vectors, tok, cot_a, cot_b, w_align, w_down, w_up, w_out, w_qkv):
    _, piece, width = tok.shape
    rows, half, wide, align = 2 * piece, width // 2, w_up.shape[1], w_align.shape[1]
    low, full = jnp.bfloat16, jnp.float32
    vmem = pl.BlockSpec(memory_space=pltpu.VMEM)
    hbm = pl.BlockSpec(memory_space=pl.ANY)
    dma = pltpu.SemaphoreType.DMA
    v = pltpu.VMEM
    shapes = [(2, 4, job[2] // 2, job[4]) for job in JOBS]
    scratch = (
        [v(shape, low) for shape in shapes]
        + [v(shape, low) for shape in shapes]
        + [v((2, 2) + shape[2:], low) for shape in shapes]
        + [v((2,) + shape[2:], low) for shape in shapes]
        + [v((2, 2) + shape[2:], low) for shape in shapes[:PLAIN]]
        + [v((3, 2) + shape[2:], low) for shape in shapes[PLAIN:]]
        + [v((5, PACK_ROWS, width), full)]
        + [v(vector.shape, full) for vector in vectors]
        + [v((PACK_ROWS, width), full), v((4 * piece, 128), full)]
        + [v(w_align.shape, low), v(w_down.shape, low), v(w_up.shape, low), v(w_out.shape, low)]
        + [v((3, width, half), low), v((piece, width), low), v((4, piece, width), low), v((4 * piece, width), low)]
        + [v((3, 4 * piece, half), low), v((3, 4 * piece, 128), low), v((2, 2, 3, piece, 128), low)]
        + [v((8, 4 * piece), full)] * 2
        + [v((rows, width), full), v((rows, width), full), v((rows, width), low), v((8, 48, wide), low)]
        + [v((rows, wide), low), v((2, 4, wide // 8, rows), low)]
        + [v((2, 4, width // 8, rows), low)] * 3
        + [v((rows, width), low)] * 2
        + [v((rows, align), low), v((rows, width), low)]
        + [v((3, 4, piece, 128), low), v((2, 4, width // 8, 4 * piece), low)]
        + [dma((11,))]
        + [dma((COUNT, 2))] * 6
        + [dma((PLAIN, 2, 2))] * 2
        + [dma((3, 3, 2))] * 2
        + [dma((PLAIN, 2)), dma((3, 2, 2))]
        + [dma((5,))] * 2
        + [dma((4, CHUNKS))] * 2
        + [dma((4, 3))] * 4
        + [dma(())] * 2
        + [dma((2,))] * 2
        + [dma((2,)), dma(())]
        + [dma((3,)), dma((12,))]
    )
    struct = jax.ShapeDtypeStruct
    return pl.pallas_call(
        layer_kernel,
        name="layer",
        out_shape=[
            struct((2, 4, 48, width), low),
            struct((2, 4, 48, align), low),
            struct((rows, width), low),
            struct((PACK_ROWS, width), full),
        ]
        + [struct((w.shape[0] // 8, w.shape[1]), low) for w in (w_qkv, w_out, w_up, w_down, w_align)],
        in_specs=[vmem, pl.BlockSpec(memory_space=pltpu.SMEM)] + [hbm] * 20,
        out_specs=[hbm, hbm, hbm, vmem] + [hbm] * 5,
        scratch_shapes=scratch,
        compiler_params=pltpu.CompilerParams(
            collective_id=0, has_side_effects=True, vmem_limit_bytes=63 * 2**20
        ),
    )(slot_mask, counts, *vectors, tok, cot_a, cot_b, w_align, w_down, w_up, w_out, w_qkv)


VECTORS = (
    N1_GAIN, N1_BIAS, Q_BIAS, V_BIAS, OUT_BIAS, N2_GAIN, N2_BIAS, DOWN_BIAS, N3_GAIN, N3_BIAS, UP_BIAS, ALIGN_BIAS,
)


def finish_kernel(*refs):
    shares, pack, through_in = refs[:5], refs[5], refs[6:9]
    wide, vectors, through_out = refs[9:14], refs[14:26], refs[26:29]
    low_v, wide_v, held, pack_v, vectors_v = refs[29:34], refs[34:39], refs[39:42], refs[42], refs[43:55]
    in_sem, out_sem, vector_sem = refs[55:]
    ins = [pltpu.make_async_copy(shares[k], low_v[k], in_sem.at[k]) for k in range(5)]
    outs = [pltpu.make_async_copy(wide_v[k], wide[k], out_sem.at[k]) for k in range(5)]
    through = [
        (
            pltpu.make_async_copy(through_in[k], held[k], in_sem.at[5 + k]),
            pltpu.make_async_copy(held[k], through_out[k], out_sem.at[5 + k]),
        )
        for k in range(3)
    ]
    pack_in = pltpu.make_async_copy(pack, pack_v, in_sem.at[8])
    for copy in [pack_in] + ins:
        copy.start()
    for copy, _ in through:
        copy.start()
    width = pack.shape[1]
    vectors_out = [
        pltpu.make_async_copy(vectors_v[k], vectors[k], vector_sem.at[k]) for k in range(len(vectors))
    ]
    pack_in.wait()
    for row, ref in zip(VECTORS, vectors_v):
        for start in range(0, ref.shape[0], width):
            size = min(width, ref.shape[0] - start)
            line = row + start // width
            ref[pl.ds(start, size)] = pack_v[line : line + 1, 0:size].reshape(size)
    for copy in vectors_out:
        copy.start()
    for k in range(5):
        ins[k].wait()
        wide_v[k][...] = low_v[k][...].astype(jnp.float32)
        outs[k].start()
    for first, second in through:
        first.wait()
        second.start()
    for copy in outs + vectors_out:
        copy.wait()
    for _, copy in through:
        copy.wait()


def finish(shares, pack, through, sizes):
    hbm = pl.BlockSpec(memory_space=pl.ANY)
    struct = jax.ShapeDtypeStruct
    results = pl.pallas_call(
        finish_kernel,
        name="finish",
        out_shape=[struct(share.shape, jnp.float32) for share in shares]
        + [struct((size,), jnp.float32) for size in sizes]
        + [struct(array.shape, array.dtype) for array in through],
        in_specs=[hbm] * 9,
        out_specs=[hbm] * 20,
        scratch_shapes=[pltpu.VMEM(share.shape, share.dtype) for share in shares]
        + [pltpu.VMEM(share.shape, jnp.float32) for share in shares]
        + [pltpu.VMEM(array.shape, array.dtype) for array in through]
        + [pltpu.VMEM(pack.shape, pack.dtype)]
        + [pltpu.VMEM((size,), jnp.float32) for size in sizes]
        + [pltpu.SemaphoreType.DMA((9,)), pltpu.SemaphoreType.DMA((8,)), pltpu.SemaphoreType.DMA((12,))],
        compiler_params=pltpu.CompilerParams(vmem_limit_bytes=62 * 2**20),
    )(*shares, pack, *through)
    return results[:5], results[5:17], results[17:]


def norm_forward(values, gain, shift):
    center = values - jnp.mean(values, axis=-1, keepdims=True)
    inverse = lax.rsqrt(jnp.mean(center * center, axis=-1, keepdims=True) + EPSILON)
    normed = center * inverse
    return (normed * gain + shift, normed, inverse)


def norm_backward(upstream, normed, inverse, gain):
    scaled = upstream * gain
    inner = (
        scaled
        - jnp.mean(scaled, axis=-1, keepdims=True)
        - normed * jnp.mean(scaled * normed, axis=-1, keepdims=True)
    )
    return (inverse * inner, jnp.sum(upstream * normed, axis=0), jnp.sum(upstream, axis=0))


def gelu_slope(values):
    return (
        0.5 * (1.0 + lax.erf(values * SQRT_HALF))
        + values * jnp.exp(-0.5 * values * values) * INV_ROOT_TAU
    )


def weight_grad(left, right):
    return lax.dot_general(
        left, right, (((0,), (0,)), ((), ())), preferred_element_type=jnp.float32
    )


def input_grad(upstream, weight):
    return lax.dot_general(
        upstream, weight, (((1,), (1,)), ((), ())), preferred_element_type=jnp.float32
    )


def masked_scores(query_heads, key_heads, key_valid, scale):
    scores = (
        jnp.einsum("cqhd,ckhd->chqk", query_heads, key_heads, preferred_element_type=jnp.float32)
        * scale
    )
    return jnp.where(key_valid, scores, -1e30)


def column_sum(values):
    return jnp.sum(values, axis=0, dtype=jnp.float32)


def local(
    tokens,
    frame_counts,
    slot_mask,
    norm1_gain,
    norm1_bias,
    w_qkv,
    q_bias,
    v_bias,
    w_out,
    out_bias,
    norm2_gain,
    norm2_bias,
    w_up,
    up_bias,
    w_down,
    down_bias,
    norm3_gain,
    norm3_bias,
    w_align,
    align_bias,
    cot_block,
    cot_align,
):
    clip_count, frame_dev, slot_count, width = tokens.shape
    align_width = w_align.shape[1]
    head_size = width // HEADS
    scale = 1.0 / math.sqrt(head_size)
    row_count = clip_count * frame_dev * slot_count
    cycle_pos = lax.axis_index("blk")
    frame_ids = cycle_pos * frame_dev + jnp.arange(frame_dev, dtype=jnp.int32)
    own_slots = lax.dynamic_slice_in_dim(slot_mask, cycle_pos * frame_dev, frame_dev, 1)
    own_mask = (frame_ids[None, :, None] < frame_counts[:, None, None]) & (own_slots > 0)
    visible = own_mask.astype(jnp.float32).reshape(row_count, 1)
    all_frames = jnp.arange(slot_mask.shape[1], dtype=jnp.int32)
    key_valid = (all_frames[None, :, None] < frame_counts[:, None, None]) & (slot_mask > 0)
    key_valid = key_valid.reshape(clip_count, 1, 1, -1)
    inputs = tokens.reshape(row_count, width).astype(jnp.float32)
    normed_one, unit_one, inverse_one = norm_forward(inputs, norm1_gain, norm1_bias)
    normed1 = normed_one.astype(jnp.bfloat16)
    projected = jnp.dot(normed1, w_qkv, preferred_element_type=jnp.float32)
    queries = (projected[:, :width] + q_bias).astype(jnp.bfloat16)
    keys_local = projected[:, width : 2 * width].astype(jnp.bfloat16)
    values_local = (projected[:, 2 * width :] + v_bias).astype(jnp.bfloat16)
    block_shape = (clip_count, frame_dev, slot_count, width)
    heads_shape = (clip_count, -1, HEADS, head_size)
    keys_all, values_all = (
        lax.all_gather(keys_local.reshape(block_shape), "blk", axis=1, tiled=True),
        lax.all_gather(values_local.reshape(block_shape), "blk", axis=1, tiled=True),
    )
    key_heads = keys_all.reshape(heads_shape)
    value_heads = values_all.reshape(heads_shape)
    query_heads = queries.reshape(heads_shape)
    scores = masked_scores(query_heads, key_heads, key_valid, scale)
    top = jnp.max(scores, axis=-1, keepdims=True)
    expo = jnp.exp(scores - top)
    total = jnp.sum(expo, axis=-1, keepdims=True)
    probs_low = (expo / total).astype(jnp.bfloat16)
    attended = jnp.einsum(
        "chqk,ckhd->cqhd", probs_low, value_heads, preferred_element_type=jnp.float32
    )
    attended = attended.astype(jnp.bfloat16).reshape(row_count, width)
    mid = inputs + jnp.dot(attended, w_out, preferred_element_type=jnp.float32) + out_bias
    normed_two, unit_two, inverse_two = norm_forward(mid, norm2_gain, norm2_bias)
    normed2 = normed_two.astype(jnp.bfloat16)
    hidden = jnp.dot(normed2, w_up, preferred_element_type=jnp.float32) + up_bias
    active = jax.nn.gelu(hidden, approximate=False).astype(jnp.bfloat16)
    after = mid + jnp.dot(active, w_down, preferred_element_type=jnp.float32) + down_bias
    block_out = (visible * after).astype(jnp.bfloat16).reshape(block_shape)
    normed_three, unit_three, inverse_three = norm_forward(after, norm3_gain, norm3_bias)
    normed3 = normed_three.astype(jnp.bfloat16)
    target = jnp.dot(normed3, w_align, preferred_element_type=jnp.float32) + align_bias
    aligned = (
        (visible * target)
        .astype(jnp.bfloat16)
        .reshape(clip_count, frame_dev, slot_count, align_width)
    )
    back_align = (visible * cot_align.reshape(row_count, align_width).astype(jnp.float32)).astype(
        jnp.bfloat16
    )
    grad_align_bias = column_sum(back_align)
    grad_w_align = weight_grad(normed3, back_align)
    back_norm3, grad_norm3_gain, grad_norm3_bias = norm_backward(
        input_grad(back_align, w_align), unit_three, inverse_three, norm3_gain
    )
    back_after = visible * cot_block.reshape(row_count, width).astype(jnp.float32) + back_norm3
    back_down = back_after.astype(jnp.bfloat16)
    grad_down_bias = column_sum(back_down)
    grad_w_down = weight_grad(active, back_down)
    back_up = (input_grad(back_down, w_down) * gelu_slope(hidden)).astype(jnp.bfloat16)
    grad_up_bias = column_sum(back_up)
    grad_w_up = weight_grad(normed2, back_up)
    back_norm2, grad_norm2_gain, grad_norm2_bias = norm_backward(
        input_grad(back_up, w_up), unit_two, inverse_two, norm2_gain
    )
    back_mid = back_after + back_norm2
    back_out = back_mid.astype(jnp.bfloat16)
    grad_out_bias = column_sum(back_out)
    grad_w_out = weight_grad(attended, back_out)
    back_attended = input_grad(back_out, w_out).astype(jnp.bfloat16).reshape(heads_shape)
    scores = masked_scores(query_heads, key_heads, key_valid, scale)
    probs = jnp.exp(scores - top) / total
    probs_low = probs.astype(jnp.bfloat16)
    back_probs = jnp.einsum(
        "cqhd,ckhd->chqk", back_attended, value_heads, preferred_element_type=jnp.float32
    )
    spread = jnp.sum(probs * back_probs, axis=-1, keepdims=True)
    back_scores = (probs * (back_probs - spread)).astype(jnp.bfloat16)
    back_queries = (
        jnp.einsum("chqk,ckhd->cqhd", back_scores, key_heads, preferred_element_type=jnp.float32)
        * scale
    )
    back_queries = back_queries.astype(jnp.bfloat16).reshape(row_count, width)
    value_terms = jnp.einsum(
        "chqk,cqhd->ckhd", probs_low, back_attended, preferred_element_type=jnp.float32
    )
    key_terms = (
        jnp.einsum("chqk,cqhd->ckhd", back_scores, query_heads, preferred_element_type=jnp.float32)
        * scale
    )
    whole_shape = (clip_count, -1, slot_count, width)
    key_share, value_share = (
        lax.psum_scatter(
            key_terms.reshape(whole_shape).astype(jnp.bfloat16),
            "blk",
            scatter_dimension=1,
            tiled=True,
        ).astype(jnp.float32),
        lax.psum_scatter(
            value_terms.reshape(whole_shape).astype(jnp.bfloat16),
            "blk",
            scatter_dimension=1,
            tiled=True,
        ).astype(jnp.float32),
    )
    back_keys = key_share.astype(jnp.bfloat16).reshape(row_count, width)
    back_values = value_share.astype(jnp.bfloat16).reshape(row_count, width)
    grad_q_bias = column_sum(back_queries)
    grad_v_bias = column_sum(back_values)
    combined = jnp.concatenate([back_queries, back_keys, back_values], axis=1)
    grad_w_qkv = weight_grad(normed1, combined)
    back_norm1, grad_norm1_gain, grad_norm1_bias = norm_backward(
        input_grad(combined, w_qkv), unit_one, inverse_one, norm1_gain
    )
    grad_tokens = (back_mid + back_norm1).astype(jnp.bfloat16).reshape(block_shape)
    vector_total = lax.psum(
        (
            grad_norm1_gain,
            grad_norm1_bias,
            grad_q_bias,
            grad_v_bias,
            grad_out_bias,
            grad_norm2_gain,
            grad_norm2_bias,
            grad_up_bias,
            grad_down_bias,
            grad_norm3_gain,
            grad_norm3_bias,
            grad_align_bias,
        ),
        ("dp", "blk"),
    )
    row_part = (
        lax.psum_scatter(grad_w_qkv, "dp", scatter_dimension=0, tiled=True),
        lax.psum_scatter(grad_w_out, "dp", scatter_dimension=0, tiled=True),
        lax.psum_scatter(grad_w_up, "dp", scatter_dimension=0, tiled=True),
        lax.psum_scatter(grad_w_down, "dp", scatter_dimension=0, tiled=True),
        lax.psum_scatter(grad_w_align, "dp", scatter_dimension=0, tiled=True),
    )
    matrix_total = (
        lax.psum(row_part[0].astype(jnp.bfloat16), "blk").astype(jnp.float32),
        lax.psum(row_part[1].astype(jnp.bfloat16), "blk").astype(jnp.float32),
        lax.psum(row_part[2].astype(jnp.bfloat16), "blk").astype(jnp.float32),
        lax.psum(row_part[3].astype(jnp.bfloat16), "blk").astype(jnp.float32),
        lax.psum(row_part[4].astype(jnp.bfloat16), "blk").astype(jnp.float32),
    )
    return (
        block_out,
        aligned,
        grad_tokens,
        vector_total[0],
        vector_total[1],
        matrix_total[0],
        vector_total[2],
        vector_total[3],
        matrix_total[1],
        vector_total[4],
        vector_total[5],
        vector_total[6],
        matrix_total[2],
        vector_total[7],
        matrix_total[3],
        vector_total[8],
        vector_total[9],
        vector_total[10],
        matrix_total[4],
        vector_total[11],
    )


def local_kernels(
    tokens, frame_counts, slot_mask, norm1_gain, norm1_bias, w_qkv, q_bias, v_bias, w_out, out_bias, norm2_gain,
    norm2_bias, w_up, up_bias, w_down, down_bias, norm3_gain, norm3_bias, w_align, align_bias, cot_block, cot_align,
):
    clip_count, frame_dev, slot_count, width = tokens.shape
    align = w_align.shape[1]
    piece = frame_dev * slot_count
    rows = clip_count * piece
    vectors = [
        norm1_gain, norm1_bias, q_bias, v_bias, out_bias, norm2_gain, norm2_bias, down_bias, norm3_gain, norm3_bias,
        up_bias, align_bias,
    ]
    block_out, align_out, grad_tokens, vec, *shares = layer(
        slot_mask, frame_counts, vectors, tokens.reshape(clip_count, piece, width), cot_align.reshape(rows, align),
        cot_block.reshape(rows, width), w_align, w_down, w_up, w_out, w_qkv,
    )
    matrices, totals, (block_out, align_out, grad_tokens) = finish(
        shares, vec, (block_out, align_out, grad_tokens), [vector.shape[0] for vector in vectors]
    )
    (
        grad_norm1_gain, grad_norm1_bias, grad_q_bias, grad_v_bias, grad_out_bias, grad_norm2_gain, grad_norm2_bias,
        grad_down_bias, grad_norm3_gain, grad_norm3_bias, grad_up_bias, grad_align_bias,
    ) = totals
    return (
        block_out.reshape(tokens.shape),
        align_out.reshape(cot_align.shape),
        grad_tokens.reshape(tokens.shape),
        grad_norm1_gain,
        grad_norm1_bias,
        matrices[0],
        grad_q_bias,
        grad_v_bias,
        matrices[1],
        grad_out_bias,
        grad_norm2_gain,
        grad_norm2_bias,
        matrices[2],
        grad_up_bias,
        matrices[3],
        grad_down_bias,
        grad_norm3_gain,
        grad_norm3_bias,
        matrices[4],
        grad_align_bias,
    )


def solution(mesh):
    in_specs = (
        P("dp", "blk", None, None),
        P("dp"),
        P("dp", None, None),
        P(),
        P(),
        P(),
        P(),
        P(),
        P(),
        P(),
        P(),
        P(),
        P(),
        P(),
        P(),
        P(),
        P(),
        P(),
        P(),
        P(),
        P("dp", "blk", None, None),
        P("dp", "blk", None, None),
    )
    out_specs = (
        P("dp", "blk", None, None),
        P("dp", "blk", None, None),
        P("dp", "blk", None, None),
        P(),
        P(),
        P("dp", None),
        P(),
        P(),
        P("dp", None),
        P(),
        P(),
        P(),
        P("dp", None),
        P(),
        P("dp", None),
        P(),
        P(),
        P(),
        P("dp", None),
        P(),
    )
    sizes = (mesh.shape["dp"], mesh.shape["blk"])
    run = local_kernels if sizes == GRID else local
    return jax.shard_map(run, mesh=mesh, in_specs=in_specs, out_specs=out_specs, check_vma=False)
```

```python
import math

import jax
import jax.numpy as jnp
from jax import lax
from jax.experimental import pallas as pl
from jax.experimental.pallas import tpu as pltpu
from jax.sharding import PartitionSpec as P

HEADS = 12


EPSILON = 1e-06
SQRT_HALF = 0.7071067811865476
INV_ROOT_TAU = 0.3989422804014327
MESH = pl.DeviceIdType.MESH
GRID = (8, 4)


NT = (((1,), (1,)), ((), ()))
TN = (((0,), (0,)), ((), ()))
CHUNKS = 4


def dot(left, right, dims=(((1,), (0,)), ((), ()))):
    return lax.dot_general(left, right, dims, preferred_element_type=jnp.float32)


def remote_copy(src, dst, send, recv, device):
    return pltpu.make_async_remote_copy(
        src_ref=src, dst_ref=dst, send_sem=send, recv_sem=recv, device_id=device, device_id_type=MESH
    )


N1_GAIN, N1_BIAS, Q_BIAS, V_BIAS, OUT_BIAS, N2_GAIN, N2_BIAS, DOWN_BIAS, N3_GAIN, N3_BIAS, UP_BIAS, ALIGN_BIAS = (
    0, 1, 2, 3, 4, 5, 6, 7, 8, 9, 10, 14,
)
PACK_ROWS = 16


def fill_pack(pack, rows, refs):
    width = pack.shape[1]
    for row, ref in zip(rows, refs):
        for start in range(0, ref.shape[0], width):
            size = min(width, ref.shape[0] - start)
            line = row + start // width
            pack[line : line + 1, 0:size] = ref[pl.ds(start, size)].reshape(1, size)


def norm_rows(values):
    center = values - jnp.mean(values, axis=-1, keepdims=True)
    inverse = lax.rsqrt(jnp.mean(center * center, axis=-1, keepdims=True) + EPSILON)
    return center * inverse, inverse


JOBS = (
    (4, 0, 96, 0, 1024, 2048),
    (3, 0, 96, 0, 768, 0),
    (3, 96, 96, 0, 768, 768),
    (3, 192, 96, 0, 768, 1536),
    (3, 288, 96, 0, 768, 2304),
    (2, 0, 96, 0, 768, 0),
    (2, 0, 96, 768, 768, 768),
    (2, 0, 96, 1536, 768, 1536),
    (2, 0, 96, 2304, 768, 2304),
    (1, 0, 96, 0, 768, 0),
    (0, 0, 96, 0, 384, 768),
    (0, 0, 96, 384, 384, 1152),
    (0, 0, 96, 768, 384, 1536),
)
COUNT = len(JOBS)
PLAIN = 10
KEY_BLOCK = 256
NORM_ROWS = 192
PLAN = (
    (0, "far"), (0, 0), "e3", "norm3", (2, "far"), (2, 0), (0, "own"), (0, 1), (2, "own"), "feed", (2, 1), "e2",
    "norm2", "back_att", (0, 2), (1, "far"), (1, 0), (3, "own"), (2, 2), (3, "far"), (3, 0), (4, "own"), (1, "own"),
    (4, "far"), (4, 0), (1, 1), (5, "far"), (5, 0), (6, "far"), (6, 0), (2, 3), (3, 1), (5, "own"), (6, "own"),
    "settle0", "pair", (0, 3), (1, 2), "pair", (4, 1), "pair", "settle1", (1, 3), (2, 4), (3, 2), "pair", (5, 1),
    (4, 2), (9, "far"), (9, 0), (0, 4), "pair", (3, 3), (2, 5), "pair", (5, 2), "settle2", (1, 4), (9, "own"),
    (4, 3), "pair", (0, 5), (9, 1), (3, 4), (5, 3), "pair", (1, 5), "pair", "dx0", (4, 4), (6, 1), (9, 2), (3, 5),
    (10, "far"), (10, 0), (8, "own"), (8, "far"), (8, 0), "dx1", (5, 4), (10, "own"), (4, 5), (11, "far"), (11, 0),
    (10, 1), (7, "far"), (7, 0), "fwd0", (7, "own"), (5, 5), (10, 2), (0, 6), (7, 1), (11, "own"), (2, 6), (9, 3),
    (12, "far"), (12, 0), (11, 1), "fwd1", (10, 3), (8, 1), "dx2", "dx3", (12, "own"), (9, 4), (11, 2), "sums",
    (10, 4), (7, 2), "vec0", (3, 6), (12, 1), (1, 6), (8, 2), (11, 3), (4, 6), (6, 2), (9, 5), (12, 2), "vec1",
    (11, 4), (7, 3), (10, 5), (7, 4), (11, 5), (5, 6), "vec2", (8, 3), (6, 3), (9, 6), (8, 4), (7, 5), (12, 3),
    (10, 6), (7, 6), (6, 4), (8, 5), (12, 4), (6, 5), "vec3", (8, 6), (11, 6), (12, 5), "norm1", "vec4", "vec5",
    (6, 6), (12, 6),
)


def add_into(target, first, second):
    lead = target.shape[:-2]

    def body(k, _):
        if len(lead) == 0:
            at = (pl.ds(pl.multiple_of(k * 16, 16), 16), slice(None))
        elif len(lead) == 1:
            at = (k,)
        else:
            at = (k // lead[1], lax.rem(k, lead[1]))
        target[at] = first[at] + second[at]
        return 0

    lax.fori_loop(0, math.prod(lead) if lead else target.shape[0] // 16, body, 0)


VIS, KEY, INV2, INV3, STATS = 0, 1, 2, 3, 8


def layer_kernel(*refs):
    slot_mask, counts, vectors_h, refs = refs[0], refs[1], refs[2:14], refs[14:]
    tok_h, cot_a_h, cot_b_h, w_align, w_down, w_up, w_out, w_qkv = refs[:8]
    block_out, align_out, grad_tokens, vec_out = refs[8:12]
    outs = refs[12:17]
    rest = refs[17:]
    own, got0, got1, got2 = (rest[i * COUNT : (i + 1) * COUNT] for i in range(4))
    rest = rest[4 * COUNT :]
    gotz, gotq = rest[:PLAIN], rest[PLAIN:COUNT]
    rest = rest[COUNT:]
    vec_got, vectors = rest[0], rest[1:13]
    (
        pack, side_v,
        align_v, down_v, up_v, out_v, low_v, tok, xall, n1, qkv, own_att, att, lse_rows, spread_rows,
        mid_v, e_v, normed, ring, slope, ld, l2, l3, la, unit2, unit3, cot_a, cot_b,
        grad_att, n1s,
        load_sem, send0, recv0, send1, recv1, send2, recv2, sendz, recvz, sendq, recvq, out_sem, outq_sem, vsend, vrecv,
        tok_send, tok_recv, att_send, att_recv, in_send, in_recv,
        pair_send, pair_recv, end_send, end_recv, out_send, out_recv, put_sem, vector_sem,
    ) = rest[13:]

    dp = lax.axis_index("dp")
    z = lax.axis_index("blk")
    core = lax.rem(dp, 2)
    x = lax.rem(dp // 2, 2)
    y = dp // 4
    clip, side = z // 2, lax.rem(z, 2)
    to_core = (dp + 1 - 2 * core, z)
    to_x = (dp + 2 - 4 * x, z)
    to_y = (dp + 4 - 8 * y, z)
    partner = z + 1 - 2 * side
    to_z1 = (dp, partner)
    to_z2 = (dp, lax.rem(z + 2, 4))
    to_z3 = (dp, 3 - z)
    is_mid = (z == 1) | (z == 2)
    is_end = (z == 0) | (z == 3)
    near, far = 3 - z, lax.rem(z + 2, 4)
    other_mid = 2 - clip
    piece, width = tok.shape
    rows, half, wide = 2 * piece, width // 2, up_v.shape[1]
    low = jnp.bfloat16
    low_d, low_o = n1.at[pl.ds(0, rows)], n1.at[pl.ds(rows, rows)]
    in_src = att
    from_end = [normed.at[pl.ds(k * piece, piece)] for k in range(2)]
    from_pair, total_in = (cot_b.at[pl.ds(k * piece, piece)] for k in range(2))

    def grad_at(m):
        return down_v.at[pl.ds((2 if m == 0 else 3) * width, width), pl.ds(half if m != 1 else 0, half)]

    def e_at(slot):
        return align_v.at[pl.ds(pl.multiple_of(slot * piece, piece), piece), pl.ds(0, width)]

    def slot_rows(slot):
        return pl.ds(pl.multiple_of(slot * piece, piece), piece)

    loads = {"mine": (tok_h.at[clip], xall.at[z]), "tok": (tok_h.at[1 - clip], tok)}
    for m in range(3):
        column = pl.multiple_of(m * width + side * half, 128)
        loads["low%d" % m] = (w_qkv.at[:, pl.ds(column, half)], low_v.at[m])
    loads["out"] = (w_out, out_v)
    loads["up"] = (w_up, up_v)
    loads["down"] = (w_down, down_v)
    loads["cot_a"] = (cot_a_h, cot_a)
    loads["align"] = (w_align, align_v)
    loads["cot_b"] = (cot_b_h, cot_b)
    loads = {
        name: pltpu.make_async_copy(src, dst, load_sem.at[k]) for k, (name, (src, dst)) in enumerate(loads.items())
    }
    early = ("mine", "tok", "low0", "low1", "low2")
    for name in early:
        loads[name].start()
    small = [pltpu.make_async_copy(src, dst, vector_sem.at[k]) for k, (src, dst) in enumerate(zip(vectors_h, vectors))]
    for copy in small:
        copy.start()

    def ready(*names):
        for name in names:
            loads[name].wait()

    barrier = pltpu.get_barrier_semaphore()
    for device in (to_core, to_x, to_y, to_z1, to_z2, to_z3):
        pl.semaphore_signal(barrier, inc=1, device_id=device, device_id_type=MESH)
    pl.semaphore_wait(barrier, 6)
    step = piece // CHUNKS

    def tok_copy(kind, slot, k):
        at = pl.ds(k * step, step)
        source = xall.at[slot, at] if kind >= 2 else tok_h.at[1 - clip if kind == 0 else clip, at]
        device = (dp, other_mid) if kind == 0 else to_z1
        return remote_copy(source, xall.at[slot, at], tok_send.at[kind, k], tok_recv.at[slot, k], device)

    for k in range(CHUNKS):
        tok_copy(0, z, k).start()
    for k in range(CHUNKS):
        tok_copy(1, z, k).start()
    for copy in small:
        copy.wait()
    fill_pack(pack, VECTORS, vectors)
    vec_out[...] = jnp.zeros_like(vec_out)
    ready("mine", "tok")
    e_v[0:128, :] = jnp.zeros((128, width), jnp.float32)
    for c in range(2):
        e_v[c : c + 1, :] = jnp.concatenate(
            [
                jnp.where((slot_mask[c, f : f + 1, :] > 0) & (f < counts[c]), 1.0, 0.0)
                for f in range(slot_mask.shape[1])
            ],
            axis=1,
        )
    side_v[...] = e_v[0:128, :].T
    seen = [side_v[slot_rows(z), c : c + 1] for c in range(2)]
    side_v[:, KEY : KEY + 1] = jnp.where(jnp.where(clip == 0, side_v[:, 0:1], side_v[:, 1:2]) > 0.0, 0.0, -1e30)
    for c in range(2):
        side_v[pl.ds(c * piece, piece), VIS : VIS + 1] = seen[c]
    row_bias = jnp.where(jnp.where(clip == 0, e_v[0:1, :], e_v[1:2, :]) > 0.0, 0.0, -1e30)
    columns = pl.ds(pl.multiple_of(side * half, 128), half)
    ready("low0", "low1", "low2")

    def project(slot):
        where = slot_rows(slot)

        def body(k, _):
            one, _ = norm_rows(xall[slot, pl.ds(pl.multiple_of(k * 96, 96), 96), :].astype(jnp.float32))
            at = pl.ds(pl.multiple_of(slot * piece + k * 96, 96), 96)
            n1[at, :] = (one * pack[N1_GAIN : N1_GAIN + 1, :] + pack[N1_BIAS : N1_BIAS + 1, :]).astype(low)
            return 0

        lax.fori_loop(0, piece // 96, body, 0)
        left = n1[where, :]
        qkv[0, where, :] = (dot(left, low_v[0]) + pack[Q_BIAS : Q_BIAS + 1, columns]).astype(low) * low(0.125)
        qkv[1, where, :] = dot(left, low_v[1]).astype(low)
        qkv[2, where, :] = (dot(left, low_v[2]) + pack[V_BIAS : V_BIAS + 1, columns]).astype(low)

    last = 3 * (1 - clip)
    third = 2 - clip
    def slot_of(number):
        return jnp.where(number == 0, z, jnp.where(number == 1, partner, jnp.where(number == 2, third, last)))

    def tokens_of(number, _):
        slot = slot_of(number)

        @pl.when(number == 1)
        def _():
            for name in loads:
                if name not in early:
                    loads[name].start()

        @pl.when(is_mid & (number == 1))
        def _():
            for which, source in enumerate((near, far)):
                for k in range(CHUNKS):
                    tok_copy(1, source, k).wait_recv()
                    tok_copy(2 + which, source, k).start()
            for k in range(CHUNKS):
                tok_copy(1, partner, k).wait_recv()

        @pl.when(is_end & (number > 0))
        def _():
            for k in range(CHUNKS):
                tok_copy(1, slot, k).wait_recv()

        project(slot)
        return 0

    lane = lax.broadcasted_iota(jnp.int32, (1, 128), 1)
    low_lane = lane < 64

    def att_copy(slot, t):
        return remote_copy(
            own_att.at[t, slot_rows(slot)], att.at[clip, side, t], att_send.at[slot, t], att_recv.at[z, t], (dp, slot)
        )

    def head(queries, a, keys, bias):
        mine = low_lane if a == 0 else jnp.logical_not(low_lane)
        return dot(jnp.where(mine, queries, jnp.zeros_like(queries)), keys, NT) + bias

    def attend_whole(slot):
        where = slot_rows(slot)
        stats = jnp.zeros((piece, 128), jnp.float32)
        for t in range(half // 128):
            at = pl.ds(t * 128, 128)
            parts = []
            for a in range(2):
                scores = head(qkv[0, where, at], a, qkv[1, :, at], row_bias)
                top = jnp.max(scores, axis=-1, keepdims=True)
                expo = jnp.exp(scores - top)
                denominator = jnp.sum(expo, axis=-1, keepdims=True)
                parts.append(dot(expo.astype(low), qkv[2, :, at]) * (1.0 / denominator))
                stats = jnp.where(lane == STATS + 2 * t + a, top + jnp.log(denominator), stats)
            own_att[t, where, :] = jnp.where(low_lane, parts[0], parts[1]).astype(low)

            @pl.when(slot != z)
            def _():
                att_copy(slot, t).start()

        side_v[where, STATS : STATS + 8] = stats[:, STATS : STATS + 8]

    lax.fori_loop(0, 3, tokens_of, 0)
    tokens_of(3, 0)

    def attend(number, _):
        attend_whole(slot_of(3 - number))

        return 0

    lax.fori_loop(0, 4, attend, 0)

    att[clip, side] = own_att[:, slot_rows(z), :]

    def tiles(count, size, body):
        def one_tile(t, _):
            body(t, pl.ds(pl.multiple_of(t * size, size), size))
            return 0

        lax.fori_loop(0, count, one_tile, 0)

    def chunks(body, carry, size=48):
        def one_chunk(k, carry):
            return body(pl.ds(pl.multiple_of(k * size, size), size), k, carry)

        return lax.fori_loop(0, rows // size, one_chunk, carry)

    def put_vector(row, start, value):
        at = 0
        while at < value.shape[1]:
            line, column = row + (start + at) // width, (start + at) % width
            take = min(value.shape[1] - at, width - column)
            vec_out[line : line + 1, column : column + take] = value[:, at : at + take]
            at += take

    def total(value):
        return jnp.sum(value.astype(jnp.float32), axis=0, keepdims=True)

    zero_row = jnp.zeros((1, width), jnp.float32)
    ready("cot_a")

    def mask(at, k, carry):
        value = (side_v[at, VIS : VIS + 1] * cot_a[at, :].astype(jnp.float32)).astype(low)
        cot_a[at, :] = value
        return carry + total(value)

    put_vector(ALIGN_BIAS, 0, chunks(mask, jnp.zeros((1, cot_a.shape[1]), jnp.float32)))
    lse_rows[...] = side_v[...].T[STATS : STATS + 8]

    def shares_of(source, target, count):
        for c in range(0, source.shape[1], 128):
            flipped = source[:, pl.ds(c, 128)].T
            at = 0
            while at < 128:
                share, inside = (c + at) // count, (c + at) % count
                take = min(128 - at, count - inside)
                rel = jnp.where(core == share % 2, 1, 0)
                target[rel, share // 2, pl.ds(inside, take), :] = flipped[at : at + take]
                at += take

    shares_of(n1, n1s, width // 8)

    def settle_att(number, _):
        slot = lax.rem(z + number, 4)
        for t in range(half // 128):
            att_copy(slot, t).wait_send()
            remote_copy(
                own_att.at[t, slot_rows(slot)], att.at[slot // 2, lax.rem(slot, 2), t],
                att_send.at[slot, t], att_recv.at[slot, t], (dp, slot),
            ).wait_recv()
        return 0

    lax.fori_loop(1, 4, settle_att, 0)
    for k in range(CHUNKS):
        tok_copy(0, z, k).wait_send()
        tok_copy(1, z, k).wait_send()

    @pl.when(is_mid)
    def _():
        for k in range(CHUNKS):
            for which, slot in enumerate((near, far)):
                tok_copy(2 + which, slot, k).wait_send()

    for c in range(2):
        for h in range(2):
            for t in range(half // 128):
                normed[pl.ds(c * piece, piece), pl.ds(h * half + t * 128, 128)] = att[c, h, t]
    shares_of(normed, la, width // 8)
    ready("out")

    def mix(t, at):
        mixed = dot(normed[...], out_v[:, at]) + pack[OUT_BIAS : OUT_BIAS + 1, at]
        for c in range(2):
            mixed_c = mixed[c * piece : (c + 1) * piece]
            source = jnp.where(clip == c, xall[z, :, at], tok[:, at])
            mid_v[pl.ds(c * piece, piece), at] = source.astype(jnp.float32) + mixed_c

    tiles(3, 256, mix)

    def norm(gain, bias, unit, inv):
        def body(at, k, _):
            one, inverse = norm_rows(mid_v[at, :])
            unit[at, :] = one.astype(low)
            side_v[at, inv : inv + 1] = inverse
            normed[at, :] = (one * pack[gain : gain + 1, :] + pack[bias : bias + 1, :]).astype(low)
            return 0

        chunks(body, 0, NORM_ROWS)

    norm(N2_GAIN, N2_BIAS, unit2, INV2)
    shares_of(normed, l2, width // 8)
    ready("up")

    def up(t, at):
        e_v[...] = dot(normed[...], up_v[:, at]) + pack[pl.ds(UP_BIAS + t, 1), :]

        def gelu(here, k, _):
            values = e_v[here, :]
            cdf = 0.5 * (1.0 + lax.erf(values * SQRT_HALF))
            ring[k, :, at] = (values * cdf).astype(low)
            slope[here, at] = (cdf + values * jnp.exp(-0.5 * values * values) * INV_ROOT_TAU).astype(low)
            return 0

        chunks(gelu, 0)
        for c in range(0, width, 128):
            rel = core if c < half else 1 - core
            columns_at = pl.ds(pl.multiple_of(t * width + c, 128), 128)
            ld[1 - rel, t, pl.ds(c % half, 128), :] = ring[:, :, columns_at].reshape(rows, 128).T

    tiles(4, width, up)
    ready("down")

    def down(t, at):
        mid_v[:, at] = (
            mid_v[:, at] + dot(ring[...].reshape(rows, wide), down_v[:, at]) + pack[DOWN_BIAS : DOWN_BIAS + 1, at]
        )

    tiles(3, 256, down)

    def staged(j, target):
        return pltpu.make_async_copy(own[j], target, put_sem.at[j])

    def put_block(at, k, _):
        own[1][k // 4, lax.rem(k, 4)] = (side_v[at, VIS : VIS + 1] * mid_v[at, :]).astype(low)
        return 0

    chunks(put_block, 0)
    staged(1, block_out).start()
    norm(N3_GAIN, N3_BIAS, unit3, INV3)
    shares_of(normed, l3, width // 8)
    ready("align", "cot_b")

    def align_tile(t, at):
        bias = pack[pl.ds(ALIGN_BIAS + t // 3, 1), pl.ds(pl.multiple_of(lax.rem(t, 3) * 256, 256), 256)]
        value = dot(normed[...], align_v[:, at]) + bias
        value = (side_v[pl.ds(0, rows), VIS : VIS + 1] * value).astype(low)
        for k in range(8):
            own[0][k // 4, k % 4, :, at] = value[k * 48 : (k + 1) * 48]

    tiles(4, 256, align_tile)
    staged(0, align_out).start()

    def buffer_of(j):
        return ring.at[:, :, pl.ds(JOBS[j][5], JOBS[j][4])]

    def copies0(j):
        for h in range(2):
            yield remote_copy(
                buffer_of(j).at[pl.ds(4 * h, 4)], got0[j].at[h], send0.at[j, h], recv0.at[j, h], to_core
            )

    def copies1(j):
        yield remote_copy(
            own[j].at[0, pl.ds(2 * (1 - x), 2)], got1[j].at[0], send1.at[j, 0], recv1.at[j, 0], to_x
        )
        yield remote_copy(
            own[j].at[1, pl.ds(2 * (1 - y), 2)], got1[j].at[1], send1.at[j, 1], recv1.at[j, 1], to_y
        )

    def copies2(j):
        yield remote_copy(own[j].at[0, 2 * x + 1 - y], got2[j].at[0], send2.at[j, 0], recv2.at[j, 0], to_y)
        yield remote_copy(own[j].at[1, 2 * y + 1 - x], got2[j].at[1], send2.at[j, 1], recv2.at[j, 1], to_x)

    def shares(j):
        return (own[j].at[0, 2 * x + y], own[j].at[1, 2 * y + x])

    def copiesz(j, slot, device):
        for h, share in enumerate(shares(j)):
            yield remote_copy(share, gotz[j].at[slot, h], sendz.at[j, slot, h], recvz.at[j, slot, h], device)

    def copiesq(j, source, slot, device):
        got, m = gotq[j - PLAIN], j - PLAIN
        for h, share in enumerate(shares(j)):
            yield remote_copy(
                share if source is None else got.at[source, h],
                got.at[slot, h], sendq.at[m, slot, h], recvq.at[m, slot, h], device,
            )

    def result(j, h, source):
        matrix, row, count, column, size, _ = JOBS[j]
        return pltpu.make_async_copy(
            source, outs[matrix].at[pl.ds(row + h * count // 2, count // 2), pl.ds(column, size)], out_sem.at[j, h]
        )

    def result_q(j, h, which, source):
        count, m = JOBS[j][2] // 2, j - PLAIN
        at = side if which == 0 else 1 - side
        column = pl.multiple_of(m * width + at * half, 128)
        return pltpu.make_async_copy(
            source, outs[0].at[pl.ds(h * count, count), pl.ds(column, half)], outq_sem.at[m, which, h]
        )

    def stage(j, number):
        if number == 0:
            for copy in copies0(j):
                copy.start()
        if number == 1:
            for h, (arrived, onward) in enumerate(zip(copies0(j), copies1(j))):
                arrived.wait()
                add_into(own[j].at[h], own[j].at[h], got0[j].at[h])
                onward.start()
        if number == 2:
            for h, (arrived, onward) in enumerate(zip(copies1(j), copies2(j))):
                arrived.wait()
                kept = own[j].at[h, pl.ds(2 * (y if h else x), 2)]
                add_into(kept, kept, got1[j].at[h])
                onward.start()
        if number == 3:
            onward = list(copiesq(j, None, 0, to_z1) if j >= PLAIN else copiesz(j, 0, to_z1))
            for h, (arrived, share) in enumerate(zip(copies2(j), shares(j))):
                arrived.wait()
                add_into(share, share, got2[j].at[h])
                pl.when(is_end)(onward[h].start)

        if number >= 4 and j >= PLAIN:
            stage_q(j, number)
            return
        if number == 4:

            @pl.when(is_mid)
            def _():
                for h, (arrived, onward) in enumerate(zip(copiesz(j, 0, to_z1), copiesz(j, 1, to_z3))):
                    arrived.wait_recv()
                    add_into(shares(j)[h], shares(j)[h], gotz[j].at[0, h])
                    onward.start()

            @pl.when(is_end)
            def _():
                for copy in copiesz(j, 0, to_z1):
                    copy.wait_send()

        if number == 5:

            @pl.when(is_mid)
            def _():
                for h, (arrived, onward) in enumerate(zip(copiesz(j, 1, to_z3), copiesz(j, 0, to_z1))):
                    arrived.wait()
                    add_into(shares(j)[h], shares(j)[h], gotz[j].at[1, h])
                    onward.start()
                    result(j, h, shares(j)[h]).start()

        if number == 6:

            @pl.when(is_mid)
            def _():
                for copy in copiesz(j, 0, to_z1):
                    copy.wait_send()

            @pl.when(is_end)
            def _():
                for copy in copiesz(j, 0, to_z1):
                    copy.wait_recv()
                for h in range(2):
                    result(j, h, gotz[j].at[0, h]).start()

    def stage_q(j, number):
        got = gotq[j - PLAIN]
        if number == 4:

            @pl.when(is_mid)
            def _():
                for copy in copiesq(j, None, 1, to_z3):
                    copy.start()
                for copy in copiesq(j, None, 0, to_z1):
                    copy.wait_recv()
                for copy in copiesq(j, 0, 2, to_z3):
                    copy.start()

            @pl.when(is_end)
            def _():
                for copy in copiesq(j, None, 0, to_z1):
                    copy.wait_send()

        if number == 5:

            @pl.when(is_mid)
            def _():
                for copy in copiesq(j, None, 1, to_z3):
                    copy.wait()
                for copy in copiesq(j, 0, 2, to_z3):
                    copy.wait()
                for h, share in enumerate(shares(j)):
                    add_into(share, share, got.at[2, h])
                    add_into(got.at[0, h], got.at[0, h], got.at[1, h])
                for copy in copiesq(j, None, 1, to_z1):
                    copy.start()
                for copy in copiesq(j, 0, 0, to_z1):
                    copy.start()
                for h, share in enumerate(shares(j)):
                    result_q(j, h, 0, share).start()
                    result_q(j, h, 1, got.at[0, h]).start()

        if number == 6:

            @pl.when(is_mid)
            def _():
                for copy in copiesq(j, None, 1, to_z1):
                    copy.wait_send()
                for copy in copiesq(j, 0, 0, to_z1):
                    copy.wait_send()

            @pl.when(is_end)
            def _():
                for copy in copiesq(j, None, 1, to_z1):
                    copy.wait_recv()
                for copy in copiesq(j, 0, 0, to_z1):
                    copy.wait_recv()
                for h in range(2):
                    result_q(j, h, 0, got.at[0, h]).start()
                    result_q(j, h, 1, got.at[1, h]).start()

    def results_done():
        for j in range(COUNT):
            for h in range(2):
                if j < PLAIN:
                    result(j, h, gotz[j].at[0, h]).wait()
                else:
                    for which in range(2):
                        result_q(j, h, which, gotq[j - PLAIN].at[0, h]).wait()

    def gradient(j, mine, left, right):
        count, size = JOBS[j][2], JOBS[j][4]
        target = own[j] if mine else buffer_of(j)
        for c in range(0, size, min(size, 384 if size % 384 == 0 else 512)):
            at = pl.ds(c, min(size, 384 if size % 384 == 0 else 512))
            value = dot(left, right(at)).astype(low)
            for chip in range(4):
                cy, cx = chip // 2, chip % 2
                for h in range(2):
                    k = 2 * cx + cy if h == 0 else 2 * cy + cx
                    start = chip * count + h * count // 2
                    part = value[start : start + count // 2]
                    if mine:
                        target[h, k, :, at] = part
                    else:
                        target[4 * h + k, :, at] = part

    def job(j, mine):
        matrix, row, count, column, size, _ = JOBS[j]
        lhs, rhs = ((n1s, None), (la, low_o), (l2, slope), (ld, low_d), (l3, cot_a))[matrix]
        left = lhs[1 if mine else 0, :, pl.ds(row, count), :].reshape(4 * count, lhs.shape[3])
        if matrix == 0:
            gradient(j, mine, left, lambda at: grad_at(j - PLAIN)[...])
        else:
            gradient(j, mine, left, lambda at: rhs[:, pl.ds(column + at.start, at.size)])

    def norm_back(e, one, inverse, gain):
        scaled = e * gain
        return inverse * (
            scaled
            - jnp.mean(scaled, axis=-1, keepdims=True)
            - one * jnp.mean(scaled * one, axis=-1, keepdims=True)
        )

    def norm_pass(unit, inv, gain_row, base, low_target, sums):
        def body(at, k, carry):
            e = e_v[at, :]
            one = unit[at, :].astype(jnp.float32)
            value = base(at) + norm_back(e, one, side_v[at, inv : inv + 1], pack[gain_row : gain_row + 1, :])
            mid_v[at, :] = value
            rounded = value.astype(low)
            low_target[at, :] = rounded
            return (carry[0] + total(e * one), carry[1] + total(e), carry[2] + total(rounded))

        for row, value in zip(sums, chunks(body, (zero_row,) * 3, NORM_ROWS)):
            put_vector(row, 0, value)

    def e3():
        def body(t, at):
            e_v[:, at] = dot(cot_a[...], align_v[at, :], NT)

        tiles(3, 256, body)

    def norm3():
        norm_pass(
            unit3, INV3, N3_GAIN, lambda at: side_v[at, VIS : VIS + 1] * cot_b[at, :].astype(jnp.float32), low_d,
            (N3_GAIN, N3_BIAS, DOWN_BIAS),
        )

    def feed():
        def body(t, at):
            value = (dot(low_d[...], down_v[at, :], NT) * slope[:, at].astype(jnp.float32)).astype(low)
            slope[:, at] = value
            vec_out[pl.ds(UP_BIAS + t, 1), :] = total(value)

        tiles(4, width, body)

    def e2():
        def body(t, at):
            e_v[:, at] = dot(slope[...], up_v[at, :], NT)

        tiles(3, 256, body)

    def norm2():
        norm_pass(unit2, INV2, N2_GAIN, lambda at: mid_v[at, :], low_o, (N2_GAIN, N2_BIAS, OUT_BIAS))

    def in_copy(slot, t):
        return remote_copy(
            in_src.at[slot // 2, lax.rem(slot, 2), t], grad_att.at[t, z],
            in_send.at[slot, t], in_recv.at[z, t], (dp, slot),
        )

    def back_att():
        for h in range(2):
            value = dot(low_o[...], out_v[pl.ds(h * half, half), :], NT).astype(low)
            for c in range(2):
                for t in range(half // 128):
                    in_src[c, h, t] = value[c * piece : (c + 1) * piece, t * 128 : (t + 1) * 128]
        for t in range(half // 128):

            def start(number, _):
                in_copy(lax.rem(z + number, 4), t).start()
                return 0

            lax.fori_loop(1, 4, start, 0)
        for t in range(half // 128):
            grad_att[t, z] = in_src[clip, side, t]

    def settle(t):
        def body(number, _):
            slot = lax.rem(z + number, 4)
            in_copy(slot, t).wait_send()
            remote_copy(
                in_src.at[0, 0, t], grad_att.at[t, slot], in_send.at[slot, t], in_recv.at[slot, t], (dp, slot)
            ).wait_recv()
            return 0

        lax.fori_loop(1, 4, body, 0)

        def spread(slot, _):
            where = slot_rows(slot)
            stats = jnp.zeros((piece, 128), jnp.float32)
            product = grad_att[t, slot].astype(jnp.float32) * own_att[t, where, :].astype(jnp.float32)
            for a in range(2):
                mine = low_lane if a == 0 else jnp.logical_not(low_lane)
                value = jnp.sum(jnp.where(mine, product, 0.0), axis=-1, keepdims=True)
                stats = jnp.where(lane == STATS + a, value, stats)
            side_v[where, STATS : STATS + 2] = stats[:, STATS : STATS + 2]
            return 0

        lax.fori_loop(0, 4, spread, 0)
        spread_rows[2 * t : 2 * t + 2, :] = side_v[...].T[STATS : STATS + 2]

    def pair(number):
        t, b = number // 3, lax.rem(number, 3)
        at = pl.ds(pl.multiple_of(t * 128, 128), 128)
        queries = qkv[0, :, at]
        grads = grad_att[t].reshape(4 * piece, 128)
        keys_at = pl.ds(pl.multiple_of(b * KEY_BLOCK, KEY_BLOCK), KEY_BLOCK)
        keys = qkv[1, keys_at, at]
        values = qkv[2, keys_at, at]
        grad_k = jnp.zeros((KEY_BLOCK, 128), jnp.float32)
        grad_v = jnp.zeros((KEY_BLOCK, 128), jnp.float32)
        held_q = (e_v.at[:, pl.ds(0, 128)], e_v.at[:, pl.ds(128, 128)])
        grad_queries = jnp.where(b == 0, 0.0, jnp.concatenate([ref[...] for ref in held_q], axis=0))
        for a in range(2):
            mine = low_lane if a == 0 else jnp.logical_not(low_lane)
            zero = jnp.zeros((), low)
            q_mine = jnp.where(mine, queries, zero)
            g_mine = jnp.where(mine, grads, zero)
            k_mine = jnp.where(mine, keys, zero)
            row = pl.ds(2 * t + a, 1)
            scores = dot(keys, q_mine, NT) + side_v[keys_at, KEY : KEY + 1]
            probs = jnp.exp(scores - lse_rows[row, :])
            back = (probs * (dot(values, g_mine, NT) - spread_rows[row, :])).astype(low)
            grad_v = grad_v + dot(probs.astype(low), g_mine)
            grad_k = grad_k + dot(back, q_mine)
            grad_queries = grad_queries + dot(back, k_mine, TN)
        grad_at(1)[keys_at, at] = grad_k.astype(low)
        grad_at(2)[keys_at, at] = grad_v.astype(low)
        for k, ref in enumerate(held_q):
            ref[...] = grad_queries[k * rows : (k + 1) * rows]

        @pl.when(b == 2)
        def _():
            for k, ref in enumerate(held_q):
                grad_at(0)[pl.ds(k * rows, rows), at] = (ref[...] * 0.125).astype(low)

    def pair_copy():
        return remote_copy(e_at(partner), from_pair, pair_send, pair_recv, to_z1)

    def end_copy(which, slot):
        return remote_copy(e_at(slot), from_end[which], end_send.at[which], end_recv.at[which], to_z1)

    def out_copy(which, slot):
        return remote_copy(e_at(slot), total_in, out_send.at[which], out_recv, (dp, slot))

    targets = (3 - 3 * clip, 2 - clip)
    mine_rows = slot_rows(clip)

    def dx(number):
        slot = (targets + (partner, z))[number]
        where = slot_rows(slot)
        value = sum(dot(grad_at(m)[where, :], low_v[m], NT) for m in range(3))
        e_at(slot)[...] = value.astype(low)
        if number == 3:
            e_v[mine_rows, :] = value
        if number < 2:

            @pl.when(is_end)
            def _():
                end_copy(number, slot).start()

        if number == 2:
            pair_copy().start()
        one, _ = norm_rows(xall[slot].astype(jnp.float32))
        for row, term in ((N1_GAIN, total(value * one)), (N1_BIAS, total(value))):
            vec_out[row : row + 1, :] = vec_out[row : row + 1, :] + term

    def sums():
        spot = lax.broadcasted_iota(jnp.int32, (1, width), 1)
        for row, m in ((Q_BIAS, 0), (V_BIAS, 2)):
            value = total(grad_at(m)[...])
            value = jnp.concatenate([value, value], axis=1)
            put_vector(row, 0, jnp.where((spot < half) == (side == 0), value, 0.0))

    def forward(which):
        @pl.when(is_mid)
        def _():
            slot = targets[which]
            end_copy(which, slot).wait_recv()
            add_into(e_at(slot), e_at(slot), from_end[which])
            out_copy(which, slot).start()

    vec_devices = (to_core, to_x, to_y, to_z1, to_z2)

    def vec_copy(k):
        return remote_copy(vec_out, vec_got.at[k], vsend.at[k], vrecv.at[k], vec_devices[k])

    def vec(k):
        if k > 0:
            vec_copy(k - 1).wait()
            vec_out[...] = vec_out[...] + vec_got[k - 1]
        if k < 5:
            vec_copy(k).start()

    def norm1():
        pair_copy().wait()
        e_v[mine_rows, :] = e_v[mine_rows, :] + from_pair[...].astype(jnp.float32)
        out_copy(0, partner).wait_recv()
        e_v[slot_rows(1 - clip), :] = total_in[...].astype(jnp.float32)

        def body(at, k, _):
            source = jnp.where(clip == k, xall[z], tok[...])
            one, inverse = norm_rows(source.astype(jnp.float32))
            value = mid_v[at, :] + norm_back(e_v[at, :], one, inverse, pack[N1_GAIN : N1_GAIN + 1, :])
            low_d[at, :] = value.astype(low)
            return 0

        chunks(body, 0, NORM_ROWS)
        pltpu.make_async_copy(low_d, grad_tokens, put_sem.at[2]).start()

    singles = dict(
        e3=e3, norm3=norm3, feed=feed, e2=e2, norm2=norm2, back_att=back_att, sums=sums, norm1=norm1
    )
    several = dict(settle=settle, dx=dx, fwd=forward, vec=vec)
    staged(0, align_out).wait()
    staged(1, block_out).wait()

    def run(entries):
        for entry in entries:
            if isinstance(entry, tuple):
                if entry[1] in ("far", "own"):
                    job(entry[0], entry[1] == "own")
                else:
                    stage(*entry)
            elif entry in singles:
                singles[entry]()
            else:
                several[entry[:-1]](int(entry[-1]))

    spots = [k for k, entry in enumerate(PLAN) if entry == "pair"]
    run(PLAN[: spots[0]])

    def pair_and_more(number, _):
        pair(number)
        for k in range(len(spots) - 1):
            if spots[k] + 1 < spots[k + 1]:

                @pl.when(number == k)
                def _():
                    run(PLAN[spots[k] + 1 : spots[k + 1]])

        return 0

    lax.fori_loop(0, len(spots), pair_and_more, 0)
    run(PLAN[spots[-1] + 1 :])
    results_done()
    pltpu.make_async_copy(low_d, grad_tokens, put_sem.at[2]).wait()

    @pl.when(is_mid)
    def _():
        for which in range(2):
            out_copy(which, targets[which]).wait_send()

    @pl.when(is_end)
    def _():
        for which in range(2):
            end_copy(which, targets[which]).wait_send()


def layer(slot_mask, counts, vectors, tok, cot_a, cot_b, w_align, w_down, w_up, w_out, w_qkv):
    _, piece, width = tok.shape
    rows, half, wide, align = 2 * piece, width // 2, w_up.shape[1], w_align.shape[1]
    low, full = jnp.bfloat16, jnp.float32
    vmem = pl.BlockSpec(memory_space=pltpu.VMEM)
    hbm = pl.BlockSpec(memory_space=pl.ANY)
    dma = pltpu.SemaphoreType.DMA
    v = pltpu.VMEM
    shapes = [(2, 4, job[2] // 2, job[4]) for job in JOBS]
    scratch = (
        [v(shape, low) for shape in shapes]
        + [v(shape, low) for shape in shapes]
        + [v((2, 2) + shape[2:], low) for shape in shapes]
        + [v((2,) + shape[2:], low) for shape in shapes]
        + [v((2, 2) + shape[2:], low) for shape in shapes[:PLAIN]]
        + [v((3, 2) + shape[2:], low) for shape in shapes[PLAIN:]]
        + [v((5, PACK_ROWS, width), full)]
        + [v(vector.shape, full) for vector in vectors]
        + [v((PACK_ROWS, width), full), v((4 * piece, 128), full)]
        + [v(w_align.shape, low), v(w_down.shape, low), v(w_up.shape, low), v(w_out.shape, low)]
        + [v((3, width, half), low), v((piece, width), low), v((4, piece, width), low), v((4 * piece, width), low)]
        + [v((3, 4 * piece, half), low), v((3, 4 * piece, 128), low), v((2, 2, 3, piece, 128), low)]
        + [v((8, 4 * piece), full)] * 2
        + [v((rows, width), full), v((rows, width), full), v((rows, width), low), v((8, 48, wide), low)]
        + [v((rows, wide), low), v((2, 4, wide // 8, rows), low)]
        + [v((2, 4, width // 8, rows), low)] * 3
        + [v((rows, width), low)] * 2
        + [v((rows, align), low), v((rows, width), low)]
        + [v((3, 4, piece, 128), low), v((2, 4, width // 8, 4 * piece), low)]
        + [dma((11,))]
        + [dma((COUNT, 2))] * 6
        + [dma((PLAIN, 2, 2))] * 2
        + [dma((3, 3, 2))] * 2
        + [dma((PLAIN, 2)), dma((3, 2, 2))]
        + [dma((5,))] * 2
        + [dma((4, CHUNKS))] * 2
        + [dma((4, 3))] * 4
        + [dma(())] * 2
        + [dma((2,))] * 2
        + [dma((2,)), dma(())]
        + [dma((3,)), dma((12,))]
    )
    struct = jax.ShapeDtypeStruct
    return pl.pallas_call(
        layer_kernel,
        name="layer",
        out_shape=[
            struct((2, 4, 48, width), low),
            struct((2, 4, 48, align), low),
            struct((rows, width), low),
            struct((PACK_ROWS, width), full),
        ]
        + [struct((w.shape[0] // 8, w.shape[1]), low) for w in (w_qkv, w_out, w_up, w_down, w_align)],
        in_specs=[vmem, pl.BlockSpec(memory_space=pltpu.SMEM)] + [hbm] * 20,
        out_specs=[hbm, hbm, hbm, vmem] + [hbm] * 5,
        scratch_shapes=scratch,
        compiler_params=pltpu.CompilerParams(
            collective_id=0, has_side_effects=True, vmem_limit_bytes=63 * 2**20
        ),
    )(slot_mask, counts, *vectors, tok, cot_a, cot_b, w_align, w_down, w_up, w_out, w_qkv)


VECTORS = (
    N1_GAIN, N1_BIAS, Q_BIAS, V_BIAS, OUT_BIAS, N2_GAIN, N2_BIAS, DOWN_BIAS, N3_GAIN, N3_BIAS, UP_BIAS, ALIGN_BIAS,
)


def finish_kernel(*refs):
    shares, pack, through_in = refs[:5], refs[5], refs[6:9]
    wide, vectors, through_out = refs[9:14], refs[14:26], refs[26:29]
    low_v, wide_v, held, pack_v, vectors_v = refs[29:34], refs[34:39], refs[39:42], refs[42], refs[43:55]
    in_sem, out_sem, vector_sem = refs[55:]
    ins = [pltpu.make_async_copy(shares[k], low_v[k], in_sem.at[k]) for k in range(5)]
    outs = [pltpu.make_async_copy(wide_v[k], wide[k], out_sem.at[k]) for k in range(5)]
    through = [
        (
            pltpu.make_async_copy(through_in[k], held[k], in_sem.at[5 + k]),
            pltpu.make_async_copy(held[k], through_out[k], out_sem.at[5 + k]),
        )
        for k in range(3)
    ]
    pack_in = pltpu.make_async_copy(pack, pack_v, in_sem.at[8])
    for copy in [pack_in] + ins:
        copy.start()
    for copy, _ in through:
        copy.start()
    width = pack.shape[1]
    vectors_out = [
        pltpu.make_async_copy(vectors_v[k], vectors[k], vector_sem.at[k]) for k in range(len(vectors))
    ]
    pack_in.wait()
    for row, ref in zip(VECTORS, vectors_v):
        for start in range(0, ref.shape[0], width):
            size = min(width, ref.shape[0] - start)
            line = row + start // width
            ref[pl.ds(start, size)] = pack_v[line : line + 1, 0:size].reshape(size)
    for copy in vectors_out:
        copy.start()
    for k in range(5):
        ins[k].wait()
        wide_v[k][...] = low_v[k][...].astype(jnp.float32)
        outs[k].start()
    for first, second in through:
        first.wait()
        second.start()
    for copy in outs + vectors_out:
        copy.wait()
    for _, copy in through:
        copy.wait()


def finish(shares, pack, through, sizes):
    hbm = pl.BlockSpec(memory_space=pl.ANY)
    struct = jax.ShapeDtypeStruct
    results = pl.pallas_call(
        finish_kernel,
        name="finish",
        out_shape=[struct(share.shape, jnp.float32) for share in shares]
        + [struct((size,), jnp.float32) for size in sizes]
        + [struct(array.shape, array.dtype) for array in through],
        in_specs=[hbm] * 9,
        out_specs=[hbm] * 20,
        scratch_shapes=[pltpu.VMEM(share.shape, share.dtype) for share in shares]
        + [pltpu.VMEM(share.shape, jnp.float32) for share in shares]
        + [pltpu.VMEM(array.shape, array.dtype) for array in through]
        + [pltpu.VMEM(pack.shape, pack.dtype)]
        + [pltpu.VMEM((size,), jnp.float32) for size in sizes]
        + [pltpu.SemaphoreType.DMA((9,)), pltpu.SemaphoreType.DMA((8,)), pltpu.SemaphoreType.DMA((12,))],
        compiler_params=pltpu.CompilerParams(vmem_limit_bytes=62 * 2**20),
    )(*shares, pack, *through)
    return results[:5], results[5:17], results[17:]


def norm_forward(values, gain, shift):
    center = values - jnp.mean(values, axis=-1, keepdims=True)
    inverse = lax.rsqrt(jnp.mean(center * center, axis=-1, keepdims=True) + EPSILON)
    normed = center * inverse
    return (normed * gain + shift, normed, inverse)


def norm_backward(upstream, normed, inverse, gain):
    scaled = upstream * gain
    inner = (
        scaled
        - jnp.mean(scaled, axis=-1, keepdims=True)
        - normed * jnp.mean(scaled * normed, axis=-1, keepdims=True)
    )
    return (inverse * inner, jnp.sum(upstream * normed, axis=0), jnp.sum(upstream, axis=0))


def gelu_slope(values):
    return (
        0.5 * (1.0 + lax.erf(values * SQRT_HALF))
        + values * jnp.exp(-0.5 * values * values) * INV_ROOT_TAU
    )


def weight_grad(left, right):
    return lax.dot_general(
        left, right, (((0,), (0,)), ((), ())), preferred_element_type=jnp.float32
    )


def input_grad(upstream, weight):
    return lax.dot_general(
        upstream, weight, (((1,), (1,)), ((), ())), preferred_element_type=jnp.float32
    )


def masked_scores(query_heads, key_heads, key_valid, scale):
    scores = (
        jnp.einsum("cqhd,ckhd->chqk", query_heads, key_heads, preferred_element_type=jnp.float32)
        * scale
    )
    return jnp.where(key_valid, scores, -1e30)


def column_sum(values):
    return jnp.sum(values, axis=0, dtype=jnp.float32)


def local(
    tokens,
    frame_counts,
    slot_mask,
    norm1_gain,
    norm1_bias,
    w_qkv,
    q_bias,
    v_bias,
    w_out,
    out_bias,
    norm2_gain,
    norm2_bias,
    w_up,
    up_bias,
    w_down,
    down_bias,
    norm3_gain,
    norm3_bias,
    w_align,
    align_bias,
    cot_block,
    cot_align,
):
    clip_count, frame_dev, slot_count, width = tokens.shape
    align_width = w_align.shape[1]
    head_size = width // HEADS
    scale = 1.0 / math.sqrt(head_size)
    row_count = clip_count * frame_dev * slot_count
    cycle_pos = lax.axis_index("blk")
    frame_ids = cycle_pos * frame_dev + jnp.arange(frame_dev, dtype=jnp.int32)
    own_slots = lax.dynamic_slice_in_dim(slot_mask, cycle_pos * frame_dev, frame_dev, 1)
    own_mask = (frame_ids[None, :, None] < frame_counts[:, None, None]) & (own_slots > 0)
    visible = own_mask.astype(jnp.float32).reshape(row_count, 1)
    all_frames = jnp.arange(slot_mask.shape[1], dtype=jnp.int32)
    key_valid = (all_frames[None, :, None] < frame_counts[:, None, None]) & (slot_mask > 0)
    key_valid = key_valid.reshape(clip_count, 1, 1, -1)
    inputs = tokens.reshape(row_count, width).astype(jnp.float32)
    normed_one, unit_one, inverse_one = norm_forward(inputs, norm1_gain, norm1_bias)
    normed1 = normed_one.astype(jnp.bfloat16)
    projected = jnp.dot(normed1, w_qkv, preferred_element_type=jnp.float32)
    queries = (projected[:, :width] + q_bias).astype(jnp.bfloat16)
    keys_local = projected[:, width : 2 * width].astype(jnp.bfloat16)
    values_local = (projected[:, 2 * width :] + v_bias).astype(jnp.bfloat16)
    block_shape = (clip_count, frame_dev, slot_count, width)
    heads_shape = (clip_count, -1, HEADS, head_size)
    keys_all, values_all = (
        lax.all_gather(keys_local.reshape(block_shape), "blk", axis=1, tiled=True),
        lax.all_gather(values_local.reshape(block_shape), "blk", axis=1, tiled=True),
    )
    key_heads = keys_all.reshape(heads_shape)
    value_heads = values_all.reshape(heads_shape)
    query_heads = queries.reshape(heads_shape)
    scores = masked_scores(query_heads, key_heads, key_valid, scale)
    top = jnp.max(scores, axis=-1, keepdims=True)
    expo = jnp.exp(scores - top)
    total = jnp.sum(expo, axis=-1, keepdims=True)
    probs_low = (expo / total).astype(jnp.bfloat16)
    attended = jnp.einsum(
        "chqk,ckhd->cqhd", probs_low, value_heads, preferred_element_type=jnp.float32
    )
    attended = attended.astype(jnp.bfloat16).reshape(row_count, width)
    mid = inputs + jnp.dot(attended, w_out, preferred_element_type=jnp.float32) + out_bias
    normed_two, unit_two, inverse_two = norm_forward(mid, norm2_gain, norm2_bias)
    normed2 = normed_two.astype(jnp.bfloat16)
    hidden = jnp.dot(normed2, w_up, preferred_element_type=jnp.float32) + up_bias
    active = jax.nn.gelu(hidden, approximate=False).astype(jnp.bfloat16)
    after = mid + jnp.dot(active, w_down, preferred_element_type=jnp.float32) + down_bias
    block_out = (visible * after).astype(jnp.bfloat16).reshape(block_shape)
    normed_three, unit_three, inverse_three = norm_forward(after, norm3_gain, norm3_bias)
    normed3 = normed_three.astype(jnp.bfloat16)
    target = jnp.dot(normed3, w_align, preferred_element_type=jnp.float32) + align_bias
    aligned = (
        (visible * target)
        .astype(jnp.bfloat16)
        .reshape(clip_count, frame_dev, slot_count, align_width)
    )
    back_align = (visible * cot_align.reshape(row_count, align_width).astype(jnp.float32)).astype(
        jnp.bfloat16
    )
    grad_align_bias = column_sum(back_align)
    grad_w_align = weight_grad(normed3, back_align)
    back_norm3, grad_norm3_gain, grad_norm3_bias = norm_backward(
        input_grad(back_align, w_align), unit_three, inverse_three, norm3_gain
    )
    back_after = visible * cot_block.reshape(row_count, width).astype(jnp.float32) + back_norm3
    back_down = back_after.astype(jnp.bfloat16)
    grad_down_bias = column_sum(back_down)
    grad_w_down = weight_grad(active, back_down)
    back_up = (input_grad(back_down, w_down) * gelu_slope(hidden)).astype(jnp.bfloat16)
    grad_up_bias = column_sum(back_up)
    grad_w_up = weight_grad(normed2, back_up)
    back_norm2, grad_norm2_gain, grad_norm2_bias = norm_backward(
        input_grad(back_up, w_up), unit_two, inverse_two, norm2_gain
    )
    back_mid = back_after + back_norm2
    back_out = back_mid.astype(jnp.bfloat16)
    grad_out_bias = column_sum(back_out)
    grad_w_out = weight_grad(attended, back_out)
    back_attended = input_grad(back_out, w_out).astype(jnp.bfloat16).reshape(heads_shape)
    scores = masked_scores(query_heads, key_heads, key_valid, scale)
    probs = jnp.exp(scores - top) / total
    probs_low = probs.astype(jnp.bfloat16)
    back_probs = jnp.einsum(
        "cqhd,ckhd->chqk", back_attended, value_heads, preferred_element_type=jnp.float32
    )
    spread = jnp.sum(probs * back_probs, axis=-1, keepdims=True)
    back_scores = (probs * (back_probs - spread)).astype(jnp.bfloat16)
    back_queries = (
        jnp.einsum("chqk,ckhd->cqhd", back_scores, key_heads, preferred_element_type=jnp.float32)
        * scale
    )
    back_queries = back_queries.astype(jnp.bfloat16).reshape(row_count, width)
    value_terms = jnp.einsum(
        "chqk,cqhd->ckhd", probs_low, back_attended, preferred_element_type=jnp.float32
    )
    key_terms = (
        jnp.einsum("chqk,cqhd->ckhd", back_scores, query_heads, preferred_element_type=jnp.float32)
        * scale
    )
    whole_shape = (clip_count, -1, slot_count, width)
    key_share, value_share = (
        lax.psum_scatter(
            key_terms.reshape(whole_shape).astype(jnp.bfloat16),
            "blk",
            scatter_dimension=1,
            tiled=True,
        ).astype(jnp.float32),
        lax.psum_scatter(
            value_terms.reshape(whole_shape).astype(jnp.bfloat16),
            "blk",
            scatter_dimension=1,
            tiled=True,
        ).astype(jnp.float32),
    )
    back_keys = key_share.astype(jnp.bfloat16).reshape(row_count, width)
    back_values = value_share.astype(jnp.bfloat16).reshape(row_count, width)
    grad_q_bias = column_sum(back_queries)
    grad_v_bias = column_sum(back_values)
    combined = jnp.concatenate([back_queries, back_keys, back_values], axis=1)
    grad_w_qkv = weight_grad(normed1, combined)
    back_norm1, grad_norm1_gain, grad_norm1_bias = norm_backward(
        input_grad(combined, w_qkv), unit_one, inverse_one, norm1_gain
    )
    grad_tokens = (back_mid + back_norm1).astype(jnp.bfloat16).reshape(block_shape)
    vector_total = lax.psum(
        (
            grad_norm1_gain,
            grad_norm1_bias,
            grad_q_bias,
            grad_v_bias,
            grad_out_bias,
            grad_norm2_gain,
            grad_norm2_bias,
            grad_up_bias,
            grad_down_bias,
            grad_norm3_gain,
            grad_norm3_bias,
            grad_align_bias,
        ),
        ("dp", "blk"),
    )
    row_part = (
        lax.psum_scatter(grad_w_qkv, "dp", scatter_dimension=0, tiled=True),
        lax.psum_scatter(grad_w_out, "dp", scatter_dimension=0, tiled=True),
        lax.psum_scatter(grad_w_up, "dp", scatter_dimension=0, tiled=True),
        lax.psum_scatter(grad_w_down, "dp", scatter_dimension=0, tiled=True),
        lax.psum_scatter(grad_w_align, "dp", scatter_dimension=0, tiled=True),
    )
    matrix_total = (
        lax.psum(row_part[0].astype(jnp.bfloat16), "blk").astype(jnp.float32),
        lax.psum(row_part[1].astype(jnp.bfloat16), "blk").astype(jnp.float32),
        lax.psum(row_part[2].astype(jnp.bfloat16), "blk").astype(jnp.float32),
        lax.psum(row_part[3].astype(jnp.bfloat16), "blk").astype(jnp.float32),
        lax.psum(row_part[4].astype(jnp.bfloat16), "blk").astype(jnp.float32),
    )
    return (
        block_out,
        aligned,
        grad_tokens,
        vector_total[0],
        vector_total[1],
        matrix_total[0],
        vector_total[2],
        vector_total[3],
        matrix_total[1],
        vector_total[4],
        vector_total[5],
        vector_total[6],
        matrix_total[2],
        vector_total[7],
        matrix_total[3],
        vector_total[8],
        vector_total[9],
        vector_total[10],
        matrix_total[4],
        vector_total[11],
    )


def local_kernels(
    tokens, frame_counts, slot_mask, norm1_gain, norm1_bias, w_qkv, q_bias, v_bias, w_out, out_bias, norm2_gain,
    norm2_bias, w_up, up_bias, w_down, down_bias, norm3_gain, norm3_bias, w_align, align_bias, cot_block, cot_align,
):
    clip_count, frame_dev, slot_count, width = tokens.shape
    align = w_align.shape[1]
    piece = frame_dev * slot_count
    rows = clip_count * piece
    vectors = [
        norm1_gain, norm1_bias, q_bias, v_bias, out_bias, norm2_gain, norm2_bias, down_bias, norm3_gain, norm3_bias,
        up_bias, align_bias,
    ]
    block_out, align_out, grad_tokens, vec, *shares = layer(
        slot_mask, frame_counts, vectors, tokens.reshape(clip_count, piece, width), cot_align.reshape(rows, align),
        cot_block.reshape(rows, width), w_align, w_down, w_up, w_out, w_qkv,
    )
    matrices, totals, (block_out, align_out, grad_tokens) = finish(
        shares, vec, (block_out, align_out, grad_tokens), [vector.shape[0] for vector in vectors]
    )
    (
        grad_norm1_gain, grad_norm1_bias, grad_q_bias, grad_v_bias, grad_out_bias, grad_norm2_gain, grad_norm2_bias,
        grad_down_bias, grad_norm3_gain, grad_norm3_bias, grad_up_bias, grad_align_bias,
    ) = totals
    return (
        block_out.reshape(tokens.shape),
        align_out.reshape(cot_align.shape),
        grad_tokens.reshape(tokens.shape),
        grad_norm1_gain,
        grad_norm1_bias,
        matrices[0],
        grad_q_bias,
        grad_v_bias,
        matrices[1],
        grad_out_bias,
        grad_norm2_gain,
        grad_norm2_bias,
        matrices[2],
        grad_up_bias,
        matrices[3],
        grad_down_bias,
        grad_norm3_gain,
        grad_norm3_bias,
        matrices[4],
        grad_align_bias,
    )


def solution(mesh):
    in_specs = (
        P("dp", "blk", None, None),
        P("dp"),
        P("dp", None, None),
        P(),
        P(),
        P(),
        P(),
        P(),
        P(),
        P(),
        P(),
        P(),
        P(),
        P(),
        P(),
        P(),
        P(),
        P(),
        P(),
        P(),
        P("dp", "blk", None, None),
        P("dp", "blk", None, None),
    )
    out_specs = (
        P("dp", "blk", None, None),
        P("dp", "blk", None, None),
        P("dp", "blk", None, None),
        P(),
        P(),
        P("dp", None),
        P(),
        P(),
        P("dp", None),
        P(),
        P(),
        P(),
        P("dp", None),
        P(),
        P("dp", None),
        P(),
        P(),
        P(),
        P("dp", None),
        P(),
    )
    sizes = (mesh.shape["dp"], mesh.shape["blk"])
    run = local_kernels if sizes == GRID else local
    return jax.shard_map(run, mesh=mesh, in_specs=in_specs, out_specs=out_specs, check_vma=False)
```

```python
import math

import jax
import jax.numpy as jnp
from jax import lax
from jax.experimental import pallas as pl
from jax.experimental.pallas import tpu as pltpu
from jax.sharding import PartitionSpec as P

HEADS = 12


EPSILON = 1e-06
SQRT_HALF = 0.7071067811865476
INV_ROOT_TAU = 0.3989422804014327
MESH = pl.DeviceIdType.MESH
GRID = (8, 4)


NT = (((1,), (1,)), ((), ()))
TN = (((0,), (0,)), ((), ()))
CHUNKS = 4


def dot(left, right, dims=(((1,), (0,)), ((), ()))):
    return lax.dot_general(left, right, dims, preferred_element_type=jnp.float32)


def remote_copy(src, dst, send, recv, device):
    return pltpu.make_async_remote_copy(
        src_ref=src, dst_ref=dst, send_sem=send, recv_sem=recv, device_id=device, device_id_type=MESH
    )


N1_GAIN, N1_BIAS, Q_BIAS, V_BIAS, OUT_BIAS, N2_GAIN, N2_BIAS, DOWN_BIAS, N3_GAIN, N3_BIAS, UP_BIAS, ALIGN_BIAS = (
    0, 1, 2, 3, 4, 5, 6, 7, 8, 9, 10, 14,
)
PACK_ROWS = 16


def fill_pack(pack, rows, refs):
    width = pack.shape[1]
    for row, ref in zip(rows, refs):
        for start in range(0, ref.shape[0], width):
            size = min(width, ref.shape[0] - start)
            line = row + start // width
            pack[line : line + 1, 0:size] = ref[pl.ds(start, size)].reshape(1, size)


def norm_rows(values):
    center = values - jnp.mean(values, axis=-1, keepdims=True)
    inverse = lax.rsqrt(jnp.mean(center * center, axis=-1, keepdims=True) + EPSILON)
    return center * inverse, inverse


JOBS = (
    (4, 0, 96, 0, 1024, 2048),
    (3, 0, 96, 0, 768, 0),
    (3, 96, 96, 0, 768, 768),
    (3, 192, 96, 0, 768, 1536),
    (3, 288, 96, 0, 768, 2304),
    (2, 0, 96, 0, 768, 0),
    (2, 0, 96, 768, 768, 768),
    (2, 0, 96, 1536, 768, 1536),
    (2, 0, 96, 2304, 768, 2304),
    (1, 0, 96, 0, 768, 0),
    (0, 0, 96, 0, 384, 768),
    (0, 0, 96, 384, 384, 1152),
    (0, 0, 96, 768, 384, 1536),
)
COUNT = len(JOBS)
PLAIN = 10
KEY_BLOCK = 256
NORM_ROWS = 192
PLAN = (
    (0, "far"), (0, 0), "e3", "norm3", (2, "far"), (2, 0), (0, "own"), (0, 1), (2, "own"), "feed", (2, 1), "e2",
    "norm2", "back_att", (0, 2), (1, "far"), (1, 0), (3, "own"), (2, 2), (3, "far"), (3, 0), (4, "own"), (1, "own"),
    (4, "far"), (4, 0), (1, 1), (5, "far"), (5, 0), (6, "far"), (6, 0), (2, 3), (3, 1), (5, "own"), (6, "own"),
    "settle0", "pair", (0, 3), (1, 2), "pair", (4, 1), "pair", "settle1", (1, 3), (2, 4), (3, 2), "pair", (5, 1),
    (4, 2), (9, "far"), (9, 0), (0, 4), "pair", (3, 3), (2, 5), "pair", (5, 2), "settle2", (1, 4), (9, "own"),
    (4, 3), "pair", (0, 5), (9, 1), (3, 4), (5, 3), "pair", (1, 5), "pair", "dx0", (4, 4), (6, 1), (9, 2), (3, 5),
    (10, "far"), (10, 0), (8, "own"), (8, "far"), (8, 0), "dx1", (5, 4), (10, "own"), (4, 5), (11, "far"), (11, 0),
    (10, 1), (7, "far"), (7, 0), "fwd0", (7, "own"), (5, 5), (10, 2), (0, 6), (7, 1), (11, "own"), (2, 6), (9, 3),
    (12, "far"), (12, 0), (11, 1), "fwd1", (10, 3), (8, 1), "dx2", "dx3", (12, "own"), (9, 4), (11, 2), "sums",
    (10, 4), (7, 2), "vec0", (3, 6), (12, 1), (1, 6), (8, 2), (11, 3), (4, 6), (6, 2), (9, 5), (12, 2), "vec1",
    (11, 4), (7, 3), (10, 5), (7, 4), (11, 5), (5, 6), "vec2", (8, 3), (6, 3), (9, 6), (8, 4), (7, 5), (12, 3),
    (10, 6), (7, 6), (6, 4), (8, 5), (12, 4), (6, 5), "vec3", (8, 6), (11, 6), (12, 5), "norm1", "vec4", "vec5",
    (6, 6), (12, 6),
)


def add_into(target, first, second):
    lead = target.shape[:-2]

    def body(k, _):
        if len(lead) == 0:
            at = (pl.ds(pl.multiple_of(k * 16, 16), 16), slice(None))
        elif len(lead) == 1:
            at = (k,)
        else:
            at = (k // lead[1], lax.rem(k, lead[1]))
        target[at] = first[at] + second[at]
        return 0

    lax.fori_loop(0, math.prod(lead) if lead else target.shape[0] // 16, body, 0)


VIS, KEY, INV2, INV3, STATS = 0, 1, 2, 3, 8


def layer_kernel(*refs):
    slot_mask, counts, vectors_h, refs = refs[0], refs[1], refs[2:14], refs[14:]
    tok_h, cot_a_h, cot_b_h, w_align, w_down, w_up, w_out, w_qkv = refs[:8]
    block_out, align_out, grad_tokens, vec_out = refs[8:12]
    outs = refs[12:17]
    rest = refs[17:]
    own, got0, got1, got2 = (rest[i * COUNT : (i + 1) * COUNT] for i in range(4))
    rest = rest[4 * COUNT :]
    gotz, gotq = rest[:PLAIN], rest[PLAIN:COUNT]
    rest = rest[COUNT:]
    vec_got, vectors = rest[0], rest[1:13]
    (
        pack, side_v,
        align_v, down_v, up_v, out_v, low_v, tok, xall, n1, qkv, own_att, att, lse_rows, spread_rows,
        mid_v, e_v, normed, ring, slope, ld, l2, l3, la, unit2, unit3, cot_a, cot_b,
        grad_att, n1s,
        load_sem, send0, recv0, send1, recv1, send2, recv2, sendz, recvz, sendq, recvq, out_sem, outq_sem, vsend, vrecv,
        tok_send, tok_recv, att_send, att_recv, in_send, in_recv,
        pair_send, pair_recv, end_send, end_recv, out_send, out_recv, put_sem, vector_sem,
    ) = rest[13:]

    dp = lax.axis_index("dp")
    z = lax.axis_index("blk")
    core = lax.rem(dp, 2)
    x = lax.rem(dp // 2, 2)
    y = dp // 4
    clip, side = z // 2, lax.rem(z, 2)
    to_core = (dp + 1 - 2 * core, z)
    to_x = (dp + 2 - 4 * x, z)
    to_y = (dp + 4 - 8 * y, z)
    partner = z + 1 - 2 * side
    to_z1 = (dp, partner)
    to_z2 = (dp, lax.rem(z + 2, 4))
    to_z3 = (dp, 3 - z)
    is_mid = (z == 1) | (z == 2)
    is_end = (z == 0) | (z == 3)
    near, far = 3 - z, lax.rem(z + 2, 4)
    other_mid = 2 - clip
    piece, width = tok.shape
    rows, half, wide = 2 * piece, width // 2, up_v.shape[1]
    low = jnp.bfloat16
    low_d, low_o = n1.at[pl.ds(0, rows)], n1.at[pl.ds(rows, rows)]
    in_src = att
    from_end = [normed.at[pl.ds(k * piece, piece)] for k in range(2)]
    from_pair, total_in = (cot_b.at[pl.ds(k * piece, piece)] for k in range(2))

    def grad_at(m):
        return down_v.at[pl.ds((2 if m == 0 else 3) * width, width), pl.ds(half if m != 1 else 0, half)]

    def e_at(slot):
        return align_v.at[pl.ds(pl.multiple_of(slot * piece, piece), piece), pl.ds(0, width)]

    def slot_rows(slot):
        return pl.ds(pl.multiple_of(slot * piece, piece), piece)

    loads = {"mine": (tok_h.at[clip], xall.at[z]), "tok": (tok_h.at[1 - clip], tok)}
    for m in range(3):
        column = pl.multiple_of(m * width + side * half, 128)
        loads["low%d" % m] = (w_qkv.at[:, pl.ds(column, half)], low_v.at[m])
    loads["out"] = (w_out, out_v)
    loads["up"] = (w_up, up_v)
    loads["down"] = (w_down, down_v)
    loads["cot_a"] = (cot_a_h, cot_a)
    loads["align"] = (w_align, align_v)
    loads["cot_b"] = (cot_b_h, cot_b)
    loads = {
        name: pltpu.make_async_copy(src, dst, load_sem.at[k]) for k, (name, (src, dst)) in enumerate(loads.items())
    }
    early = ("mine", "tok", "low0", "low1", "low2")
    for name in early:
        loads[name].start()
    small = [pltpu.make_async_copy(src, dst, vector_sem.at[k]) for k, (src, dst) in enumerate(zip(vectors_h, vectors))]
    for copy in small:
        copy.start()

    def ready(*names):
        for name in names:
            loads[name].wait()

    barrier = pltpu.get_barrier_semaphore()
    for device in (to_core, to_x, to_y, to_z1, to_z2, to_z3):
        pl.semaphore_signal(barrier, inc=1, device_id=device, device_id_type=MESH)
    pl.semaphore_wait(barrier, 6)
    step = piece // CHUNKS

    def tok_copy(kind, slot, k):
        at = pl.ds(k * step, step)
        source = xall.at[slot, at] if kind >= 2 else tok_h.at[1 - clip if kind == 0 else clip, at]
        device = (dp, other_mid) if kind == 0 else to_z1
        return remote_copy(source, xall.at[slot, at], tok_send.at[kind, k], tok_recv.at[slot, k], device)

    for k in range(CHUNKS):
        tok_copy(0, z, k).start()
    for k in range(CHUNKS):
        tok_copy(1, z, k).start()
    for copy in small:
        copy.wait()
    fill_pack(pack, VECTORS, vectors)
    vec_out[...] = jnp.zeros_like(vec_out)
    ready("mine", "tok")
    e_v[0:128, :] = jnp.zeros((128, width), jnp.float32)
    for c in range(2):
        e_v[c : c + 1, :] = jnp.concatenate(
            [
                jnp.where((slot_mask[c, f : f + 1, :] > 0) & (f < counts[c]), 1.0, 0.0)
                for f in range(slot_mask.shape[1])
            ],
            axis=1,
        )
    side_v[...] = e_v[0:128, :].T
    seen = [side_v[slot_rows(z), c : c + 1] for c in range(2)]
    side_v[:, KEY : KEY + 1] = jnp.where(jnp.where(clip == 0, side_v[:, 0:1], side_v[:, 1:2]) > 0.0, 0.0, -1e30)
    for c in range(2):
        side_v[pl.ds(c * piece, piece), VIS : VIS + 1] = seen[c]
    row_bias = jnp.where(jnp.where(clip == 0, e_v[0:1, :], e_v[1:2, :]) > 0.0, 0.0, -1e30)
    columns = pl.ds(pl.multiple_of(side * half, 128), half)
    ready("low0", "low1", "low2")

    def project(slot):
        where = slot_rows(slot)

        def body(k, _):
            one, _ = norm_rows(xall[slot, pl.ds(pl.multiple_of(k * 96, 96), 96), :].astype(jnp.float32))
            at = pl.ds(pl.multiple_of(slot * piece + k * 96, 96), 96)
            n1[at, :] = (one * pack[N1_GAIN : N1_GAIN + 1, :] + pack[N1_BIAS : N1_BIAS + 1, :]).astype(low)
            return 0

        lax.fori_loop(0, piece // 96, body, 0)
        left = n1[where, :]
        qkv[0, where, :] = (dot(left, low_v[0]) + pack[Q_BIAS : Q_BIAS + 1, columns]).astype(low) * low(0.125)
        qkv[1, where, :] = dot(left, low_v[1]).astype(low)
        qkv[2, where, :] = (dot(left, low_v[2]) + pack[V_BIAS : V_BIAS + 1, columns]).astype(low)

    last = 3 * (1 - clip)
    third = 2 - clip
    def slot_of(number):
        return jnp.where(number == 0, z, jnp.where(number == 1, partner, jnp.where(number == 2, third, last)))

    def tokens_of(number, _):
        slot = slot_of(number)

        @pl.when(number == 1)
        def _():
            for name in loads:
                if name not in early:
                    loads[name].start()

        @pl.when(is_mid & (number == 1))
        def _():
            for which, source in enumerate((near, far)):
                for k in range(CHUNKS):
                    tok_copy(1, source, k).wait_recv()
                    tok_copy(2 + which, source, k).start()
            for k in range(CHUNKS):
                tok_copy(1, partner, k).wait_recv()

        @pl.when(is_end & (number > 0))
        def _():
            for k in range(CHUNKS):
                tok_copy(1, slot, k).wait_recv()

        project(slot)
        return 0

    lane = lax.broadcasted_iota(jnp.int32, (1, 128), 1)
    low_lane = lane < 64

    def att_copy(slot, t):
        return remote_copy(
            own_att.at[t, slot_rows(slot)], att.at[clip, side, t], att_send.at[slot, t], att_recv.at[z, t], (dp, slot)
        )

    def head(queries, a, keys, bias):
        mine = low_lane if a == 0 else jnp.logical_not(low_lane)
        return dot(jnp.where(mine, queries, jnp.zeros_like(queries)), keys, NT) + bias

    def attend_whole(slot):
        where = slot_rows(slot)
        stats = jnp.zeros((piece, 128), jnp.float32)
        for t in range(half // 128):
            at = pl.ds(t * 128, 128)
            parts = []
            for a in range(2):
                scores = head(qkv[0, where, at], a, qkv[1, :, at], row_bias)
                top = jnp.max(scores, axis=-1, keepdims=True)
                expo = jnp.exp(scores - top)
                denominator = jnp.sum(expo, axis=-1, keepdims=True)
                parts.append(dot(expo.astype(low), qkv[2, :, at]) * (1.0 / denominator))
                stats = jnp.where(lane == STATS + 2 * t + a, top + jnp.log(denominator), stats)
            own_att[t, where, :] = jnp.where(low_lane, parts[0], parts[1]).astype(low)

            @pl.when(slot != z)
            def _():
                att_copy(slot, t).start()

        side_v[where, STATS : STATS + 8] = stats[:, STATS : STATS + 8]

    lax.fori_loop(0, 3, tokens_of, 0)
    tokens_of(3, 0)

    def attend(number, _):
        attend_whole(slot_of(3 - number))

        return 0

    lax.fori_loop(0, 4, attend, 0)

    att[clip, side] = own_att[:, slot_rows(z), :]

    def tiles(count, size, body):
        def one_tile(t, _):
            body(t, pl.ds(pl.multiple_of(t * size, size), size))
            return 0

        lax.fori_loop(0, count, one_tile, 0)

    def chunks(body, carry, size=48):
        def one_chunk(k, carry):
            return body(pl.ds(pl.multiple_of(k * size, size), size), k, carry)

        return lax.fori_loop(0, rows // size, one_chunk, carry)

    def put_vector(row, start, value):
        at = 0
        while at < value.shape[1]:
            line, column = row + (start + at) // width, (start + at) % width
            take = min(value.shape[1] - at, width - column)
            vec_out[line : line + 1, column : column + take] = value[:, at : at + take]
            at += take

    def total(value):
        return jnp.sum(value.astype(jnp.float32), axis=0, keepdims=True)

    zero_row = jnp.zeros((1, width), jnp.float32)
    ready("cot_a")

    def mask(at, k, carry):
        value = (side_v[at, VIS : VIS + 1] * cot_a[at, :].astype(jnp.float32)).astype(low)
        cot_a[at, :] = value
        return carry + total(value)

    put_vector(ALIGN_BIAS, 0, chunks(mask, jnp.zeros((1, cot_a.shape[1]), jnp.float32)))
    lse_rows[...] = side_v[...].T[STATS : STATS + 8]

    def shares_of(source, target, count):
        for c in range(0, source.shape[1], 128):
            flipped = source[:, pl.ds(c, 128)].T
            at = 0
            while at < 128:
                share, inside = (c + at) // count, (c + at) % count
                take = min(128 - at, count - inside)
                rel = jnp.where(core == share % 2, 1, 0)
                target[rel, share // 2, pl.ds(inside, take), :] = flipped[at : at + take]
                at += take

    shares_of(n1, n1s, width // 8)

    def settle_att(number, _):
        slot = lax.rem(z + number, 4)
        for t in range(half // 128):
            att_copy(slot, t).wait_send()
            remote_copy(
                own_att.at[t, slot_rows(slot)], att.at[slot // 2, lax.rem(slot, 2), t],
                att_send.at[slot, t], att_recv.at[slot, t], (dp, slot),
            ).wait_recv()
        return 0

    lax.fori_loop(1, 4, settle_att, 0)
    for k in range(CHUNKS):
        tok_copy(0, z, k).wait_send()
        tok_copy(1, z, k).wait_send()

    @pl.when(is_mid)
    def _():
        for k in range(CHUNKS):
            for which, slot in enumerate((near, far)):
                tok_copy(2 + which, slot, k).wait_send()

    for c in range(2):
        for h in range(2):
            for t in range(half // 128):
                normed[pl.ds(c * piece, piece), pl.ds(h * half + t * 128, 128)] = att[c, h, t]
    shares_of(normed, la, width // 8)
    ready("out")

    def mix(t, at):
        mixed = dot(normed[...], out_v[:, at]) + pack[OUT_BIAS : OUT_BIAS + 1, at]
        for c in range(2):
            mixed_c = mixed[c * piece : (c + 1) * piece]
            source = jnp.where(clip == c, xall[z, :, at], tok[:, at])
            mid_v[pl.ds(c * piece, piece), at] = source.astype(jnp.float32) + mixed_c

    tiles(3, 256, mix)

    def norm(gain, bias, unit, inv):
        def body(at, k, _):
            one, inverse = norm_rows(mid_v[at, :])
            unit[at, :] = one.astype(low)
            side_v[at, inv : inv + 1] = inverse
            normed[at, :] = (one * pack[gain : gain + 1, :] + pack[bias : bias + 1, :]).astype(low)
            return 0

        chunks(body, 0, NORM_ROWS)

    norm(N2_GAIN, N2_BIAS, unit2, INV2)
    shares_of(normed, l2, width // 8)
    ready("up")

    def up(t, at):
        e_v[...] = dot(normed[...], up_v[:, at]) + pack[pl.ds(UP_BIAS + t, 1), :]

        def gelu(here, k, _):
            values = e_v[here, :]
            cdf = 0.5 * (1.0 + lax.erf(values * SQRT_HALF))
            ring[k, :, at] = (values * cdf).astype(low)
            slope[here, at] = (cdf + values * jnp.exp(-0.5 * values * values) * INV_ROOT_TAU).astype(low)
            return 0

        chunks(gelu, 0)
        for c in range(0, width, 128):
            rel = core if c < half else 1 - core
            columns_at = pl.ds(pl.multiple_of(t * width + c, 128), 128)
            ld[1 - rel, t, pl.ds(c % half, 128), :] = ring[:, :, columns_at].reshape(rows, 128).T

    tiles(4, width, up)
    ready("down")

    def down(t, at):
        mid_v[:, at] = (
            mid_v[:, at] + dot(ring[...].reshape(rows, wide), down_v[:, at]) + pack[DOWN_BIAS : DOWN_BIAS + 1, at]
        )

    tiles(3, 256, down)

    def staged(j, target):
        return pltpu.make_async_copy(own[j], target, put_sem.at[j])

    def put_block(at, k, _):
        own[1][k // 4, lax.rem(k, 4)] = (side_v[at, VIS : VIS + 1] * mid_v[at, :]).astype(low)
        return 0

    chunks(put_block, 0)
    staged(1, block_out).start()
    norm(N3_GAIN, N3_BIAS, unit3, INV3)
    shares_of(normed, l3, width // 8)
    ready("align", "cot_b")

    def align_tile(t, at):
        bias = pack[pl.ds(ALIGN_BIAS + t // 3, 1), pl.ds(pl.multiple_of(lax.rem(t, 3) * 256, 256), 256)]
        value = dot(normed[...], align_v[:, at]) + bias
        value = (side_v[pl.ds(0, rows), VIS : VIS + 1] * value).astype(low)
        for k in range(8):
            own[0][k // 4, k % 4, :, at] = value[k * 48 : (k + 1) * 48]

    tiles(4, 256, align_tile)
    staged(0, align_out).start()

    def buffer_of(j):
        return ring.at[:, :, pl.ds(JOBS[j][5], JOBS[j][4])]

    def copies0(j):
        for h in range(2):
            yield remote_copy(
                buffer_of(j).at[pl.ds(4 * h, 4)], got0[j].at[h], send0.at[j, h], recv0.at[j, h], to_core
            )

    def copies1(j):
        yield remote_copy(
            own[j].at[0, pl.ds(2 * (1 - x), 2)], got1[j].at[0], send1.at[j, 0], recv1.at[j, 0], to_x
        )
        yield remote_copy(
            own[j].at[1, pl.ds(2 * (1 - y), 2)], got1[j].at[1], send1.at[j, 1], recv1.at[j, 1], to_y
        )

    def copies2(j):
        yield remote_copy(own[j].at[0, 2 * x + 1 - y], got2[j].at[0], send2.at[j, 0], recv2.at[j, 0], to_y)
        yield remote_copy(own[j].at[1, 2 * y + 1 - x], got2[j].at[1], send2.at[j, 1], recv2.at[j, 1], to_x)

    def shares(j):
        return (own[j].at[0, 2 * x + y], own[j].at[1, 2 * y + x])

    def copiesz(j, slot, device):
        for h, share in enumerate(shares(j)):
            yield remote_copy(share, gotz[j].at[slot, h], sendz.at[j, slot, h], recvz.at[j, slot, h], device)

    def copiesq(j, source, slot, device):
        got, m = gotq[j - PLAIN], j - PLAIN
        for h, share in enumerate(shares(j)):
            yield remote_copy(
                share if source is None else got.at[source, h],
                got.at[slot, h], sendq.at[m, slot, h], recvq.at[m, slot, h], device,
            )

    def result(j, h, source):
        matrix, row, count, column, size, _ = JOBS[j]
        return pltpu.make_async_copy(
            source, outs[matrix].at[pl.ds(row + h * count // 2, count // 2), pl.ds(column, size)], out_sem.at[j, h]
        )

    def result_q(j, h, which, source):
        count, m = JOBS[j][2] // 2, j - PLAIN
        at = side if which == 0 else 1 - side
        column = pl.multiple_of(m * width + at * half, 128)
        return pltpu.make_async_copy(
            source, outs[0].at[pl.ds(h * count, count), pl.ds(column, half)], outq_sem.at[m, which, h]
        )

    def stage(j, number):
        if number == 0:
            for copy in copies0(j):
                copy.start()
        if number == 1:
            for h, (arrived, onward) in enumerate(zip(copies0(j), copies1(j))):
                arrived.wait()
                add_into(own[j].at[h], own[j].at[h], got0[j].at[h])
                onward.start()
        if number == 2:
            for h, (arrived, onward) in enumerate(zip(copies1(j), copies2(j))):
                arrived.wait()
                kept = own[j].at[h, pl.ds(2 * (y if h else x), 2)]
                add_into(kept, kept, got1[j].at[h])
                onward.start()
        if number == 3:
            onward = list(copiesq(j, None, 0, to_z1) if j >= PLAIN else copiesz(j, 0, to_z1))
            for h, (arrived, share) in enumerate(zip(copies2(j), shares(j))):
                arrived.wait()
                add_into(share, share, got2[j].at[h])
                pl.when(is_end)(onward[h].start)

        if number >= 4 and j >= PLAIN:
            stage_q(j, number)
            return
        if number == 4:

            @pl.when(is_mid)
            def _():
                for h, (arrived, onward) in enumerate(zip(copiesz(j, 0, to_z1), copiesz(j, 1, to_z3))):
                    arrived.wait_recv()
                    add_into(shares(j)[h], shares(j)[h], gotz[j].at[0, h])
                    onward.start()

            @pl.when(is_end)
            def _():
                for copy in copiesz(j, 0, to_z1):
                    copy.wait_send()

        if number == 5:

            @pl.when(is_mid)
            def _():
                for h, (arrived, onward) in enumerate(zip(copiesz(j, 1, to_z3), copiesz(j, 0, to_z1))):
                    arrived.wait()
                    add_into(shares(j)[h], shares(j)[h], gotz[j].at[1, h])
                    onward.start()
                    result(j, h, shares(j)[h]).start()

        if number == 6:

            @pl.when(is_mid)
            def _():
                for copy in copiesz(j, 0, to_z1):
                    copy.wait_send()

            @pl.when(is_end)
            def _():
                for copy in copiesz(j, 0, to_z1):
                    copy.wait_recv()
                for h in range(2):
                    result(j, h, gotz[j].at[0, h]).start()

    def stage_q(j, number):
        got = gotq[j - PLAIN]
        if number == 4:

            @pl.when(is_mid)
            def _():
                for copy in copiesq(j, None, 1, to_z3):
                    copy.start()
                for copy in copiesq(j, None, 0, to_z1):
                    copy.wait_recv()
                for copy in copiesq(j, 0, 2, to_z3):
                    copy.start()

            @pl.when(is_end)
            def _():
                for copy in copiesq(j, None, 0, to_z1):
                    copy.wait_send()

        if number == 5:

            @pl.when(is_mid)
            def _():
                for copy in copiesq(j, None, 1, to_z3):
                    copy.wait()
                for copy in copiesq(j, 0, 2, to_z3):
                    copy.wait()
                for h, share in enumerate(shares(j)):
                    add_into(share, share, got.at[2, h])
                    add_into(got.at[0, h], got.at[0, h], got.at[1, h])
                for copy in copiesq(j, None, 1, to_z1):
                    copy.start()
                for copy in copiesq(j, 0, 0, to_z1):
                    copy.start()
                for h, share in enumerate(shares(j)):
                    result_q(j, h, 0, share).start()
                    result_q(j, h, 1, got.at[0, h]).start()

        if number == 6:

            @pl.when(is_mid)
            def _():
                for copy in copiesq(j, None, 1, to_z1):
                    copy.wait_send()
                for copy in copiesq(j, 0, 0, to_z1):
                    copy.wait_send()

            @pl.when(is_end)
            def _():
                for copy in copiesq(j, None, 1, to_z1):
                    copy.wait_recv()
                for copy in copiesq(j, 0, 0, to_z1):
                    copy.wait_recv()
                for h in range(2):
                    result_q(j, h, 0, got.at[0, h]).start()
                    result_q(j, h, 1, got.at[1, h]).start()

    def results_done():
        for j in range(COUNT):
            for h in range(2):
                if j < PLAIN:
                    result(j, h, gotz[j].at[0, h]).wait()
                else:
                    for which in range(2):
                        result_q(j, h, which, gotq[j - PLAIN].at[0, h]).wait()

    def gradient(j, mine, left, right):
        count, size = JOBS[j][2], JOBS[j][4]
        target = own[j] if mine else buffer_of(j)
        for c in range(0, size, min(size, 384 if size % 384 == 0 else 512)):
            at = pl.ds(c, min(size, 384 if size % 384 == 0 else 512))
            value = dot(left, right(at)).astype(low)
            for chip in range(4):
                cy, cx = chip // 2, chip % 2
                for h in range(2):
                    k = 2 * cx + cy if h == 0 else 2 * cy + cx
                    start = chip * count + h * count // 2
                    part = value[start : start + count // 2]
                    if mine:
                        target[h, k, :, at] = part
                    else:
                        target[4 * h + k, :, at] = part

    def job(j, mine):
        matrix, row, count, column, size, _ = JOBS[j]
        lhs, rhs = ((n1s, None), (la, low_o), (l2, slope), (ld, low_d), (l3, cot_a))[matrix]
        left = lhs[1 if mine else 0, :, pl.ds(row, count), :].reshape(4 * count, lhs.shape[3])
        if matrix == 0:
            gradient(j, mine, left, lambda at: grad_at(j - PLAIN)[...])
        else:
            gradient(j, mine, left, lambda at: rhs[:, pl.ds(column + at.start, at.size)])

    def norm_back(e, one, inverse, gain):
        scaled = e * gain
        return inverse * (
            scaled
            - jnp.mean(scaled, axis=-1, keepdims=True)
            - one * jnp.mean(scaled * one, axis=-1, keepdims=True)
        )

    def norm_pass(unit, inv, gain_row, base, low_target, sums):
        def body(at, k, carry):
            e = e_v[at, :]
            one = unit[at, :].astype(jnp.float32)
            value = base(at) + norm_back(e, one, side_v[at, inv : inv + 1], pack[gain_row : gain_row + 1, :])
            mid_v[at, :] = value
            rounded = value.astype(low)
            low_target[at, :] = rounded
            return (carry[0] + total(e * one), carry[1] + total(e), carry[2] + total(rounded))

        for row, value in zip(sums, chunks(body, (zero_row,) * 3, NORM_ROWS)):
            put_vector(row, 0, value)

    def e3():
        def body(t, at):
            e_v[:, at] = dot(cot_a[...], align_v[at, :], NT)

        tiles(3, 256, body)

    def norm3():
        norm_pass(
            unit3, INV3, N3_GAIN, lambda at: side_v[at, VIS : VIS + 1] * cot_b[at, :].astype(jnp.float32), low_d,
            (N3_GAIN, N3_BIAS, DOWN_BIAS),
        )

    def feed():
        def body(t, at):
            value = (dot(low_d[...], down_v[at, :], NT) * slope[:, at].astype(jnp.float32)).astype(low)
            slope[:, at] = value
            vec_out[pl.ds(UP_BIAS + t, 1), :] = total(value)

        tiles(4, width, body)

    def e2():
        def body(t, at):
            e_v[:, at] = dot(slope[...], up_v[at, :], NT)

        tiles(3, 256, body)

    def norm2():
        norm_pass(unit2, INV2, N2_GAIN, lambda at: mid_v[at, :], low_o, (N2_GAIN, N2_BIAS, OUT_BIAS))

    def in_copy(slot, t):
        return remote_copy(
            in_src.at[slot // 2, lax.rem(slot, 2), t], grad_att.at[t, z],
            in_send.at[slot, t], in_recv.at[z, t], (dp, slot),
        )

    def back_att():
        for h in range(2):
            value = dot(low_o[...], out_v[pl.ds(h * half, half), :], NT).astype(low)
            for c in range(2):
                for t in range(half // 128):
                    in_src[c, h, t] = value[c * piece : (c + 1) * piece, t * 128 : (t + 1) * 128]
        for t in range(half // 128):

            def start(number, _):
                in_copy(lax.rem(z + number, 4), t).start()
                return 0

            lax.fori_loop(1, 4, start, 0)
        for t in range(half // 128):
            grad_att[t, z] = in_src[clip, side, t]

    def settle(t):
        def body(number, _):
            slot = lax.rem(z + number, 4)
            in_copy(slot, t).wait_send()
            remote_copy(
                in_src.at[0, 0, t], grad_att.at[t, slot], in_send.at[slot, t], in_recv.at[slot, t], (dp, slot)
            ).wait_recv()
            return 0

        lax.fori_loop(1, 4, body, 0)

        def spread(slot, _):
            where = slot_rows(slot)
            stats = jnp.zeros((piece, 128), jnp.float32)
            product = grad_att[t, slot].astype(jnp.float32) * own_att[t, where, :].astype(jnp.float32)
            for a in range(2):
                mine = low_lane if a == 0 else jnp.logical_not(low_lane)
                value = jnp.sum(jnp.where(mine, product, 0.0), axis=-1, keepdims=True)
                stats = jnp.where(lane == STATS + a, value, stats)
            side_v[where, STATS : STATS + 2] = stats[:, STATS : STATS + 2]
            return 0

        lax.fori_loop(0, 4, spread, 0)
        spread_rows[2 * t : 2 * t + 2, :] = side_v[...].T[STATS : STATS + 2]

    def pair(number):
        t, b = number // 3, lax.rem(number, 3)
        at = pl.ds(pl.multiple_of(t * 128, 128), 128)
        queries = qkv[0, :, at]
        grads = grad_att[t].reshape(4 * piece, 128)
        keys_at = pl.ds(pl.multiple_of(b * KEY_BLOCK, KEY_BLOCK), KEY_BLOCK)
        keys = qkv[1, keys_at, at]
        values = qkv[2, keys_at, at]
        grad_k = jnp.zeros((KEY_BLOCK, 128), jnp.float32)
        grad_v = jnp.zeros((KEY_BLOCK, 128), jnp.float32)
        held_q = (e_v.at[:, pl.ds(0, 128)], e_v.at[:, pl.ds(128, 128)])
        grad_queries = jnp.where(b == 0, 0.0, jnp.concatenate([ref[...] for ref in held_q], axis=0))
        for a in range(2):
            mine = low_lane if a == 0 else jnp.logical_not(low_lane)
            zero = jnp.zeros((), low)
            q_mine = jnp.where(mine, queries, zero)
            g_mine = jnp.where(mine, grads, zero)
            k_mine = jnp.where(mine, keys, zero)
            row = pl.ds(2 * t + a, 1)
            scores = dot(keys, q_mine, NT) + side_v[keys_at, KEY : KEY + 1]
            probs = jnp.exp(scores - lse_rows[row, :])
            back = (probs * (dot(values, g_mine, NT) - spread_rows[row, :])).astype(low)
            grad_v = grad_v + dot(probs.astype(low), g_mine)
            grad_k = grad_k + dot(back, q_mine)
            grad_queries = grad_queries + dot(back, k_mine, TN)
        grad_at(1)[keys_at, at] = grad_k.astype(low)
        grad_at(2)[keys_at, at] = grad_v.astype(low)
        for k, ref in enumerate(held_q):
            ref[...] = grad_queries[k * rows : (k + 1) * rows]

        @pl.when(b == 2)
        def _():
            for k, ref in enumerate(held_q):
                grad_at(0)[pl.ds(k * rows, rows), at] = (ref[...] * 0.125).astype(low)

    def pair_copy():
        return remote_copy(e_at(partner), from_pair, pair_send, pair_recv, to_z1)

    def end_copy(which, slot):
        return remote_copy(e_at(slot), from_end[which], end_send.at[which], end_recv.at[which], to_z1)

    def out_copy(which, slot):
        return remote_copy(e_at(slot), total_in, out_send.at[which], out_recv, (dp, slot))

    targets = (3 - 3 * clip, 2 - clip)
    mine_rows = slot_rows(clip)

    def dx(number):
        slot = (targets + (partner, z))[number]
        where = slot_rows(slot)
        value = sum(dot(grad_at(m)[where, :], low_v[m], NT) for m in range(3))
        e_at(slot)[...] = value.astype(low)
        if number == 3:
            e_v[mine_rows, :] = value
        if number < 2:

            @pl.when(is_end)
            def _():
                end_copy(number, slot).start()

        if number == 2:
            pair_copy().start()
        one, _ = norm_rows(xall[slot].astype(jnp.float32))
        for row, term in ((N1_GAIN, total(value * one)), (N1_BIAS, total(value))):
            vec_out[row : row + 1, :] = vec_out[row : row + 1, :] + term

    def sums():
        spot = lax.broadcasted_iota(jnp.int32, (1, width), 1)
        for row, m in ((Q_BIAS, 0), (V_BIAS, 2)):
            value = total(grad_at(m)[...])
            value = jnp.concatenate([value, value], axis=1)
            put_vector(row, 0, jnp.where((spot < half) == (side == 0), value, 0.0))

    def forward(which):
        @pl.when(is_mid)
        def _():
            slot = targets[which]
            end_copy(which, slot).wait_recv()
            add_into(e_at(slot), e_at(slot), from_end[which])
            out_copy(which, slot).start()

    vec_devices = (to_core, to_x, to_y, to_z1, to_z2)

    def vec_copy(k):
        return remote_copy(vec_out, vec_got.at[k], vsend.at[k], vrecv.at[k], vec_devices[k])

    def vec(k):
        if k > 0:
            vec_copy(k - 1).wait()
            vec_out[...] = vec_out[...] + vec_got[k - 1]
        if k < 5:
            vec_copy(k).start()

    def norm1():
        pair_copy().wait()
        e_v[mine_rows, :] = e_v[mine_rows, :] + from_pair[...].astype(jnp.float32)
        out_copy(0, partner).wait_recv()
        e_v[slot_rows(1 - clip), :] = total_in[...].astype(jnp.float32)

        def body(at, k, _):
            source = jnp.where(clip == k, xall[z], tok[...])
            one, inverse = norm_rows(source.astype(jnp.float32))
            value = mid_v[at, :] + norm_back(e_v[at, :], one, inverse, pack[N1_GAIN : N1_GAIN + 1, :])
            low_d[at, :] = value.astype(low)
            return 0

        chunks(body, 0, NORM_ROWS)
        pltpu.make_async_copy(low_d, grad_tokens, put_sem.at[2]).start()

    singles = dict(
        e3=e3, norm3=norm3, feed=feed, e2=e2, norm2=norm2, back_att=back_att, sums=sums, norm1=norm1
    )
    several = dict(settle=settle, dx=dx, fwd=forward, vec=vec)
    staged(0, align_out).wait()
    staged(1, block_out).wait()

    def run(entries):
        for entry in entries:
            if isinstance(entry, tuple):
                if entry[1] in ("far", "own"):
                    job(entry[0], entry[1] == "own")
                else:
                    stage(*entry)
            elif entry in singles:
                singles[entry]()
            else:
                several[entry[:-1]](int(entry[-1]))

    spots = [k for k, entry in enumerate(PLAN) if entry == "pair"]
    run(PLAN[: spots[0]])

    def pair_and_more(number, _):
        pair(number)
        for k in range(len(spots) - 1):
            if spots[k] + 1 < spots[k + 1]:

                @pl.when(number == k)
                def _():
                    run(PLAN[spots[k] + 1 : spots[k + 1]])

        return 0

    lax.fori_loop(0, len(spots), pair_and_more, 0)
    run(PLAN[spots[-1] + 1 :])
    results_done()
    pltpu.make_async_copy(low_d, grad_tokens, put_sem.at[2]).wait()

    @pl.when(is_mid)
    def _():
        for which in range(2):
            out_copy(which, targets[which]).wait_send()

    @pl.when(is_end)
    def _():
        for which in range(2):
            end_copy(which, targets[which]).wait_send()


def layer(slot_mask, counts, vectors, tok, cot_a, cot_b, w_align, w_down, w_up, w_out, w_qkv):
    _, piece, width = tok.shape
    rows, half, wide, align = 2 * piece, width // 2, w_up.shape[1], w_align.shape[1]
    low, full = jnp.bfloat16, jnp.float32
    vmem = pl.BlockSpec(memory_space=pltpu.VMEM)
    hbm = pl.BlockSpec(memory_space=pl.ANY)
    dma = pltpu.SemaphoreType.DMA
    v = pltpu.VMEM
    shapes = [(2, 4, job[2] // 2, job[4]) for job in JOBS]
    scratch = (
        [v(shape, low) for shape in shapes]
        + [v(shape, low) for shape in shapes]
        + [v((2, 2) + shape[2:], low) for shape in shapes]
        + [v((2,) + shape[2:], low) for shape in shapes]
        + [v((2, 2) + shape[2:], low) for shape in shapes[:PLAIN]]
        + [v((3, 2) + shape[2:], low) for shape in shapes[PLAIN:]]
        + [v((5, PACK_ROWS, width), full)]
        + [v(vector.shape, full) for vector in vectors]
        + [v((PACK_ROWS, width), full), v((4 * piece, 128), full)]
        + [v(w_align.shape, low), v(w_down.shape, low), v(w_up.shape, low), v(w_out.shape, low)]
        + [v((3, width, half), low), v((piece, width), low), v((4, piece, width), low), v((4 * piece, width), low)]
        + [v((3, 4 * piece, half), low), v((3, 4 * piece, 128), low), v((2, 2, 3, piece, 128), low)]
        + [v((8, 4 * piece), full)] * 2
        + [v((rows, width), full), v((rows, width), full), v((rows, width), low), v((8, 48, wide), low)]
        + [v((rows, wide), low), v((2, 4, wide // 8, rows), low)]
        + [v((2, 4, width // 8, rows), low)] * 3
        + [v((rows, width), low)] * 2
        + [v((rows, align), low), v((rows, width), low)]
        + [v((3, 4, piece, 128), low), v((2, 4, width // 8, 4 * piece), low)]
        + [dma((11,))]
        + [dma((COUNT, 2))] * 6
        + [dma((PLAIN, 2, 2))] * 2
        + [dma((3, 3, 2))] * 2
        + [dma((PLAIN, 2)), dma((3, 2, 2))]
        + [dma((5,))] * 2
        + [dma((4, CHUNKS))] * 2
        + [dma((4, 3))] * 4
        + [dma(())] * 2
        + [dma((2,))] * 2
        + [dma((2,)), dma(())]
        + [dma((3,)), dma((12,))]
    )
    struct = jax.ShapeDtypeStruct
    return pl.pallas_call(
        layer_kernel,
        name="layer",
        out_shape=[
            struct((2, 4, 48, width), low),
            struct((2, 4, 48, align), low),
            struct((rows, width), low),
            struct((PACK_ROWS, width), full),
        ]
        + [struct((w.shape[0] // 8, w.shape[1]), low) for w in (w_qkv, w_out, w_up, w_down, w_align)],
        in_specs=[vmem, pl.BlockSpec(memory_space=pltpu.SMEM)] + [hbm] * 20,
        out_specs=[hbm, hbm, hbm, vmem] + [hbm] * 5,
        scratch_shapes=scratch,
        compiler_params=pltpu.CompilerParams(
            collective_id=0, has_side_effects=True, vmem_limit_bytes=63 * 2**20
        ),
    )(slot_mask, counts, *vectors, tok, cot_a, cot_b, w_align, w_down, w_up, w_out, w_qkv)


VECTORS = (
    N1_GAIN, N1_BIAS, Q_BIAS, V_BIAS, OUT_BIAS, N2_GAIN, N2_BIAS, DOWN_BIAS, N3_GAIN, N3_BIAS, UP_BIAS, ALIGN_BIAS,
)


def finish_kernel(*refs):
    shares, pack, through_in = refs[:5], refs[5], refs[6:9]
    wide, vectors, through_out = refs[9:14], refs[14:26], refs[26:29]
    low_v, wide_v, held, pack_v, vectors_v = refs[29:34], refs[34:39], refs[39:42], refs[42], refs[43:55]
    in_sem, out_sem, vector_sem = refs[55:]
    ins = [pltpu.make_async_copy(shares[k], low_v[k], in_sem.at[k]) for k in range(5)]
    outs = [pltpu.make_async_copy(wide_v[k], wide[k], out_sem.at[k]) for k in range(5)]
    through = [
        (
            pltpu.make_async_copy(through_in[k], held[k], in_sem.at[5 + k]),
            pltpu.make_async_copy(held[k], through_out[k], out_sem.at[5 + k]),
        )
        for k in range(3)
    ]
    pack_in = pltpu.make_async_copy(pack, pack_v, in_sem.at[8])
    for copy, _ in through:
        copy.start()
    for copy in [pack_in] + ins:
        copy.start()
    width = pack.shape[1]
    vectors_out = [
        pltpu.make_async_copy(vectors_v[k], vectors[k], vector_sem.at[k]) for k in range(len(vectors))
    ]
    pack_in.wait()
    for row, ref in zip(VECTORS, vectors_v):
        for start in range(0, ref.shape[0], width):
            size = min(width, ref.shape[0] - start)
            line = row + start // width
            ref[pl.ds(start, size)] = pack_v[line : line + 1, 0:size].reshape(size)
    for copy in vectors_out:
        copy.start()
    for first, second in through:
        first.wait()
        second.start()
    for k in range(5):
        ins[k].wait()
        wide_v[k][...] = low_v[k][...].astype(jnp.float32)
        outs[k].start()
    for copy in outs + vectors_out:
        copy.wait()
    for _, copy in through:
        copy.wait()


def finish(shares, pack, through, sizes):
    hbm = pl.BlockSpec(memory_space=pl.ANY)
    struct = jax.ShapeDtypeStruct
    results = pl.pallas_call(
        finish_kernel,
        name="finish",
        out_shape=[struct(share.shape, jnp.float32) for share in shares]
        + [struct((size,), jnp.float32) for size in sizes]
        + [struct(array.shape, array.dtype) for array in through],
        in_specs=[hbm] * 9,
        out_specs=[hbm] * 20,
        scratch_shapes=[pltpu.VMEM(share.shape, share.dtype) for share in shares]
        + [pltpu.VMEM(share.shape, jnp.float32) for share in shares]
        + [pltpu.VMEM(array.shape, array.dtype) for array in through]
        + [pltpu.VMEM(pack.shape, pack.dtype)]
        + [pltpu.VMEM((size,), jnp.float32) for size in sizes]
        + [pltpu.SemaphoreType.DMA((9,)), pltpu.SemaphoreType.DMA((8,)), pltpu.SemaphoreType.DMA((12,))],
        compiler_params=pltpu.CompilerParams(vmem_limit_bytes=62 * 2**20),
    )(*shares, pack, *through)
    return results[:5], results[5:17], results[17:]


def norm_forward(values, gain, shift):
    center = values - jnp.mean(values, axis=-1, keepdims=True)
    inverse = lax.rsqrt(jnp.mean(center * center, axis=-1, keepdims=True) + EPSILON)
    normed = center * inverse
    return (normed * gain + shift, normed, inverse)


def norm_backward(upstream, normed, inverse, gain):
    scaled = upstream * gain
    inner = (
        scaled
        - jnp.mean(scaled, axis=-1, keepdims=True)
        - normed * jnp.mean(scaled * normed, axis=-1, keepdims=True)
    )
    return (inverse * inner, jnp.sum(upstream * normed, axis=0), jnp.sum(upstream, axis=0))


def gelu_slope(values):
    return (
        0.5 * (1.0 + lax.erf(values * SQRT_HALF))
        + values * jnp.exp(-0.5 * values * values) * INV_ROOT_TAU
    )


def weight_grad(left, right):
    return lax.dot_general(
        left, right, (((0,), (0,)), ((), ())), preferred_element_type=jnp.float32
    )


def input_grad(upstream, weight):
    return lax.dot_general(
        upstream, weight, (((1,), (1,)), ((), ())), preferred_element_type=jnp.float32
    )


def masked_scores(query_heads, key_heads, key_valid, scale):
    scores = (
        jnp.einsum("cqhd,ckhd->chqk", query_heads, key_heads, preferred_element_type=jnp.float32)
        * scale
    )
    return jnp.where(key_valid, scores, -1e30)


def column_sum(values):
    return jnp.sum(values, axis=0, dtype=jnp.float32)


def local(
    tokens,
    frame_counts,
    slot_mask,
    norm1_gain,
    norm1_bias,
    w_qkv,
    q_bias,
    v_bias,
    w_out,
    out_bias,
    norm2_gain,
    norm2_bias,
    w_up,
    up_bias,
    w_down,
    down_bias,
    norm3_gain,
    norm3_bias,
    w_align,
    align_bias,
    cot_block,
    cot_align,
):
    clip_count, frame_dev, slot_count, width = tokens.shape
    align_width = w_align.shape[1]
    head_size = width // HEADS
    scale = 1.0 / math.sqrt(head_size)
    row_count = clip_count * frame_dev * slot_count
    cycle_pos = lax.axis_index("blk")
    frame_ids = cycle_pos * frame_dev + jnp.arange(frame_dev, dtype=jnp.int32)
    own_slots = lax.dynamic_slice_in_dim(slot_mask, cycle_pos * frame_dev, frame_dev, 1)
    own_mask = (frame_ids[None, :, None] < frame_counts[:, None, None]) & (own_slots > 0)
    visible = own_mask.astype(jnp.float32).reshape(row_count, 1)
    all_frames = jnp.arange(slot_mask.shape[1], dtype=jnp.int32)
    key_valid = (all_frames[None, :, None] < frame_counts[:, None, None]) & (slot_mask > 0)
    key_valid = key_valid.reshape(clip_count, 1, 1, -1)
    inputs = tokens.reshape(row_count, width).astype(jnp.float32)
    normed_one, unit_one, inverse_one = norm_forward(inputs, norm1_gain, norm1_bias)
    normed1 = normed_one.astype(jnp.bfloat16)
    projected = jnp.dot(normed1, w_qkv, preferred_element_type=jnp.float32)
    queries = (projected[:, :width] + q_bias).astype(jnp.bfloat16)
    keys_local = projected[:, width : 2 * width].astype(jnp.bfloat16)
    values_local = (projected[:, 2 * width :] + v_bias).astype(jnp.bfloat16)
    block_shape = (clip_count, frame_dev, slot_count, width)
    heads_shape = (clip_count, -1, HEADS, head_size)
    keys_all, values_all = (
        lax.all_gather(keys_local.reshape(block_shape), "blk", axis=1, tiled=True),
        lax.all_gather(values_local.reshape(block_shape), "blk", axis=1, tiled=True),
    )
    key_heads = keys_all.reshape(heads_shape)
    value_heads = values_all.reshape(heads_shape)
    query_heads = queries.reshape(heads_shape)
    scores = masked_scores(query_heads, key_heads, key_valid, scale)
    top = jnp.max(scores, axis=-1, keepdims=True)
    expo = jnp.exp(scores - top)
    total = jnp.sum(expo, axis=-1, keepdims=True)
    probs_low = (expo / total).astype(jnp.bfloat16)
    attended = jnp.einsum(
        "chqk,ckhd->cqhd", probs_low, value_heads, preferred_element_type=jnp.float32
    )
    attended = attended.astype(jnp.bfloat16).reshape(row_count, width)
    mid = inputs + jnp.dot(attended, w_out, preferred_element_type=jnp.float32) + out_bias
    normed_two, unit_two, inverse_two = norm_forward(mid, norm2_gain, norm2_bias)
    normed2 = normed_two.astype(jnp.bfloat16)
    hidden = jnp.dot(normed2, w_up, preferred_element_type=jnp.float32) + up_bias
    active = jax.nn.gelu(hidden, approximate=False).astype(jnp.bfloat16)
    after = mid + jnp.dot(active, w_down, preferred_element_type=jnp.float32) + down_bias
    block_out = (visible * after).astype(jnp.bfloat16).reshape(block_shape)
    normed_three, unit_three, inverse_three = norm_forward(after, norm3_gain, norm3_bias)
    normed3 = normed_three.astype(jnp.bfloat16)
    target = jnp.dot(normed3, w_align, preferred_element_type=jnp.float32) + align_bias
    aligned = (
        (visible * target)
        .astype(jnp.bfloat16)
        .reshape(clip_count, frame_dev, slot_count, align_width)
    )
    back_align = (visible * cot_align.reshape(row_count, align_width).astype(jnp.float32)).astype(
        jnp.bfloat16
    )
    grad_align_bias = column_sum(back_align)
    grad_w_align = weight_grad(normed3, back_align)
    back_norm3, grad_norm3_gain, grad_norm3_bias = norm_backward(
        input_grad(back_align, w_align), unit_three, inverse_three, norm3_gain
    )
    back_after = visible * cot_block.reshape(row_count, width).astype(jnp.float32) + back_norm3
    back_down = back_after.astype(jnp.bfloat16)
    grad_down_bias = column_sum(back_down)
    grad_w_down = weight_grad(active, back_down)
    back_up = (input_grad(back_down, w_down) * gelu_slope(hidden)).astype(jnp.bfloat16)
    grad_up_bias = column_sum(back_up)
    grad_w_up = weight_grad(normed2, back_up)
    back_norm2, grad_norm2_gain, grad_norm2_bias = norm_backward(
        input_grad(back_up, w_up), unit_two, inverse_two, norm2_gain
    )
    back_mid = back_after + back_norm2
    back_out = back_mid.astype(jnp.bfloat16)
    grad_out_bias = column_sum(back_out)
    grad_w_out = weight_grad(attended, back_out)
    back_attended = input_grad(back_out, w_out).astype(jnp.bfloat16).reshape(heads_shape)
    scores = masked_scores(query_heads, key_heads, key_valid, scale)
    probs = jnp.exp(scores - top) / total
    probs_low = probs.astype(jnp.bfloat16)
    back_probs = jnp.einsum(
        "cqhd,ckhd->chqk", back_attended, value_heads, preferred_element_type=jnp.float32
    )
    spread = jnp.sum(probs * back_probs, axis=-1, keepdims=True)
    back_scores = (probs * (back_probs - spread)).astype(jnp.bfloat16)
    back_queries = (
        jnp.einsum("chqk,ckhd->cqhd", back_scores, key_heads, preferred_element_type=jnp.float32)
        * scale
    )
    back_queries = back_queries.astype(jnp.bfloat16).reshape(row_count, width)
    value_terms = jnp.einsum(
        "chqk,cqhd->ckhd", probs_low, back_attended, preferred_element_type=jnp.float32
    )
    key_terms = (
        jnp.einsum("chqk,cqhd->ckhd", back_scores, query_heads, preferred_element_type=jnp.float32)
        * scale
    )
    whole_shape = (clip_count, -1, slot_count, width)
    key_share, value_share = (
        lax.psum_scatter(
            key_terms.reshape(whole_shape).astype(jnp.bfloat16),
            "blk",
            scatter_dimension=1,
            tiled=True,
        ).astype(jnp.float32),
        lax.psum_scatter(
            value_terms.reshape(whole_shape).astype(jnp.bfloat16),
            "blk",
            scatter_dimension=1,
            tiled=True,
        ).astype(jnp.float32),
    )
    back_keys = key_share.astype(jnp.bfloat16).reshape(row_count, width)
    back_values = value_share.astype(jnp.bfloat16).reshape(row_count, width)
    grad_q_bias = column_sum(back_queries)
    grad_v_bias = column_sum(back_values)
    combined = jnp.concatenate([back_queries, back_keys, back_values], axis=1)
    grad_w_qkv = weight_grad(normed1, combined)
    back_norm1, grad_norm1_gain, grad_norm1_bias = norm_backward(
        input_grad(combined, w_qkv), unit_one, inverse_one, norm1_gain
    )
    grad_tokens = (back_mid + back_norm1).astype(jnp.bfloat16).reshape(block_shape)
    vector_total = lax.psum(
        (
            grad_norm1_gain,
            grad_norm1_bias,
            grad_q_bias,
            grad_v_bias,
            grad_out_bias,
            grad_norm2_gain,
            grad_norm2_bias,
            grad_up_bias,
            grad_down_bias,
            grad_norm3_gain,
            grad_norm3_bias,
            grad_align_bias,
        ),
        ("dp", "blk"),
    )
    row_part = (
        lax.psum_scatter(grad_w_qkv, "dp", scatter_dimension=0, tiled=True),
        lax.psum_scatter(grad_w_out, "dp", scatter_dimension=0, tiled=True),
        lax.psum_scatter(grad_w_up, "dp", scatter_dimension=0, tiled=True),
        lax.psum_scatter(grad_w_down, "dp", scatter_dimension=0, tiled=True),
        lax.psum_scatter(grad_w_align, "dp", scatter_dimension=0, tiled=True),
    )
    matrix_total = (
        lax.psum(row_part[0].astype(jnp.bfloat16), "blk").astype(jnp.float32),
        lax.psum(row_part[1].astype(jnp.bfloat16), "blk").astype(jnp.float32),
        lax.psum(row_part[2].astype(jnp.bfloat16), "blk").astype(jnp.float32),
        lax.psum(row_part[3].astype(jnp.bfloat16), "blk").astype(jnp.float32),
        lax.psum(row_part[4].astype(jnp.bfloat16), "blk").astype(jnp.float32),
    )
    return (
        block_out,
        aligned,
        grad_tokens,
        vector_total[0],
        vector_total[1],
        matrix_total[0],
        vector_total[2],
        vector_total[3],
        matrix_total[1],
        vector_total[4],
        vector_total[5],
        vector_total[6],
        matrix_total[2],
        vector_total[7],
        matrix_total[3],
        vector_total[8],
        vector_total[9],
        vector_total[10],
        matrix_total[4],
        vector_total[11],
    )


def local_kernels(
    tokens, frame_counts, slot_mask, norm1_gain, norm1_bias, w_qkv, q_bias, v_bias, w_out, out_bias, norm2_gain,
    norm2_bias, w_up, up_bias, w_down, down_bias, norm3_gain, norm3_bias, w_align, align_bias, cot_block, cot_align,
):
    clip_count, frame_dev, slot_count, width = tokens.shape
    align = w_align.shape[1]
    piece = frame_dev * slot_count
    rows = clip_count * piece
    vectors = [
        norm1_gain, norm1_bias, q_bias, v_bias, out_bias, norm2_gain, norm2_bias, down_bias, norm3_gain, norm3_bias,
        up_bias, align_bias,
    ]
    block_out, align_out, grad_tokens, vec, *shares = layer(
        slot_mask, frame_counts, vectors, tokens.reshape(clip_count, piece, width), cot_align.reshape(rows, align),
        cot_block.reshape(rows, width), w_align, w_down, w_up, w_out, w_qkv,
    )
    matrices, totals, (block_out, align_out, grad_tokens) = finish(
        shares, vec, (block_out, align_out, grad_tokens), [vector.shape[0] for vector in vectors]
    )
    (
        grad_norm1_gain, grad_norm1_bias, grad_q_bias, grad_v_bias, grad_out_bias, grad_norm2_gain, grad_norm2_bias,
        grad_down_bias, grad_norm3_gain, grad_norm3_bias, grad_up_bias, grad_align_bias,
    ) = totals
    return (
        block_out.reshape(tokens.shape),
        align_out.reshape(cot_align.shape),
        grad_tokens.reshape(tokens.shape),
        grad_norm1_gain,
        grad_norm1_bias,
        matrices[0],
        grad_q_bias,
        grad_v_bias,
        matrices[1],
        grad_out_bias,
        grad_norm2_gain,
        grad_norm2_bias,
        matrices[2],
        grad_up_bias,
        matrices[3],
        grad_down_bias,
        grad_norm3_gain,
        grad_norm3_bias,
        matrices[4],
        grad_align_bias,
    )


def solution(mesh):
    in_specs = (
        P("dp", "blk", None, None),
        P("dp"),
        P("dp", None, None),
        P(),
        P(),
        P(),
        P(),
        P(),
        P(),
        P(),
        P(),
        P(),
        P(),
        P(),
        P(),
        P(),
        P(),
        P(),
        P(),
        P(),
        P("dp", "blk", None, None),
        P("dp", "blk", None, None),
    )
    out_specs = (
        P("dp", "blk", None, None),
        P("dp", "blk", None, None),
        P("dp", "blk", None, None),
        P(),
        P(),
        P("dp", None),
        P(),
        P(),
        P("dp", None),
        P(),
        P(),
        P(),
        P("dp", None),
        P(),
        P("dp", None),
        P(),
        P(),
        P(),
        P("dp", None),
        P(),
    )
    sizes = (mesh.shape["dp"], mesh.shape["blk"])
    run = local_kernels if sizes == GRID else local
    return jax.shard_map(run, mesh=mesh, in_specs=in_specs, out_specs=out_specs, check_vma=False)
```
